32 devices in a mesh: dp: 8 (over y, x, core), mp: 4 (over z).
Axes of the slice: x: 2, y: 2, z: 4, core: 2. Of those that a mesh axis runs over, the one named last changes fastest.
Arguments:
- language_input: bfloat16 [2080, 768], P(('dp', 'mp')), may hold values from -6 to 6
- vision_input: bfloat16 [3744, 768], P(('dp', 'mp')), may hold values from -6 to 6
- word_lengths: int32 [104], P('dp'), may hold values from 1 to 20, as said below
- region_counts: int32 [104], P('dp'), may hold values from 1 to 36, as said below
- task_flags: int32 [104, 2], P('dp'), may hold values from 0 to 1, as said below
- language_cotangent: bfloat16 [2080, 768], P(('dp', 'mp')), may hold values from -6 to 6
- vision_cotangent: bfloat16 [3744, 768], P(('dp', 'mp')), may hold values from -6 to 6
- projection_weight: bfloat16 [3, 3, 768, 768], P(None, None, 'dp', 'mp'), may hold values from -0.21875 to 0.21875
- query_value_bias: float32 [3, 2, 768], P(None, None, 'mp'), may hold values from -3 to 3
- output_weight: bfloat16 [3, 768, 768], P(None, 'mp', 'dp'), may hold values from -0.4375 to 0.4375
- output_bias: float32 [3, 768], replicated, may hold values from -3 to 3
- expand_weight: bfloat16 [2, 768, 3072], P(None, 'dp', 'mp'), may hold values from -0.21875 to 0.21875
- expand_bias: float32 [2, 3072], P(None, 'mp'), may hold values from -3 to 3
- contract_weight: bfloat16 [2, 3072, 768], P(None, 'mp', 'dp'), may hold values from -0.109375 to 0.109375
- contract_bias: float32 [2, 768], replicated, may hold values from -3 to 3
- norm_gain: float32 [5, 768], replicated, may hold values from 0.1 to 1.9
- norm_bias: float32 [5, 768], replicated, may hold values from -2 to 2
Outputs:
- language_out: bfloat16 [2080, 768], P(('dp', 'mp'))
- vision_out: bfloat16 [3744, 768], P(('dp', 'mp'))
- language_grad: float32 [2080, 768], P(('dp', 'mp'))
- vision_grad: float32 [3744, 768], P(('dp', 'mp'))
- projection_grad: float32 [3, 3, 768, 768], P(None, None, 'dp', 'mp')
- query_value_grad: float32 [3, 2, 768], P(None, None, 'mp')
- output_weight_grad: float32 [3, 768, 768], P(None, 'mp', 'dp')
- output_bias_grad: float32 [3, 768], replicated
- expand_grad: float32 [2, 768, 3072], P(None, 'dp', 'mp')
- expand_bias_grad: float32 [2, 3072], P(None, 'mp')
- contract_grad: float32 [2, 3072, 768], P(None, 'mp', 'dp')
- contract_bias_grad: float32 [2, 768], replicated
- norm_gain_grad: float32 [5, 768], replicated
- norm_bias_grad: float32 [5, 768], replicated
The draws below stay inside these ranges and needn't reach their ends.
Inputs may be any that keep to these rules, and one draw needn't show every extreme that they name: `word_lengths`: some item has all 20 words valid. `region_counts`: some item has all 36 regions valid. `task_flags`: item 0 has both flags set.
All inputs are finite; a program needn't handle non-finite values.
Results may differ from the reference program's by a relative error of at most 0.018.
Values may be sent and summed in bfloat16 or wider, within the bound.
A program may use at most 192 MiB of HBM per device.

```python
import math
import jax
import jax.numpy as jnp
from jax import lax

D = 768
HEADS = 12
FF = 3072
WORDS = 20
REGIONS = 36
ITEMS_DP = 13
ITEMS = 104
LANG_ROWS = 2080
VIS_ROWS = 3744
N_DP = 8


def filled_count(key, most):
    draw_key, pick_key = jax.random.split(key)
    drawn = jax.random.randint(draw_key, (ITEMS,), 1, most + 1, dtype=jnp.int32)
    chosen = jax.random.randint(pick_key, (), 0, ITEMS, dtype=jnp.int32)
    return jnp.where(jnp.arange(ITEMS, dtype=jnp.int32) == chosen, most, drawn).astype(jnp.int32)


def draw_word_lengths(key, part):
    key = jax.random.fold_in(key, 11)
    return filled_count(key, WORDS)


def draw_region_counts(key, part):
    key = jax.random.fold_in(key, 12)
    return filled_count(key, REGIONS)


def draw_task_flags(key, part):
    key = jax.random.fold_in(key, 13)
    position = jnp.arange(ITEMS, dtype=jnp.int32)[:, None]
    level = 2 + 6 * position // ITEMS
    rolled = jax.random.randint(key, (ITEMS, 2), 0, 8, dtype=jnp.int32)
    flags = (rolled < level).astype(jnp.int32)
    return jnp.where(position == 0, 1, flags).astype(jnp.int32)


def shard_levels(rng, extent, shards, smallest, largest):
    loudness, own = 1.0, jax.random.fold_in(rng, 6)
    for dim, parts in shards:
        draws = jnp.exp(jax.random.uniform(jax.random.fold_in(own, dim), (parts,), jnp.float32, smallest / len(shards), largest / len(shards)))
        loudness = loudness * jnp.repeat(draws, extent[dim] // parts).reshape([-1 if axis == dim else 1 for axis in range(len(extent))])
    return loudness


def normal_values(own_key, dims, deviation, most, cuts=(), kind=jnp.bfloat16):
    result = jax.random.normal(own_key, dims, jnp.float32) * deviation
    if len(cuts) > 0:
        result = shard_levels(own_key, dims, cuts, -0.22, 0.18) * result
    return jnp.clip(result, min=-most, max=most).astype(kind)


def setup_inputs(seed: int = 0) -> dict:
    splits = jax.random.split(jax.random.key(seed), 18)
    return {
        "language_input": normal_values(splits[0], (LANG_ROWS, D), 1.0, 6.0, ((0, 32),)),
        "vision_input": normal_values(splits[1], (VIS_ROWS, D), 1.0, 6.0, ((0, 32),)),
        "word_lengths": draw_word_lengths(jax.random.fold_in(splits[17], 71), 0),
        "region_counts": draw_region_counts(jax.random.fold_in(splits[17], 71), 0),
        "task_flags": draw_task_flags(jax.random.fold_in(splits[17], 71), 0),
        "language_cotangent": normal_values(splits[5], (LANG_ROWS, D), 1.0, 6.0, ((0, 32),)),
        "vision_cotangent": normal_values(splits[6], (VIS_ROWS, D), 1.0, 6.0, ((0, 32),)),
        "projection_weight": normal_values(splits[7], (3, 3, D, D), D ** -0.5, 0.21875, ((2, 8), (3, 4))),
        "query_value_bias": normal_values(splits[8], (3, 2, D), 0.5, 3.0, ((2, 4),), jnp.float32),
        "output_weight": normal_values(splits[9], (3, D, D), (D // 4) ** -0.5, 0.4375, ((1, 4), (2, 8))),
        "output_bias": normal_values(splits[10], (3, D), 0.5, 3.0, (), jnp.float32),
        "expand_weight": normal_values(splits[11], (2, D, FF), D ** -0.5, 0.21875, ((1, 8), (2, 4))),
        "expand_bias": normal_values(splits[12], (2, FF), 0.5, 3.0, ((1, 4),), jnp.float32),
        "contract_weight": normal_values(splits[13], (2, FF, D), FF ** -0.5, 0.109375, ((1, 4), (2, 8))),
        "contract_bias": normal_values(splits[14], (2, D), 0.5, 3.0, (), jnp.float32),
        "norm_gain": jnp.clip(1.0 + 0.18 * jax.random.normal(splits[15], (5, D), jnp.float32), 0.1, 1.9),
        "norm_bias": normal_values(splits[16], (5, D), 0.3, 2.0, (), jnp.float32),
    }


@jax.custom_vjp
def low(v):
    return lax.optimization_barrier(v.astype(jnp.bfloat16)).astype(jnp.float32)

@jax.custom_vjp
def low_back(v):
    return v

def low_keep(v):
    return (low(v), None)

def low_pass(kept, grad):
    return (grad,)

def back_keep(v):
    return (v, None)

def back_low(kept, grad):
    return (low(grad),)
low.defvjp(low_keep, low_pass)
low_back.defvjp(back_keep, back_low)
EPSILON = 1e-12
MASKED = -1e+30
HIGHEST = lax.Precision.HIGHEST

def matmul(left, right):
    return jnp.dot(left, right, precision=HIGHEST, preferred_element_type=jnp.float32)

def rounded_both(value):
    return low(low_back(value))

def norm(summed, gain, shift):
    center = summed - lax.optimization_barrier(jnp.mean(summed, -1, keepdims=True))
    return center * lax.rsqrt(lax.optimization_barrier(jnp.mean(center * center, -1, keepdims=True)) + EPSILON) * gain + shift

def split_heads(rows, item_count):
    return rows.reshape(item_count, rows.shape[0] // item_count, HEADS, D // HEADS)

def attention(query_rows, key_rows, valid, projection, query_value, out_weight, item_count):
    query = split_heads(rounded_both(matmul(query_rows, projection[0]) + query_value[0]), item_count)
    keys = split_heads(rounded_both(matmul(key_rows, projection[1])), item_count)
    values = split_heads(rounded_both(matmul(key_rows, projection[2]) + query_value[1]), item_count)
    scores = jnp.einsum('inhd,imhd->ihnm', query, keys, precision=HIGHEST) * (1.0 / math.sqrt(D // HEADS))
    scores = low_back(jnp.where(valid[:, None, None, :], scores, MASKED))
    weights = jax.nn.softmax(scores, axis=-1)
    context = jnp.einsum('ihnm,imhd->inhd', low(weights), values, precision=HIGHEST)
    context = rounded_both(context.reshape(query_rows.shape[0], D))
    return low_back(matmul(context, out_weight))

def feed(rows, expand, expand_bias, contract):
    hidden = low(jax.nn.gelu(low_back(matmul(rows, expand) + expand_bias), approximate=False))
    return low_back(matmul(hidden, contract))

def layer(weights, language, vision, word_valid, region_valid):
    projection, query_value, out_weight, out_bias, expand, expand_bias, contract, contract_bias, gain, shift = weights
    item_count = word_valid.shape[0]
    language_cross = attention(language, vision, region_valid, projection[0], query_value[0], out_weight[0], item_count)
    vision_cross = attention(vision, language, word_valid, projection[0], query_value[0], out_weight[0], item_count)
    language_first = low(norm(language_cross + out_bias[0] + language, gain[0], shift[0]))
    vision_first = low(norm(vision_cross + out_bias[0] + vision, gain[0], shift[0]))
    language_self = attention(language_first, language_first, word_valid, projection[1], query_value[1], out_weight[1], item_count)
    vision_self = attention(vision_first, vision_first, region_valid, projection[2], query_value[2], out_weight[2], item_count)
    language_second = low(norm(language_self + out_bias[1] + language_first, gain[1], shift[1]))
    vision_second = low(norm(vision_self + out_bias[2] + vision_first, gain[2], shift[2]))
    language_out = norm(feed(language_second, expand[0], expand_bias[0], contract[0]) + contract_bias[0] + language_second, gain[3], shift[3])
    vision_out = norm(feed(vision_second, expand[1], expand_bias[1], contract[1]) + contract_bias[1] + vision_second, gain[4], shift[4])
    return (language_out, vision_out)

def reference(language_input, vision_input, word_lengths, region_counts, task_flags, language_cotangent, vision_cotangent, projection_weight, query_value_bias, output_weight, output_bias, expand_weight, expand_bias, contract_weight, contract_bias, norm_gain, norm_bias):
    params = tuple((array.astype(jnp.float32) for array in (projection_weight, query_value_bias, output_weight, output_bias, expand_weight, expand_bias, contract_weight, contract_bias, norm_gain, norm_bias)))
    counts = lax.optimization_barrier(jnp.sum(task_flags, 0)).astype(jnp.float32)
    item_scale = task_flags.astype(jnp.float32) * (ITEMS / counts)
    blocks = (language_input.reshape(N_DP, ITEMS_DP * WORDS, D), vision_input.reshape(N_DP, ITEMS_DP * REGIONS, D), word_lengths.reshape(N_DP, ITEMS_DP), region_counts.reshape(N_DP, ITEMS_DP), language_cotangent.reshape(N_DP, ITEMS_DP * WORDS, D), vision_cotangent.reshape(N_DP, ITEMS_DP * REGIONS, D), item_scale.reshape(N_DP, ITEMS_DP, 2))

    def step(carry, block):
        language, vision, lengths, regions, language_cot, vision_cot, scale = block
        word_valid = jnp.arange(WORDS, dtype=jnp.int32)[None, :] < lengths[:, None]
        region_valid = jnp.arange(REGIONS, dtype=jnp.int32)[None, :] < regions[:, None]

        def forward(weights, language_rows, vision_rows):
            return layer(weights, language_rows, vision_rows, word_valid, region_valid)
        outputs, pull = jax.vjp(forward, params, language.astype(jnp.float32), vision.astype(jnp.float32))
        language_up = language_cot.astype(jnp.float32) * jnp.repeat(scale[:, 0], WORDS, total_repeat_length=ITEMS_DP * WORDS)[:, None]
        vision_up = vision_cot.astype(jnp.float32) * jnp.repeat(scale[:, 1], REGIONS, total_repeat_length=ITEMS_DP * REGIONS)[:, None]
        grads = pull((language_up, vision_up))
        carry = jax.tree.map(jnp.add, carry, grads[0])
        return (carry, (outputs[0].astype(jnp.bfloat16), outputs[1].astype(jnp.bfloat16), grads[1], grads[2]))
    zeros = jax.tree.map(jnp.zeros_like, params)
    totals, stacked = lax.scan(step, zeros, blocks)
    return (stacked[0].reshape(LANG_ROWS, D), stacked[1].reshape(VIS_ROWS, D), stacked[2].reshape(LANG_ROWS, D), stacked[3].reshape(VIS_ROWS, D), totals[0], totals[1], totals[2], totals[3], totals[4], totals[5], totals[6], totals[7], totals[8], totals[9])
```

```python
from functools import partial
import math

import jax
import jax.numpy as jnp
from jax import lax
from jax.experimental import pallas as pl
from jax.experimental.pallas import tpu as pltpu
from jax.sharding import PartitionSpec as P

D = 768
HEADS = 12
WORDS = 20
REGIONS = 36
D_MODEL = D
D_HEAD = D // HEADS

EPSILON = 1e-12
MASKED = -1e30


def layer_norm(summed, gain, shift):
    center = summed - jnp.mean(summed, -1, keepdims=True)
    scaled = lax.rsqrt(jnp.mean(center * center, -1, keepdims=True) + EPSILON)
    normed = center * scaled
    return (normed * gain + shift, normed, scaled)


def norm_back(upstream, normed, scaled, gain):
    through = upstream * gain
    inner = (
        through
        - jnp.mean(through, -1, keepdims=True)
        - normed * jnp.mean(through * normed, -1, keepdims=True)
    )
    return (scaled * inner, jnp.sum(upstream * normed, 0), jnp.sum(upstream, 0))


def split_heads(rows, item_count):
    head_size = D // HEADS
    return rows.reshape(
        item_count, rows.shape[0] // item_count, rows.shape[1] // head_size, head_size
    )


def join_heads(block):
    return block.reshape(block.shape[0] * block.shape[1], block.shape[2] * block.shape[3])


def project(rows, weight, bias, item_count):
    mapped = jnp.einsum("rd,jde->jre", rows, weight, preferred_element_type=jnp.float32)
    query = split_heads((mapped[0] + bias[0]).astype(jnp.bfloat16), item_count)
    keys = split_heads(mapped[1].astype(jnp.bfloat16), item_count)
    values = split_heads((mapped[2] + bias[1]).astype(jnp.bfloat16), item_count)
    return (query, keys, values)


def masked_scores(query, keys, valid):
    scores = jnp.einsum("inhd,imhd->ihnm", query, keys, preferred_element_type=jnp.float32) * (
        1.0 / math.sqrt(D // HEADS)
    )
    return jnp.where(valid[:, None, None, :], scores, MASKED)


def attend(query, keys, values, valid):
    scores = masked_scores(query, keys, valid)
    highest = jnp.max(scores, -1, keepdims=True)
    raised = jnp.exp(scores - highest)
    summed = jnp.sum(raised, -1, keepdims=True)
    context = jnp.einsum(
        "ihnm,imhd->inhd",
        (raised / summed).astype(jnp.bfloat16),
        values,
        preferred_element_type=jnp.float32,
    )
    return (join_heads(context).astype(jnp.bfloat16), highest + jnp.log(summed))


def attend_back(query, keys, values, valid, log_total, context_grad):
    factor = 1.0 / math.sqrt(D // HEADS)
    upstream = context_grad.reshape(query.shape)
    weights = jnp.exp(masked_scores(query, keys, valid) - log_total)
    weight_grad = jnp.einsum(
        "inhd,imhd->ihnm", upstream, values, preferred_element_type=jnp.float32
    )
    score_grad = (
        weights * (weight_grad - jnp.sum(weight_grad * weights, -1, keepdims=True))
    ).astype(jnp.bfloat16)
    query_grad = (
        jnp.einsum("ihnm,imhd->inhd", score_grad, keys, preferred_element_type=jnp.float32) * factor
    ).astype(jnp.bfloat16)
    keys_grad = (
        jnp.einsum("ihnm,inhd->imhd", score_grad, query, preferred_element_type=jnp.float32)
        * factor
    ).astype(jnp.bfloat16)
    values_grad = jnp.einsum(
        "ihnm,inhd->imhd",
        weights.astype(jnp.bfloat16),
        upstream,
        preferred_element_type=jnp.float32,
    ).astype(jnp.bfloat16)
    return (join_heads(query_grad), join_heads(keys_grad), join_heads(values_grad))


def project_back(rows, query_grad, keys_grad, values_grad):
    stacked = jnp.stack([query_grad, keys_grad, values_grad])
    weight_grad = jnp.einsum("rd,jre->jde", rows, stacked, preferred_element_type=jnp.float32)
    bias_grad = jnp.stack(
        [jnp.sum(query_grad.astype(jnp.float32), 0), jnp.sum(values_grad.astype(jnp.float32), 0)]
    )
    return (weight_grad, bias_grad, stacked)


def gather_rows(language_rows, vision_rows):
    return (
        lax.all_gather(language_rows, "mp", axis=0, tiled=True),
        lax.all_gather(vision_rows, "mp", axis=0, tiled=True),
    )


def rows_of(language_part, vision_part):
    return (
        lax.all_to_all(language_part, "mp", split_axis=0, concat_axis=1, tiled=True),
        lax.all_to_all(vision_part, "mp", split_axis=0, concat_axis=1, tiled=True),
    )


def gather_grads(language_rows, vision_rows):
    return (
        lax.all_gather(language_rows, "mp", axis=0, tiled=True),
        lax.all_gather(vision_rows, "mp", axis=0, tiled=True),
    )


def grads_of(language_part, vision_part):
    return (
        lax.all_to_all(language_part, "mp", split_axis=1, concat_axis=2, tiled=True),
        lax.all_to_all(vision_part, "mp", split_axis=1, concat_axis=2, tiled=True),
    )


def matmul(left, right):
    return jnp.dot(left, right, preferred_element_type=jnp.float32)


def on_device(
    language_input,
    vision_input,
    word_lengths,
    region_counts,
    task_flags,
    language_cotangent,
    vision_cotangent,
    projection_weight,
    query_value_bias,
    output_weight,
    output_bias,
    expand_weight,
    expand_bias,
    contract_weight,
    contract_bias,
    norm_gain,
    norm_bias,
):
    item_count = word_lengths.shape[0]
    flag_total = lax.psum(jnp.sum(task_flags, 0), "dp")
    projection, out_weight, expand, contract = (
        lax.all_gather(projection_weight, "dp", axis=2, tiled=True),
        lax.all_gather(output_weight, "dp", axis=2, tiled=True),
        lax.all_gather(expand_weight, "dp", axis=1, tiled=True),
        lax.all_gather(contract_weight, "dp", axis=2, tiled=True),
    )
    projection_full, out_full, expand_full, contract_full = (
        lax.all_gather(projection, "mp", axis=3, tiled=True),
        lax.all_gather(out_weight, "mp", axis=1, tiled=True),
        lax.all_gather(expand, "mp", axis=2, tiled=True),
        lax.all_gather(contract, "mp", axis=1, tiled=True),
    )
    valid = [
        jnp.arange(WORDS, dtype=jnp.int32)[None, :] < word_lengths[:, None],
        jnp.arange(REGIONS, dtype=jnp.int32)[None, :] < region_counts[:, None],
    ]
    row_counts = [WORDS, REGIONS]
    inputs = [language_input.astype(jnp.float32), vision_input.astype(jnp.float32)]
    cross_rows = gather_rows(language_input, vision_input)
    cross_parts = [
        project(cross_rows[stream], projection[0], query_value_bias[0], item_count)
        for stream in range(2)
    ]
    cross_context = []
    cross_total = []
    for stream in range(2):
        other = 1 - stream
        context, log_total = attend(
            cross_parts[stream][0], cross_parts[other][1], cross_parts[other][2], valid[other]
        )
        cross_context.append(context)
        cross_total.append(log_total)
    moved = rows_of(cross_context[0], cross_context[1])
    branch = [matmul(moved[stream], out_full[0]) for stream in range(2)]
    first = [
        layer_norm(branch[stream] + output_bias[0] + inputs[stream], norm_gain[0], norm_bias[0])
        for stream in range(2)
    ]
    first_out = [first[stream][0].astype(jnp.bfloat16) for stream in range(2)]
    self_rows = gather_rows(first_out[0], first_out[1])
    self_parts = [
        project(self_rows[stream], projection[1 + stream], query_value_bias[1 + stream], item_count)
        for stream in range(2)
    ]
    self_context = []
    self_total = []
    for stream in range(2):
        context, log_total = attend(
            self_parts[stream][0], self_parts[stream][1], self_parts[stream][2], valid[stream]
        )
        self_context.append(context)
        self_total.append(log_total)
    moved = rows_of(self_context[0], self_context[1])
    branch = [matmul(moved[stream], out_full[1 + stream]) for stream in range(2)]
    second = [
        layer_norm(
            branch[stream] + output_bias[1 + stream] + first_out[stream].astype(jnp.float32),
            norm_gain[1 + stream],
            norm_bias[1 + stream],
        )
        for stream in range(2)
    ]
    second_out = [second[stream][0].astype(jnp.bfloat16) for stream in range(2)]
    feed_rows = gather_rows(second_out[0], second_out[1])
    before = [
        matmul(feed_rows[stream], expand[stream]) + expand_bias[stream] for stream in range(2)
    ]
    hidden = [
        jax.nn.gelu(before[stream], approximate=False).astype(jnp.bfloat16) for stream in range(2)
    ]
    moved = rows_of(hidden[0], hidden[1])
    branch = [matmul(moved[stream], contract_full[stream]) for stream in range(2)]
    third = [
        layer_norm(
            branch[stream] + contract_bias[stream] + second_out[stream].astype(jnp.float32),
            norm_gain[3 + stream],
            norm_bias[3 + stream],
        )
        for stream in range(2)
    ]
    language_out = third[0][0].astype(jnp.bfloat16)
    vision_out = third[1][0].astype(jnp.bfloat16)
    item_scale = task_flags.astype(jnp.float32) * (
        item_count * lax.axis_size("dp") / flag_total.astype(jnp.float32)
    )
    shard_index = lax.axis_index("mp")
    upstream = []
    for stream, cotangent in enumerate([language_cotangent, vision_cotangent]):
        per_row = jnp.repeat(
            item_scale[:, stream],
            row_counts[stream],
            total_repeat_length=item_count * row_counts[stream],
        )
        shard_rows = cotangent.shape[0]
        row_scale = lax.dynamic_slice_in_dim(per_row, shard_index * shard_rows, shard_rows)
        upstream.append(cotangent.astype(jnp.float32) * row_scale[:, None])
    third_back = [
        norm_back(upstream[stream], third[stream][1], third[stream][2], norm_gain[3 + stream])
        for stream in range(2)
    ]
    sent = gather_grads(
        third_back[0][0].astype(jnp.bfloat16), third_back[1][0].astype(jnp.bfloat16)
    )
    expand_local = []
    expand_bias_local = []
    contract_local = []
    before_grads = []
    for stream in range(2):
        hidden_grad = jnp.einsum(
            "rd,fd->rf", sent[stream], contract[stream], preferred_element_type=jnp.float32
        )
        contract_local.append(
            jnp.einsum(
                "rf,rd->fd", hidden[stream], sent[stream], preferred_element_type=jnp.float32
            )
        )
        unused, pull = jax.vjp(partial(jax.nn.gelu, approximate=False), before[stream])
        before_grad = pull(hidden_grad)[0].astype(jnp.bfloat16)
        expand_local.append(
            jnp.einsum(
                "rd,rf->df", feed_rows[stream], before_grad, preferred_element_type=jnp.float32
            )
        )
        expand_bias_local.append(jnp.sum(before_grad.astype(jnp.float32), 0))
        before_grads.append(before_grad[None])
    moved = grads_of(before_grads[0], before_grads[1])
    back = [
        jnp.einsum(
            "rf,df->rd", moved[stream][0], expand_full[stream], preferred_element_type=jnp.float32
        )
        for stream in range(2)
    ]
    second_grad = [third_back[stream][0] + back[stream] for stream in range(2)]
    second_back = [
        norm_back(second_grad[stream], second[stream][1], second[stream][2], norm_gain[1 + stream])
        for stream in range(2)
    ]
    sent = gather_grads(
        second_back[0][0].astype(jnp.bfloat16), second_back[1][0].astype(jnp.bfloat16)
    )
    self_weight = []
    self_bias = []
    self_out = []
    stacks = []
    for stream in range(2):
        context_grad = jnp.einsum(
            "rd,ed->re", sent[stream], out_weight[1 + stream], preferred_element_type=jnp.float32
        ).astype(jnp.bfloat16)
        self_out.append(
            jnp.einsum(
                "re,rd->ed", self_context[stream], sent[stream], preferred_element_type=jnp.float32
            )
        )
        grads = attend_back(
            self_parts[stream][0],
            self_parts[stream][1],
            self_parts[stream][2],
            valid[stream],
            self_total[stream],
            context_grad,
        )
        weight_part, bias_part, stacked = project_back(
            self_rows[stream], grads[0], grads[1], grads[2]
        )
        self_weight.append(weight_part)
        self_bias.append(bias_part)
        stacks.append(stacked)
    moved = grads_of(stacks[0], stacks[1])
    back = [
        jnp.einsum(
            "jre,jde->rd",
            moved[stream],
            projection_full[1 + stream],
            preferred_element_type=jnp.float32,
        )
        for stream in range(2)
    ]
    first_grad = [second_back[stream][0] + back[stream] for stream in range(2)]
    first_back = [
        norm_back(first_grad[stream], first[stream][1], first[stream][2], norm_gain[0])
        for stream in range(2)
    ]
    sent = gather_grads(
        first_back[0][0].astype(jnp.bfloat16), first_back[1][0].astype(jnp.bfloat16)
    )
    cross_out = jnp.einsum(
        "re,rd->ed", cross_context[0], sent[0], preferred_element_type=jnp.float32
    ) + jnp.einsum("re,rd->ed", cross_context[1], sent[1], preferred_element_type=jnp.float32)
    triples = [[None, None, None], [None, None, None]]
    for stream in range(2):
        other = 1 - stream
        context_grad = jnp.einsum(
            "rd,ed->re", sent[stream], out_weight[0], preferred_element_type=jnp.float32
        ).astype(jnp.bfloat16)
        grads = attend_back(
            cross_parts[stream][0],
            cross_parts[other][1],
            cross_parts[other][2],
            valid[other],
            cross_total[stream],
            context_grad,
        )
        triples[stream][0] = grads[0]
        triples[other][1] = grads[1]
        triples[other][2] = grads[2]
    results = [
        project_back(cross_rows[stream], triples[stream][0], triples[stream][1], triples[stream][2])
        for stream in range(2)
    ]
    cross_weight = results[0][0] + results[1][0]
    cross_bias = results[0][1] + results[1][1]
    moved = grads_of(results[0][2], results[1][2])
    back = [
        jnp.einsum(
            "jre,jde->rd", moved[stream], projection_full[0], preferred_element_type=jnp.float32
        )
        for stream in range(2)
    ]
    language_grad = first_back[0][0] + back[0]
    vision_grad = first_back[1][0] + back[1]
    projection_stack = jnp.stack([cross_weight, self_weight[0], self_weight[1]])
    output_stack = jnp.stack([cross_out, self_out[0], self_out[1]])
    projection_grad, output_weight_grad, expand_grad, contract_grad = (
        lax.psum_scatter(projection_stack, "dp", scatter_dimension=2, tiled=True),
        lax.psum_scatter(output_stack, "dp", scatter_dimension=2, tiled=True),
        lax.psum_scatter(jnp.stack(expand_local), "dp", scatter_dimension=1, tiled=True),
        lax.psum_scatter(jnp.stack(contract_local), "dp", scatter_dimension=2, tiled=True),
    )
    query_value_grad, expand_bias_grad = lax.psum(
        (jnp.stack([cross_bias, self_bias[0], self_bias[1]]), jnp.stack(expand_bias_local)), "dp"
    )
    output_bias_local = jnp.stack(
        [
            jnp.sum(first_back[0][0], 0) + jnp.sum(first_back[1][0], 0),
            jnp.sum(second_back[0][0], 0),
            jnp.sum(second_back[1][0], 0),
        ]
    )
    contract_bias_local = jnp.stack([jnp.sum(third_back[0][0], 0), jnp.sum(third_back[1][0], 0)])
    gain_local = jnp.stack(
        [
            first_back[0][1] + first_back[1][1],
            second_back[0][1],
            second_back[1][1],
            third_back[0][1],
            third_back[1][1],
        ]
    )
    shift_local = jnp.stack(
        [
            first_back[0][2] + first_back[1][2],
            second_back[0][2],
            second_back[1][2],
            third_back[0][2],
            third_back[1][2],
        ]
    )
    output_bias_grad, contract_bias_grad, norm_gain_grad, norm_bias_grad = lax.psum(
        (output_bias_local, contract_bias_local, gain_local, shift_local), ("dp", "mp")
    )
    return (
        language_out,
        vision_out,
        language_grad,
        vision_grad,
        projection_grad,
        query_value_grad,
        output_weight_grad,
        output_bias_grad,
        expand_grad,
        expand_bias_grad,
        contract_grad,
        contract_bias_grad,
        norm_gain_grad,
        norm_bias_grad,
    )


MESH = pl.DeviceIdType.MESH
BF = jnp.bfloat16
F32 = jnp.float32
SLOTS = 4
RL = SLOTS * WORDS
RV = SLOTS * REGIONS
ROWS = RL + RV
SHARE = 96
HALF_PAIR = 2 * SHARE
LANG_HEAD = 16
VIS_HEAD = 32
LANG_TAIL = 32
VIS_TAIL = 64
N_AR = 48
NT = 3
TILE = 256
VMEM_LIMIT = 63 * 1024 * 1024


def dot_nn(left, right):
    return lax.dot_general(left, right, (((1,), (0,)), ((), ())), preferred_element_type=F32)


def dot_nt(left, right):
    return lax.dot_general(left, right, (((1,), (1,)), ((), ())), preferred_element_type=F32)


def dot_tn(left, right):
    return lax.dot_general(left, right, (((0,), (0,)), ((), ())), preferred_element_type=F32)


def head_mask(first_lane, dtype):
    lane = lax.broadcasted_iota(jnp.int32, (1, TILE), 1) - first_lane
    return [
        jnp.where((lane >= 64 * h) & (lane < 64 * h + 64), 1.0, 0.0).astype(dtype) for h in range(3)
    ]


def select_rows(shape, shift, low, high):
    row = lax.broadcasted_iota(jnp.int32, shape, 0)
    column = lax.broadcasted_iota(jnp.int32, shape, 1)
    return jnp.where((column - row == shift) & (row >= low) & (row < high), 1.0, 0.0)


def layer_kernel(
    total_items,
    lang,
    vis,
    lcot,
    vcot,
    share,
    colid,
    rowflag,
    cnt,
    qbias,
    vecs,
    lang_out,
    vis_out,
    lang_grad,
    vis_grad,
    wgrad,
    vec_out,
    qb_out,
    W,
    G,
    R1,
    R2,
    A,
    KV,
    RSB,
    STG,
    QVK,
    D,
    C,
    H,
    GP,
    PCL,
    PCV,
    PSL,
    PSV,
    PART,
    PZ,
    NORM,
    RSTD,
    DZ,
    COT,
    QB,
    QR,
    CA,
    CR,
    VG,
    QG,
    AVA,
    AVR,
    HL,
    HV,
    OUTS,
    TLO,
    TVO,
    TLG,
    TVG,
    ssem,
    rsem,
    wsem,
    wsem_z,
    gsem,
    gsem2,
    lsem,
):
    d = lax.axis_index("dp")
    z = lax.axis_index("mp")
    c = d % 2
    k = d // 2
    k_flip = [k + 1 - 2 * (k % 2), (k + 2) % 4, 3 - k]
    sib = (d + 1 - 2 * c, z)
    zp = (d, z + 1 - 2 * (z % 2))
    z2 = (z + 2) % 4
    up = (d, (z + 1) % 4)
    down = (d, (z + 3) % 4)
    plane = [(2 * kf + c, z) for kf in k_flip]
    far = (2 * k + 1, z2)

    pending = []
    counter = [0, 0]

    def remote(src, dst, send, recv, device):
        return pltpu.make_async_remote_copy(
            src_ref=src, dst_ref=dst, send_sem=send, recv_sem=recv, device_id=device, device_id_type=MESH
        )

    def send(src, dst, device, recv=None, keep=True):
        slot = counter[0]
        counter[0] += 1
        if recv is None:
            recv = rsem.at[counter[1]]
            counter[1] += 1
        copy = remote(src, dst, ssem.at[slot], recv, device)
        copy.start()
        if keep:
            pending.append(copy)
        return copy

    def wait_bytes(ref, sem):
        pltpu.make_async_copy(ref, ref, sem).wait()

    barrier = pltpu.get_barrier_semaphore()
    peers = [sib, up, down, (d, z2), (d + 1 - 2 * c, z2)] + plane
    for peer in peers:
        pl.semaphore_signal(barrier, inc=1, device_id=peer, device_id_type=MESH)
    pl.semaphore_wait(barrier, len(peers))

    def weight_first(w):
        row = pl.ds(pl.multiple_of(d * SHARE, 16), SHARE)
        slot = counter[0]
        counter[0] += 1
        near = remote(share.at[w], W.at[w, row], ssem.at[slot], wsem_z.at[w], sib)
        own = pltpu.make_async_copy(share.at[w], W.at[w, row], wsem_z.at[w])

        @pl.when(c == 1)
        def _():
            near.start()

        @pl.when(c == 0)
        def _():
            own.start()

        send(share.at[w], W.at[w, row], far, wsem_z.at[w])
        return near

    nears = []
    heads = [
        send(lang.at[pl.ds(0, LANG_HEAD)], HL.at[0], down),
        send(vis.at[pl.ds(0, VIS_HEAD)], HV.at[0], down),
        send(lcot.at[pl.ds(0, LANG_HEAD)], HL.at[1], down),
        send(vcot.at[pl.ds(0, VIS_HEAD)], HV.at[1], down),
    ]
    nears.append(weight_first(0))
    KV[0] = colid[...]
    kv_sib = send(KV.at[0], KV.at[1], sib)
    kv_zp = send(KV.at[0], KV.at[2], zp)
    bias_swap = send(qbias, QR, (d, z2))
    CA[0] = cnt[...]
    count_copies = [send(CA.at[0], CR.at[0], sib)]
    for w in range(1, 7):
        nears.append(weight_first(w))

    pair_rows = pl.ds(pl.multiple_of(k * HALF_PAIR, 16), HALF_PAIR)

    def weight_second(w):
        wait_bytes(W.at[w, pair_rows], wsem_z.at[w])
        for peer in plane:
            send(W.at[w, pair_rows], W.at[w, pair_rows], peer, wsem.at[w])

    def weight_ready(w):
        wait_bytes(W.at[w, pl.ds(0, 3 * HALF_PAIR)], wsem.at[w])

    off_l = jnp.where(z == 0, 0, 20 - 5 * z)
    off_v = jnp.where(z == 0, 0, 36 - 9 * z)
    n_l = jnp.where(z == 0, 4 * WORDS, 3 * WORDS)
    n_v = jnp.where(z == 0, 4 * REGIONS, 3 * REGIONS)
    own_l = lang.shape[0]
    own_v = vis.shape[0]
    for copy in heads:
        copy.wait_recv()
    for index, (source_l, source_v) in enumerate([(lang, vis), (lcot, vcot)]):
        slab_l = dot_nn(select_rows((RL, own_l), off_l, 0, n_l).astype(BF), source_l[...]) + dot_nn(
            select_rows((RL, LANG_HEAD), off_l - own_l, 0, n_l).astype(BF), HL[index]
        )
        slab_v = dot_nn(select_rows((RV, own_v), off_v, 0, n_v).astype(BF), source_v[...]) + dot_nn(
            select_rows((RV, VIS_HEAD), off_v - own_v, 0, n_v).astype(BF), HV[index]
        )
        if index == 0:
            A[0, 0, 0:RL] = slab_l.astype(BF)
            A[0, 0, RL:ROWS] = slab_v.astype(BF)
        else:
            COT[0:RL] = slab_l.astype(BF)
            COT[RL:ROWS] = slab_v.astype(BF)

    def gather_start(p):
        return (send(A.at[p, 0], A.at[p, 1], sib), send(A.at[p, 0], A.at[p, 2], zp))

    def gather_forward(p, copies):
        copies[1].wait_recv()
        return send(A.at[p, 2], A.at[p, 3], sib)

    stage_used = [None, None, None]

    def stage_free(index):
        if stage_used[index] is not None:
            stage_used[index].wait_send()
            stage_used[index] = None

    def partial_nt(g, lhs_ref, r0, r1, w, lanes):
        rows = r1 - r0

        def body(n, carry):
            column = pl.ds(pl.multiple_of(n * TILE, TILE), TILE)
            lhs = lhs_ref[2 * g : 2 * g + 2, r0:r1, :]
            lhs = lhs.reshape(2 * rows, lhs.shape[-1])
            out = dot_nt(lhs, W[w, column, lanes])
            if g == 0:
                PART[r0:r1, column] = out[:rows]
                STG[0, r0:r1, column] = out[rows:].astype(BF)
            else:
                PZ[r0:r1, column] = out[:rows]
                STG[1, r0:r1, column] = out[rows:].astype(BF)
            return carry

        lax.fori_loop(0, NT, body, 0)

    def reduce_first():
        copy = send(STG.at[0], RSB.at[0], sib, keep=False)
        stage_used[0] = copy
        return copy

    def reduce_second():
        across = send(STG.at[1], RSB.at[1], sib, keep=False)
        stage_used[1] = across
        across.wait_recv()
        stage_free(2)
        STG[2] = (PZ[...] + RSB[1].astype(F32)).astype(BF)
        copy = send(STG.at[2], RSB.at[2], zp, keep=False)
        stage_used[2] = copy
        return copy

    def reduced(r0, r1):
        return PART[r0:r1] + RSB[0, r0:r1].astype(F32) + RSB[2, r0:r1].astype(F32)

    mask_q = head_mask(0, BF)
    mask_c = head_mask(64, BF)
    mask_q32 = head_mask(0, F32)
    mask_c32 = head_mask(64, F32)
    factor = 1.0 / math.sqrt(D_HEAD)

    def attend_slab(QV, Cb, PL, PV, crossed, s):
        def one(q0, q1, k0, k1, words_keys, P):
            nq, nk = q1 - q0, k1 - k0
            query = QV[s, q0:q1, 0:256]
            keys = QV[s, k0:k1, 384:640]
            values = QV[s, k0:k1, 128:384]
            query_size = WORDS if q0 == 0 else REGIONS
            spread = jnp.concatenate([query * mask_q[h] for h in range(3)], 0)
            scores = dot_nt(spread, keys) * factor
            row = lax.broadcasted_iota(jnp.int32, (nq, nk), 0)
            item = jnp.zeros((nq, nk), F32)
            for j in range(1, SLOTS):
                item = item + jnp.where(row >= j * query_size, 1.0, 0.0)
            column = KV[s, 0:1, 0:nk] if words_keys else KV[s, 1:2, 0:nk]
            same = item == column
            scores = jnp.where(same[None], scores.reshape(3, nq, nk), MASKED)
            raised = jnp.exp(scores - jnp.max(scores, -1, keepdims=True))
            weights = (raised / jnp.sum(raised, -1, keepdims=True)).astype(BF).reshape(3 * nq, nk)
            P[s] = weights
            context = dot_nn(weights, values).reshape(3, nq, TILE)
            Cb[s, q0:q1] = (
                context[0] * mask_c32[0] + context[1] * mask_c32[1] + context[2] * mask_c32[2]
            ).astype(BF)

        if crossed:
            one(0, RL, RL, ROWS, False, PL)
            one(RL, ROWS, 0, RL, True, PV)
        else:
            one(0, RL, 0, RL, True, PL)
            one(RL, ROWS, RL, ROWS, False, PV)

    def attend_back_slab(QV, Cb, PL, PV, crossed, s):
        def one(q0, q1, k0, k1, P):
            nq, nk = q1 - q0, k1 - k0
            query = QV[s, q0:q1, 0:256]
            keys = QV[s, k0:k1, 384:640]
            values = QV[s, k0:k1, 128:384]
            spread = jnp.concatenate([query * mask_q[h] for h in range(3)], 0)
            upstream = D[s, q0:q1, 512:768]
            up_spread = jnp.concatenate([upstream * mask_c[h] for h in range(3)], 0)
            weights = P[s]
            weights32 = weights.astype(F32)
            weight_grad = dot_nt(up_spread, values)
            score_grad = (
                weights32
                * (weight_grad - jnp.sum(weight_grad * weights32, -1, keepdims=True))
            ).astype(BF)
            dq = dot_nn(score_grad, keys).reshape(3, nq, TILE)
            dq = (dq[0] * mask_q32[0] + dq[1] * mask_q32[1] + dq[2] * mask_q32[2]) * factor
            dk = dot_tn(score_grad, spread) * factor
            dv = dot_tn(weights, up_spread)
            return dq, dk, dv

        if crossed:
            dq_l, dk_v, dv_v = one(0, RL, RL, ROWS, PL)
            dq_v, dk_l, dv_l = one(RL, ROWS, 0, RL, PV)
        else:
            dq_l, dk_l, dv_l = one(0, RL, 0, RL, PL)
            dq_v, dk_v, dv_v = one(RL, ROWS, RL, ROWS, PV)
        for r0, r1, dq, dk, dv in ((0, RL, dq_l, dk_l, dv_l), (RL, ROWS, dq_v, dk_v, dv_v)):
            D[s, r0:r1, 0:128] = dq[:, :128].astype(BF)
            D[s, r0:r1, 128:256] = (dq[:, 128:] + dv[:, :128]).astype(BF)
            D[s, r0:r1, 256:384] = dv[:, 128:].astype(BF)
            D[s, r0:r1, 384:640] = dk.astype(BF)
            D[s, r0:r1, 640:768] = jnp.zeros((r1 - r0, 128), BF)

    def grouped(g, body):
        lax.fori_loop(2 * g, 2 * g + 2, lambda s, carry: (body(s), carry)[1], 0)

    def over_tiles(body):
        def step(n, carry):
            body(pl.ds(pl.multiple_of(n * TILE, TILE), TILE))
            return carry

        lax.fori_loop(0, NT, step, 0)

    def forward_norm(value, index, gain_row, r0, r1):
        center = value - jnp.mean(value, -1, keepdims=True)
        scaled = lax.rsqrt(jnp.mean(center * center, -1, keepdims=True) + EPSILON)
        normed = center * scaled
        NORM[index, r0:r1] = normed
        RSTD[index, r0:r1] = scaled
        return normed * vecs[5 + gain_row : 6 + gain_row] + vecs[10 + gain_row : 11 + gain_row]

    def backward_norm(upstream, index, gain_row, bias_row, r0, r1):
        normed = NORM[index, r0:r1]
        through = upstream * vecs[5 + gain_row : 6 + gain_row]
        inner = (
            through
            - jnp.mean(through, -1, keepdims=True)
            - normed * jnp.mean(through * normed, -1, keepdims=True)
        )
        result = RSTD[index, r0:r1] * inner
        VG[5 + gain_row : 6 + gain_row] += jnp.sum(upstream * normed, 0, keepdims=True)
        VG[10 + gain_row : 11 + gain_row] += jnp.sum(upstream, 0, keepdims=True)
        VG[bias_row : bias_row + 1] += jnp.sum(result, 0, keepdims=True)
        return result

    both = ((0, RL), (RL, ROWS))
    all_rows = ((0, ROWS),)

    def rows_of_group(p, g, r0, r1):
        return A[p, 2 * g : 2 * g + 2, r0:r1, :].reshape(2 * (r1 - r0), D_MODEL)

    def attention_forward(p, streams, QV, Cb, PL, PV, crossed, ready, between):
        copies = gather_start(p)
        ready()
        for g in range(2):
            if g == 0:
                copies[0].wait_recv()
            else:
                forward.wait_recv()
            for r0, r1, w in streams:
                rows = r1 - r0

                def project_tile(column, r0=r0, r1=r1, w=w, rows=rows):
                    mapped = dot_nn(rows_of_group(p, g, r0, r1), W[w, :, column]) + QB[w : w + 1, column]
                    QV[2 * g : 2 * g + 2, r0:r1, column] = mapped.astype(BF).reshape(2, rows, TILE)

                over_tiles(project_tile)
            if g == 0:
                forward = gather_forward(p, copies)
            grouped(g, lambda s: attend_slab(QV, Cb, PL, PV, crossed, s))
            stage_free(g)
            for r0, r1, w in streams:
                partial_nt(g, Cb, r0, r1, w, slice(512, 768))
            if g == 0:
                first = reduce_first()
                between()
            else:
                second = reduce_second()
        first.wait_recv()
        second.wait_recv()

    VG[...] = jnp.zeros_like(VG)
    QG[...] = jnp.zeros_like(QG)

    def ready_cross():
        weight_second(0)
        kv_sib.wait_recv()
        kv_zp.wait_recv()
        kv_far = send(KV.at[2], KV.at[3], sib)
        bias_swap.wait_recv()
        QB[...] = jnp.where(c == 1, QR[...], qbias[...])
        weight_ready(0)
        kv_far.wait_recv()

    def between_cross():
        weight_second(1)
        weight_second(2)
        count_copies[0].wait_recv()
        CA[1] = CA[0] + CR[0]
        count_copies.append(send(CA.at[1], CR.at[1], plane[0]))

    attention_forward(
        0, ((0, ROWS, 0),), QVK.at[0], C.at[0], PCL, PCV, True, ready_cross, between_cross
    )
    for r0, r1 in both:
        value = reduced(r0, r1) + vecs[0:1] + A[0, 0, r0:r1].astype(F32)
        A[1, 0, r0:r1] = forward_norm(value, 0, 0, r0, r1).astype(BF)

    def ready_self():
        weight_ready(1)
        weight_ready(2)

    def between_self():
        weight_second(3)
        weight_second(4)
        count_copies[1].wait_recv()
        CA[2] = CA[1] + CR[1]
        count_copies.append(send(CA.at[2], CR.at[2], plane[1]))

    attention_forward(
        1, ((0, RL, 1), (RL, ROWS, 2)), QVK.at[1], C.at[1], PSL, PSV, False, ready_self, between_self
    )
    for stream, (r0, r1) in enumerate(both):
        value = reduced(r0, r1) + vecs[1 + stream : 2 + stream] + A[1, 0, r0:r1].astype(F32)
        A[2, 0, r0:r1] = forward_norm(value, 1, 1 + stream, r0, r1).astype(BF)

    copies = gather_start(2)
    for g in range(2):
        if g == 0:
            copies[0].wait_recv()
            weight_ready(3)
            weight_ready(4)
        else:
            forward.wait_recv()
        for stream, (r0, r1) in enumerate(both):
            rows = r1 - r0

            def expand_tile(column, r0=r0, r1=r1, stream=stream, rows=rows):
                before = (
                    dot_nn(rows_of_group(2, g, r0, r1), W[3 + stream, :, column])
                    + QB[3 + stream : 4 + stream, column]
                )
                half = 0.5 * (1.0 + lax.erf(before * math.sqrt(0.5)))
                slope = half + before * jnp.exp(-0.5 * before * before) * (
                    1.0 / math.sqrt(2.0 * math.pi)
                )
                H[2 * g : 2 * g + 2, r0:r1, column] = (before * half).astype(BF).reshape(2, rows, TILE)
                GP[2 * g : 2 * g + 2, r0:r1, column] = slope.astype(BF).reshape(2, rows, TILE)

            over_tiles(expand_tile)
        if g == 0:
            forward = gather_forward(2, copies)
            weight_second(5)
            weight_second(6)
            weight_ready(5)
            weight_ready(6)
        stage_free(g)
        for stream, (r0, r1) in enumerate(both):
            partial_nt(g, H, r0, r1, 5 + stream, slice(0, 768))
        if g == 0:
            first = reduce_first()
            count_copies[2].wait_recv()
            CA[3] = CA[2] + CR[2]
        else:
            second = reduce_second()
    first.wait_recv()
    second.wait_recv()

    for stream, (r0, r1) in enumerate(both):
        value = reduced(r0, r1) + vecs[3 + stream : 4 + stream] + A[2, 0, r0:r1].astype(F32)
        OUTS[r0:r1] = forward_norm(value, 2, 3 + stream, r0, r1).astype(BF)
        scale = total_items / CA[3, stream : stream + 1, 0:1]
        upstream = COT[r0:r1].astype(F32) * (rowflag[r0:r1] * scale)
        result = backward_norm(upstream, 2, 3 + stream, 3 + stream, r0, r1)
        DZ[r0:r1] = result
        A[3, 0, r0:r1] = result.astype(BF)
    copies = gather_start(3)
    tail_out = [
        send(OUTS.at[pl.ds(RL - LANG_TAIL, LANG_TAIL)], TLO, up),
        send(OUTS.at[pl.ds(ROWS - VIS_TAIL, VIS_TAIL)], TVO, up),
    ]

    def weight_grad(w, lhs_p, rhs_ref, r0, r1, rhs_lanes=slice(0, 768)):
        rows = SLOTS * (r1 - r0)

        def step(m, carry):
            column = pl.ds(pl.multiple_of(m * TILE, TILE), TILE)
            left = A[lhs_p, :, r0:r1, column].reshape(rows, TILE)
            right = rhs_ref[:, r0:r1, rhs_lanes]
            right = right.reshape(rows, right.shape[-1])
            G[w, column, rhs_lanes] = dot_tn(left, right).astype(BF)
            return carry

        lax.fori_loop(0, NT, step, 0)

    def attention_weight_grad(w, x_p, b_p, Cb, r0, r1):
        weight_grad(w, x_p, D, r0, r1, slice(0, 512))
        rows = SLOTS * (r1 - r0)

        def step(m, carry):
            column = pl.ds(pl.multiple_of(m * TILE, TILE), TILE)
            left = A[x_p, :, r0:r1, column].reshape(rows, TILE)
            right = D[:, r0:r1, 512:768].reshape(rows, TILE)
            left_b = A[b_p, :, r0:r1, column].reshape(rows, TILE)
            right_b = Cb[:, r0:r1, :].reshape(rows, TILE)
            G[w, column, 512:768] = (dot_tn(left, right) + dot_tn(left_b, right_b)).astype(BF)
            return carry

        lax.fori_loop(0, NT, step, 0)

    def bias_grad(row, r0, r1):
        total = jnp.zeros((1, D_MODEL), F32)
        for s in range(SLOTS):
            total = total + jnp.sum(D[s, r0:r1].astype(F32), 0, keepdims=True)
        QG[row : row + 1] = total

    def grad_first(w):
        for j in range(3):
            rows = pl.ds(pl.multiple_of(k_flip[j] * HALF_PAIR, 16), HALF_PAIR)
            send(G.at[w, rows], R1.at[j, w], plane[j], gsem.at[w])

    grad_nears = []

    def grad_second(w):
        wait_bytes(R1.at[:, w], gsem.at[w])
        total = G[w, pair_rows].astype(F32)
        for j in range(3):
            total = total + R1[j, w].astype(F32)
        G[w, pair_rows] = total.astype(BF)
        low = pl.ds(pl.multiple_of(k * HALF_PAIR, 16), SHARE)
        high = pl.ds(pl.multiple_of(k * HALF_PAIR + SHARE, 16), SHARE)
        slot = counter[0]
        counter[0] += 2
        own = pltpu.make_async_copy(G.at[w, low], R2.at[0, w], gsem2.at[w])
        near = remote(G.at[w, high], R2.at[0, w], ssem.at[slot], gsem2.at[w], sib)
        far_low = remote(G.at[w, low], R2.at[1, w], ssem.at[slot], gsem2.at[w], (2 * k, z2))
        far_high = remote(G.at[w, high], R2.at[1, w], ssem.at[slot + 1], gsem2.at[w], (2 * k + 1, z2))

        @pl.when(c == 0)
        def _():
            own.start()
            near.start()

        @pl.when(c == 1)
        def _():
            far_low.start()
            far_high.start()

        grad_nears.append((near, far_low, far_high))

    def grad_last(w):
        wait_bytes(R2.at[:, w], gsem2.at[w])
        wgrad[w] = R2[0, w].astype(F32) + R2[1, w].astype(F32)

    for g in range(2):
        if g == 0:
            copies[0].wait_recv()
        else:
            forward.wait_recv()
        for stream, (r0, r1) in enumerate(both):
            rows = r1 - r0

            def hidden_tile(column, r0=r0, r1=r1, stream=stream, rows=rows):
                up_hidden = dot_nn(rows_of_group(3, g, r0, r1), W[5 + stream, :, column])
                slope = GP[2 * g : 2 * g + 2, r0:r1, column].reshape(2 * rows, TILE)
                D[2 * g : 2 * g + 2, r0:r1, column] = (
                    (up_hidden * slope.astype(F32)).astype(BF).reshape(2, rows, TILE)
                )

            over_tiles(hidden_tile)
        if g == 0:
            forward = gather_forward(3, copies)
        stage_free(g)
        for stream, (r0, r1) in enumerate(both):
            partial_nt(g, D, r0, r1, 3 + stream, slice(0, 768))
        if g == 0:
            first = reduce_first()
        else:
            second = reduce_second()
    for stream, (r0, r1) in enumerate(both):
        weight_grad(5 + stream, 3, H, r0, r1)
        grad_first(5 + stream)
        weight_grad(3 + stream, 2, D, r0, r1)
        grad_first(3 + stream)
        bias_grad(3 + stream, r0, r1)
    first.wait_recv()
    second.wait_recv()
    for stream, (r0, r1) in enumerate(both):
        result = backward_norm(DZ[r0:r1] + reduced(r0, r1), 1, 1 + stream, 1 + stream, r0, r1)
        DZ[r0:r1] = result
        A[4, 0, r0:r1] = result.astype(BF)

    def attention_backward(p, x_p, streams, QV, Cb, PL, PV, crossed):
        copies = gather_start(p)
        for g in range(2):
            if g == 0:
                copies[0].wait_recv()
            else:
                forward.wait_recv()
            for r0, r1, w in streams:
                context_grad = dot_nn(rows_of_group(p, g, r0, r1), W[w, :, 512:768])
                D[2 * g : 2 * g + 2, r0:r1, 512:768] = context_grad.astype(BF).reshape(2, r1 - r0, TILE)
            if g == 0:
                forward = gather_forward(p, copies)
            grouped(g, lambda s: attend_back_slab(QV, Cb, PL, PV, crossed, s))
            stage_free(g)
            for r0, r1, w in streams:
                partial_nt(g, D, r0, r1, w, slice(0, 768))
            if g == 0:
                first = reduce_first()
            else:
                second = reduce_second()
        for r0, r1, w in streams:
            attention_weight_grad(w, x_p, p, Cb, r0, r1)
            grad_first(w)
            bias_grad(w, r0, r1)
        return first, second

    first, second = attention_backward(
        4, 1, ((0, RL, 1), (RL, ROWS, 2)), QVK.at[1], C.at[1], PSL, PSV, False
    )
    grad_second(5)
    grad_second(3)
    first.wait_recv()
    second.wait_recv()
    for r0, r1 in both:
        result = backward_norm(DZ[r0:r1] + reduced(r0, r1), 0, 0, 0, r0, r1)
        DZ[r0:r1] = result
        A[5, 0, r0:r1] = result.astype(BF)
    first, second = attention_backward(5, 0, ((0, ROWS, 0),), QVK.at[0], C.at[0], PCL, PCV, True)

    quarter = jnp.where(c == 0, z, z2)
    AVA[0, 0:16] = VG[...]
    for j in range(4):
        AVA[0, 16 + 8 * j : 24 + 8 * j] = jnp.where(quarter == j, QG[...], 0.0)
    vector_peers = [sib, plane[0], plane[1], zp, (d, z2)]
    vector_copy = send(AVA.at[0], AVR.at[0], vector_peers[0])
    grad_second(6)
    grad_second(4)
    for stage in range(5):
        if stage == 1:
            first.wait_recv()
            second.wait_recv()
            for r0, r1 in both:
                DZ[r0:r1] = DZ[r0:r1] + reduced(r0, r1)
            tail_grad = [
                send(DZ.at[pl.ds(RL - LANG_TAIL, LANG_TAIL)], TLG, up),
                send(DZ.at[pl.ds(ROWS - VIS_TAIL, VIS_TAIL)], TVG, up),
            ]
            grad_second(1)
            grad_second(2)
        vector_copy.wait_recv()
        AVA[stage + 1] = AVA[stage] + AVR[stage]
        if stage < 4:
            vector_copy = send(AVA.at[stage + 1], AVR.at[stage + 1], vector_peers[stage + 1])
    vec_out[...] = AVA[5, 0:16]
    qb_out[...] = AVA[5, pl.ds(pl.multiple_of(16 + 8 * z, 8), 8)]

    for copy in tail_out + tail_grad:
        copy.wait_recv()
    before_l = jnp.where(z == 1, 0, 25 - 5 * z)
    before_v = jnp.where(z == 1, 0, 45 - 9 * z)
    tail_shift_l = own_l - before_l - (RL - LANG_TAIL)
    tail_shift_v = own_v - before_v - (RV - VIS_TAIL)
    for own_rows, off, tail_rows, shift, out_ref, grad_ref, r0, r1, t_out, t_grad in (
        (own_l, off_l, LANG_TAIL, tail_shift_l, lang_out, lang_grad, 0, RL, TLO, TLG),
        (own_v, off_v, VIS_TAIL, tail_shift_v, vis_out, vis_grad, RL, ROWS, TVO, TVG),
    ):
        from_own = select_rows((own_rows, r1 - r0), -off, off, own_rows)
        from_tail = select_rows((own_rows, tail_rows), shift, 0, off)
        out_ref[...] = (
            dot_nn(from_own.astype(BF), OUTS[r0:r1]) + dot_nn(from_tail.astype(BF), t_out[...])
        ).astype(BF)
        exact = lax.Precision.HIGHEST
        grad_ref[...] = jnp.dot(
            from_own, DZ[r0:r1], precision=exact, preferred_element_type=F32
        ) + jnp.dot(from_tail, t_grad[...], precision=exact, preferred_element_type=F32)

    grad_second(0)
    for w in (5, 3, 6, 4, 1, 2, 0):
        grad_last(w)

    for copy in pending:
        copy.wait_send()
    for index in range(3):
        stage_free(index)

    @pl.when(c == 1)
    def _():
        for copy in nears:
            copy.wait_send()
        for _, far_low, far_high in grad_nears:
            far_low.wait_send()
            far_high.wait_send()

    @pl.when(c == 0)
    def _():
        for near, _, _ in grad_nears:
            near.wait_send()
    assert counter[0] <= ssem.shape[0] and counter[1] <= rsem.shape[0], counter


N_SEND = 160
N_RECV = 80


def fused_layer(total_items, *operands):
    own_l, own_v = operands[0].shape[0], operands[1].shape[0]
    vmem = pl.BlockSpec(memory_space=pltpu.VMEM)
    shapes = [
        ((own_l, D), BF),
        ((own_v, D), BF),
        ((own_l, D), F32),
        ((own_v, D), F32),
        ((7, SHARE, D), F32),
        ((16, D), F32),
        ((8, D), F32),
    ]
    scratch = [
        ((7, D, D), BF),
        ((7, D, D), BF),
        ((3, 7, HALF_PAIR, D), BF),
        ((2, 7, SHARE, D), BF),
        ((6, SLOTS, ROWS, D), BF),
        ((SLOTS, 8, TILE), F32),
        ((3, ROWS, D), BF),
        ((3, ROWS, D), BF),
        ((2, SLOTS, ROWS, D), BF),
        ((SLOTS, ROWS, D), BF),
        ((2, SLOTS, ROWS, TILE), BF),
        ((SLOTS, ROWS, D), BF),
        ((SLOTS, ROWS, D), BF),
        ((SLOTS, 3 * RL, RV), BF),
        ((SLOTS, 3 * RV, RL), BF),
        ((SLOTS, 3 * RL, RL), BF),
        ((SLOTS, 3 * RV, RV), BF),
        ((ROWS, D), F32),
        ((ROWS, D), F32),
        ((3, ROWS, D), F32),
        ((3, ROWS, 1), F32),
        ((ROWS, D), F32),
        ((ROWS, D), BF),
        ((8, D), F32),
        ((8, D), F32),
        ((4, 8, 128), F32),
        ((3, 8, 128), F32),
        ((16, D), F32),
        ((8, D), F32),
        ((6, N_AR, D), F32),
        ((5, N_AR, D), F32),
        ((2, LANG_HEAD, D), BF),
        ((2, VIS_HEAD, D), BF),
        ((ROWS, D), BF),
        ((LANG_TAIL, D), BF),
        ((VIS_TAIL, D), BF),
        ((LANG_TAIL, D), F32),
        ((VIS_TAIL, D), F32),
    ]
    dma = pltpu.SemaphoreType.DMA
    return pl.pallas_call(
        partial(layer_kernel, total_items),
        out_shape=[jax.ShapeDtypeStruct(s, t) for s, t in shapes],
        in_specs=[vmem] * len(operands),
        out_specs=[vmem] * len(shapes),
        scratch_shapes=[pltpu.VMEM(s, t) for s, t in scratch]
        + [dma((N_SEND,)), dma((N_RECV,)), dma((7,)), dma((7,)), dma((7,)), dma((7,)), dma((1,))],
        compiler_params=pltpu.CompilerParams(
            collective_id=0, has_side_effects=True, vmem_limit_bytes=VMEM_LIMIT
        ),
    )(*operands)


def on_device_fused(
    language_input,
    vision_input,
    word_lengths,
    region_counts,
    task_flags,
    language_cotangent,
    vision_cotangent,
    projection_weight,
    query_value_bias,
    output_weight,
    output_bias,
    expand_weight,
    expand_bias,
    contract_weight,
    contract_bias,
    norm_gain,
    norm_bias,
):
    item_count = word_lengths.shape[0]
    z = lax.axis_index("mp")
    share = jnp.concatenate(
        [
            jnp.concatenate(
                [
                    projection_weight[:, 0],
                    projection_weight[:, 2],
                    projection_weight[:, 1],
                    output_weight.transpose(0, 2, 1),
                ],
                -1,
            ),
            expand_weight,
            contract_weight.transpose(0, 2, 1),
        ],
        0,
    )
    first_item = 3 * z + jnp.minimum(z, 1)
    picked = jnp.minimum(first_item + jnp.arange(SLOTS), item_count - 1)

    def key_items(lengths, size):
        slot = jnp.arange(SLOTS * size, dtype=jnp.int32)
        valid = slot % size < lengths[picked][slot // size]
        return jnp.pad(
            jnp.where(valid, slot // size, -1).astype(F32), (0, TILE - SLOTS * size), constant_values=-1.0
        )

    colid = jnp.pad(
        jnp.stack([key_items(word_lengths, WORDS), key_items(region_counts, REGIONS)]), ((0, 6), (0, 0))
    )
    flags = task_flags.astype(F32)
    slab_flags = flags[picked]
    rowflag = jnp.concatenate([jnp.repeat(slab_flags[:, 0], WORDS), jnp.repeat(slab_flags[:, 1], REGIONS)])
    cnt = jnp.pad(jnp.broadcast_to(jnp.sum(flags, 0)[:, None], (2, 128)), ((0, 6), (0, 0)))
    zero_row = jnp.zeros((3, HALF_PAIR), F32)
    qbias = jnp.pad(
        jnp.concatenate(
            [
                jnp.concatenate([query_value_bias[:, 0], query_value_bias[:, 1], zero_row, zero_row], -1),
                expand_bias,
            ],
            0,
        ),
        ((0, 3), (0, 0)),
    )
    vecs = jnp.pad(
        jnp.concatenate([output_bias, contract_bias, norm_gain, norm_bias], 0), ((0, 1), (0, 0))
    )
    lang_out, vis_out, lang_grad, vis_grad, wgrad, vec, qb = fused_layer(
        float(item_count * lax.axis_size("dp")),
        language_input,
        vision_input,
        language_cotangent,
        vision_cotangent,
        share,
        colid,
        rowflag[:, None],
        cnt,
        qbias,
        vecs,
    )
    attention = wgrad[0:3]
    width = HALF_PAIR
    projection_grad = jnp.stack(
        [
            attention[:, :, 0:width],
            attention[:, :, 2 * width : 3 * width],
            attention[:, :, width : 2 * width],
        ],
        1,
    )
    return (
        lang_out,
        vis_out,
        lang_grad,
        vis_grad,
        projection_grad,
        jnp.stack([qb[0:3, 0:width], qb[0:3, width : 2 * width]], 1),
        attention[:, :, 3 * width :].transpose(0, 2, 1),
        vec[0:3],
        wgrad[3:5],
        qb[3:5],
        wgrad[5:7].transpose(0, 2, 1),
        vec[3:5],
        vec[5:10],
        vec[10:15],
    )


def solution(mesh):
    in_specs = (
        P(("dp", "mp"), None),
        P(("dp", "mp"), None),
        P("dp"),
        P("dp"),
        P("dp", None),
        P(("dp", "mp"), None),
        P(("dp", "mp"), None),
        P(None, None, "dp", "mp"),
        P(None, None, "mp"),
        P(None, "mp", "dp"),
        P(),
        P(None, "dp", "mp"),
        P(None, "mp"),
        P(None, "mp", "dp"),
        P(),
        P(),
        P(),
    )
    out_specs = (
        P(("dp", "mp"), None),
        P(("dp", "mp"), None),
        P(("dp", "mp"), None),
        P(("dp", "mp"), None),
        P(None, None, "dp", "mp"),
        P(None, None, "mp"),
        P(None, "mp", "dp"),
        P(),
        P(None, "dp", "mp"),
        P(None, "mp"),
        P(None, "mp", "dp"),
        P(),
        P(),
        P(),
    )
    fused = dict(mesh.shape) == {"dp": 8, "mp": 4}
    return jax.shard_map(
        on_device_fused if fused else on_device, mesh=mesh, in_specs=in_specs, out_specs=out_specs, check_vma=False
    )
```

```python
from functools import partial
import math

import jax
import jax.numpy as jnp
from jax import lax
from jax.experimental import pallas as pl
from jax.experimental.pallas import tpu as pltpu
from jax.sharding import PartitionSpec as P

D = 768
HEADS = 12
WORDS = 20
REGIONS = 36
D_MODEL = D
D_HEAD = D // HEADS

EPSILON = 1e-12
MASKED = -1e30


def layer_norm(summed, gain, shift):
    center = summed - jnp.mean(summed, -1, keepdims=True)
    scaled = lax.rsqrt(jnp.mean(center * center, -1, keepdims=True) + EPSILON)
    normed = center * scaled
    return (normed * gain + shift, normed, scaled)


def norm_back(upstream, normed, scaled, gain):
    through = upstream * gain
    inner = (
        through
        - jnp.mean(through, -1, keepdims=True)
        - normed * jnp.mean(through * normed, -1, keepdims=True)
    )
    return (scaled * inner, jnp.sum(upstream * normed, 0), jnp.sum(upstream, 0))


def split_heads(rows, item_count):
    head_size = D // HEADS
    return rows.reshape(
        item_count, rows.shape[0] // item_count, rows.shape[1] // head_size, head_size
    )


def join_heads(block):
    return block.reshape(block.shape[0] * block.shape[1], block.shape[2] * block.shape[3])


def project(rows, weight, bias, item_count):
    mapped = jnp.einsum("rd,jde->jre", rows, weight, preferred_element_type=jnp.float32)
    query = split_heads((mapped[0] + bias[0]).astype(jnp.bfloat16), item_count)
    keys = split_heads(mapped[1].astype(jnp.bfloat16), item_count)
    values = split_heads((mapped[2] + bias[1]).astype(jnp.bfloat16), item_count)
    return (query, keys, values)


def masked_scores(query, keys, valid):
    scores = jnp.einsum("inhd,imhd->ihnm", query, keys, preferred_element_type=jnp.float32) * (
        1.0 / math.sqrt(D // HEADS)
    )
    return jnp.where(valid[:, None, None, :], scores, MASKED)


def attend(query, keys, values, valid):
    scores = masked_scores(query, keys, valid)
    highest = jnp.max(scores, -1, keepdims=True)
    raised = jnp.exp(scores - highest)
    summed = jnp.sum(raised, -1, keepdims=True)
    context = jnp.einsum(
        "ihnm,imhd->inhd",
        (raised / summed).astype(jnp.bfloat16),
        values,
        preferred_element_type=jnp.float32,
    )
    return (join_heads(context).astype(jnp.bfloat16), highest + jnp.log(summed))


def attend_back(query, keys, values, valid, log_total, context_grad):
    factor = 1.0 / math.sqrt(D // HEADS)
    upstream = context_grad.reshape(query.shape)
    weights = jnp.exp(masked_scores(query, keys, valid) - log_total)
    weight_grad = jnp.einsum(
        "inhd,imhd->ihnm", upstream, values, preferred_element_type=jnp.float32
    )
    score_grad = (
        weights * (weight_grad - jnp.sum(weight_grad * weights, -1, keepdims=True))
    ).astype(jnp.bfloat16)
    query_grad = (
        jnp.einsum("ihnm,imhd->inhd", score_grad, keys, preferred_element_type=jnp.float32) * factor
    ).astype(jnp.bfloat16)
    keys_grad = (
        jnp.einsum("ihnm,inhd->imhd", score_grad, query, preferred_element_type=jnp.float32)
        * factor
    ).astype(jnp.bfloat16)
    values_grad = jnp.einsum(
        "ihnm,inhd->imhd",
        weights.astype(jnp.bfloat16),
        upstream,
        preferred_element_type=jnp.float32,
    ).astype(jnp.bfloat16)
    return (join_heads(query_grad), join_heads(keys_grad), join_heads(values_grad))


def project_back(rows, query_grad, keys_grad, values_grad):
    stacked = jnp.stack([query_grad, keys_grad, values_grad])
    weight_grad = jnp.einsum("rd,jre->jde", rows, stacked, preferred_element_type=jnp.float32)
    bias_grad = jnp.stack(
        [jnp.sum(query_grad.astype(jnp.float32), 0), jnp.sum(values_grad.astype(jnp.float32), 0)]
    )
    return (weight_grad, bias_grad, stacked)


def gather_rows(language_rows, vision_rows):
    return (
        lax.all_gather(language_rows, "mp", axis=0, tiled=True),
        lax.all_gather(vision_rows, "mp", axis=0, tiled=True),
    )


def rows_of(language_part, vision_part):
    return (
        lax.all_to_all(language_part, "mp", split_axis=0, concat_axis=1, tiled=True),
        lax.all_to_all(vision_part, "mp", split_axis=0, concat_axis=1, tiled=True),
    )


def gather_grads(language_rows, vision_rows):
    return (
        lax.all_gather(language_rows, "mp", axis=0, tiled=True),
        lax.all_gather(vision_rows, "mp", axis=0, tiled=True),
    )


def grads_of(language_part, vision_part):
    return (
        lax.all_to_all(language_part, "mp", split_axis=1, concat_axis=2, tiled=True),
        lax.all_to_all(vision_part, "mp", split_axis=1, concat_axis=2, tiled=True),
    )


def matmul(left, right):
    return jnp.dot(left, right, preferred_element_type=jnp.float32)


def on_device(
    language_input,
    vision_input,
    word_lengths,
    region_counts,
    task_flags,
    language_cotangent,
    vision_cotangent,
    projection_weight,
    query_value_bias,
    output_weight,
    output_bias,
    expand_weight,
    expand_bias,
    contract_weight,
    contract_bias,
    norm_gain,
    norm_bias,
):
    item_count = word_lengths.shape[0]
    flag_total = lax.psum(jnp.sum(task_flags, 0), "dp")
    projection, out_weight, expand, contract = (
        lax.all_gather(projection_weight, "dp", axis=2, tiled=True),
        lax.all_gather(output_weight, "dp", axis=2, tiled=True),
        lax.all_gather(expand_weight, "dp", axis=1, tiled=True),
        lax.all_gather(contract_weight, "dp", axis=2, tiled=True),
    )
    projection_full, out_full, expand_full, contract_full = (
        lax.all_gather(projection, "mp", axis=3, tiled=True),
        lax.all_gather(out_weight, "mp", axis=1, tiled=True),
        lax.all_gather(expand, "mp", axis=2, tiled=True),
        lax.all_gather(contract, "mp", axis=1, tiled=True),
    )
    valid = [
        jnp.arange(WORDS, dtype=jnp.int32)[None, :] < word_lengths[:, None],
        jnp.arange(REGIONS, dtype=jnp.int32)[None, :] < region_counts[:, None],
    ]
    row_counts = [WORDS, REGIONS]
    inputs = [language_input.astype(jnp.float32), vision_input.astype(jnp.float32)]
    cross_rows = gather_rows(language_input, vision_input)
    cross_parts = [
        project(cross_rows[stream], projection[0], query_value_bias[0], item_count)
        for stream in range(2)
    ]
    cross_context = []
    cross_total = []
    for stream in range(2):
        other = 1 - stream
        context, log_total = attend(
            cross_parts[stream][0], cross_parts[other][1], cross_parts[other][2], valid[other]
        )
        cross_context.append(context)
        cross_total.append(log_total)
    moved = rows_of(cross_context[0], cross_context[1])
    branch = [matmul(moved[stream], out_full[0]) for stream in range(2)]
    first = [
        layer_norm(branch[stream] + output_bias[0] + inputs[stream], norm_gain[0], norm_bias[0])
        for stream in range(2)
    ]
    first_out = [first[stream][0].astype(jnp.bfloat16) for stream in range(2)]
    self_rows = gather_rows(first_out[0], first_out[1])
    self_parts = [
        project(self_rows[stream], projection[1 + stream], query_value_bias[1 + stream], item_count)
        for stream in range(2)
    ]
    self_context = []
    self_total = []
    for stream in range(2):
        context, log_total = attend(
            self_parts[stream][0], self_parts[stream][1], self_parts[stream][2], valid[stream]
        )
        self_context.append(context)
        self_total.append(log_total)
    moved = rows_of(self_context[0], self_context[1])
    branch = [matmul(moved[stream], out_full[1 + stream]) for stream in range(2)]
    second = [
        layer_norm(
            branch[stream] + output_bias[1 + stream] + first_out[stream].astype(jnp.float32),
            norm_gain[1 + stream],
            norm_bias[1 + stream],
        )
        for stream in range(2)
    ]
    second_out = [second[stream][0].astype(jnp.bfloat16) for stream in range(2)]
    feed_rows = gather_rows(second_out[0], second_out[1])
    before = [
        matmul(feed_rows[stream], expand[stream]) + expand_bias[stream] for stream in range(2)
    ]
    hidden = [
        jax.nn.gelu(before[stream], approximate=False).astype(jnp.bfloat16) for stream in range(2)
    ]
    moved = rows_of(hidden[0], hidden[1])
    branch = [matmul(moved[stream], contract_full[stream]) for stream in range(2)]
    third = [
        layer_norm(
            branch[stream] + contract_bias[stream] + second_out[stream].astype(jnp.float32),
            norm_gain[3 + stream],
            norm_bias[3 + stream],
        )
        for stream in range(2)
    ]
    language_out = third[0][0].astype(jnp.bfloat16)
    vision_out = third[1][0].astype(jnp.bfloat16)
    item_scale = task_flags.astype(jnp.float32) * (
        item_count * lax.axis_size("dp") / flag_total.astype(jnp.float32)
    )
    shard_index = lax.axis_index("mp")
    upstream = []
    for stream, cotangent in enumerate([language_cotangent, vision_cotangent]):
        per_row = jnp.repeat(
            item_scale[:, stream],
            row_counts[stream],
            total_repeat_length=item_count * row_counts[stream],
        )
        shard_rows = cotangent.shape[0]
        row_scale = lax.dynamic_slice_in_dim(per_row, shard_index * shard_rows, shard_rows)
        upstream.append(cotangent.astype(jnp.float32) * row_scale[:, None])
    third_back = [
        norm_back(upstream[stream], third[stream][1], third[stream][2], norm_gain[3 + stream])
        for stream in range(2)
    ]
    sent = gather_grads(
        third_back[0][0].astype(jnp.bfloat16), third_back[1][0].astype(jnp.bfloat16)
    )
    expand_local = []
    expand_bias_local = []
    contract_local = []
    before_grads = []
    for stream in range(2):
        hidden_grad = jnp.einsum(
            "rd,fd->rf", sent[stream], contract[stream], preferred_element_type=jnp.float32
        )
        contract_local.append(
            jnp.einsum(
                "rf,rd->fd", hidden[stream], sent[stream], preferred_element_type=jnp.float32
            )
        )
        unused, pull = jax.vjp(partial(jax.nn.gelu, approximate=False), before[stream])
        before_grad = pull(hidden_grad)[0].astype(jnp.bfloat16)
        expand_local.append(
            jnp.einsum(
                "rd,rf->df", feed_rows[stream], before_grad, preferred_element_type=jnp.float32
            )
        )
        expand_bias_local.append(jnp.sum(before_grad.astype(jnp.float32), 0))
        before_grads.append(before_grad[None])
    moved = grads_of(before_grads[0], before_grads[1])
    back = [
        jnp.einsum(
            "rf,df->rd", moved[stream][0], expand_full[stream], preferred_element_type=jnp.float32
        )
        for stream in range(2)
    ]
    second_grad = [third_back[stream][0] + back[stream] for stream in range(2)]
    second_back = [
        norm_back(second_grad[stream], second[stream][1], second[stream][2], norm_gain[1 + stream])
        for stream in range(2)
    ]
    sent = gather_grads(
        second_back[0][0].astype(jnp.bfloat16), second_back[1][0].astype(jnp.bfloat16)
    )
    self_weight = []
    self_bias = []
    self_out = []
    stacks = []
    for stream in range(2):
        context_grad = jnp.einsum(
            "rd,ed->re", sent[stream], out_weight[1 + stream], preferred_element_type=jnp.float32
        ).astype(jnp.bfloat16)
        self_out.append(
            jnp.einsum(
                "re,rd->ed", self_context[stream], sent[stream], preferred_element_type=jnp.float32
            )
        )
        grads = attend_back(
            self_parts[stream][0],
            self_parts[stream][1],
            self_parts[stream][2],
            valid[stream],
            self_total[stream],
            context_grad,
        )
        weight_part, bias_part, stacked = project_back(
            self_rows[stream], grads[0], grads[1], grads[2]
        )
        self_weight.append(weight_part)
        self_bias.append(bias_part)
        stacks.append(stacked)
    moved = grads_of(stacks[0], stacks[1])
    back = [
        jnp.einsum(
            "jre,jde->rd",
            moved[stream],
            projection_full[1 + stream],
            preferred_element_type=jnp.float32,
        )
        for stream in range(2)
    ]
    first_grad = [second_back[stream][0] + back[stream] for stream in range(2)]
    first_back = [
        norm_back(first_grad[stream], first[stream][1], first[stream][2], norm_gain[0])
        for stream in range(2)
    ]
    sent = gather_grads(
        first_back[0][0].astype(jnp.bfloat16), first_back[1][0].astype(jnp.bfloat16)
    )
    cross_out = jnp.einsum(
        "re,rd->ed", cross_context[0], sent[0], preferred_element_type=jnp.float32
    ) + jnp.einsum("re,rd->ed", cross_context[1], sent[1], preferred_element_type=jnp.float32)
    triples = [[None, None, None], [None, None, None]]
    for stream in range(2):
        other = 1 - stream
        context_grad = jnp.einsum(
            "rd,ed->re", sent[stream], out_weight[0], preferred_element_type=jnp.float32
        ).astype(jnp.bfloat16)
        grads = attend_back(
            cross_parts[stream][0],
            cross_parts[other][1],
            cross_parts[other][2],
            valid[other],
            cross_total[stream],
            context_grad,
        )
        triples[stream][0] = grads[0]
        triples[other][1] = grads[1]
        triples[other][2] = grads[2]
    results = [
        project_back(cross_rows[stream], triples[stream][0], triples[stream][1], triples[stream][2])
        for stream in range(2)
    ]
    cross_weight = results[0][0] + results[1][0]
    cross_bias = results[0][1] + results[1][1]
    moved = grads_of(results[0][2], results[1][2])
    back = [
        jnp.einsum(
            "jre,jde->rd", moved[stream], projection_full[0], preferred_element_type=jnp.float32
        )
        for stream in range(2)
    ]
    language_grad = first_back[0][0] + back[0]
    vision_grad = first_back[1][0] + back[1]
    projection_stack = jnp.stack([cross_weight, self_weight[0], self_weight[1]])
    output_stack = jnp.stack([cross_out, self_out[0], self_out[1]])
    projection_grad, output_weight_grad, expand_grad, contract_grad = (
        lax.psum_scatter(projection_stack, "dp", scatter_dimension=2, tiled=True),
        lax.psum_scatter(output_stack, "dp", scatter_dimension=2, tiled=True),
        lax.psum_scatter(jnp.stack(expand_local), "dp", scatter_dimension=1, tiled=True),
        lax.psum_scatter(jnp.stack(contract_local), "dp", scatter_dimension=2, tiled=True),
    )
    query_value_grad, expand_bias_grad = lax.psum(
        (jnp.stack([cross_bias, self_bias[0], self_bias[1]]), jnp.stack(expand_bias_local)), "dp"
    )
    output_bias_local = jnp.stack(
        [
            jnp.sum(first_back[0][0], 0) + jnp.sum(first_back[1][0], 0),
            jnp.sum(second_back[0][0], 0),
            jnp.sum(second_back[1][0], 0),
        ]
    )
    contract_bias_local = jnp.stack([jnp.sum(third_back[0][0], 0), jnp.sum(third_back[1][0], 0)])
    gain_local = jnp.stack(
        [
            first_back[0][1] + first_back[1][1],
            second_back[0][1],
            second_back[1][1],
            third_back[0][1],
            third_back[1][1],
        ]
    )
    shift_local = jnp.stack(
        [
            first_back[0][2] + first_back[1][2],
            second_back[0][2],
            second_back[1][2],
            third_back[0][2],
            third_back[1][2],
        ]
    )
    output_bias_grad, contract_bias_grad, norm_gain_grad, norm_bias_grad = lax.psum(
        (output_bias_local, contract_bias_local, gain_local, shift_local), ("dp", "mp")
    )
    return (
        language_out,
        vision_out,
        language_grad,
        vision_grad,
        projection_grad,
        query_value_grad,
        output_weight_grad,
        output_bias_grad,
        expand_grad,
        expand_bias_grad,
        contract_grad,
        contract_bias_grad,
        norm_gain_grad,
        norm_bias_grad,
    )


MESH = pl.DeviceIdType.MESH
BF = jnp.bfloat16
F32 = jnp.float32
SLOTS = 4
RL = SLOTS * WORDS
RV = SLOTS * REGIONS
ROWS = RL + RV
SHARE = 96
HALF_PAIR = 2 * SHARE
LANG_HEAD = 16
VIS_HEAD = 32
LANG_TAIL = 32
VIS_TAIL = 64
N_AR = 48
NT = 3
TILE = 256
VMEM_LIMIT = 63 * 1024 * 1024


def dot_nn(left, right):
    return lax.dot_general(left, right, (((1,), (0,)), ((), ())), preferred_element_type=F32)


def dot_nt(left, right):
    return lax.dot_general(left, right, (((1,), (1,)), ((), ())), preferred_element_type=F32)


def dot_tn(left, right):
    return lax.dot_general(left, right, (((0,), (0,)), ((), ())), preferred_element_type=F32)


def head_mask(first_lane, dtype):
    lane = lax.broadcasted_iota(jnp.int32, (1, TILE), 1) - first_lane
    return [
        jnp.where((lane >= 64 * h) & (lane < 64 * h + 64), 1.0, 0.0).astype(dtype) for h in range(3)
    ]


def select_rows(shape, shift, low, high):
    row = lax.broadcasted_iota(jnp.int32, shape, 0)
    column = lax.broadcasted_iota(jnp.int32, shape, 1)
    return jnp.where((column - row == shift) & (row >= low) & (row < high), 1.0, 0.0)


def layer_kernel(
    total_items,
    lang,
    vis,
    lcot,
    vcot,
    lengths,
    regions,
    flags,
    projection,
    query_value,
    out_weight,
    expand,
    expand_b,
    contract,
    out_bias,
    contract_b,
    gains,
    shifts,
    lang_out,
    vis_out,
    lang_grad,
    vis_grad,
    wgrad,
    vec_out,
    qb_out,
    W,
    G,
    R1,
    R2,
    A,
    KV,
    RSB,
    STG,
    QVK,
    D,
    C,
    H,
    GP,
    PCL,
    PCV,
    PSL,
    PSV,
    PART,
    PZ,
    NORM,
    RSTD,
    DZ,
    COT,
    SH,
    FLAG,
    QO,
    QB,
    QR,
    CA,
    CR,
    VG,
    QG,
    AVA,
    AVR,
    HL,
    HV,
    OUTS,
    TLO,
    TVO,
    TLG,
    TVG,
    ssem,
    rsem,
    wsem,
    wsem_z,
    gsem,
    gsem2,
    lsem,
):
    d = lax.axis_index("dp")
    z = lax.axis_index("mp")
    c = d % 2
    k = d // 2
    k_flip = [k + 1 - 2 * (k % 2), (k + 2) % 4, 3 - k]
    sib = (d + 1 - 2 * c, z)
    zp = (d, z + 1 - 2 * (z % 2))
    z2 = (z + 2) % 4
    up = (d, (z + 1) % 4)
    down = (d, (z + 3) % 4)
    plane = [(2 * kf + c, z) for kf in k_flip]
    far = (2 * k + 1, z2)

    pending = []
    counter = [0, 0]

    def remote(src, dst, send, recv, device):
        return pltpu.make_async_remote_copy(
            src_ref=src, dst_ref=dst, send_sem=send, recv_sem=recv, device_id=device, device_id_type=MESH
        )

    def send(src, dst, device, recv=None, keep=True):
        slot = counter[0]
        counter[0] += 1
        if recv is None:
            recv = rsem.at[counter[1]]
            counter[1] += 1
        copy = remote(src, dst, ssem.at[slot], recv, device)
        copy.start()
        if keep:
            pending.append(copy)
        return copy

    def wait_bytes(ref, sem):
        pltpu.make_async_copy(ref, ref, sem).wait()

    def arrived(name, *copies):
        with jax.named_scope("wait_" + name):
            for copy in copies:
                copy.wait_recv()

    barrier = pltpu.get_barrier_semaphore()
    peers = [sib, up, down, (d, z2), (d + 1 - 2 * c, z2)] + plane
    with jax.named_scope("barrier"):
        for peer in peers:
            pl.semaphore_signal(barrier, inc=1, device_id=peer, device_id_type=MESH)
        pl.semaphore_wait(barrier, len(peers))

    def weight_first(w):
        row = pl.ds(pl.multiple_of(d * SHARE, 16), SHARE)
        slot = counter[0]
        counter[0] += 1
        share = expand.at[w - 3] if w in (3, 4) else SH.at[w if w < 3 else w - 2]
        near = remote(share, W.at[w, row], ssem.at[slot], wsem_z.at[w], sib)
        own = pltpu.make_async_copy(share, W.at[w, row], wsem_z.at[w])

        @pl.when(c == 1)
        def _():
            near.start()

        @pl.when(c == 0)
        def _():
            own.start()

        send(share, W.at[w, row], far, wsem_z.at[w])
        return near

    def place(width, first):
        row = lax.broadcasted_iota(jnp.int32, (width, D_MODEL), 0)
        column = lax.broadcasted_iota(jnp.int32, (width, D_MODEL), 1)
        return jnp.where(column - row == first, 1.0, 0.0).astype(BF)

    @jax.named_scope("share")
    def attention_share(b):
        SH[b] = (
            dot_nn(projection[b, 0], place(HALF_PAIR, 0))
            + dot_nn(projection[b, 2], place(HALF_PAIR, HALF_PAIR))
            + dot_nn(projection[b, 1], place(HALF_PAIR, 2 * HALF_PAIR))
            + dot_tn(out_weight[b], place(HALF_PAIR, 3 * HALF_PAIR))
        ).astype(BF)

    @jax.named_scope("share")
    def contract_share(stream):
        SH[3 + stream] = dot_tn(contract[stream], place(D_MODEL, 0)).astype(BF)

    nears = []
    heads = [
        send(lang.at[pl.ds(0, LANG_HEAD)], HL.at[0], down),
        send(vis.at[pl.ds(0, VIS_HEAD)], HV.at[0], down),
        send(lcot.at[pl.ds(0, LANG_HEAD)], HL.at[1], down),
        send(vcot.at[pl.ds(0, VIS_HEAD)], HV.at[1], down),
    ]
    attention_share(0)
    nears.append(weight_first(0))

    n_items = lengths.shape[0]
    first_item = 3 * z + jnp.minimum(z, 1)
    KV[0] = jnp.full(KV.shape[1:], -1.0, F32)
    for row, source, size in ((0, lengths, WORDS), (1, regions, REGIONS)):
        lane = lax.broadcasted_iota(jnp.int32, (1, TILE), 1)
        owner = jnp.full((1, TILE), -1.0, F32)
        slab_row = lax.broadcasted_iota(jnp.int32, (SLOTS * size, 1), 0)
        flag = jnp.zeros((SLOTS * size, 1), F32)
        for j in range(SLOTS):
            item = jnp.minimum(first_item + j, n_items - 1)
            valid = (lane >= j * size) & (lane < j * size + source[item]) & (lane < (j + 1) * size)
            owner = jnp.where(valid, float(j), owner)
            inside = (slab_row >= j * size) & (slab_row < (j + 1) * size)
            flag = jnp.where(inside, flags[item, row].astype(F32), flag)
        KV[0, row : row + 1] = owner
        FLAG[row * RL : row * RL + SLOTS * size] = flag
        count = flags[0, row]
        for j in range(1, n_items):
            count = count + flags[j, row]
        CA[0, row : row + 1] = jnp.full((1, 128), count.astype(F32), F32)
    kv_sib = send(KV.at[0], KV.at[1], sib)
    kv_zp = send(KV.at[0], KV.at[2], zp)
    count_copies = [send(CA.at[0], CR.at[0], sib)]
    QO[...] = jnp.zeros_like(QO)
    for b in range(3):
        QO[b : b + 1, 0:HALF_PAIR] = query_value[b, 0:1]
        QO[b : b + 1, HALF_PAIR : 2 * HALF_PAIR] = query_value[b, 1:2]
    QO[3:5] = expand_b[...]
    bias_swap = send(QO, QR, (d, z2))
    for w in (1, 2, 3, 4, 5, 6):
        if w < 3:
            attention_share(w)
        elif w > 4:
            contract_share(w - 5)
        nears.append(weight_first(w))

    pair_rows = pl.ds(pl.multiple_of(k * HALF_PAIR, 16), HALF_PAIR)

    def weight_second(w):
        with jax.named_scope("wait_weight_pair"):
            wait_bytes(W.at[w, pair_rows], wsem_z.at[w])
        for peer in plane:
            send(W.at[w, pair_rows], W.at[w, pair_rows], peer, wsem.at[w])

    def weight_ready(w):
        with jax.named_scope("wait_weight_full"):
            wait_bytes(W.at[w, pl.ds(0, 3 * HALF_PAIR)], wsem.at[w])

    off_l = jnp.where(z == 0, 0, 20 - 5 * z)
    off_v = jnp.where(z == 0, 0, 36 - 9 * z)
    n_l = jnp.where(z == 0, 4 * WORDS, 3 * WORDS)
    n_v = jnp.where(z == 0, 4 * REGIONS, 3 * REGIONS)
    own_l = lang.shape[0]
    own_v = vis.shape[0]
    arrived("heads", *heads)
    for index, (source_l, source_v) in enumerate([(lang, vis), (lcot, vcot)]):
        slab_l = dot_nn(select_rows((RL, own_l), off_l, 0, n_l).astype(BF), source_l[...]) + dot_nn(
            select_rows((RL, LANG_HEAD), off_l - own_l, 0, n_l).astype(BF), HL[index]
        )
        slab_v = dot_nn(select_rows((RV, own_v), off_v, 0, n_v).astype(BF), source_v[...]) + dot_nn(
            select_rows((RV, VIS_HEAD), off_v - own_v, 0, n_v).astype(BF), HV[index]
        )
        if index == 0:
            A[0, 0, 0:RL] = slab_l.astype(BF)
            A[0, 0, RL:ROWS] = slab_v.astype(BF)
        else:
            COT[0:RL] = slab_l.astype(BF)
            COT[RL:ROWS] = slab_v.astype(BF)

    def gather_start(p):
        return (send(A.at[p, 0], A.at[p, 1], sib), send(A.at[p, 0], A.at[p, 2], zp))

    def gather_forward(p, copies):
        arrived("rows_z", copies[1])
        return send(A.at[p, 2], A.at[p, 3], sib)

    stage_used = [None, None, None]

    def stage_free(index):
        if stage_used[index] is not None:
            stage_used[index].wait_send()
            stage_used[index] = None

    def partial_nt(g, lhs_ref, r0, r1, w, lanes):
        rows = r1 - r0

        def body(n, carry):
            column = pl.ds(pl.multiple_of(n * TILE, TILE), TILE)
            lhs = lhs_ref[2 * g : 2 * g + 2, r0:r1, :]
            lhs = lhs.reshape(2 * rows, lhs.shape[-1])
            out = dot_nt(lhs, W[w, column, lanes])
            if g == 0:
                PART[r0:r1, column] = out[:rows]
                STG[0, r0:r1, column] = out[rows:].astype(BF)
            else:
                PZ[r0:r1, column] = out[:rows]
                STG[1, r0:r1, column] = out[rows:].astype(BF)
            return carry

        with jax.named_scope("partial_sums"):
            lax.fori_loop(0, NT, body, 0)

    def reduce_first():
        copy = send(STG.at[0], RSB.at[0], sib, keep=False)
        stage_used[0] = copy
        return copy

    def reduce_second():
        across = send(STG.at[1], RSB.at[1], sib, keep=False)
        stage_used[1] = across
        arrived("sums_core", across)
        stage_free(2)
        STG[2] = (PZ[...] + RSB[1].astype(F32)).astype(BF)
        copy = send(STG.at[2], RSB.at[2], zp, keep=False)
        stage_used[2] = copy
        return copy

    def reduced(r0, r1):
        return PART[r0:r1] + RSB[0, r0:r1].astype(F32) + RSB[2, r0:r1].astype(F32)

    mask_q = head_mask(0, BF)
    mask_c = head_mask(64, BF)
    mask_q32 = head_mask(0, F32)
    mask_c32 = head_mask(64, F32)
    factor = 1.0 / math.sqrt(D_HEAD)

    def attend_slab(QV, Cb, PL, PV, crossed, s):
        def one(q0, q1, k0, k1, words_keys, P):
            nq, nk = q1 - q0, k1 - k0
            query = QV[s, q0:q1, 0:256]
            keys = QV[s, k0:k1, 384:640]
            values = QV[s, k0:k1, 128:384]
            query_size = WORDS if q0 == 0 else REGIONS
            spread = jnp.concatenate([query * mask_q[h] for h in range(3)], 0)
            scores = dot_nt(spread, keys) * factor
            row = lax.broadcasted_iota(jnp.int32, (nq, nk), 0)
            item = jnp.zeros((nq, nk), F32)
            for j in range(1, SLOTS):
                item = item + jnp.where(row >= j * query_size, 1.0, 0.0)
            column = KV[s, 0:1, 0:nk] if words_keys else KV[s, 1:2, 0:nk]
            same = item == column
            scores = jnp.where(same[None], scores.reshape(3, nq, nk), MASKED)
            raised = jnp.exp(scores - jnp.max(scores, -1, keepdims=True))
            weights = (raised / jnp.sum(raised, -1, keepdims=True)).astype(BF).reshape(3 * nq, nk)
            P[s] = weights
            context = dot_nn(weights, values).reshape(3, nq, TILE)
            Cb[s, q0:q1] = (
                context[0] * mask_c32[0] + context[1] * mask_c32[1] + context[2] * mask_c32[2]
            ).astype(BF)

        if crossed:
            one(0, RL, RL, ROWS, False, PL)
            one(RL, ROWS, 0, RL, True, PV)
        else:
            one(0, RL, 0, RL, True, PL)
            one(RL, ROWS, RL, ROWS, False, PV)

    def attend_back_slab(QV, Cb, PL, PV, crossed, s):
        def one(q0, q1, k0, k1, P):
            nq, nk = q1 - q0, k1 - k0
            query = QV[s, q0:q1, 0:256]
            keys = QV[s, k0:k1, 384:640]
            values = QV[s, k0:k1, 128:384]
            spread = jnp.concatenate([query * mask_q[h] for h in range(3)], 0)
            upstream = D[s, q0:q1, 512:768]
            up_spread = jnp.concatenate([upstream * mask_c[h] for h in range(3)], 0)
            weights = P[s]
            weights32 = weights.astype(F32)
            weight_grad = dot_nt(up_spread, values)
            score_grad = (
                weights32
                * (weight_grad - jnp.sum(weight_grad * weights32, -1, keepdims=True))
            ).astype(BF)
            dq = dot_nn(score_grad, keys).reshape(3, nq, TILE)
            dq = (dq[0] * mask_q32[0] + dq[1] * mask_q32[1] + dq[2] * mask_q32[2]) * factor
            dk = dot_tn(score_grad, spread) * factor
            dv = dot_tn(weights, up_spread)
            return dq, dk, dv

        if crossed:
            dq_l, dk_v, dv_v = one(0, RL, RL, ROWS, PL)
            dq_v, dk_l, dv_l = one(RL, ROWS, 0, RL, PV)
        else:
            dq_l, dk_l, dv_l = one(0, RL, 0, RL, PL)
            dq_v, dk_v, dv_v = one(RL, ROWS, RL, ROWS, PV)
        for r0, r1, dq, dk, dv in ((0, RL, dq_l, dk_l, dv_l), (RL, ROWS, dq_v, dk_v, dv_v)):
            D[s, r0:r1, 0:128] = dq[:, :128].astype(BF)
            D[s, r0:r1, 128:256] = (dq[:, 128:] + dv[:, :128]).astype(BF)
            D[s, r0:r1, 256:384] = dv[:, 128:].astype(BF)
            D[s, r0:r1, 384:640] = dk.astype(BF)
            D[s, r0:r1, 640:768] = jnp.zeros((r1 - r0, 128), BF)

    def grouped(g, body):
        lax.fori_loop(2 * g, 2 * g + 2, lambda s, carry: (body(s), carry)[1], 0)

    def over_tiles(body):
        def step(n, carry):
            body(pl.ds(pl.multiple_of(n * TILE, TILE), TILE))
            return carry

        lax.fori_loop(0, NT, step, 0)

    @jax.named_scope("norm")
    def forward_norm(value, index, gain_row, r0, r1):
        center = value - jnp.mean(value, -1, keepdims=True)
        scaled = lax.rsqrt(jnp.mean(center * center, -1, keepdims=True) + EPSILON)
        normed = center * scaled
        NORM[index, r0:r1] = normed
        RSTD[index, r0:r1] = scaled
        return normed * gains[gain_row : gain_row + 1] + shifts[gain_row : gain_row + 1]

    @jax.named_scope("norm_gradient")
    def backward_norm(upstream, index, gain_row, bias_row, r0, r1):
        normed = NORM[index, r0:r1]
        through = upstream * gains[gain_row : gain_row + 1]
        inner = (
            through
            - jnp.mean(through, -1, keepdims=True)
            - normed * jnp.mean(through * normed, -1, keepdims=True)
        )
        result = RSTD[index, r0:r1] * inner
        VG[5 + gain_row : 6 + gain_row] += jnp.sum(upstream * normed, 0, keepdims=True)
        VG[10 + gain_row : 11 + gain_row] += jnp.sum(upstream, 0, keepdims=True)
        VG[bias_row : bias_row + 1] += jnp.sum(result, 0, keepdims=True)
        return result

    both = ((0, RL), (RL, ROWS))
    all_rows = ((0, ROWS),)

    def rows_of_group(p, g, r0, r1):
        return A[p, 2 * g : 2 * g + 2, r0:r1, :].reshape(2 * (r1 - r0), D_MODEL)

    def attention_forward(p, streams, QV, Cb, PL, PV, crossed, ready, between):
        copies = gather_start(p)
        ready()
        for g in range(2):
            if g == 0:
                arrived("rows_core", copies[0])
            else:
                arrived("rows_far", forward)
            for r0, r1, w in streams:
                rows = r1 - r0

                def project_tile(column, r0=r0, r1=r1, w=w, rows=rows):
                    mapped = dot_nn(rows_of_group(p, g, r0, r1), W[w, :, column]) + QB[w : w + 1, column]
                    QV[2 * g : 2 * g + 2, r0:r1, column] = mapped.astype(BF).reshape(2, rows, TILE)

                with jax.named_scope("project"):
                    over_tiles(project_tile)
            if g == 0:
                forward = gather_forward(p, copies)
            with jax.named_scope("attend"):
                grouped(g, lambda s: attend_slab(QV, Cb, PL, PV, crossed, s))
            stage_free(g)
            for r0, r1, w in streams:
                partial_nt(g, Cb, r0, r1, w, slice(512, 768))
            if g == 0:
                first = reduce_first()
                between()
            else:
                second = reduce_second()
        arrived("sums", first, second)

    VG[...] = jnp.zeros_like(VG)
    QG[...] = jnp.zeros_like(QG)

    def ready_cross():
        weight_second(0)
        kv_sib.wait_recv()
        kv_zp.wait_recv()
        kv_far = send(KV.at[2], KV.at[3], sib)
        bias_swap.wait_recv()
        QB[...] = jnp.where(c == 1, QR[...], QO[...])
        weight_ready(0)
        kv_far.wait_recv()

    def between_cross():
        weight_second(1)
        weight_second(2)
        count_copies[0].wait_recv()
        CA[1] = CA[0] + CR[0]
        count_copies.append(send(CA.at[1], CR.at[1], plane[0]))

    attention_forward(
        0, ((0, ROWS, 0),), QVK.at[0], C.at[0], PCL, PCV, True, ready_cross, between_cross
    )
    for r0, r1 in both:
        value = reduced(r0, r1) + out_bias[0:1] + A[0, 0, r0:r1].astype(F32)
        A[1, 0, r0:r1] = forward_norm(value, 0, 0, r0, r1).astype(BF)

    def ready_self():
        weight_ready(1)
        weight_ready(2)

    def between_self():
        weight_second(3)
        weight_second(4)
        count_copies[1].wait_recv()
        CA[2] = CA[1] + CR[1]
        count_copies.append(send(CA.at[2], CR.at[2], plane[1]))

    attention_forward(
        1, ((0, RL, 1), (RL, ROWS, 2)), QVK.at[1], C.at[1], PSL, PSV, False, ready_self, between_self
    )
    for stream, (r0, r1) in enumerate(both):
        value = reduced(r0, r1) + out_bias[1 + stream : 2 + stream] + A[1, 0, r0:r1].astype(F32)
        A[2, 0, r0:r1] = forward_norm(value, 1, 1 + stream, r0, r1).astype(BF)

    copies = gather_start(2)
    for g in range(2):
        if g == 0:
            arrived("rows_core", copies[0])
            weight_ready(3)
            weight_ready(4)
        else:
            arrived("rows_far", forward)
        for stream, (r0, r1) in enumerate(both):
            rows = r1 - r0

            def expand_tile(column, r0=r0, r1=r1, stream=stream, rows=rows):
                before = (
                    dot_nn(rows_of_group(2, g, r0, r1), W[3 + stream, :, column])
                    + QB[3 + stream : 4 + stream, column]
                )
                half = 0.5 * (1.0 + lax.erf(before * math.sqrt(0.5)))
                slope = half + before * jnp.exp(-0.5 * before * before) * (
                    1.0 / math.sqrt(2.0 * math.pi)
                )
                H[2 * g : 2 * g + 2, r0:r1, column] = (before * half).astype(BF).reshape(2, rows, TILE)
                GP[2 * g : 2 * g + 2, r0:r1, column] = slope.astype(BF).reshape(2, rows, TILE)

            with jax.named_scope("expand"):
                over_tiles(expand_tile)
        if g == 0:
            forward = gather_forward(2, copies)
            weight_second(5)
            weight_second(6)
            weight_ready(5)
            weight_ready(6)
        stage_free(g)
        for stream, (r0, r1) in enumerate(both):
            partial_nt(g, H, r0, r1, 5 + stream, slice(0, 768))
        if g == 0:
            first = reduce_first()
            count_copies[2].wait_recv()
            CA[3] = CA[2] + CR[2]
        else:
            second = reduce_second()
    arrived("sums", first, second)

    for stream, (r0, r1) in enumerate(both):
        value = reduced(r0, r1) + contract_b[stream : stream + 1] + A[2, 0, r0:r1].astype(F32)
        OUTS[r0:r1] = forward_norm(value, 2, 3 + stream, r0, r1).astype(BF)
        scale = total_items / CA[3, stream : stream + 1, 0:1]
        upstream = COT[r0:r1].astype(F32) * (FLAG[r0:r1] * scale)
        result = backward_norm(upstream, 2, 3 + stream, 3 + stream, r0, r1)
        DZ[r0:r1] = result
        A[3, 0, r0:r1] = result.astype(BF)
    copies = gather_start(3)
    tail_out = [
        send(OUTS.at[pl.ds(RL - LANG_TAIL, LANG_TAIL)], TLO, up),
        send(OUTS.at[pl.ds(ROWS - VIS_TAIL, VIS_TAIL)], TVO, up),
    ]

    def weight_grad(w, lhs_p, rhs_ref, r0, r1, rhs_lanes=slice(0, 768)):
        rows = SLOTS * (r1 - r0)

        def step(m, carry):
            column = pl.ds(pl.multiple_of(m * TILE, TILE), TILE)
            left = A[lhs_p, :, r0:r1, column].reshape(rows, TILE)
            right = rhs_ref[:, r0:r1, rhs_lanes]
            right = right.reshape(rows, right.shape[-1])
            G[w, column, rhs_lanes] = dot_tn(left, right).astype(BF)
            return carry

        with jax.named_scope("weight_gradient"):
            lax.fori_loop(0, NT, step, 0)

    def attention_weight_grad(w, x_p, b_p, Cb, r0, r1):
        weight_grad(w, x_p, D, r0, r1, slice(0, 512))
        rows = SLOTS * (r1 - r0)

        def step(m, carry):
            column = pl.ds(pl.multiple_of(m * TILE, TILE), TILE)
            left = A[x_p, :, r0:r1, column].reshape(rows, TILE)
            right = D[:, r0:r1, 512:768].reshape(rows, TILE)
            left_b = A[b_p, :, r0:r1, column].reshape(rows, TILE)
            right_b = Cb[:, r0:r1, :].reshape(rows, TILE)
            G[w, column, 512:768] = (dot_tn(left, right) + dot_tn(left_b, right_b)).astype(BF)
            return carry

        with jax.named_scope("weight_gradient"):
            lax.fori_loop(0, NT, step, 0)

    @jax.named_scope("bias_gradient")
    def bias_grad(row, r0, r1):
        total = jnp.zeros((1, D_MODEL), F32)
        for s in range(SLOTS):
            total = total + jnp.sum(D[s, r0:r1].astype(F32), 0, keepdims=True)
        QG[row : row + 1] = total

    def grad_first(w):
        for j in range(3):
            rows = pl.ds(pl.multiple_of(k_flip[j] * HALF_PAIR, 16), HALF_PAIR)
            send(G.at[w, rows], R1.at[j, w], plane[j], gsem.at[w])

    grad_nears = []

    def grad_second(w):
        with jax.named_scope("wait_grad_plane"):
            wait_bytes(R1.at[:, w], gsem.at[w])
        total = G[w, pair_rows].astype(F32)
        for j in range(3):
            total = total + R1[j, w].astype(F32)
        G[w, pair_rows] = total.astype(BF)
        low = pl.ds(pl.multiple_of(k * HALF_PAIR, 16), SHARE)
        high = pl.ds(pl.multiple_of(k * HALF_PAIR + SHARE, 16), SHARE)
        slot = counter[0]
        counter[0] += 2
        own = pltpu.make_async_copy(G.at[w, low], R2.at[0, w], gsem2.at[w])
        near = remote(G.at[w, high], R2.at[0, w], ssem.at[slot], gsem2.at[w], sib)
        far_low = remote(G.at[w, low], R2.at[1, w], ssem.at[slot], gsem2.at[w], (2 * k, z2))
        far_high = remote(G.at[w, high], R2.at[1, w], ssem.at[slot + 1], gsem2.at[w], (2 * k + 1, z2))

        @pl.when(c == 0)
        def _():
            own.start()
            near.start()

        @pl.when(c == 1)
        def _():
            far_low.start()
            far_high.start()

        grad_nears.append((near, far_low, far_high))

    def grad_last(w):
        with jax.named_scope("wait_grad_last"):
            wait_bytes(R2.at[:, w], gsem2.at[w])
        wgrad[w] = R2[0, w].astype(F32) + R2[1, w].astype(F32)

    for g in range(2):
        if g == 0:
            arrived("rows_core", copies[0])
        else:
            arrived("rows_far", forward)
        for stream, (r0, r1) in enumerate(both):
            rows = r1 - r0

            def hidden_tile(column, r0=r0, r1=r1, stream=stream, rows=rows):
                up_hidden = dot_nn(rows_of_group(3, g, r0, r1), W[5 + stream, :, column])
                slope = GP[2 * g : 2 * g + 2, r0:r1, column].reshape(2 * rows, TILE)
                D[2 * g : 2 * g + 2, r0:r1, column] = (
                    (up_hidden * slope.astype(F32)).astype(BF).reshape(2, rows, TILE)
                )

            with jax.named_scope("hidden_gradient"):
                over_tiles(hidden_tile)
        if g == 0:
            forward = gather_forward(3, copies)
        stage_free(g)
        for stream, (r0, r1) in enumerate(both):
            partial_nt(g, D, r0, r1, 3 + stream, slice(0, 768))
        if g == 0:
            first = reduce_first()
        else:
            second = reduce_second()
    for stream, (r0, r1) in enumerate(both):
        weight_grad(5 + stream, 3, H, r0, r1)
        grad_first(5 + stream)
        weight_grad(3 + stream, 2, D, r0, r1)
        grad_first(3 + stream)
        bias_grad(3 + stream, r0, r1)
    arrived("sums", first, second)
    for stream, (r0, r1) in enumerate(both):
        result = backward_norm(DZ[r0:r1] + reduced(r0, r1), 1, 1 + stream, 1 + stream, r0, r1)
        DZ[r0:r1] = result
        A[4, 0, r0:r1] = result.astype(BF)

    def attention_backward(p, x_p, streams, QV, Cb, PL, PV, crossed):
        copies = gather_start(p)
        for g in range(2):
            if g == 0:
                arrived("rows_core", copies[0])
            else:
                arrived("rows_far", forward)
            for r0, r1, w in streams:
                context_grad = dot_nn(rows_of_group(p, g, r0, r1), W[w, :, 512:768])
                D[2 * g : 2 * g + 2, r0:r1, 512:768] = context_grad.astype(BF).reshape(2, r1 - r0, TILE)
            if g == 0:
                forward = gather_forward(p, copies)
            with jax.named_scope("attend_gradient"):
                grouped(g, lambda s: attend_back_slab(QV, Cb, PL, PV, crossed, s))
            stage_free(g)
            for r0, r1, w in streams:
                partial_nt(g, D, r0, r1, w, slice(0, 768))
            if g == 0:
                first = reduce_first()
            else:
                second = reduce_second()
        for r0, r1, w in streams:
            attention_weight_grad(w, x_p, p, Cb, r0, r1)
            grad_first(w)
            bias_grad(w, r0, r1)
        return first, second

    first, second = attention_backward(
        4, 1, ((0, RL, 1), (RL, ROWS, 2)), QVK.at[1], C.at[1], PSL, PSV, False
    )
    grad_second(5)
    grad_second(3)
    arrived("sums", first, second)
    for r0, r1 in both:
        result = backward_norm(DZ[r0:r1] + reduced(r0, r1), 0, 0, 0, r0, r1)
        DZ[r0:r1] = result
        A[5, 0, r0:r1] = result.astype(BF)
    first, second = attention_backward(5, 0, ((0, ROWS, 0),), QVK.at[0], C.at[0], PCL, PCV, True)

    quarter = jnp.where(c == 0, z, z2)
    AVA[0, 0:16] = VG[...]
    for j in range(4):
        AVA[0, 16 + 8 * j : 24 + 8 * j] = jnp.where(quarter == j, QG[...], 0.0)
    vector_peers = [sib, plane[0], plane[1], zp, (d, z2)]
    vector_copy = send(AVA.at[0], AVR.at[0], vector_peers[0])
    grad_second(6)
    grad_second(4)
    for stage in range(5):
        if stage == 1:
            arrived("sums", first, second)
            for r0, r1 in both:
                DZ[r0:r1] = DZ[r0:r1] + reduced(r0, r1)
            tail_grad = [
                send(DZ.at[pl.ds(RL - LANG_TAIL, LANG_TAIL)], TLG, up),
                send(DZ.at[pl.ds(ROWS - VIS_TAIL, VIS_TAIL)], TVG, up),
            ]
            grad_second(1)
            grad_second(2)
        arrived("vectors", vector_copy)
        AVA[stage + 1] = AVA[stage] + AVR[stage]
        if stage < 4:
            vector_copy = send(AVA.at[stage + 1], AVR.at[stage + 1], vector_peers[stage + 1])
    vec_out[...] = AVA[5, 0:16]
    qb_out[...] = AVA[5, pl.ds(pl.multiple_of(16 + 8 * z, 8), 8)]

    arrived("tails", *tail_out, *tail_grad)
    before_l = jnp.where(z == 1, 0, 25 - 5 * z)
    before_v = jnp.where(z == 1, 0, 45 - 9 * z)
    tail_shift_l = own_l - before_l - (RL - LANG_TAIL)
    tail_shift_v = own_v - before_v - (RV - VIS_TAIL)
    for own_rows, off, tail_rows, shift, out_ref, grad_ref, r0, r1, t_out, t_grad in (
        (own_l, off_l, LANG_TAIL, tail_shift_l, lang_out, lang_grad, 0, RL, TLO, TLG),
        (own_v, off_v, VIS_TAIL, tail_shift_v, vis_out, vis_grad, RL, ROWS, TVO, TVG),
    ):
        from_own = select_rows((own_rows, r1 - r0), -off, off, own_rows)
        from_tail = select_rows((own_rows, tail_rows), shift, 0, off)
        out_ref[...] = (
            dot_nn(from_own.astype(BF), OUTS[r0:r1]) + dot_nn(from_tail.astype(BF), t_out[...])
        ).astype(BF)
        exact = lax.Precision.HIGHEST
        grad_ref[...] = jnp.dot(
            from_own, DZ[r0:r1], precision=exact, preferred_element_type=F32
        ) + jnp.dot(from_tail, t_grad[...], precision=exact, preferred_element_type=F32)

    grad_second(0)
    for w in (5, 3, 6, 4, 1, 2, 0):
        grad_last(w)

    for copy in pending:
        copy.wait_send()
    for index in range(3):
        stage_free(index)

    @pl.when(c == 1)
    def _():
        for copy in nears:
            copy.wait_send()
        for _, far_low, far_high in grad_nears:
            far_low.wait_send()
            far_high.wait_send()

    @pl.when(c == 0)
    def _():
        for near, _, _ in grad_nears:
            near.wait_send()
    assert counter[0] <= ssem.shape[0] and counter[1] <= rsem.shape[0], counter


N_SEND = 160
N_RECV = 80


def fused_layer(total_items, *operands):
    own_l, own_v = operands[0].shape[0], operands[1].shape[0]
    vmem = pl.BlockSpec(memory_space=pltpu.VMEM)
    smem = pl.BlockSpec(memory_space=pltpu.SMEM)
    shapes = [
        ((own_l, D), BF),
        ((own_v, D), BF),
        ((own_l, D), F32),
        ((own_v, D), F32),
        ((7, SHARE, D), F32),
        ((16, D), F32),
        ((8, D), F32),
    ]
    scratch = [
        ((7, D, D), BF),
        ((7, D, D), BF),
        ((3, 7, HALF_PAIR, D), BF),
        ((2, 7, SHARE, D), BF),
        ((6, SLOTS, ROWS, D), BF),
        ((SLOTS, 8, TILE), F32),
        ((3, ROWS, D), BF),
        ((3, ROWS, D), BF),
        ((2, SLOTS, ROWS, D), BF),
        ((SLOTS, ROWS, D), BF),
        ((2, SLOTS, ROWS, TILE), BF),
        ((SLOTS, ROWS, D), BF),
        ((SLOTS, ROWS, D), BF),
        ((SLOTS, 3 * RL, RV), BF),
        ((SLOTS, 3 * RV, RL), BF),
        ((SLOTS, 3 * RL, RL), BF),
        ((SLOTS, 3 * RV, RV), BF),
        ((ROWS, D), F32),
        ((ROWS, D), F32),
        ((3, ROWS, D), F32),
        ((3, ROWS, 1), F32),
        ((ROWS, D), F32),
        ((ROWS, D), BF),
        ((5, SHARE, D), BF),
        ((ROWS, 1), F32),
        ((8, D), F32),
        ((8, D), F32),
        ((8, D), F32),
        ((4, 8, 128), F32),
        ((3, 8, 128), F32),
        ((16, D), F32),
        ((8, D), F32),
        ((6, N_AR, D), F32),
        ((5, N_AR, D), F32),
        ((2, LANG_HEAD, D), BF),
        ((2, VIS_HEAD, D), BF),
        ((ROWS, D), BF),
        ((LANG_TAIL, D), BF),
        ((VIS_TAIL, D), BF),
        ((LANG_TAIL, D), F32),
        ((VIS_TAIL, D), F32),
    ]
    dma = pltpu.SemaphoreType.DMA
    return pl.pallas_call(
        partial(layer_kernel, total_items),
        out_shape=[jax.ShapeDtypeStruct(s, t) for s, t in shapes],
        in_specs=[vmem] * 4 + [smem] * 3 + [vmem] * (len(operands) - 7),
        out_specs=[vmem] * len(shapes),
        scratch_shapes=[pltpu.VMEM(s, t) for s, t in scratch]
        + [dma((N_SEND,)), dma((N_RECV,)), dma((7,)), dma((7,)), dma((7,)), dma((7,)), dma((1,))],
        compiler_params=pltpu.CompilerParams(
            collective_id=0, has_side_effects=True, vmem_limit_bytes=VMEM_LIMIT
        ),
    )(*operands)


def unpack_kernel(lo, vo, lg, vg, wgrad, vec, qb, *outs):
    (lo_out, vo_out, lg_out, vg_out, proj, qv, outw, outb, exp, expb, con, conb, gain, shift) = outs
    lo_out[...] = lo[...]
    vo_out[...] = vo[...]
    lg_out[...] = lg[...]
    vg_out[...] = vg[...]
    width = HALF_PAIR
    for b in range(3):
        for j, lane in enumerate((0, 2 * width, width)):
            proj[b, j] = wgrad[b, :, lane : lane + width]
        outw[b] = wgrad[b, :, 3 * width :].T
        for j in range(2):
            qv[b, j : j + 1] = qb[b : b + 1, j * width : (j + 1) * width]
    for stream in range(2):
        exp[stream] = wgrad[3 + stream]
        con[stream] = wgrad[5 + stream].T
    expb[...] = qb[3:5]
    outb[...] = vec[0:3]
    conb[...] = vec[3:5]
    gain[...] = vec[5:10]
    shift[...] = vec[10:15]


def unpack(packed, shapes):
    vmem = pl.BlockSpec(memory_space=pltpu.VMEM)
    return pl.pallas_call(
        unpack_kernel,
        out_shape=shapes,
        in_specs=[vmem] * len(packed),
        out_specs=[vmem] * len(shapes),
        compiler_params=pltpu.CompilerParams(vmem_limit_bytes=VMEM_LIMIT),
    )(*packed)


def on_device_fused(
    language_input,
    vision_input,
    word_lengths,
    region_counts,
    task_flags,
    language_cotangent,
    vision_cotangent,
    projection_weight,
    query_value_bias,
    output_weight,
    output_bias,
    expand_weight,
    expand_bias,
    contract_weight,
    contract_bias,
    norm_gain,
    norm_bias,
):
    packed = fused_layer(
        float(word_lengths.shape[0] * lax.axis_size("dp")),
        language_input,
        vision_input,
        language_cotangent,
        vision_cotangent,
        word_lengths,
        region_counts,
        task_flags,
        projection_weight,
        query_value_bias,
        output_weight,
        expand_weight,
        expand_bias,
        contract_weight,
        output_bias,
        contract_bias,
        norm_gain,
        norm_bias,
    )
    like = [
        (language_input, BF),
        (vision_input, BF),
        (language_input, F32),
        (vision_input, F32),
        (projection_weight, F32),
        (query_value_bias, F32),
        (output_weight, F32),
        (output_bias, F32),
        (expand_weight, F32),
        (expand_bias, F32),
        (contract_weight, F32),
        (contract_bias, F32),
        (norm_gain, F32),
        (norm_bias, F32),
    ]
    return tuple(unpack(packed, [jax.ShapeDtypeStruct(a.shape, t) for a, t in like]))


def solution(mesh):
    in_specs = (
        P(("dp", "mp"), None),
        P(("dp", "mp"), None),
        P("dp"),
        P("dp"),
        P("dp", None),
        P(("dp", "mp"), None),
        P(("dp", "mp"), None),
        P(None, None, "dp", "mp"),
        P(None, None, "mp"),
        P(None, "mp", "dp"),
        P(),
        P(None, "dp", "mp"),
        P(None, "mp"),
        P(None, "mp", "dp"),
        P(),
        P(),
        P(),
    )
    out_specs = (
        P(("dp", "mp"), None),
        P(("dp", "mp"), None),
        P(("dp", "mp"), None),
        P(("dp", "mp"), None),
        P(None, None, "dp", "mp"),
        P(None, None, "mp"),
        P(None, "mp", "dp"),
        P(),
        P(None, "dp", "mp"),
        P(None, "mp"),
        P(None, "mp", "dp"),
        P(),
        P(),
        P(),
    )
    fused = dict(mesh.shape) == {"dp": 8, "mp": 4}
    return jax.shard_map(
        on_device_fused if fused else on_device, mesh=mesh, in_specs=in_specs, out_specs=out_specs, check_vma=False
    )
```

```python
from functools import partial
import math

import jax
import jax.numpy as jnp
from jax import lax
from jax.experimental import pallas as pl
from jax.experimental.pallas import tpu as pltpu
from jax.sharding import PartitionSpec as P

D = 768
HEADS = 12
WORDS = 20
REGIONS = 36
D_MODEL = D
D_HEAD = D // HEADS

EPSILON = 1e-12
MASKED = -1e30


def layer_norm(summed, gain, shift):
    center = summed - jnp.mean(summed, -1, keepdims=True)
    scaled = lax.rsqrt(jnp.mean(center * center, -1, keepdims=True) + EPSILON)
    normed = center * scaled
    return (normed * gain + shift, normed, scaled)


def norm_back(upstream, normed, scaled, gain):
    through = upstream * gain
    inner = (
        through
        - jnp.mean(through, -1, keepdims=True)
        - normed * jnp.mean(through * normed, -1, keepdims=True)
    )
    return (scaled * inner, jnp.sum(upstream * normed, 0), jnp.sum(upstream, 0))


def split_heads(rows, item_count):
    head_size = D // HEADS
    return rows.reshape(
        item_count, rows.shape[0] // item_count, rows.shape[1] // head_size, head_size
    )


def join_heads(block):
    return block.reshape(block.shape[0] * block.shape[1], block.shape[2] * block.shape[3])


def project(rows, weight, bias, item_count):
    mapped = jnp.einsum("rd,jde->jre", rows, weight, preferred_element_type=jnp.float32)
    query = split_heads((mapped[0] + bias[0]).astype(jnp.bfloat16), item_count)
    keys = split_heads(mapped[1].astype(jnp.bfloat16), item_count)
    values = split_heads((mapped[2] + bias[1]).astype(jnp.bfloat16), item_count)
    return (query, keys, values)


def masked_scores(query, keys, valid):
    scores = jnp.einsum("inhd,imhd->ihnm", query, keys, preferred_element_type=jnp.float32) * (
        1.0 / math.sqrt(D // HEADS)
    )
    return jnp.where(valid[:, None, None, :], scores, MASKED)


def attend(query, keys, values, valid):
    scores = masked_scores(query, keys, valid)
    highest = jnp.max(scores, -1, keepdims=True)
    raised = jnp.exp(scores - highest)
    summed = jnp.sum(raised, -1, keepdims=True)
    context = jnp.einsum(
        "ihnm,imhd->inhd",
        (raised / summed).astype(jnp.bfloat16),
        values,
        preferred_element_type=jnp.float32,
    )
    return (join_heads(context).astype(jnp.bfloat16), highest + jnp.log(summed))


def attend_back(query, keys, values, valid, log_total, context_grad):
    factor = 1.0 / math.sqrt(D // HEADS)
    upstream = context_grad.reshape(query.shape)
    weights = jnp.exp(masked_scores(query, keys, valid) - log_total)
    weight_grad = jnp.einsum(
        "inhd,imhd->ihnm", upstream, values, preferred_element_type=jnp.float32
    )
    score_grad = (
        weights * (weight_grad - jnp.sum(weight_grad * weights, -1, keepdims=True))
    ).astype(jnp.bfloat16)
    query_grad = (
        jnp.einsum("ihnm,imhd->inhd", score_grad, keys, preferred_element_type=jnp.float32) * factor
    ).astype(jnp.bfloat16)
    keys_grad = (
        jnp.einsum("ihnm,inhd->imhd", score_grad, query, preferred_element_type=jnp.float32)
        * factor
    ).astype(jnp.bfloat16)
    values_grad = jnp.einsum(
        "ihnm,inhd->imhd",
        weights.astype(jnp.bfloat16),
        upstream,
        preferred_element_type=jnp.float32,
    ).astype(jnp.bfloat16)
    return (join_heads(query_grad), join_heads(keys_grad), join_heads(values_grad))


def project_back(rows, query_grad, keys_grad, values_grad):
    stacked = jnp.stack([query_grad, keys_grad, values_grad])
    weight_grad = jnp.einsum("rd,jre->jde", rows, stacked, preferred_element_type=jnp.float32)
    bias_grad = jnp.stack(
        [jnp.sum(query_grad.astype(jnp.float32), 0), jnp.sum(values_grad.astype(jnp.float32), 0)]
    )
    return (weight_grad, bias_grad, stacked)


def gather_rows(language_rows, vision_rows):
    return (
        lax.all_gather(language_rows, "mp", axis=0, tiled=True),
        lax.all_gather(vision_rows, "mp", axis=0, tiled=True),
    )


def rows_of(language_part, vision_part):
    return (
        lax.all_to_all(language_part, "mp", split_axis=0, concat_axis=1, tiled=True),
        lax.all_to_all(vision_part, "mp", split_axis=0, concat_axis=1, tiled=True),
    )


def gather_grads(language_rows, vision_rows):
    return (
        lax.all_gather(language_rows, "mp", axis=0, tiled=True),
        lax.all_gather(vision_rows, "mp", axis=0, tiled=True),
    )


def grads_of(language_part, vision_part):
    return (
        lax.all_to_all(language_part, "mp", split_axis=1, concat_axis=2, tiled=True),
        lax.all_to_all(vision_part, "mp", split_axis=1, concat_axis=2, tiled=True),
    )


def matmul(left, right):
    return jnp.dot(left, right, preferred_element_type=jnp.float32)


def on_device(
    language_input,
    vision_input,
    word_lengths,
    region_counts,
    task_flags,
    language_cotangent,
    vision_cotangent,
    projection_weight,
    query_value_bias,
    output_weight,
    output_bias,
    expand_weight,
    expand_bias,
    contract_weight,
    contract_bias,
    norm_gain,
    norm_bias,
):
    item_count = word_lengths.shape[0]
    flag_total = lax.psum(jnp.sum(task_flags, 0), "dp")
    projection, out_weight, expand, contract = (
        lax.all_gather(projection_weight, "dp", axis=2, tiled=True),
        lax.all_gather(output_weight, "dp", axis=2, tiled=True),
        lax.all_gather(expand_weight, "dp", axis=1, tiled=True),
        lax.all_gather(contract_weight, "dp", axis=2, tiled=True),
    )
    projection_full, out_full, expand_full, contract_full = (
        lax.all_gather(projection, "mp", axis=3, tiled=True),
        lax.all_gather(out_weight, "mp", axis=1, tiled=True),
        lax.all_gather(expand, "mp", axis=2, tiled=True),
        lax.all_gather(contract, "mp", axis=1, tiled=True),
    )
    valid = [
        jnp.arange(WORDS, dtype=jnp.int32)[None, :] < word_lengths[:, None],
        jnp.arange(REGIONS, dtype=jnp.int32)[None, :] < region_counts[:, None],
    ]
    row_counts = [WORDS, REGIONS]
    inputs = [language_input.astype(jnp.float32), vision_input.astype(jnp.float32)]
    cross_rows = gather_rows(language_input, vision_input)
    cross_parts = [
        project(cross_rows[stream], projection[0], query_value_bias[0], item_count)
        for stream in range(2)
    ]
    cross_context = []
    cross_total = []
    for stream in range(2):
        other = 1 - stream
        context, log_total = attend(
            cross_parts[stream][0], cross_parts[other][1], cross_parts[other][2], valid[other]
        )
        cross_context.append(context)
        cross_total.append(log_total)
    moved = rows_of(cross_context[0], cross_context[1])
    branch = [matmul(moved[stream], out_full[0]) for stream in range(2)]
    first = [
        layer_norm(branch[stream] + output_bias[0] + inputs[stream], norm_gain[0], norm_bias[0])
        for stream in range(2)
    ]
    first_out = [first[stream][0].astype(jnp.bfloat16) for stream in range(2)]
    self_rows = gather_rows(first_out[0], first_out[1])
    self_parts = [
        project(self_rows[stream], projection[1 + stream], query_value_bias[1 + stream], item_count)
        for stream in range(2)
    ]
    self_context = []
    self_total = []
    for stream in range(2):
        context, log_total = attend(
            self_parts[stream][0], self_parts[stream][1], self_parts[stream][2], valid[stream]
        )
        self_context.append(context)
        self_total.append(log_total)
    moved = rows_of(self_context[0], self_context[1])
    branch = [matmul(moved[stream], out_full[1 + stream]) for stream in range(2)]
    second = [
        layer_norm(
            branch[stream] + output_bias[1 + stream] + first_out[stream].astype(jnp.float32),
            norm_gain[1 + stream],
            norm_bias[1 + stream],
        )
        for stream in range(2)
    ]
    second_out = [second[stream][0].astype(jnp.bfloat16) for stream in range(2)]
    feed_rows = gather_rows(second_out[0], second_out[1])
    before = [
        matmul(feed_rows[stream], expand[stream]) + expand_bias[stream] for stream in range(2)
    ]
    hidden = [
        jax.nn.gelu(before[stream], approximate=False).astype(jnp.bfloat16) for stream in range(2)
    ]
    moved = rows_of(hidden[0], hidden[1])
    branch = [matmul(moved[stream], contract_full[stream]) for stream in range(2)]
    third = [
        layer_norm(
            branch[stream] + contract_bias[stream] + second_out[stream].astype(jnp.float32),
            norm_gain[3 + stream],
            norm_bias[3 + stream],
        )
        for stream in range(2)
    ]
    language_out = third[0][0].astype(jnp.bfloat16)
    vision_out = third[1][0].astype(jnp.bfloat16)
    item_scale = task_flags.astype(jnp.float32) * (
        item_count * lax.axis_size("dp") / flag_total.astype(jnp.float32)
    )
    shard_index = lax.axis_index("mp")
    upstream = []
    for stream, cotangent in enumerate([language_cotangent, vision_cotangent]):
        per_row = jnp.repeat(
            item_scale[:, stream],
            row_counts[stream],
            total_repeat_length=item_count * row_counts[stream],
        )
        shard_rows = cotangent.shape[0]
        row_scale = lax.dynamic_slice_in_dim(per_row, shard_index * shard_rows, shard_rows)
        upstream.append(cotangent.astype(jnp.float32) * row_scale[:, None])
    third_back = [
        norm_back(upstream[stream], third[stream][1], third[stream][2], norm_gain[3 + stream])
        for stream in range(2)
    ]
    sent = gather_grads(
        third_back[0][0].astype(jnp.bfloat16), third_back[1][0].astype(jnp.bfloat16)
    )
    expand_local = []
    expand_bias_local = []
    contract_local = []
    before_grads = []
    for stream in range(2):
        hidden_grad = jnp.einsum(
            "rd,fd->rf", sent[stream], contract[stream], preferred_element_type=jnp.float32
        )
        contract_local.append(
            jnp.einsum(
                "rf,rd->fd", hidden[stream], sent[stream], preferred_element_type=jnp.float32
            )
        )
        unused, pull = jax.vjp(partial(jax.nn.gelu, approximate=False), before[stream])
        before_grad = pull(hidden_grad)[0].astype(jnp.bfloat16)
        expand_local.append(
            jnp.einsum(
                "rd,rf->df", feed_rows[stream], before_grad, preferred_element_type=jnp.float32
            )
        )
        expand_bias_local.append(jnp.sum(before_grad.astype(jnp.float32), 0))
        before_grads.append(before_grad[None])
    moved = grads_of(before_grads[0], before_grads[1])
    back = [
        jnp.einsum(
            "rf,df->rd", moved[stream][0], expand_full[stream], preferred_element_type=jnp.float32
        )
        for stream in range(2)
    ]
    second_grad = [third_back[stream][0] + back[stream] for stream in range(2)]
    second_back = [
        norm_back(second_grad[stream], second[stream][1], second[stream][2], norm_gain[1 + stream])
        for stream in range(2)
    ]
    sent = gather_grads(
        second_back[0][0].astype(jnp.bfloat16), second_back[1][0].astype(jnp.bfloat16)
    )
    self_weight = []
    self_bias = []
    self_out = []
    stacks = []
    for stream in range(2):
        context_grad = jnp.einsum(
            "rd,ed->re", sent[stream], out_weight[1 + stream], preferred_element_type=jnp.float32
        ).astype(jnp.bfloat16)
        self_out.append(
            jnp.einsum(
                "re,rd->ed", self_context[stream], sent[stream], preferred_element_type=jnp.float32
            )
        )
        grads = attend_back(
            self_parts[stream][0],
            self_parts[stream][1],
            self_parts[stream][2],
            valid[stream],
            self_total[stream],
            context_grad,
        )
        weight_part, bias_part, stacked = project_back(
            self_rows[stream], grads[0], grads[1], grads[2]
        )
        self_weight.append(weight_part)
        self_bias.append(bias_part)
        stacks.append(stacked)
    moved = grads_of(stacks[0], stacks[1])
    back = [
        jnp.einsum(
            "jre,jde->rd",
            moved[stream],
            projection_full[1 + stream],
            preferred_element_type=jnp.float32,
        )
        for stream in range(2)
    ]
    first_grad = [second_back[stream][0] + back[stream] for stream in range(2)]
    first_back = [
        norm_back(first_grad[stream], first[stream][1], first[stream][2], norm_gain[0])
        for stream in range(2)
    ]
    sent = gather_grads(
        first_back[0][0].astype(jnp.bfloat16), first_back[1][0].astype(jnp.bfloat16)
    )
    cross_out = jnp.einsum(
        "re,rd->ed", cross_context[0], sent[0], preferred_element_type=jnp.float32
    ) + jnp.einsum("re,rd->ed", cross_context[1], sent[1], preferred_element_type=jnp.float32)
    triples = [[None, None, None], [None, None, None]]
    for stream in range(2):
        other = 1 - stream
        context_grad = jnp.einsum(
            "rd,ed->re", sent[stream], out_weight[0], preferred_element_type=jnp.float32
        ).astype(jnp.bfloat16)
        grads = attend_back(
            cross_parts[stream][0],
            cross_parts[other][1],
            cross_parts[other][2],
            valid[other],
            cross_total[stream],
            context_grad,
        )
        triples[stream][0] = grads[0]
        triples[other][1] = grads[1]
        triples[other][2] = grads[2]
    results = [
        project_back(cross_rows[stream], triples[stream][0], triples[stream][1], triples[stream][2])
        for stream in range(2)
    ]
    cross_weight = results[0][0] + results[1][0]
    cross_bias = results[0][1] + results[1][1]
    moved = grads_of(results[0][2], results[1][2])
    back = [
        jnp.einsum(
            "jre,jde->rd", moved[stream], projection_full[0], preferred_element_type=jnp.float32
        )
        for stream in range(2)
    ]
    language_grad = first_back[0][0] + back[0]
    vision_grad = first_back[1][0] + back[1]
    projection_stack = jnp.stack([cross_weight, self_weight[0], self_weight[1]])
    output_stack = jnp.stack([cross_out, self_out[0], self_out[1]])
    projection_grad, output_weight_grad, expand_grad, contract_grad = (
        lax.psum_scatter(projection_stack, "dp", scatter_dimension=2, tiled=True),
        lax.psum_scatter(output_stack, "dp", scatter_dimension=2, tiled=True),
        lax.psum_scatter(jnp.stack(expand_local), "dp", scatter_dimension=1, tiled=True),
        lax.psum_scatter(jnp.stack(contract_local), "dp", scatter_dimension=2, tiled=True),
    )
    query_value_grad, expand_bias_grad = lax.psum(
        (jnp.stack([cross_bias, self_bias[0], self_bias[1]]), jnp.stack(expand_bias_local)), "dp"
    )
    output_bias_local = jnp.stack(
        [
            jnp.sum(first_back[0][0], 0) + jnp.sum(first_back[1][0], 0),
            jnp.sum(second_back[0][0], 0),
            jnp.sum(second_back[1][0], 0),
        ]
    )
    contract_bias_local = jnp.stack([jnp.sum(third_back[0][0], 0), jnp.sum(third_back[1][0], 0)])
    gain_local = jnp.stack(
        [
            first_back[0][1] + first_back[1][1],
            second_back[0][1],
            second_back[1][1],
            third_back[0][1],
            third_back[1][1],
        ]
    )
    shift_local = jnp.stack(
        [
            first_back[0][2] + first_back[1][2],
            second_back[0][2],
            second_back[1][2],
            third_back[0][2],
            third_back[1][2],
        ]
    )
    output_bias_grad, contract_bias_grad, norm_gain_grad, norm_bias_grad = lax.psum(
        (output_bias_local, contract_bias_local, gain_local, shift_local), ("dp", "mp")
    )
    return (
        language_out,
        vision_out,
        language_grad,
        vision_grad,
        projection_grad,
        query_value_grad,
        output_weight_grad,
        output_bias_grad,
        expand_grad,
        expand_bias_grad,
        contract_grad,
        contract_bias_grad,
        norm_gain_grad,
        norm_bias_grad,
    )


MESH = pl.DeviceIdType.MESH
BF = jnp.bfloat16
F32 = jnp.float32
SLOTS = 4
RL = SLOTS * WORDS
RV = SLOTS * REGIONS
ROWS = RL + RV
SHARE = 96
HALF_PAIR = 2 * SHARE
LANG_HEAD = 16
VIS_HEAD = 32
LANG_TAIL = 32
VIS_TAIL = 64
N_AR = 48
NT = 3
TILE = 256
VMEM_LIMIT = 63 * 1024 * 1024


def dot_nn(left, right):
    return lax.dot_general(left, right, (((1,), (0,)), ((), ())), preferred_element_type=F32)


def dot_nt(left, right):
    return lax.dot_general(left, right, (((1,), (1,)), ((), ())), preferred_element_type=F32)


def dot_tn(left, right):
    return lax.dot_general(left, right, (((0,), (0,)), ((), ())), preferred_element_type=F32)


def head_mask(first_lane, dtype):
    lane = lax.broadcasted_iota(jnp.int32, (1, TILE), 1) - first_lane
    return [
        jnp.where((lane >= 64 * h) & (lane < 64 * h + 64), 1.0, 0.0).astype(dtype) for h in range(3)
    ]


def select_rows(shape, shift, low, high):
    row = lax.broadcasted_iota(jnp.int32, shape, 0)
    column = lax.broadcasted_iota(jnp.int32, shape, 1)
    return jnp.where((column - row == shift) & (row >= low) & (row < high), 1.0, 0.0)


def layer_kernel(
    total_items,
    lang,
    vis,
    lcot,
    vcot,
    lengths,
    regions,
    flags,
    projection,
    query_value,
    out_weight,
    expand,
    expand_b,
    contract,
    out_bias,
    contract_b,
    gains,
    shifts,
    lang_out,
    vis_out,
    lang_grad,
    vis_grad,
    wgrad,
    vec_out,
    qb_out,
    W,
    G,
    R1,
    R2,
    A,
    KV,
    RSB,
    STG,
    QVK,
    D,
    C,
    H,
    GP,
    PCL,
    PCV,
    PSL,
    PSV,
    PART,
    PZ,
    NORM,
    RSTD,
    DZ,
    COT,
    SH,
    FLAG,
    QO,
    QB,
    QR,
    CA,
    CR,
    VG,
    QG,
    AVA,
    AVR,
    HL,
    HV,
    OUTS,
    TLO,
    TVO,
    TLG,
    TVG,
    ssem,
    rsem,
    wsem,
    wsem_z,
    gsem,
    gsem2,
    lsem,
):
    d = lax.axis_index("dp")
    z = lax.axis_index("mp")
    c = d % 2
    k = d // 2
    k_flip = [k + 1 - 2 * (k % 2), (k + 2) % 4, 3 - k]
    sib = (d + 1 - 2 * c, z)
    zp = (d, z + 1 - 2 * (z % 2))
    z2 = (z + 2) % 4
    up = (d, (z + 1) % 4)
    down = (d, (z + 3) % 4)
    plane = [(2 * kf + c, z) for kf in k_flip]
    far = (2 * k + 1, z2)

    pending = []
    counter = [0, 0]

    def remote(src, dst, send, recv, device):
        return pltpu.make_async_remote_copy(
            src_ref=src, dst_ref=dst, send_sem=send, recv_sem=recv, device_id=device, device_id_type=MESH
        )

    def send(src, dst, device, recv=None, keep=True):
        slot = counter[0]
        counter[0] += 1
        if recv is None:
            recv = rsem.at[counter[1]]
            counter[1] += 1
        copy = remote(src, dst, ssem.at[slot], recv, device)
        copy.start()
        if keep:
            pending.append(copy)
        return copy

    def wait_bytes(ref, sem):
        pltpu.make_async_copy(ref, ref, sem).wait()

    def arrived(name, *copies):
        with jax.named_scope("wait_" + name):
            for copy in copies:
                copy.wait_recv()

    barrier = pltpu.get_barrier_semaphore()
    peers = [sib, up, down, (d, z2), (d + 1 - 2 * c, z2)] + plane
    with jax.named_scope("barrier"):
        for peer in peers:
            pl.semaphore_signal(barrier, inc=1, device_id=peer, device_id_type=MESH)
        pl.semaphore_wait(barrier, len(peers))

    def weight_first(w):
        row = pl.ds(pl.multiple_of(d * SHARE, 16), SHARE)
        slot = counter[0]
        counter[0] += 1
        share = SH.at[w] if w < 3 else (expand.at[w - 3] if w < 5 else contract.at[w - 5])
        near = remote(share, W.at[w, row], ssem.at[slot], wsem_z.at[w], sib)
        own = pltpu.make_async_copy(share, W.at[w, row], wsem_z.at[w])

        @pl.when(c == 1)
        def _():
            near.start()

        @pl.when(c == 0)
        def _():
            own.start()

        send(share, W.at[w, row], far, wsem_z.at[w])
        return near

    def place(width, first):
        row = lax.broadcasted_iota(jnp.int32, (width, D_MODEL), 0)
        column = lax.broadcasted_iota(jnp.int32, (width, D_MODEL), 1)
        return jnp.where(column - row == first, 1.0, 0.0).astype(BF)

    @jax.named_scope("share")
    def attention_share(b):
        SH[b] = (
            dot_nn(projection[b, 0], place(HALF_PAIR, 0))
            + dot_nn(projection[b, 2], place(HALF_PAIR, HALF_PAIR))
            + dot_nn(projection[b, 1], place(HALF_PAIR, 2 * HALF_PAIR))
            + dot_tn(out_weight[b], place(HALF_PAIR, 3 * HALF_PAIR))
        ).astype(BF)

    nears = []
    heads = [
        send(lang.at[pl.ds(0, LANG_HEAD)], HL.at[0], down),
        send(vis.at[pl.ds(0, VIS_HEAD)], HV.at[0], down),
        send(lcot.at[pl.ds(0, LANG_HEAD)], HL.at[1], down),
        send(vcot.at[pl.ds(0, VIS_HEAD)], HV.at[1], down),
    ]
    attention_share(0)
    nears.append(weight_first(0))

    n_items = lengths.shape[0]
    first_item = 3 * z + jnp.minimum(z, 1)
    KV[0] = jnp.full(KV.shape[1:], -1.0, F32)
    for row, source, size in ((0, lengths, WORDS), (1, regions, REGIONS)):
        lane = lax.broadcasted_iota(jnp.int32, (1, TILE), 1)
        owner = jnp.full((1, TILE), -1.0, F32)
        slab_row = lax.broadcasted_iota(jnp.int32, (SLOTS * size, 1), 0)
        flag = jnp.zeros((SLOTS * size, 1), F32)
        for j in range(SLOTS):
            item = jnp.minimum(first_item + j, n_items - 1)
            valid = (lane >= j * size) & (lane < j * size + source[item]) & (lane < (j + 1) * size)
            owner = jnp.where(valid, float(j), owner)
            inside = (slab_row >= j * size) & (slab_row < (j + 1) * size)
            flag = jnp.where(inside, flags[row, item].astype(F32), flag)
        KV[0, row : row + 1] = owner
        FLAG[row * RL : row * RL + SLOTS * size] = flag
        count = flags[row, 0]
        for j in range(1, n_items):
            count = count + flags[row, j]
        CA[0, row : row + 1] = jnp.full((1, 128), count.astype(F32), F32)
    kv_sib = send(KV.at[0], KV.at[1], sib)
    kv_zp = send(KV.at[0], KV.at[2], zp)
    count_copies = [send(CA.at[0], CR.at[0], sib)]
    QO[...] = jnp.zeros_like(QO)
    for b in range(3):
        QO[b : b + 1, 0:HALF_PAIR] = query_value[b, 0:1]
        QO[b : b + 1, HALF_PAIR : 2 * HALF_PAIR] = query_value[b, 1:2]
    QO[3:5] = expand_b[...]
    bias_swap = send(QO, QR, (d, z2))
    attention_share(1)
    attention_share(2)

    pair_rows = pl.ds(pl.multiple_of(k * HALF_PAIR, 16), HALF_PAIR)

    def weight_second(w):
        with jax.named_scope("wait_weight_pair"):
            wait_bytes(W.at[w, pair_rows], wsem_z.at[w])
        for peer in plane:
            send(W.at[w, pair_rows], W.at[w, pair_rows], peer, wsem.at[w])

    def weight_ready(w):
        with jax.named_scope("wait_weight_full"):
            wait_bytes(W.at[w, pl.ds(0, 3 * HALF_PAIR)], wsem.at[w])

    off_l = jnp.where(z == 0, 0, 20 - 5 * z)
    off_v = jnp.where(z == 0, 0, 36 - 9 * z)
    n_l = jnp.where(z == 0, 4 * WORDS, 3 * WORDS)
    n_v = jnp.where(z == 0, 4 * REGIONS, 3 * REGIONS)
    own_l = lang.shape[0]
    own_v = vis.shape[0]
    arrived("heads", *heads)
    for index, (source_l, source_v) in enumerate([(lang, vis), (lcot, vcot)]):
        slab_l = dot_nn(select_rows((RL, own_l), off_l, 0, n_l).astype(BF), source_l[...]) + dot_nn(
            select_rows((RL, LANG_HEAD), off_l - own_l, 0, n_l).astype(BF), HL[index]
        )
        slab_v = dot_nn(select_rows((RV, own_v), off_v, 0, n_v).astype(BF), source_v[...]) + dot_nn(
            select_rows((RV, VIS_HEAD), off_v - own_v, 0, n_v).astype(BF), HV[index]
        )
        if index == 0:
            A[0, 0, 0:RL] = slab_l.astype(BF)
            A[0, 0, RL:ROWS] = slab_v.astype(BF)
        else:
            COT[0:RL] = slab_l.astype(BF)
            COT[RL:ROWS] = slab_v.astype(BF)

    def gather_start(p):
        return (send(A.at[p, 0], A.at[p, 1], sib), send(A.at[p, 0], A.at[p, 2], zp))

    def gather_forward(p, copies):
        arrived("rows_z", copies[1])
        return send(A.at[p, 2], A.at[p, 3], sib)

    stage_used = [None, None, None]

    def stage_free(index):
        if stage_used[index] is not None:
            stage_used[index].wait_send()
            stage_used[index] = None

    def partial_nt(g, lhs_ref, r0, r1, w, lanes):
        rows = r1 - r0

        def body(column):
            lhs = lhs_ref[2 * g : 2 * g + 2, r0:r1, :]
            lhs = lhs.reshape(2 * rows, lhs.shape[-1])
            out = dot_nt(lhs, W[w, column, lanes])
            if g == 0:
                PART[r0:r1, column] = out[:rows]
                STG[0, r0:r1, column] = out[rows:].astype(BF)
            else:
                PZ[r0:r1, column] = out[:rows]
                STG[1, r0:r1, column] = out[rows:].astype(BF)

        with jax.named_scope("partial_sums"):
            over_tiles(body)

    def reduce_first():
        copy = send(STG.at[0], RSB.at[0], sib, keep=False)
        stage_used[0] = copy
        return copy

    def reduce_second():
        across = send(STG.at[1], RSB.at[1], sib, keep=False)
        stage_used[1] = across
        arrived("sums_core", across)
        stage_free(2)
        STG[2] = (PZ[...] + RSB[1].astype(F32)).astype(BF)
        copy = send(STG.at[2], RSB.at[2], zp, keep=False)
        stage_used[2] = copy
        return copy

    def reduced(r0, r1):
        return PART[r0:r1] + RSB[0, r0:r1].astype(F32) + RSB[2, r0:r1].astype(F32)

    mask_q = head_mask(0, BF)
    mask_c = head_mask(64, BF)
    mask_q32 = head_mask(0, F32)
    mask_c32 = head_mask(64, F32)
    factor = 1.0 / math.sqrt(D_HEAD)

    def attend_slab(QV, Cb, PL, PV, crossed, s):
        def one(q0, q1, k0, k1, words_keys, P):
            nq, nk = q1 - q0, k1 - k0
            query = QV[s, q0:q1, 0:256]
            keys = QV[s, k0:k1, 384:640]
            values = QV[s, k0:k1, 128:384]
            query_size = WORDS if q0 == 0 else REGIONS
            spread = jnp.concatenate([query * mask_q[h] for h in range(3)], 0)
            scores = dot_nt(spread, keys) * factor
            row = lax.broadcasted_iota(jnp.int32, (nq, nk), 0)
            item = jnp.zeros((nq, nk), F32)
            for j in range(1, SLOTS):
                item = item + jnp.where(row >= j * query_size, 1.0, 0.0)
            column = KV[s, 0:1, 0:nk] if words_keys else KV[s, 1:2, 0:nk]
            same = item == column
            scores = jnp.where(same[None], scores.reshape(3, nq, nk), MASKED)
            raised = jnp.exp(scores - jnp.max(scores, -1, keepdims=True))
            weights = (raised / jnp.sum(raised, -1, keepdims=True)).astype(BF).reshape(3 * nq, nk)
            P[s] = weights
            context = dot_nn(weights, values).reshape(3, nq, TILE)
            Cb[s, q0:q1] = (
                context[0] * mask_c32[0] + context[1] * mask_c32[1] + context[2] * mask_c32[2]
            ).astype(BF)

        if crossed:
            one(0, RL, RL, ROWS, False, PL)
            one(RL, ROWS, 0, RL, True, PV)
        else:
            one(0, RL, 0, RL, True, PL)
            one(RL, ROWS, RL, ROWS, False, PV)

    def attend_back_slab(QV, Cb, PL, PV, crossed, s):
        def one(q0, q1, k0, k1, P):
            nq, nk = q1 - q0, k1 - k0
            query = QV[s, q0:q1, 0:256]
            keys = QV[s, k0:k1, 384:640]
            values = QV[s, k0:k1, 128:384]
            spread = jnp.concatenate([query * mask_q[h] for h in range(3)], 0)
            upstream = D[s, q0:q1, 512:768]
            up_spread = jnp.concatenate([upstream * mask_c[h] for h in range(3)], 0)
            weights = P[s]
            weights32 = weights.astype(F32)
            weight_grad = dot_nt(up_spread, values)
            score_grad = (
                weights32
                * (weight_grad - jnp.sum(weight_grad * weights32, -1, keepdims=True))
            ).astype(BF)
            dq = dot_nn(score_grad, keys).reshape(3, nq, TILE)
            dq = (dq[0] * mask_q32[0] + dq[1] * mask_q32[1] + dq[2] * mask_q32[2]) * factor
            dk = dot_tn(score_grad, spread) * factor
            dv = dot_tn(weights, up_spread)
            return dq, dk, dv

        if crossed:
            dq_l, dk_v, dv_v = one(0, RL, RL, ROWS, PL)
            dq_v, dk_l, dv_l = one(RL, ROWS, 0, RL, PV)
        else:
            dq_l, dk_l, dv_l = one(0, RL, 0, RL, PL)
            dq_v, dk_v, dv_v = one(RL, ROWS, RL, ROWS, PV)
        for r0, r1, dq, dk, dv in ((0, RL, dq_l, dk_l, dv_l), (RL, ROWS, dq_v, dk_v, dv_v)):
            D[s, r0:r1, 0:128] = dq[:, :128].astype(BF)
            D[s, r0:r1, 128:256] = (dq[:, 128:] + dv[:, :128]).astype(BF)
            D[s, r0:r1, 256:384] = dv[:, 128:].astype(BF)
            D[s, r0:r1, 384:640] = dk.astype(BF)
            D[s, r0:r1, 640:768] = jnp.zeros((r1 - r0, 128), BF)

    def grouped(g, body):
        for s in (2 * g, 2 * g + 1):
            body(s)

    def over_tiles(body):
        for n in range(NT):
            body(slice(n * TILE, (n + 1) * TILE))

    @jax.named_scope("norm")
    def forward_norm(value, index, gain_row, r0, r1):
        center = value - jnp.mean(value, -1, keepdims=True)
        scaled = lax.rsqrt(jnp.mean(center * center, -1, keepdims=True) + EPSILON)
        normed = center * scaled
        NORM[index, r0:r1] = normed
        RSTD[index, r0:r1] = scaled
        return normed * gains[gain_row : gain_row + 1] + shifts[gain_row : gain_row + 1]

    @jax.named_scope("norm_gradient")
    def backward_norm(upstream, index, gain_row, bias_row, r0, r1):
        normed = NORM[index, r0:r1]
        through = upstream * gains[gain_row : gain_row + 1]
        inner = (
            through
            - jnp.mean(through, -1, keepdims=True)
            - normed * jnp.mean(through * normed, -1, keepdims=True)
        )
        result = RSTD[index, r0:r1] * inner
        VG[5 + gain_row : 6 + gain_row] += jnp.sum(upstream * normed, 0, keepdims=True)
        VG[10 + gain_row : 11 + gain_row] += jnp.sum(upstream, 0, keepdims=True)
        VG[bias_row : bias_row + 1] += jnp.sum(result, 0, keepdims=True)
        return result

    both = ((0, RL), (RL, ROWS))
    all_rows = ((0, ROWS),)

    def rows_of_group(p, g, r0, r1):
        return A[p, 2 * g : 2 * g + 2, r0:r1, :].reshape(2 * (r1 - r0), D_MODEL)

    def attention_forward(p, streams, QV, Cb, PL, PV, crossed, ready, between):
        copies = gather_start(p)
        ready()
        for g in range(2):
            if g == 0:
                arrived("rows_core", copies[0])
            else:
                arrived("rows_far", forward)
            for r0, r1, w in streams:
                rows = r1 - r0

                def project_tile(column, r0=r0, r1=r1, w=w, rows=rows):
                    mapped = dot_nn(rows_of_group(p, g, r0, r1), W[w, :, column]) + QB[w : w + 1, column]
                    QV[2 * g : 2 * g + 2, r0:r1, column] = mapped.astype(BF).reshape(2, rows, TILE)

                with jax.named_scope("project"):
                    over_tiles(project_tile)
            if g == 0:
                forward = gather_forward(p, copies)
            with jax.named_scope("attend"):
                grouped(g, lambda s: attend_slab(QV, Cb, PL, PV, crossed, s))
            stage_free(g)
            for r0, r1, w in streams:
                partial_nt(g, Cb, r0, r1, w, slice(512, 768))
            if g == 0:
                first = reduce_first()
                between()
            else:
                second = reduce_second()
        arrived("sums", first, second)

    VG[...] = jnp.zeros_like(VG)
    QG[...] = jnp.zeros_like(QG)

    def ready_cross():
        weight_second(0)
        nears.append(weight_first(1))
        nears.append(weight_first(2))
        kv_sib.wait_recv()
        kv_zp.wait_recv()
        kv_far = send(KV.at[2], KV.at[3], sib)
        bias_swap.wait_recv()
        QB[...] = jnp.where(c == 1, QR[...], QO[...])
        weight_ready(0)
        kv_far.wait_recv()

    def between_cross():
        weight_second(1)
        weight_second(2)
        nears.append(weight_first(3))
        nears.append(weight_first(4))
        count_copies[0].wait_recv()
        CA[1] = CA[0] + CR[0]
        count_copies.append(send(CA.at[1], CR.at[1], plane[0]))

    attention_forward(
        0, ((0, ROWS, 0),), QVK.at[0], C.at[0], PCL, PCV, True, ready_cross, between_cross
    )
    for r0, r1 in both:
        value = reduced(r0, r1) + out_bias[0:1] + A[0, 0, r0:r1].astype(F32)
        A[1, 0, r0:r1] = forward_norm(value, 0, 0, r0, r1).astype(BF)

    def ready_self():
        weight_second(3)
        weight_second(4)
        nears.append(weight_first(5))
        nears.append(weight_first(6))
        weight_ready(1)
        weight_ready(2)

    def between_self():
        weight_second(5)
        weight_second(6)
        count_copies[1].wait_recv()
        CA[2] = CA[1] + CR[1]
        count_copies.append(send(CA.at[2], CR.at[2], plane[1]))

    attention_forward(
        1, ((0, RL, 1), (RL, ROWS, 2)), QVK.at[1], C.at[1], PSL, PSV, False, ready_self, between_self
    )
    for stream, (r0, r1) in enumerate(both):
        value = reduced(r0, r1) + out_bias[1 + stream : 2 + stream] + A[1, 0, r0:r1].astype(F32)
        A[2, 0, r0:r1] = forward_norm(value, 1, 1 + stream, r0, r1).astype(BF)

    copies = gather_start(2)
    for g in range(2):
        if g == 0:
            arrived("rows_core", copies[0])
            weight_ready(3)
            weight_ready(4)
        else:
            arrived("rows_far", forward)
        for stream, (r0, r1) in enumerate(both):
            rows = r1 - r0

            def expand_tile(column, r0=r0, r1=r1, stream=stream, rows=rows):
                before = (
                    dot_nn(rows_of_group(2, g, r0, r1), W[3 + stream, :, column])
                    + QB[3 + stream : 4 + stream, column]
                )
                half = 0.5 * (1.0 + lax.erf(before * math.sqrt(0.5)))
                slope = half + before * jnp.exp(-0.5 * before * before) * (
                    1.0 / math.sqrt(2.0 * math.pi)
                )
                H[2 * g : 2 * g + 2, r0:r1, column] = (before * half).astype(BF).reshape(2, rows, TILE)
                GP[2 * g : 2 * g + 2, r0:r1, column] = slope.astype(BF).reshape(2, rows, TILE)

            with jax.named_scope("expand"):
                over_tiles(expand_tile)
        if g == 0:
            forward = gather_forward(2, copies)
            weight_ready(5)
            weight_ready(6)
        stage_free(g)
        for stream, (r0, r1) in enumerate(both):
            partial_nt(g, H, r0, r1, 5 + stream, slice(0, 768))
        if g == 0:
            first = reduce_first()
            count_copies[2].wait_recv()
            CA[3] = CA[2] + CR[2]
        else:
            second = reduce_second()
    arrived("sums", first, second)

    for stream, (r0, r1) in enumerate(both):
        value = reduced(r0, r1) + contract_b[stream : stream + 1] + A[2, 0, r0:r1].astype(F32)
        OUTS[r0:r1] = forward_norm(value, 2, 3 + stream, r0, r1).astype(BF)
        scale = total_items / CA[3, stream : stream + 1, 0:1]
        upstream = COT[r0:r1].astype(F32) * (FLAG[r0:r1] * scale)
        result = backward_norm(upstream, 2, 3 + stream, 3 + stream, r0, r1)
        DZ[r0:r1] = result
        A[3, 0, r0:r1] = result.astype(BF)
    copies = gather_start(3)
    tail_out = [
        send(OUTS.at[pl.ds(RL - LANG_TAIL, LANG_TAIL)], TLO, up),
        send(OUTS.at[pl.ds(ROWS - VIS_TAIL, VIS_TAIL)], TVO, up),
    ]

    def weight_grad(w, lhs_p, rhs_ref, r0, r1, rhs_lanes=slice(0, 768)):
        rows = SLOTS * (r1 - r0)

        def step(column):
            left = A[lhs_p, :, r0:r1, column].reshape(rows, TILE)
            right = rhs_ref[:, r0:r1, rhs_lanes]
            right = right.reshape(rows, right.shape[-1])
            G[w, column, rhs_lanes] = dot_tn(left, right).astype(BF)

        with jax.named_scope("weight_gradient"):
            over_tiles(step)

    def attention_weight_grad(w, x_p, b_p, Cb, r0, r1):
        weight_grad(w, x_p, D, r0, r1, slice(0, 512))
        rows = SLOTS * (r1 - r0)

        def step(column):
            left = A[x_p, :, r0:r1, column].reshape(rows, TILE)
            right = D[:, r0:r1, 512:768].reshape(rows, TILE)
            left_b = A[b_p, :, r0:r1, column].reshape(rows, TILE)
            right_b = Cb[:, r0:r1, :].reshape(rows, TILE)
            G[w, column, 512:768] = (dot_tn(left, right) + dot_tn(left_b, right_b)).astype(BF)

        with jax.named_scope("weight_gradient"):
            over_tiles(step)

    @jax.named_scope("bias_gradient")
    def bias_grad(row, r0, r1):
        total = jnp.zeros((1, D_MODEL), F32)
        for s in range(SLOTS):
            total = total + jnp.sum(D[s, r0:r1].astype(F32), 0, keepdims=True)
        QG[row : row + 1] = total

    def grad_first(w):
        for j in range(3):
            rows = pl.ds(pl.multiple_of(k_flip[j] * HALF_PAIR, 16), HALF_PAIR)
            send(G.at[w, rows], R1.at[j, w], plane[j], gsem.at[w])

    grad_nears = []

    def grad_second(w):
        with jax.named_scope("wait_grad_plane"):
            wait_bytes(R1.at[:, w], gsem.at[w])
        total = G[w, pair_rows].astype(F32)
        for j in range(3):
            total = total + R1[j, w].astype(F32)
        G[w, pair_rows] = total.astype(BF)
        low = pl.ds(pl.multiple_of(k * HALF_PAIR, 16), SHARE)
        high = pl.ds(pl.multiple_of(k * HALF_PAIR + SHARE, 16), SHARE)
        slot = counter[0]
        counter[0] += 2
        own = pltpu.make_async_copy(G.at[w, low], R2.at[0, w], gsem2.at[w])
        near = remote(G.at[w, high], R2.at[0, w], ssem.at[slot], gsem2.at[w], sib)
        far_low = remote(G.at[w, low], R2.at[1, w], ssem.at[slot], gsem2.at[w], (2 * k, z2))
        far_high = remote(G.at[w, high], R2.at[1, w], ssem.at[slot + 1], gsem2.at[w], (2 * k + 1, z2))

        @pl.when(c == 0)
        def _():
            own.start()
            near.start()

        @pl.when(c == 1)
        def _():
            far_low.start()
            far_high.start()

        grad_nears.append((near, far_low, far_high))

    def grad_last(w):
        with jax.named_scope("wait_grad_last"):
            wait_bytes(R2.at[:, w], gsem2.at[w])
        wgrad[w] = R2[0, w].astype(F32) + R2[1, w].astype(F32)

    for g in range(2):
        if g == 0:
            arrived("rows_core", copies[0])
        else:
            arrived("rows_far", forward)
        for stream, (r0, r1) in enumerate(both):
            rows = r1 - r0

            def hidden_tile(column, r0=r0, r1=r1, stream=stream, rows=rows):
                up_hidden = dot_nn(rows_of_group(3, g, r0, r1), W[5 + stream, :, column])
                slope = GP[2 * g : 2 * g + 2, r0:r1, column].reshape(2 * rows, TILE)
                D[2 * g : 2 * g + 2, r0:r1, column] = (
                    (up_hidden * slope.astype(F32)).astype(BF).reshape(2, rows, TILE)
                )

            with jax.named_scope("hidden_gradient"):
                over_tiles(hidden_tile)
        if g == 0:
            forward = gather_forward(3, copies)
        stage_free(g)
        for stream, (r0, r1) in enumerate(both):
            partial_nt(g, D, r0, r1, 3 + stream, slice(0, 768))
        if g == 0:
            first = reduce_first()
        else:
            second = reduce_second()
    for stream, (r0, r1) in enumerate(both):
        weight_grad(5 + stream, 3, H, r0, r1)
        grad_first(5 + stream)
        weight_grad(3 + stream, 2, D, r0, r1)
        grad_first(3 + stream)
        bias_grad(3 + stream, r0, r1)
    arrived("sums", first, second)
    for stream, (r0, r1) in enumerate(both):
        result = backward_norm(DZ[r0:r1] + reduced(r0, r1), 1, 1 + stream, 1 + stream, r0, r1)
        DZ[r0:r1] = result
        A[4, 0, r0:r1] = result.astype(BF)

    def attention_backward(p, x_p, streams, QV, Cb, PL, PV, crossed):
        copies = gather_start(p)
        for g in range(2):
            if g == 0:
                arrived("rows_core", copies[0])
            else:
                arrived("rows_far", forward)
            for r0, r1, w in streams:
                context_grad = dot_nn(rows_of_group(p, g, r0, r1), W[w, :, 512:768])
                D[2 * g : 2 * g + 2, r0:r1, 512:768] = context_grad.astype(BF).reshape(2, r1 - r0, TILE)
            if g == 0:
                forward = gather_forward(p, copies)
            with jax.named_scope("attend_gradient"):
                grouped(g, lambda s: attend_back_slab(QV, Cb, PL, PV, crossed, s))
            stage_free(g)
            for r0, r1, w in streams:
                partial_nt(g, D, r0, r1, w, slice(0, 768))
            if g == 0:
                first = reduce_first()
            else:
                second = reduce_second()
        for r0, r1, w in streams:
            attention_weight_grad(w, x_p, p, Cb, r0, r1)
            grad_first(w)
            bias_grad(w, r0, r1)
        return first, second

    first, second = attention_backward(
        4, 1, ((0, RL, 1), (RL, ROWS, 2)), QVK.at[1], C.at[1], PSL, PSV, False
    )
    grad_second(5)
    grad_second(3)
    arrived("sums", first, second)
    for r0, r1 in both:
        result = backward_norm(DZ[r0:r1] + reduced(r0, r1), 0, 0, 0, r0, r1)
        DZ[r0:r1] = result
        A[5, 0, r0:r1] = result.astype(BF)
    first, second = attention_backward(5, 0, ((0, ROWS, 0),), QVK.at[0], C.at[0], PCL, PCV, True)

    quarter = jnp.where(c == 0, z, z2)
    AVA[0, 0:16] = VG[...]
    for j in range(4):
        AVA[0, 16 + 8 * j : 24 + 8 * j] = jnp.where(quarter == j, QG[...], 0.0)
    vector_peers = [sib, plane[0], plane[1], zp, (d, z2)]
    vector_copy = send(AVA.at[0], AVR.at[0], vector_peers[0])
    grad_second(6)
    grad_second(4)
    for stage in range(5):
        if stage == 1:
            arrived("sums", first, second)
            for r0, r1 in both:
                DZ[r0:r1] = DZ[r0:r1] + reduced(r0, r1)
            tail_grad = [
                send(DZ.at[pl.ds(RL - LANG_TAIL, LANG_TAIL)], TLG, up),
                send(DZ.at[pl.ds(ROWS - VIS_TAIL, VIS_TAIL)], TVG, up),
            ]
            grad_second(1)
            grad_second(2)
        arrived("vectors", vector_copy)
        AVA[stage + 1] = AVA[stage] + AVR[stage]
        if stage < 4:
            vector_copy = send(AVA.at[stage + 1], AVR.at[stage + 1], vector_peers[stage + 1])
    vec_out[...] = AVA[5, 0:16]
    qb_out[...] = AVA[5, pl.ds(pl.multiple_of(16 + 8 * z, 8), 8)]

    arrived("tails", *tail_out, *tail_grad)
    before_l = jnp.where(z == 1, 0, 25 - 5 * z)
    before_v = jnp.where(z == 1, 0, 45 - 9 * z)
    tail_shift_l = own_l - before_l - (RL - LANG_TAIL)
    tail_shift_v = own_v - before_v - (RV - VIS_TAIL)
    for own_rows, off, tail_rows, shift, out_ref, grad_ref, r0, r1, t_out, t_grad in (
        (own_l, off_l, LANG_TAIL, tail_shift_l, lang_out, lang_grad, 0, RL, TLO, TLG),
        (own_v, off_v, VIS_TAIL, tail_shift_v, vis_out, vis_grad, RL, ROWS, TVO, TVG),
    ):
        from_own = select_rows((own_rows, r1 - r0), -off, off, own_rows)
        from_tail = select_rows((own_rows, tail_rows), shift, 0, off)
        out_ref[...] = (
            dot_nn(from_own.astype(BF), OUTS[r0:r1]) + dot_nn(from_tail.astype(BF), t_out[...])
        ).astype(BF)
        exact = lax.Precision.HIGHEST
        grad_ref[...] = jnp.dot(
            from_own, DZ[r0:r1], precision=exact, preferred_element_type=F32
        ) + jnp.dot(from_tail, t_grad[...], precision=exact, preferred_element_type=F32)

    grad_second(0)
    for w in (5, 3, 6, 4, 1, 2, 0):
        grad_last(w)

    for copy in pending:
        copy.wait_send()
    for index in range(3):
        stage_free(index)

    @pl.when(c == 1)
    def _():
        for copy in nears:
            copy.wait_send()
        for _, far_low, far_high in grad_nears:
            far_low.wait_send()
            far_high.wait_send()

    @pl.when(c == 0)
    def _():
        for near, _, _ in grad_nears:
            near.wait_send()
    assert counter[0] <= ssem.shape[0] and counter[1] <= rsem.shape[0], counter


N_SEND = 160
N_RECV = 80


def fused_layer(total_items, *operands):
    own_l, own_v = operands[0].shape[0], operands[1].shape[0]
    vmem = pl.BlockSpec(memory_space=pltpu.VMEM)
    smem = pl.BlockSpec(memory_space=pltpu.SMEM)
    shapes = [
        ((own_l, D), BF),
        ((own_v, D), BF),
        ((own_l, D), F32),
        ((own_v, D), F32),
        ((7, SHARE, D), F32),
        ((16, D), F32),
        ((8, D), F32),
    ]
    scratch = [
        ((7, D, D), BF),
        ((7, D, D), BF),
        ((3, 7, HALF_PAIR, D), BF),
        ((2, 7, SHARE, D), BF),
        ((6, SLOTS, ROWS, D), BF),
        ((SLOTS, 8, TILE), F32),
        ((3, ROWS, D), BF),
        ((3, ROWS, D), BF),
        ((2, SLOTS, ROWS, D), BF),
        ((SLOTS, ROWS, D), BF),
        ((2, SLOTS, ROWS, TILE), BF),
        ((SLOTS, ROWS, D), BF),
        ((SLOTS, ROWS, D), BF),
        ((SLOTS, 3 * RL, RV), BF),
        ((SLOTS, 3 * RV, RL), BF),
        ((SLOTS, 3 * RL, RL), BF),
        ((SLOTS, 3 * RV, RV), BF),
        ((ROWS, D), F32),
        ((ROWS, D), F32),
        ((3, ROWS, D), F32),
        ((3, ROWS, 1), F32),
        ((ROWS, D), F32),
        ((ROWS, D), BF),
        ((3, SHARE, D), BF),
        ((ROWS, 1), F32),
        ((8, D), F32),
        ((8, D), F32),
        ((8, D), F32),
        ((4, 8, 128), F32),
        ((3, 8, 128), F32),
        ((16, D), F32),
        ((8, D), F32),
        ((6, N_AR, D), F32),
        ((5, N_AR, D), F32),
        ((2, LANG_HEAD, D), BF),
        ((2, VIS_HEAD, D), BF),
        ((ROWS, D), BF),
        ((LANG_TAIL, D), BF),
        ((VIS_TAIL, D), BF),
        ((LANG_TAIL, D), F32),
        ((VIS_TAIL, D), F32),
    ]
    dma = pltpu.SemaphoreType.DMA
    return pl.pallas_call(
        partial(layer_kernel, total_items),
        out_shape=[jax.ShapeDtypeStruct(s, t) for s, t in shapes],
        in_specs=[vmem] * 4 + [smem] * 3 + [vmem] * (len(operands) - 7),
        out_specs=[vmem] * len(shapes),
        scratch_shapes=[pltpu.VMEM(s, t) for s, t in scratch]
        + [dma((N_SEND,)), dma((N_RECV,)), dma((7,)), dma((7,)), dma((7,)), dma((7,)), dma((1,))],
        compiler_params=pltpu.CompilerParams(
            collective_id=0, has_side_effects=True, vmem_limit_bytes=VMEM_LIMIT
        ),
    )(*operands)


def unpack_kernel(lo, vo, lg, vg, wgrad, vec, qb, *outs):
    (lo_out, vo_out, lg_out, vg_out, proj, qv, outw, outb, exp, expb, con, conb, gain, shift) = outs
    lo_out[...] = lo[...]
    vo_out[...] = vo[...]
    lg_out[...] = lg[...]
    vg_out[...] = vg[...]
    width = HALF_PAIR
    for b in range(3):
        for j, lane in enumerate((0, 2 * width, width)):
            proj[b, j] = wgrad[b, :, lane : lane + width]
        outw[b] = wgrad[b, :, 3 * width :].T
        for j in range(2):
            qv[b, j : j + 1] = qb[b : b + 1, j * width : (j + 1) * width]
    for stream in range(2):
        exp[stream] = wgrad[3 + stream]
        con[stream] = wgrad[5 + stream]
    expb[...] = qb[3:5]
    outb[...] = vec[0:3]
    conb[...] = vec[3:5]
    gain[...] = vec[5:10]
    shift[...] = vec[10:15]


def unpack(packed, shapes):
    vmem = pl.BlockSpec(memory_space=pltpu.VMEM)
    return pl.pallas_call(
        unpack_kernel,
        out_shape=shapes,
        in_specs=[vmem] * len(packed),
        out_specs=[vmem] * len(shapes),
        compiler_params=pltpu.CompilerParams(vmem_limit_bytes=VMEM_LIMIT),
    )(*packed)


def on_device_fused(
    language_input,
    vision_input,
    word_lengths,
    region_counts,
    task_flags,
    language_cotangent,
    vision_cotangent,
    projection_weight,
    query_value_bias,
    output_weight,
    output_bias,
    expand_weight,
    expand_bias,
    contract_weight,
    contract_bias,
    norm_gain,
    norm_bias,
):
    packed = fused_layer(
        float(word_lengths.shape[0] * lax.axis_size("dp")),
        language_input,
        vision_input,
        language_cotangent,
        vision_cotangent,
        word_lengths,
        region_counts,
        task_flags.T,
        projection_weight,
        query_value_bias,
        output_weight,
        expand_weight,
        expand_bias,
        contract_weight.transpose(0, 2, 1),
        output_bias,
        contract_bias,
        norm_gain,
        norm_bias,
    )
    like = [
        (language_input, BF),
        (vision_input, BF),
        (language_input, F32),
        (vision_input, F32),
        (projection_weight, F32),
        (query_value_bias, F32),
        (output_weight, F32),
        (output_bias, F32),
        (expand_weight, F32),
        (expand_bias, F32),
        (contract_weight.transpose(0, 2, 1), F32),
        (contract_bias, F32),
        (norm_gain, F32),
        (norm_bias, F32),
    ]
    outs = list(unpack(packed, [jax.ShapeDtypeStruct(a.shape, t) for a, t in like]))
    outs[10] = outs[10].transpose(0, 2, 1)
    return tuple(outs)


def solution(mesh):
    in_specs = (
        P(("dp", "mp"), None),
        P(("dp", "mp"), None),
        P("dp"),
        P("dp"),
        P("dp", None),
        P(("dp", "mp"), None),
        P(("dp", "mp"), None),
        P(None, None, "dp", "mp"),
        P(None, None, "mp"),
        P(None, "mp", "dp"),
        P(),
        P(None, "dp", "mp"),
        P(None, "mp"),
        P(None, "mp", "dp"),
        P(),
        P(),
        P(),
    )
    out_specs = (
        P(("dp", "mp"), None),
        P(("dp", "mp"), None),
        P(("dp", "mp"), None),
        P(("dp", "mp"), None),
        P(None, None, "dp", "mp"),
        P(None, None, "mp"),
        P(None, "mp", "dp"),
        P(),
        P(None, "dp", "mp"),
        P(None, "mp"),
        P(None, "mp", "dp"),
        P(),
        P(),
        P(),
    )
    fused = dict(mesh.shape) == {"dp": 8, "mp": 4}
    return jax.shard_map(
        on_device_fused if fused else on_device, mesh=mesh, in_specs=in_specs, out_specs=out_specs, check_vma=False
    )
```

```python
from functools import partial
import math

import jax
import jax.numpy as jnp
from jax import lax
from jax.experimental import pallas as pl
from jax.experimental.pallas import tpu as pltpu
from jax.sharding import PartitionSpec as P

D = 768
HEADS = 12
WORDS = 20
REGIONS = 36
D_MODEL = D
D_HEAD = D // HEADS

EPSILON = 1e-12
MASKED = -1e30


def layer_norm(summed, gain, shift):
    center = summed - jnp.mean(summed, -1, keepdims=True)
    scaled = lax.rsqrt(jnp.mean(center * center, -1, keepdims=True) + EPSILON)
    normed = center * scaled
    return (normed * gain + shift, normed, scaled)


def norm_back(upstream, normed, scaled, gain):
    through = upstream * gain
    inner = (
        through
        - jnp.mean(through, -1, keepdims=True)
        - normed * jnp.mean(through * normed, -1, keepdims=True)
    )
    return (scaled * inner, jnp.sum(upstream * normed, 0), jnp.sum(upstream, 0))


def split_heads(rows, item_count):
    head_size = D // HEADS
    return rows.reshape(
        item_count, rows.shape[0] // item_count, rows.shape[1] // head_size, head_size
    )


def join_heads(block):
    return block.reshape(block.shape[0] * block.shape[1], block.shape[2] * block.shape[3])


def project(rows, weight, bias, item_count):
    mapped = jnp.einsum("rd,jde->jre", rows, weight, preferred_element_type=jnp.float32)
    query = split_heads((mapped[0] + bias[0]).astype(jnp.bfloat16), item_count)
    keys = split_heads(mapped[1].astype(jnp.bfloat16), item_count)
    values = split_heads((mapped[2] + bias[1]).astype(jnp.bfloat16), item_count)
    return (query, keys, values)


def masked_scores(query, keys, valid):
    scores = jnp.einsum("inhd,imhd->ihnm", query, keys, preferred_element_type=jnp.float32) * (
        1.0 / math.sqrt(D // HEADS)
    )
    return jnp.where(valid[:, None, None, :], scores, MASKED)


def attend(query, keys, values, valid):
    scores = masked_scores(query, keys, valid)
    highest = jnp.max(scores, -1, keepdims=True)
    raised = jnp.exp(scores - highest)
    summed = jnp.sum(raised, -1, keepdims=True)
    context = jnp.einsum(
        "ihnm,imhd->inhd",
        (raised / summed).astype(jnp.bfloat16),
        values,
        preferred_element_type=jnp.float32,
    )
    return (join_heads(context).astype(jnp.bfloat16), highest + jnp.log(summed))


def attend_back(query, keys, values, valid, log_total, context_grad):
    factor = 1.0 / math.sqrt(D // HEADS)
    upstream = context_grad.reshape(query.shape)
    weights = jnp.exp(masked_scores(query, keys, valid) - log_total)
    weight_grad = jnp.einsum(
        "inhd,imhd->ihnm", upstream, values, preferred_element_type=jnp.float32
    )
    score_grad = (
        weights * (weight_grad - jnp.sum(weight_grad * weights, -1, keepdims=True))
    ).astype(jnp.bfloat16)
    query_grad = (
        jnp.einsum("ihnm,imhd->inhd", score_grad, keys, preferred_element_type=jnp.float32) * factor
    ).astype(jnp.bfloat16)
    keys_grad = (
        jnp.einsum("ihnm,inhd->imhd", score_grad, query, preferred_element_type=jnp.float32)
        * factor
    ).astype(jnp.bfloat16)
    values_grad = jnp.einsum(
        "ihnm,inhd->imhd",
        weights.astype(jnp.bfloat16),
        upstream,
        preferred_element_type=jnp.float32,
    ).astype(jnp.bfloat16)
    return (join_heads(query_grad), join_heads(keys_grad), join_heads(values_grad))


def project_back(rows, query_grad, keys_grad, values_grad):
    stacked = jnp.stack([query_grad, keys_grad, values_grad])
    weight_grad = jnp.einsum("rd,jre->jde", rows, stacked, preferred_element_type=jnp.float32)
    bias_grad = jnp.stack(
        [jnp.sum(query_grad.astype(jnp.float32), 0), jnp.sum(values_grad.astype(jnp.float32), 0)]
    )
    return (weight_grad, bias_grad, stacked)


def gather_rows(language_rows, vision_rows):
    return (
        lax.all_gather(language_rows, "mp", axis=0, tiled=True),
        lax.all_gather(vision_rows, "mp", axis=0, tiled=True),
    )


def rows_of(language_part, vision_part):
    return (
        lax.all_to_all(language_part, "mp", split_axis=0, concat_axis=1, tiled=True),
        lax.all_to_all(vision_part, "mp", split_axis=0, concat_axis=1, tiled=True),
    )


def gather_grads(language_rows, vision_rows):
    return (
        lax.all_gather(language_rows, "mp", axis=0, tiled=True),
        lax.all_gather(vision_rows, "mp", axis=0, tiled=True),
    )


def grads_of(language_part, vision_part):
    return (
        lax.all_to_all(language_part, "mp", split_axis=1, concat_axis=2, tiled=True),
        lax.all_to_all(vision_part, "mp", split_axis=1, concat_axis=2, tiled=True),
    )


def matmul(left, right):
    return jnp.dot(left, right, preferred_element_type=jnp.float32)


def on_device(
    language_input,
    vision_input,
    word_lengths,
    region_counts,
    task_flags,
    language_cotangent,
    vision_cotangent,
    projection_weight,
    query_value_bias,
    output_weight,
    output_bias,
    expand_weight,
    expand_bias,
    contract_weight,
    contract_bias,
    norm_gain,
    norm_bias,
):
    item_count = word_lengths.shape[0]
    flag_total = lax.psum(jnp.sum(task_flags, 0), "dp")
    projection, out_weight, expand, contract = (
        lax.all_gather(projection_weight, "dp", axis=2, tiled=True),
        lax.all_gather(output_weight, "dp", axis=2, tiled=True),
        lax.all_gather(expand_weight, "dp", axis=1, tiled=True),
        lax.all_gather(contract_weight, "dp", axis=2, tiled=True),
    )
    projection_full, out_full, expand_full, contract_full = (
        lax.all_gather(projection, "mp", axis=3, tiled=True),
        lax.all_gather(out_weight, "mp", axis=1, tiled=True),
        lax.all_gather(expand, "mp", axis=2, tiled=True),
        lax.all_gather(contract, "mp", axis=1, tiled=True),
    )
    valid = [
        jnp.arange(WORDS, dtype=jnp.int32)[None, :] < word_lengths[:, None],
        jnp.arange(REGIONS, dtype=jnp.int32)[None, :] < region_counts[:, None],
    ]
    row_counts = [WORDS, REGIONS]
    inputs = [language_input.astype(jnp.float32), vision_input.astype(jnp.float32)]
    cross_rows = gather_rows(language_input, vision_input)
    cross_parts = [
        project(cross_rows[stream], projection[0], query_value_bias[0], item_count)
        for stream in range(2)
    ]
    cross_context = []
    cross_total = []
    for stream in range(2):
        other = 1 - stream
        context, log_total = attend(
            cross_parts[stream][0], cross_parts[other][1], cross_parts[other][2], valid[other]
        )
        cross_context.append(context)
        cross_total.append(log_total)
    moved = rows_of(cross_context[0], cross_context[1])
    branch = [matmul(moved[stream], out_full[0]) for stream in range(2)]
    first = [
        layer_norm(branch[stream] + output_bias[0] + inputs[stream], norm_gain[0], norm_bias[0])
        for stream in range(2)
    ]
    first_out = [first[stream][0].astype(jnp.bfloat16) for stream in range(2)]
    self_rows = gather_rows(first_out[0], first_out[1])
    self_parts = [
        project(self_rows[stream], projection[1 + stream], query_value_bias[1 + stream], item_count)
        for stream in range(2)
    ]
    self_context = []
    self_total = []
    for stream in range(2):
        context, log_total = attend(
            self_parts[stream][0], self_parts[stream][1], self_parts[stream][2], valid[stream]
        )
        self_context.append(context)
        self_total.append(log_total)
    moved = rows_of(self_context[0], self_context[1])
    branch = [matmul(moved[stream], out_full[1 + stream]) for stream in range(2)]
    second = [
        layer_norm(
            branch[stream] + output_bias[1 + stream] + first_out[stream].astype(jnp.float32),
            norm_gain[1 + stream],
            norm_bias[1 + stream],
        )
        for stream in range(2)
    ]
    second_out = [second[stream][0].astype(jnp.bfloat16) for stream in range(2)]
    feed_rows = gather_rows(second_out[0], second_out[1])
    before = [
        matmul(feed_rows[stream], expand[stream]) + expand_bias[stream] for stream in range(2)
    ]
    hidden = [
        jax.nn.gelu(before[stream], approximate=False).astype(jnp.bfloat16) for stream in range(2)
    ]
    moved = rows_of(hidden[0], hidden[1])
    branch = [matmul(moved[stream], contract_full[stream]) for stream in range(2)]
    third = [
        layer_norm(
            branch[stream] + contract_bias[stream] + second_out[stream].astype(jnp.float32),
            norm_gain[3 + stream],
            norm_bias[3 + stream],
        )
        for stream in range(2)
    ]
    language_out = third[0][0].astype(jnp.bfloat16)
    vision_out = third[1][0].astype(jnp.bfloat16)
    item_scale = task_flags.astype(jnp.float32) * (
        item_count * lax.axis_size("dp") / flag_total.astype(jnp.float32)
    )
    shard_index = lax.axis_index("mp")
    upstream = []
    for stream, cotangent in enumerate([language_cotangent, vision_cotangent]):
        per_row = jnp.repeat(
            item_scale[:, stream],
            row_counts[stream],
            total_repeat_length=item_count * row_counts[stream],
        )
        shard_rows = cotangent.shape[0]
        row_scale = lax.dynamic_slice_in_dim(per_row, shard_index * shard_rows, shard_rows)
        upstream.append(cotangent.astype(jnp.float32) * row_scale[:, None])
    third_back = [
        norm_back(upstream[stream], third[stream][1], third[stream][2], norm_gain[3 + stream])
        for stream in range(2)
    ]
    sent = gather_grads(
        third_back[0][0].astype(jnp.bfloat16), third_back[1][0].astype(jnp.bfloat16)
    )
    expand_local = []
    expand_bias_local = []
    contract_local = []
    before_grads = []
    for stream in range(2):
        hidden_grad = jnp.einsum(
            "rd,fd->rf", sent[stream], contract[stream], preferred_element_type=jnp.float32
        )
        contract_local.append(
            jnp.einsum(
                "rf,rd->fd", hidden[stream], sent[stream], preferred_element_type=jnp.float32
            )
        )
        unused, pull = jax.vjp(partial(jax.nn.gelu, approximate=False), before[stream])
        before_grad = pull(hidden_grad)[0].astype(jnp.bfloat16)
        expand_local.append(
            jnp.einsum(
                "rd,rf->df", feed_rows[stream], before_grad, preferred_element_type=jnp.float32
            )
        )
        expand_bias_local.append(jnp.sum(before_grad.astype(jnp.float32), 0))
        before_grads.append(before_grad[None])
    moved = grads_of(before_grads[0], before_grads[1])
    back = [
        jnp.einsum(
            "rf,df->rd", moved[stream][0], expand_full[stream], preferred_element_type=jnp.float32
        )
        for stream in range(2)
    ]
    second_grad = [third_back[stream][0] + back[stream] for stream in range(2)]
    second_back = [
        norm_back(second_grad[stream], second[stream][1], second[stream][2], norm_gain[1 + stream])
        for stream in range(2)
    ]
    sent = gather_grads(
        second_back[0][0].astype(jnp.bfloat16), second_back[1][0].astype(jnp.bfloat16)
    )
    self_weight = []
    self_bias = []
    self_out = []
    stacks = []
    for stream in range(2):
        context_grad = jnp.einsum(
            "rd,ed->re", sent[stream], out_weight[1 + stream], preferred_element_type=jnp.float32
        ).astype(jnp.bfloat16)
        self_out.append(
            jnp.einsum(
                "re,rd->ed", self_context[stream], sent[stream], preferred_element_type=jnp.float32
            )
        )
        grads = attend_back(
            self_parts[stream][0],
            self_parts[stream][1],
            self_parts[stream][2],
            valid[stream],
            self_total[stream],
            context_grad,
        )
        weight_part, bias_part, stacked = project_back(
            self_rows[stream], grads[0], grads[1], grads[2]
        )
        self_weight.append(weight_part)
        self_bias.append(bias_part)
        stacks.append(stacked)
    moved = grads_of(stacks[0], stacks[1])
    back = [
        jnp.einsum(
            "jre,jde->rd",
            moved[stream],
            projection_full[1 + stream],
            preferred_element_type=jnp.float32,
        )
        for stream in range(2)
    ]
    first_grad = [second_back[stream][0] + back[stream] for stream in range(2)]
    first_back = [
        norm_back(first_grad[stream], first[stream][1], first[stream][2], norm_gain[0])
        for stream in range(2)
    ]
    sent = gather_grads(
        first_back[0][0].astype(jnp.bfloat16), first_back[1][0].astype(jnp.bfloat16)
    )
    cross_out = jnp.einsum(
        "re,rd->ed", cross_context[0], sent[0], preferred_element_type=jnp.float32
    ) + jnp.einsum("re,rd->ed", cross_context[1], sent[1], preferred_element_type=jnp.float32)
    triples = [[None, None, None], [None, None, None]]
    for stream in range(2):
        other = 1 - stream
        context_grad = jnp.einsum(
            "rd,ed->re", sent[stream], out_weight[0], preferred_element_type=jnp.float32
        ).astype(jnp.bfloat16)
        grads = attend_back(
            cross_parts[stream][0],
            cross_parts[other][1],
            cross_parts[other][2],
            valid[other],
            cross_total[stream],
            context_grad,
        )
        triples[stream][0] = grads[0]
        triples[other][1] = grads[1]
        triples[other][2] = grads[2]
    results = [
        project_back(cross_rows[stream], triples[stream][0], triples[stream][1], triples[stream][2])
        for stream in range(2)
    ]
    cross_weight = results[0][0] + results[1][0]
    cross_bias = results[0][1] + results[1][1]
    moved = grads_of(results[0][2], results[1][2])
    back = [
        jnp.einsum(
            "jre,jde->rd", moved[stream], projection_full[0], preferred_element_type=jnp.float32
        )
        for stream in range(2)
    ]
    language_grad = first_back[0][0] + back[0]
    vision_grad = first_back[1][0] + back[1]
    projection_stack = jnp.stack([cross_weight, self_weight[0], self_weight[1]])
    output_stack = jnp.stack([cross_out, self_out[0], self_out[1]])
    projection_grad, output_weight_grad, expand_grad, contract_grad = (
        lax.psum_scatter(projection_stack, "dp", scatter_dimension=2, tiled=True),
        lax.psum_scatter(output_stack, "dp", scatter_dimension=2, tiled=True),
        lax.psum_scatter(jnp.stack(expand_local), "dp", scatter_dimension=1, tiled=True),
        lax.psum_scatter(jnp.stack(contract_local), "dp", scatter_dimension=2, tiled=True),
    )
    query_value_grad, expand_bias_grad = lax.psum(
        (jnp.stack([cross_bias, self_bias[0], self_bias[1]]), jnp.stack(expand_bias_local)), "dp"
    )
    output_bias_local = jnp.stack(
        [
            jnp.sum(first_back[0][0], 0) + jnp.sum(first_back[1][0], 0),
            jnp.sum(second_back[0][0], 0),
            jnp.sum(second_back[1][0], 0),
        ]
    )
    contract_bias_local = jnp.stack([jnp.sum(third_back[0][0], 0), jnp.sum(third_back[1][0], 0)])
    gain_local = jnp.stack(
        [
            first_back[0][1] + first_back[1][1],
            second_back[0][1],
            second_back[1][1],
            third_back[0][1],
            third_back[1][1],
        ]
    )
    shift_local = jnp.stack(
        [
            first_back[0][2] + first_back[1][2],
            second_back[0][2],
            second_back[1][2],
            third_back[0][2],
            third_back[1][2],
        ]
    )
    output_bias_grad, contract_bias_grad, norm_gain_grad, norm_bias_grad = lax.psum(
        (output_bias_local, contract_bias_local, gain_local, shift_local), ("dp", "mp")
    )
    return (
        language_out,
        vision_out,
        language_grad,
        vision_grad,
        projection_grad,
        query_value_grad,
        output_weight_grad,
        output_bias_grad,
        expand_grad,
        expand_bias_grad,
        contract_grad,
        contract_bias_grad,
        norm_gain_grad,
        norm_bias_grad,
    )


MESH = pl.DeviceIdType.MESH
BF = jnp.bfloat16
F32 = jnp.float32
SLOTS = 4
RL = SLOTS * WORDS
RV = SLOTS * REGIONS
ROWS = RL + RV
SHARE = 96
HALF_PAIR = 2 * SHARE
LANG_HEAD = 16
VIS_HEAD = 32
LANG_TAIL = 32
VIS_TAIL = 64
N_AR = 48
NT = 3
TILE = 256
LANG = (0, RL)
VIS = (RL, ROWS)
BOTH = (0, ROWS)
SELF = {LANG: 1, VIS: 2}
EXPAND = {LANG: 3, VIS: 4}
CONTRACT = {LANG: 5, VIS: 6}
VMEM_LIMIT = 63 * 1024 * 1024


def dot_nn(left, right):
    return lax.dot_general(left, right, (((1,), (0,)), ((), ())), preferred_element_type=F32)


def dot_nt(left, right):
    return lax.dot_general(left, right, (((1,), (1,)), ((), ())), preferred_element_type=F32)


def dot_tn(left, right):
    return lax.dot_general(left, right, (((0,), (0,)), ((), ())), preferred_element_type=F32)


def head_mask(first_lane, dtype):
    lane = lax.broadcasted_iota(jnp.int32, (1, TILE), 1) - first_lane
    return [
        jnp.where((lane >= 64 * h) & (lane < 64 * h + 64), 1.0, 0.0).astype(dtype) for h in range(3)
    ]


def select_rows(shape, shift, low, high):
    row = lax.broadcasted_iota(jnp.int32, shape, 0)
    column = lax.broadcasted_iota(jnp.int32, shape, 1)
    return jnp.where((column - row == shift) & (row >= low) & (row < high), 1.0, 0.0)


def layer_kernel(
    total_items,
    lang,
    vis,
    lcot,
    vcot,
    lengths,
    regions,
    flags,
    projection,
    query_value,
    out_weight,
    expand,
    expand_b,
    contract,
    out_bias,
    contract_b,
    gains,
    shifts,
    lang_out,
    vis_out,
    lang_grad,
    vis_grad,
    wgrad,
    vec_out,
    qb_out,
    W,
    G,
    RD,
    RX,
    R2,
    A,
    KV,
    RSB,
    STG,
    QVK,
    D,
    C,
    H,
    GP,
    PCL,
    PCV,
    PSL,
    PSV,
    PART,
    PZ,
    NORM,
    RSTD,
    DZ,
    COT,
    SH,
    FLAG,
    QO,
    QB,
    QR,
    CA,
    CR,
    VG,
    QG,
    AVA,
    AVR,
    HL,
    HV,
    OUTS,
    TLO,
    TVO,
    TLG,
    TVG,
    ssem,
    rsem,
    wsem,
    wsem_z,
    gsem,
    gsem2,
    lsem,
):
    d = lax.axis_index("dp")
    z = lax.axis_index("mp")
    c = d % 2
    k = d // 2
    k_flip = [k + 1 - 2 * (k % 2), (k + 2) % 4, 3 - k]
    sib = (d + 1 - 2 * c, z)
    zp = (d, z + 1 - 2 * (z % 2))
    z2 = (z + 2) % 4
    up = (d, (z + 1) % 4)
    down = (d, (z + 3) % 4)
    plane = [(2 * kf + c, z) for kf in k_flip]
    far = (2 * k + 1, z2)

    pending = []
    counter = [0, 0]

    def remote(src, dst, send, recv, device):
        return pltpu.make_async_remote_copy(
            src_ref=src, dst_ref=dst, send_sem=send, recv_sem=recv, device_id=device, device_id_type=MESH
        )

    def send(src, dst, device, recv=None, keep=True):
        slot = counter[0]
        counter[0] += 1
        if recv is None:
            recv = rsem.at[counter[1]]
            counter[1] += 1
        copy = remote(src, dst, ssem.at[slot], recv, device)
        copy.start()
        if keep:
            pending.append(copy)
        return copy

    def wait_bytes(ref, sem):
        pltpu.make_async_copy(ref, ref, sem).wait()

    def arrived(name, *copies):
        with jax.named_scope("wait_" + name):
            for copy in copies:
                copy.wait_recv()

    barrier = pltpu.get_barrier_semaphore()
    peers = [sib, up, down, (d, z2), (d + 1 - 2 * c, z2)] + plane
    with jax.named_scope("barrier"):
        for peer in peers:
            pl.semaphore_signal(barrier, inc=1, device_id=peer, device_id_type=MESH)
        pl.semaphore_wait(barrier, len(peers))

    def weight_first(w):
        row = pl.ds(pl.multiple_of(d * SHARE, 16), SHARE)
        slot = counter[0]
        counter[0] += 1
        share = SH.at[w] if w < 3 else (expand.at[w - 3] if w < 5 else contract.at[w - 5])
        near = remote(share, W.at[w, row], ssem.at[slot], wsem_z.at[w], sib)
        own = pltpu.make_async_copy(share, W.at[w, row], wsem_z.at[w])

        @pl.when(c == 1)
        def _():
            near.start()

        @pl.when(c == 0)
        def _():
            own.start()

        send(share, W.at[w, row], far, wsem_z.at[w])
        return near

    def place(width, first):
        row = lax.broadcasted_iota(jnp.int32, (width, D_MODEL), 0)
        column = lax.broadcasted_iota(jnp.int32, (width, D_MODEL), 1)
        return jnp.where(column - row == first, 1.0, 0.0).astype(BF)

    @jax.named_scope("share")
    def attention_share(b):
        SH[b] = (
            dot_nn(projection[b, 0], place(HALF_PAIR, 0))
            + dot_nn(projection[b, 2], place(HALF_PAIR, HALF_PAIR))
            + dot_nn(projection[b, 1], place(HALF_PAIR, 2 * HALF_PAIR))
            + dot_tn(out_weight[b], place(HALF_PAIR, 3 * HALF_PAIR))
        ).astype(BF)

    nears = []
    heads = [
        send(lang.at[pl.ds(0, LANG_HEAD)], HL.at[0], down),
        send(vis.at[pl.ds(0, VIS_HEAD)], HV.at[0], down),
        send(lcot.at[pl.ds(0, LANG_HEAD)], HL.at[1], down),
        send(vcot.at[pl.ds(0, VIS_HEAD)], HV.at[1], down),
    ]
    attention_share(0)
    nears.append(weight_first(0))

    n_items = lengths.shape[0]
    first_item = 3 * z + jnp.minimum(z, 1)
    KV[0] = jnp.full(KV.shape[1:], -1.0, F32)
    for row, source, size in ((0, lengths, WORDS), (1, regions, REGIONS)):
        lane = lax.broadcasted_iota(jnp.int32, (1, TILE), 1)
        owner = jnp.full((1, TILE), -1.0, F32)
        slab_row = lax.broadcasted_iota(jnp.int32, (SLOTS * size, 1), 0)
        flag = jnp.zeros((SLOTS * size, 1), F32)
        for j in range(SLOTS):
            item = jnp.minimum(first_item + j, n_items - 1)
            valid = (lane >= j * size) & (lane < j * size + source[item]) & (lane < (j + 1) * size)
            owner = jnp.where(valid, float(j), owner)
            inside = (slab_row >= j * size) & (slab_row < (j + 1) * size)
            flag = jnp.where(inside, flags[row, item].astype(F32), flag)
        KV[0, row : row + 1] = owner
        FLAG[row * RL : row * RL + SLOTS * size] = flag
        count = flags[row, 0]
        for j in range(1, n_items):
            count = count + flags[row, j]
        CA[0, row : row + 1] = jnp.full((1, 128), count.astype(F32), F32)
    kv_sib = send(KV.at[0], KV.at[1], sib)
    kv_zp = send(KV.at[0], KV.at[2], zp)
    count_copies = [send(CA.at[0], CR.at[0], sib)]
    QO[...] = jnp.zeros_like(QO)
    for b in range(3):
        QO[b : b + 1, 0:HALF_PAIR] = query_value[b, 0:1]
        QO[b : b + 1, HALF_PAIR : 2 * HALF_PAIR] = query_value[b, 1:2]
    QO[3:5] = expand_b[...]
    bias_swap = send(QO, QR, (d, z2))

    pair_rows = pl.ds(pl.multiple_of(k * HALF_PAIR, 16), HALF_PAIR)

    def rows_of_chip(chip, first=0, count=HALF_PAIR):
        return pl.ds(pl.multiple_of(chip * HALF_PAIR + first, 16), count)

    def weight_second(w):
        wait_bytes(W.at[w, pair_rows], wsem_z.at[w])
        for j in range(2):
            send(W.at[w, pair_rows], W.at[w, pair_rows], plane[j], wsem.at[j, w])

    def weight_third(w):
        for j in range(2):
            wait_bytes(W.at[w, pair_rows], wsem.at[j, w])
            half = rows_of_chip(k_flip[j], j * SHARE, SHARE)
            send(W.at[w, half], W.at[w, half], plane[1 - j], wsem.at[2, w])

    def weight_ready(w):
        wait_bytes(W.at[w, pair_rows], wsem.at[2, w])

    off_l = jnp.where(z == 0, 0, 20 - 5 * z)
    off_v = jnp.where(z == 0, 0, 36 - 9 * z)
    n_l = jnp.where(z == 0, 4 * WORDS, 3 * WORDS)
    n_v = jnp.where(z == 0, 4 * REGIONS, 3 * REGIONS)
    own_l = lang.shape[0]
    own_v = vis.shape[0]
    arrived("heads", *heads)

    def gather_start(p, stream):
        rows = pl.ds(stream[0], stream[1] - stream[0])
        return (
            p,
            rows,
            send(A.at[p, 0, rows], A.at[p, 1, rows], sib),
            send(A.at[p, 0, rows], A.at[p, 2, rows], zp),
        )

    def gather_forward(handle):
        p, rows, _, across = handle
        arrived("rows_z", across)
        return send(A.at[p, 2, rows], A.at[p, 3, rows], sib)

    for index, (source_l, source_v) in enumerate([(lang, vis), (lcot, vcot)]):
        slab_l = dot_nn(select_rows((RL, own_l), off_l, 0, n_l).astype(BF), source_l[...]) + dot_nn(
            select_rows((RL, LANG_HEAD), off_l - own_l, 0, n_l).astype(BF), HL[index]
        )
        slab_v = dot_nn(select_rows((RV, own_v), off_v, 0, n_v).astype(BF), source_v[...]) + dot_nn(
            select_rows((RV, VIS_HEAD), off_v - own_v, 0, n_v).astype(BF), HV[index]
        )
        if index == 0:
            A[0, 0, 0:RL] = slab_l.astype(BF)
            A[0, 0, RL:ROWS] = slab_v.astype(BF)
            rows_x = {stream: gather_start(0, stream) for stream in (VIS, LANG)}
        else:
            COT[0:RL] = slab_l.astype(BF)
            COT[RL:ROWS] = slab_v.astype(BF)

    stage_used = {}

    def stage_free(index, stream):
        copy = stage_used.pop((index, stream), None)
        if copy is not None:
            copy.wait_send()

    def partial_nt(g, lhs_ref, stream, w, lanes):
        r0, r1 = stream
        rows = r1 - r0
        stage_free(g, stream)
        for n in range(NT):
            column = slice(n * TILE, (n + 1) * TILE)
            lhs = lhs_ref[2 * g : 2 * g + 2, r0:r1, :]
            lhs = lhs.reshape(2 * rows, lhs.shape[-1])
            out = dot_nt(lhs, W[w, column, lanes])
            target = PART if g == 0 else PZ
            target[r0:r1, column] = out[:rows]
            STG[g, r0:r1, column] = out[rows:].astype(BF)

    def stage_send(index, stream, device):
        rows = pl.ds(stream[0], stream[1] - stream[0])
        copy = send(STG.at[index, rows], RSB.at[index, rows], device, keep=False)
        stage_used[index, stream] = copy
        return copy

    def sums_near(stream):
        return stage_send(0, stream, sib)

    def sums_far(stream):
        return stage_send(1, stream, sib)

    def sums_z(stream, far):
        r0, r1 = stream
        arrived("sums_core", far)
        stage_free(2, stream)
        STG[2, r0:r1] = (PZ[r0:r1] + RSB[1, r0:r1].astype(F32)).astype(BF)
        return stage_send(2, stream, zp)

    def reduced(stream, *copies):
        r0, r1 = stream
        arrived("sums", *copies)
        return PART[r0:r1] + RSB[0, r0:r1].astype(F32) + RSB[2, r0:r1].astype(F32)

    mask_q = head_mask(0, BF)
    mask_c = head_mask(64, BF)
    mask_q32 = head_mask(0, F32)
    mask_c32 = head_mask(64, F32)
    factor = 1.0 / math.sqrt(D_HEAD)

    def attend_slab(QV, Cb, PL, PV, crossed, stream, s):
        def one(q0, q1, k0, k1, words_keys, P):
            nq, nk = q1 - q0, k1 - k0
            query = QV[s, q0:q1, 0:256]
            keys = QV[s, k0:k1, 384:640]
            values = QV[s, k0:k1, 128:384]
            query_size = WORDS if q0 == 0 else REGIONS
            spread = jnp.concatenate([query * mask_q[h] for h in range(3)], 0)
            scores = dot_nt(spread, keys) * factor
            row = lax.broadcasted_iota(jnp.int32, (nq, nk), 0)
            item = jnp.zeros((nq, nk), F32)
            for j in range(1, SLOTS):
                item = item + jnp.where(row >= j * query_size, 1.0, 0.0)
            column = KV[s, 0:1, 0:nk] if words_keys else KV[s, 1:2, 0:nk]
            same = item == column
            scores = jnp.where(same[None], scores.reshape(3, nq, nk), MASKED)
            raised = jnp.exp(scores - jnp.max(scores, -1, keepdims=True))
            weights = (raised / jnp.sum(raised, -1, keepdims=True)).astype(BF).reshape(3 * nq, nk)
            P[s] = weights
            context = dot_nn(weights, values).reshape(3, nq, TILE)
            Cb[s, q0:q1] = (
                context[0] * mask_c32[0] + context[1] * mask_c32[1] + context[2] * mask_c32[2]
            ).astype(BF)

        if stream == LANG:
            if crossed:
                one(0, RL, RL, ROWS, False, PL)
            else:
                one(0, RL, 0, RL, True, PL)
        elif crossed:
            one(RL, ROWS, 0, RL, True, PV)
        else:
            one(RL, ROWS, RL, ROWS, False, PV)

    def attend_back_slab(QV, PL, PV, crossed, streams, s):
        def one(q0, q1, k0, k1, P):
            nq, nk = q1 - q0, k1 - k0
            query = QV[s, q0:q1, 0:256]
            keys = QV[s, k0:k1, 384:640]
            values = QV[s, k0:k1, 128:384]
            spread = jnp.concatenate([query * mask_q[h] for h in range(3)], 0)
            upstream = D[s, q0:q1, 512:768]
            up_spread = jnp.concatenate([upstream * mask_c[h] for h in range(3)], 0)
            weights = P[s]
            weights32 = weights.astype(F32)
            weight_grad = dot_nt(up_spread, values)
            score_grad = (
                weights32
                * (weight_grad - jnp.sum(weight_grad * weights32, -1, keepdims=True))
            ).astype(BF)
            dq = dot_nn(score_grad, keys).reshape(3, nq, TILE)
            dq = (dq[0] * mask_q32[0] + dq[1] * mask_q32[1] + dq[2] * mask_q32[2]) * factor
            dk = dot_tn(score_grad, spread) * factor
            dv = dot_tn(weights, up_spread)
            return dq, dk, dv

        if crossed:
            dq_l, dk_v, dv_v = one(0, RL, RL, ROWS, PL)
            dq_v, dk_l, dv_l = one(RL, ROWS, 0, RL, PV)
            results = {LANG: (dq_l, dk_l, dv_l), VIS: (dq_v, dk_v, dv_v)}
        else:
            results = {stream: one(*stream, *stream, PL if stream == LANG else PV) for stream in streams}
        for (r0, r1), (dq, dk, dv) in results.items():
            D[s, r0:r1, 0:128] = dq[:, :128].astype(BF)
            D[s, r0:r1, 128:256] = (dq[:, 128:] + dv[:, :128]).astype(BF)
            D[s, r0:r1, 256:384] = dv[:, 128:].astype(BF)
            D[s, r0:r1, 384:640] = dk.astype(BF)
            D[s, r0:r1, 640:768] = jnp.zeros((r1 - r0, 128), BF)

    def over_tiles(body):
        for n in range(NT):
            body(slice(n * TILE, (n + 1) * TILE))

    @jax.named_scope("norm")
    def forward_norm(value, index, gain_row, r0, r1):
        center = value - jnp.mean(value, -1, keepdims=True)
        scaled = lax.rsqrt(jnp.mean(center * center, -1, keepdims=True) + EPSILON)
        normed = center * scaled
        NORM[index, r0:r1] = normed
        RSTD[index, r0:r1] = scaled
        return normed * gains[gain_row : gain_row + 1] + shifts[gain_row : gain_row + 1]

    @jax.named_scope("norm_gradient")
    def backward_norm(upstream, index, gain_row, bias_row, r0, r1):
        normed = NORM[index, r0:r1]
        through = upstream * gains[gain_row : gain_row + 1]
        inner = (
            through
            - jnp.mean(through, -1, keepdims=True)
            - normed * jnp.mean(through * normed, -1, keepdims=True)
        )
        result = RSTD[index, r0:r1] * inner
        VG[5 + gain_row : 6 + gain_row] += jnp.sum(upstream * normed, 0, keepdims=True)
        VG[10 + gain_row : 11 + gain_row] += jnp.sum(upstream, 0, keepdims=True)
        VG[bias_row : bias_row + 1] += jnp.sum(result, 0, keepdims=True)
        return result

    def rows_of_group(p, g, stream):
        r0, r1 = stream
        return A[p, 2 * g : 2 * g + 2, r0:r1, :].reshape(2 * (r1 - r0), D_MODEL)

    def project(p, g, stream, w, QV):
        r0, r1 = stream
        for n in range(NT):
            column = slice(n * TILE, (n + 1) * TILE)
            mapped = dot_nn(rows_of_group(p, g, stream), W[w, :, column]) + QB[w : w + 1, column]
            QV[2 * g : 2 * g + 2, r0:r1, column] = mapped.astype(BF).reshape(2, r1 - r0, TILE)

    def attend(g, stream, QV, Cb, PL, PV, crossed):
        for s in (2 * g, 2 * g + 1):
            attend_slab(QV, Cb, PL, PV, crossed, stream, s)

    def expand_rows(g, stream):
        r0, r1 = stream
        rows = r1 - r0
        w = EXPAND[stream]
        for n in range(NT):
            column = slice(n * TILE, (n + 1) * TILE)
            before = dot_nn(rows_of_group(2, g, stream), W[w, :, column]) + QB[w : w + 1, column]
            half = 0.5 * (1.0 + lax.erf(before * math.sqrt(0.5)))
            slope = half + before * jnp.exp(-0.5 * before * before) * (1.0 / math.sqrt(2.0 * math.pi))
            H[2 * g : 2 * g + 2, r0:r1, column] = (before * half).astype(BF).reshape(2, rows, TILE)
            GP[2 * g : 2 * g + 2, r0:r1, column] = slope.astype(BF).reshape(2, rows, TILE)

    def hidden_gradient(g, stream):
        r0, r1 = stream
        rows = r1 - r0
        for n in range(NT):
            column = slice(n * TILE, (n + 1) * TILE)
            up_hidden = dot_nn(rows_of_group(3, g, stream), W[CONTRACT[stream], :, column])
            slope = GP[2 * g : 2 * g + 2, r0:r1, column].reshape(2 * rows, TILE)
            D[2 * g : 2 * g + 2, r0:r1, column] = (
                (up_hidden * slope.astype(F32)).astype(BF).reshape(2, rows, TILE)
            )

    def context_gradient(p, g, stream, w):
        r0, r1 = stream
        upstream = dot_nn(rows_of_group(p, g, stream), W[w, :, 512:768])
        D[2 * g : 2 * g + 2, r0:r1, 512:768] = upstream.astype(BF).reshape(2, r1 - r0, TILE)

    def attend_gradient(g, streams, QV, PL, PV, crossed):
        for s in (2 * g, 2 * g + 1):
            attend_back_slab(QV, PL, PV, crossed, streams, s)

    def all_rows(ref, r0, r1, lanes):
        value = ref[:, r0:r1, lanes]
        return value.reshape(SLOTS * (r1 - r0), value.shape[-1])

    def weight_grad(w, lhs_p, rhs_ref, r0, r1, lanes=slice(0, 768)):
        for m in range(NT):
            column = slice(m * TILE, (m + 1) * TILE)
            left = all_rows(A.at[lhs_p], r0, r1, column)
            G[w, column, lanes] = dot_tn(left, all_rows(rhs_ref, r0, r1, lanes)).astype(BF)

    def attention_weight_grad(w, x_p, b_p, Cb, r0, r1):
        weight_grad(w, x_p, D, r0, r1, slice(0, 512))
        for m in range(NT):
            column = slice(m * TILE, (m + 1) * TILE)
            G[w, column, 512:768] = (
                dot_tn(all_rows(A.at[x_p], r0, r1, column), all_rows(D, r0, r1, slice(512, 768)))
                + dot_tn(all_rows(A.at[b_p], r0, r1, column), all_rows(Cb, r0, r1, slice(0, 256)))
            ).astype(BF)

    def bias_grad(row, r0, r1):
        total = jnp.zeros((1, D_MODEL), F32)
        for s in range(SLOTS):
            total = total + jnp.sum(D[s, r0:r1].astype(F32), 0, keepdims=True)
        QG[row : row + 1] = total

    def grad_first(w):
        for j in range(2):
            half = rows_of_chip(k_flip[2], (1 - j) * SHARE, SHARE)
            send(G.at[w, half], RD.at[j, w], plane[j], gsem.at[2, w])

    def grad_second(w):
        wait_bytes(RD.at[:, w], gsem.at[2, w])
        for j in range(2):
            half = rows_of_chip(k_flip[1 - j], (1 - j) * SHARE, SHARE)
            G[w, half] = (G[w, half].astype(F32) + RD[j, w].astype(F32)).astype(BF)
        for j in range(2):
            send(G.at[w, rows_of_chip(k_flip[j])], RX.at[j, w], plane[j], gsem.at[j, w])

    grad_nears = []

    def grad_third(w):
        for j in range(2):
            wait_bytes(RX.at[j, w], gsem.at[j, w])
        total = G[w, pair_rows].astype(F32) + RX[0, w].astype(F32) + RX[1, w].astype(F32)
        G[w, pair_rows] = total.astype(BF)
        low, high = rows_of_chip(k, 0, SHARE), rows_of_chip(k, SHARE, SHARE)
        slot = counter[0]
        counter[0] += 2
        own = pltpu.make_async_copy(G.at[w, low], R2.at[0, w], gsem2.at[w])
        near = remote(G.at[w, high], R2.at[0, w], ssem.at[slot], gsem2.at[w], sib)
        far_low = remote(G.at[w, low], R2.at[1, w], ssem.at[slot], gsem2.at[w], (2 * k, z2))
        far_high = remote(G.at[w, high], R2.at[1, w], ssem.at[slot + 1], gsem2.at[w], (2 * k + 1, z2))

        @pl.when(c == 0)
        def _():
            own.start()
            near.start()

        @pl.when(c == 1)
        def _():
            far_low.start()
            far_high.start()

        grad_nears.append((near, far_low, far_high))

    def grad_last(w):
        wait_bytes(R2.at[:, w], gsem2.at[w])
        wgrad[w] = R2[0, w].astype(F32) + R2[1, w].astype(F32)

    def count_step(stage, peer):
        count_copies[stage].wait_recv()
        CA[stage + 1] = CA[stage] + CR[stage]
        if peer is not None:
            count_copies.append(send(CA.at[stage + 1], CR.at[stage + 1], peer))

    VG[...] = jnp.zeros_like(VG)
    QG[...] = jnp.zeros_like(QG)
    cross = (QVK.at[0], C.at[0], PCL, PCV, True)
    inner = (QVK.at[1], C.at[1], PSL, PSV, False)

    weight_second(0)
    attention_share(2)
    nears.append(weight_first(2))
    attention_share(1)
    nears.append(weight_first(1))
    far_x = {stream: gather_forward(rows_x[stream]) for stream in (VIS, LANG)}
    kv_sib.wait_recv()
    kv_zp.wait_recv()
    kv_far = send(KV.at[2], KV.at[3], sib)
    bias_swap.wait_recv()
    QB[...] = jnp.where(c == 1, QR[...], QO[...])
    weight_third(0)
    kv_far.wait_recv()
    arrived("rows", rows_x[VIS][2], rows_x[LANG][2])
    weight_ready(0)

    project(0, 0, BOTH, 0, QVK.at[0])
    weight_second(2)
    nears.append(weight_first(4))
    attend(0, VIS, *cross)
    partial_nt(0, C.at[0], VIS, 0, slice(512, 768))
    near_v = sums_near(VIS)
    weight_second(1)
    nears.append(weight_first(6))
    attend(0, LANG, *cross)
    partial_nt(0, C.at[0], LANG, 0, slice(512, 768))
    near_l = sums_near(LANG)
    arrived("rows", far_x[VIS], far_x[LANG])
    project(0, 1, BOTH, 0, QVK.at[0])
    attend(1, VIS, *cross)
    partial_nt(1, C.at[0], VIS, 0, slice(512, 768))
    far_v = sums_far(VIS)
    attend(1, LANG, *cross)
    z_v = sums_z(VIS, far_v)
    partial_nt(1, C.at[0], LANG, 0, slice(512, 768))
    far_l = sums_far(LANG)
    weight_third(2)
    z_l = sums_z(LANG, far_l)
    count_step(0, plane[0])
    weight_third(1)

    def first_norm(stream, *copies):
        r0, r1 = stream
        value = reduced(stream, *copies) + out_bias[0:1] + A[0, 0, r0:r1].astype(F32)
        A[1, 0, r0:r1] = forward_norm(value, 0, 0, r0, r1).astype(BF)
        return gather_start(1, stream)

    rows_v = first_norm(VIS, near_v, z_v)
    rows_l = first_norm(LANG, near_l, z_l)

    def self_rows(g, stream):
        w = SELF[stream]
        project(1, g, stream, w, QVK.at[1])
        attend(g, stream, *inner)
        partial_nt(g, C.at[1], stream, w, slice(512, 768))

    weight_second(4)
    weight_ready(2)
    arrived("rows", rows_v[2])
    self_rows(0, VIS)
    near_v = sums_near(VIS)
    far_x = gather_forward(rows_v)
    weight_second(6)
    nears.append(weight_first(3))
    weight_ready(1)
    arrived("rows", rows_l[2])
    self_rows(0, LANG)
    near_l = sums_near(LANG)
    far_y = gather_forward(rows_l)
    arrived("rows", far_x)
    self_rows(1, VIS)
    far_v = sums_far(VIS)
    weight_third(4)
    nears.append(weight_first(5))
    arrived("rows", far_y)
    self_rows(1, LANG)
    z_v = sums_z(VIS, far_v)
    far_l = sums_far(LANG)
    count_step(1, plane[1])
    z_l = sums_z(LANG, far_l)
    weight_third(6)

    def second_norm(stream, *copies):
        r0, r1 = stream
        n = 1 if stream == LANG else 2
        value = reduced(stream, *copies) + out_bias[n : n + 1] + A[1, 0, r0:r1].astype(F32)
        A[2, 0, r0:r1] = forward_norm(value, 1, n, r0, r1).astype(BF)
        return gather_start(2, stream)

    rows_v = second_norm(VIS, near_v, z_v)
    rows_l = second_norm(LANG, near_l, z_l)

    weight_second(3)
    weight_ready(4)
    arrived("rows", rows_v[2])
    expand_rows(0, VIS)
    far_x = gather_forward(rows_v)
    weight_second(5)
    arrived("rows", far_x)
    expand_rows(1, VIS)
    far_y = gather_forward(rows_l)
    weight_ready(6)
    partial_nt(1, H, VIS, 6, slice(0, 768))
    far_v = sums_far(VIS)
    weight_third(3)
    partial_nt(0, H, VIS, 6, slice(0, 768))
    near_v = sums_near(VIS)
    z_v = sums_z(VIS, far_v)
    weight_ready(3)
    arrived("rows", rows_l[2], far_y)
    expand_rows(0, LANG)
    expand_rows(1, LANG)
    weight_third(5)
    count_step(2, None)

    def last_norm(stream, *copies):
        r0, r1 = stream
        n = 0 if stream == LANG else 1
        value = reduced(stream, *copies) + contract_b[n : n + 1] + A[2, 0, r0:r1].astype(F32)
        OUTS[r0:r1] = forward_norm(value, 2, 3 + n, r0, r1).astype(BF)
        scale = total_items / CA[3, n : n + 1, 0:1]
        upstream = COT[r0:r1].astype(F32) * (FLAG[r0:r1] * scale)
        result = backward_norm(upstream, 2, 3 + n, 3 + n, r0, r1)
        DZ[r0:r1] = result
        A[3, 0, r0:r1] = result.astype(BF)
        return gather_start(3, stream)

    rows_v = last_norm(VIS, near_v, z_v)
    weight_ready(5)
    partial_nt(1, H, LANG, 5, slice(0, 768))
    far_l = sums_far(LANG)
    partial_nt(0, H, LANG, 5, slice(0, 768))
    near_l = sums_near(LANG)
    z_l = sums_z(LANG, far_l)

    def feed_gradient(g, stream):
        hidden_gradient(g, stream)
        partial_nt(g, D, stream, EXPAND[stream], slice(0, 768))

    arrived("rows", rows_v[2])
    feed_gradient(0, VIS)
    near_v = sums_near(VIS)
    far_x = gather_forward(rows_v)
    rows_l = last_norm(LANG, near_l, z_l)
    arrived("rows", far_x)
    feed_gradient(1, VIS)
    far_v = sums_far(VIS)
    arrived("rows", rows_l[2])
    feed_gradient(0, LANG)
    near_l = sums_near(LANG)
    z_v = sums_z(VIS, far_v)
    far_y = gather_forward(rows_l)
    weight_grad(6, 3, H, *VIS)
    grad_first(6)
    arrived("rows", far_y)
    feed_gradient(1, LANG)
    far_l = sums_far(LANG)
    weight_grad(4, 2, D, *VIS)
    grad_first(4)
    z_l = sums_z(LANG, far_l)
    bias_grad(4, *VIS)

    def second_norm_back(stream, *copies):
        r0, r1 = stream
        n = 1 if stream == LANG else 2
        result = backward_norm(DZ[r0:r1] + reduced(stream, *copies), 1, n, n, r0, r1)
        DZ[r0:r1] = result
        A[4, 0, r0:r1] = result.astype(BF)
        return gather_start(4, stream)

    rows_v = second_norm_back(VIS, near_v, z_v)
    tail_out = [
        send(OUTS.at[pl.ds(RL - LANG_TAIL, LANG_TAIL)], TLO, up),
        send(OUTS.at[pl.ds(ROWS - VIS_TAIL, VIS_TAIL)], TVO, up),
    ]
    weight_grad(5, 3, H, *LANG)
    grad_first(5)
    grad_second(6)
    rows_l = second_norm_back(LANG, near_l, z_l)
    weight_grad(3, 2, D, *LANG)
    grad_first(3)
    bias_grad(3, *LANG)
    grad_second(4)

    def self_gradient(g, stream):
        w = SELF[stream]
        context_gradient(4, g, stream, w)
        attend_gradient(g, (stream,), QVK.at[1], PSL, PSV, False)
        partial_nt(g, D, stream, w, slice(0, 768))

    arrived("rows", rows_v[2])
    self_gradient(0, VIS)
    near_v = sums_near(VIS)
    far_x = gather_forward(rows_v)
    grad_second(5)
    arrived("rows", rows_l[2])
    self_gradient(0, LANG)
    near_l = sums_near(LANG)
    far_y = gather_forward(rows_l)
    arrived("rows", far_x)
    self_gradient(1, VIS)
    far_v = sums_far(VIS)
    grad_second(3)
    arrived("rows", far_y)
    self_gradient(1, LANG)
    z_v = sums_z(VIS, far_v)
    far_l = sums_far(LANG)
    grad_third(6)
    z_l = sums_z(LANG, far_l)
    attention_weight_grad(2, 1, 4, C.at[1], *VIS)
    grad_first(2)
    bias_grad(2, *VIS)
    grad_third(4)

    def first_norm_back(stream, *copies):
        r0, r1 = stream
        result = backward_norm(DZ[r0:r1] + reduced(stream, *copies), 0, 0, 0, r0, r1)
        DZ[r0:r1] = result
        A[5, 0, r0:r1] = result.astype(BF)
        return gather_start(5, stream)

    rows_v = first_norm_back(VIS, near_v, z_v)
    rows_l = first_norm_back(LANG, near_l, z_l)
    attention_weight_grad(1, 1, 4, C.at[1], *LANG)
    grad_first(1)
    bias_grad(1, *LANG)
    grad_third(5)
    grad_second(2)

    arrived("rows", rows_v[2], rows_l[2])
    for stream in (VIS, LANG):
        context_gradient(5, 0, stream, 0)
    attend_gradient(0, None, QVK.at[0], PCL, PCV, True)
    far_x = gather_forward(rows_v)
    far_y = gather_forward(rows_l)
    for stream in (VIS, LANG):
        partial_nt(0, D, stream, 0, slice(0, 768))
    near_v = sums_near(VIS)
    near_l = sums_near(LANG)
    grad_second(1)
    grad_third(3)
    arrived("rows", far_x, far_y)
    for stream in (VIS, LANG):
        context_gradient(5, 1, stream, 0)
    attend_gradient(1, None, QVK.at[0], PCL, PCV, True)
    attention_weight_grad(0, 0, 5, C.at[0], *BOTH)
    grad_first(0)
    bias_grad(0, *BOTH)
    quarter = jnp.where(c == 0, z, z2)
    AVA[0, 0:16] = VG[...]
    for j in range(4):
        AVA[0, 16 + 8 * j : 24 + 8 * j] = jnp.where(quarter == j, QG[...], 0.0)
    vector_peers = [sib, plane[0], plane[1], zp, (d, z2)]
    vector_copies = [send(AVA.at[0], AVR.at[0], vector_peers[0])]

    def vector_step(stage):
        arrived("vectors", vector_copies[stage])
        AVA[stage + 1] = AVA[stage] + AVR[stage]
        if stage < 4:
            vector_copies.append(send(AVA.at[stage + 1], AVR.at[stage + 1], vector_peers[stage + 1]))

    partial_nt(1, D, VIS, 0, slice(0, 768))
    far_v = sums_far(VIS)
    partial_nt(1, D, LANG, 0, slice(0, 768))
    far_l = sums_far(LANG)
    z_v = sums_z(VIS, far_v)
    z_l = sums_z(LANG, far_l)
    vector_step(0)
    grad_second(0)
    grad_third(2)
    vector_step(1)
    grad_third(1)
    vector_step(2)
    for w in (6, 4, 5, 3):
        grad_last(w)
    grad_third(0)
    vector_step(3)
    for stream, copies in ((VIS, (near_v, z_v)), (LANG, (near_l, z_l))):
        r0, r1 = stream
        DZ[r0:r1] = DZ[r0:r1] + reduced(stream, *copies)
    tail_grad = [
        send(DZ.at[pl.ds(RL - LANG_TAIL, LANG_TAIL)], TLG, up),
        send(DZ.at[pl.ds(ROWS - VIS_TAIL, VIS_TAIL)], TVG, up),
    ]
    for w in (2, 1):
        grad_last(w)
    vector_step(4)
    vec_out[...] = AVA[5, 0:16]
    qb_out[...] = AVA[5, pl.ds(pl.multiple_of(16 + 8 * z, 8), 8)]

    arrived("tails", *tail_out, *tail_grad)
    before_l = jnp.where(z == 1, 0, 25 - 5 * z)
    before_v = jnp.where(z == 1, 0, 45 - 9 * z)
    tail_shift_l = own_l - before_l - (RL - LANG_TAIL)
    tail_shift_v = own_v - before_v - (RV - VIS_TAIL)
    for own_rows, off, tail_rows, shift, out_ref, grad_ref, r0, r1, t_out, t_grad in (
        (own_l, off_l, LANG_TAIL, tail_shift_l, lang_out, lang_grad, 0, RL, TLO, TLG),
        (own_v, off_v, VIS_TAIL, tail_shift_v, vis_out, vis_grad, RL, ROWS, TVO, TVG),
    ):
        from_own = select_rows((own_rows, r1 - r0), -off, off, own_rows)
        from_tail = select_rows((own_rows, tail_rows), shift, 0, off)
        out_ref[...] = (
            dot_nn(from_own.astype(BF), OUTS[r0:r1]) + dot_nn(from_tail.astype(BF), t_out[...])
        ).astype(BF)
        exact = lax.Precision.HIGHEST
        grad_ref[...] = jnp.dot(
            from_own, DZ[r0:r1], precision=exact, preferred_element_type=F32
        ) + jnp.dot(from_tail, t_grad[...], precision=exact, preferred_element_type=F32)

    grad_last(0)

    for copy in pending:
        copy.wait_send()
    for index, stream in list(stage_used):
        stage_free(index, stream)

    @pl.when(c == 1)
    def _():
        for copy in nears:
            copy.wait_send()
        for _, far_low, far_high in grad_nears:
            far_low.wait_send()
            far_high.wait_send()

    @pl.when(c == 0)
    def _():
        for near, _, _ in grad_nears:
            near.wait_send()
    assert counter[0] <= ssem.shape[0] and counter[1] <= rsem.shape[0], counter


N_SEND = 192
N_RECV = 112


def fused_layer(total_items, *operands):
    own_l, own_v = operands[0].shape[0], operands[1].shape[0]
    vmem = pl.BlockSpec(memory_space=pltpu.VMEM)
    smem = pl.BlockSpec(memory_space=pltpu.SMEM)
    shapes = [
        ((own_l, D), BF),
        ((own_v, D), BF),
        ((own_l, D), F32),
        ((own_v, D), F32),
        ((7, SHARE, D), F32),
        ((16, D), F32),
        ((8, D), F32),
    ]
    scratch = [
        ((7, D, D), BF),
        ((7, D, D), BF),
        ((2, 7, SHARE, D), BF),
        ((2, 7, HALF_PAIR, D), BF),
        ((2, 7, SHARE, D), BF),
        ((6, SLOTS, ROWS, D), BF),
        ((SLOTS, 8, TILE), F32),
        ((3, ROWS, D), BF),
        ((3, ROWS, D), BF),
        ((2, SLOTS, ROWS, D), BF),
        ((SLOTS, ROWS, D), BF),
        ((2, SLOTS, ROWS, TILE), BF),
        ((SLOTS, ROWS, D), BF),
        ((SLOTS, ROWS, D), BF),
        ((SLOTS, 3 * RL, RV), BF),
        ((SLOTS, 3 * RV, RL), BF),
        ((SLOTS, 3 * RL, RL), BF),
        ((SLOTS, 3 * RV, RV), BF),
        ((ROWS, D), F32),
        ((ROWS, D), F32),
        ((3, ROWS, D), F32),
        ((3, ROWS, 1), F32),
        ((ROWS, D), F32),
        ((ROWS, D), BF),
        ((3, SHARE, D), BF),
        ((ROWS, 1), F32),
        ((8, D), F32),
        ((8, D), F32),
        ((8, D), F32),
        ((4, 8, 128), F32),
        ((3, 8, 128), F32),
        ((16, D), F32),
        ((8, D), F32),
        ((6, N_AR, D), F32),
        ((5, N_AR, D), F32),
        ((2, LANG_HEAD, D), BF),
        ((2, VIS_HEAD, D), BF),
        ((ROWS, D), BF),
        ((LANG_TAIL, D), BF),
        ((VIS_TAIL, D), BF),
        ((LANG_TAIL, D), F32),
        ((VIS_TAIL, D), F32),
    ]
    dma = pltpu.SemaphoreType.DMA
    return pl.pallas_call(
        partial(layer_kernel, total_items),
        out_shape=[jax.ShapeDtypeStruct(s, t) for s, t in shapes],
        in_specs=[vmem] * 4 + [smem] * 3 + [vmem] * (len(operands) - 7),
        out_specs=[vmem] * len(shapes),
        scratch_shapes=[pltpu.VMEM(s, t) for s, t in scratch]
        + [dma((N_SEND,)), dma((N_RECV,)), dma((3, 7)), dma((7,)), dma((3, 7)), dma((7,)), dma((1,))],
        compiler_params=pltpu.CompilerParams(
            collective_id=0, has_side_effects=True, vmem_limit_bytes=VMEM_LIMIT
        ),
    )(*operands)


def unpack_kernel(lo, vo, lg, vg, wgrad, vec, qb, *outs):
    (lo_out, vo_out, lg_out, vg_out, proj, qv, outw, outb, exp, expb, con, conb, gain, shift) = outs
    lo_out[...] = lo[...]
    vo_out[...] = vo[...]
    lg_out[...] = lg[...]
    vg_out[...] = vg[...]
    width = HALF_PAIR
    for b in range(3):
        for j, lane in enumerate((0, 2 * width, width)):
            proj[b, j] = wgrad[b, :, lane : lane + width]
        outw[b] = wgrad[b, :, 3 * width :].T
        for j in range(2):
            qv[b, j : j + 1] = qb[b : b + 1, j * width : (j + 1) * width]
    for stream in range(2):
        exp[stream] = wgrad[3 + stream]
        con[stream] = wgrad[5 + stream]
    expb[...] = qb[3:5]
    outb[...] = vec[0:3]
    conb[...] = vec[3:5]
    gain[...] = vec[5:10]
    shift[...] = vec[10:15]


def unpack(packed, shapes):
    vmem = pl.BlockSpec(memory_space=pltpu.VMEM)
    return pl.pallas_call(
        unpack_kernel,
        out_shape=shapes,
        in_specs=[vmem] * len(packed),
        out_specs=[vmem] * len(shapes),
        compiler_params=pltpu.CompilerParams(vmem_limit_bytes=VMEM_LIMIT),
    )(*packed)


def on_device_fused(
    language_input,
    vision_input,
    word_lengths,
    region_counts,
    task_flags,
    language_cotangent,
    vision_cotangent,
    projection_weight,
    query_value_bias,
    output_weight,
    output_bias,
    expand_weight,
    expand_bias,
    contract_weight,
    contract_bias,
    norm_gain,
    norm_bias,
):
    packed = fused_layer(
        float(word_lengths.shape[0] * lax.axis_size("dp")),
        language_input,
        vision_input,
        language_cotangent,
        vision_cotangent,
        word_lengths,
        region_counts,
        task_flags.T,
        projection_weight,
        query_value_bias,
        output_weight,
        expand_weight,
        expand_bias,
        contract_weight.transpose(0, 2, 1),
        output_bias,
        contract_bias,
        norm_gain,
        norm_bias,
    )
    like = [
        (language_input, BF),
        (vision_input, BF),
        (language_input, F32),
        (vision_input, F32),
        (projection_weight, F32),
        (query_value_bias, F32),
        (output_weight, F32),
        (output_bias, F32),
        (expand_weight, F32),
        (expand_bias, F32),
        (contract_weight.transpose(0, 2, 1), F32),
        (contract_bias, F32),
        (norm_gain, F32),
        (norm_bias, F32),
    ]
    outs = list(unpack(packed, [jax.ShapeDtypeStruct(a.shape, t) for a, t in like]))
    outs[10] = outs[10].transpose(0, 2, 1)
    return tuple(outs)


def solution(mesh):
    in_specs = (
        P(("dp", "mp"), None),
        P(("dp", "mp"), None),
        P("dp"),
        P("dp"),
        P("dp", None),
        P(("dp", "mp"), None),
        P(("dp", "mp"), None),
        P(None, None, "dp", "mp"),
        P(None, None, "mp"),
        P(None, "mp", "dp"),
        P(),
        P(None, "dp", "mp"),
        P(None, "mp"),
        P(None, "mp", "dp"),
        P(),
        P(),
        P(),
    )
    out_specs = (
        P(("dp", "mp"), None),
        P(("dp", "mp"), None),
        P(("dp", "mp"), None),
        P(("dp", "mp"), None),
        P(None, None, "dp", "mp"),
        P(None, None, "mp"),
        P(None, "mp", "dp"),
        P(),
        P(None, "dp", "mp"),
        P(None, "mp"),
        P(None, "mp", "dp"),
        P(),
        P(),
        P(),
    )
    fused = dict(mesh.shape) == {"dp": 8, "mp": 4}
    return jax.shard_map(
        on_device_fused if fused else on_device, mesh=mesh, in_specs=in_specs, out_specs=out_specs, check_vma=False
    )
```

```python
from functools import partial
import math

import jax
import jax.numpy as jnp
from jax import lax
from jax.experimental import pallas as pl
from jax.experimental.pallas import tpu as pltpu
from jax.sharding import PartitionSpec as P

D = 768
HEADS = 12
WORDS = 20
REGIONS = 36
D_MODEL = D
D_HEAD = D // HEADS

EPSILON = 1e-12
MASKED = -1e30


def layer_norm(summed, gain, shift):
    center = summed - jnp.mean(summed, -1, keepdims=True)
    scaled = lax.rsqrt(jnp.mean(center * center, -1, keepdims=True) + EPSILON)
    normed = center * scaled
    return (normed * gain + shift, normed, scaled)


def norm_back(upstream, normed, scaled, gain):
    through = upstream * gain
    inner = (
        through
        - jnp.mean(through, -1, keepdims=True)
        - normed * jnp.mean(through * normed, -1, keepdims=True)
    )
    return (scaled * inner, jnp.sum(upstream * normed, 0), jnp.sum(upstream, 0))


def split_heads(rows, item_count):
    head_size = D // HEADS
    return rows.reshape(
        item_count, rows.shape[0] // item_count, rows.shape[1] // head_size, head_size
    )


def join_heads(block):
    return block.reshape(block.shape[0] * block.shape[1], block.shape[2] * block.shape[3])


def project(rows, weight, bias, item_count):
    mapped = jnp.einsum("rd,jde->jre", rows, weight, preferred_element_type=jnp.float32)
    query = split_heads((mapped[0] + bias[0]).astype(jnp.bfloat16), item_count)
    keys = split_heads(mapped[1].astype(jnp.bfloat16), item_count)
    values = split_heads((mapped[2] + bias[1]).astype(jnp.bfloat16), item_count)
    return (query, keys, values)


def masked_scores(query, keys, valid):
    scores = jnp.einsum("inhd,imhd->ihnm", query, keys, preferred_element_type=jnp.float32) * (
        1.0 / math.sqrt(D // HEADS)
    )
    return jnp.where(valid[:, None, None, :], scores, MASKED)


def attend(query, keys, values, valid):
    scores = masked_scores(query, keys, valid)
    highest = jnp.max(scores, -1, keepdims=True)
    raised = jnp.exp(scores - highest)
    summed = jnp.sum(raised, -1, keepdims=True)
    context = jnp.einsum(
        "ihnm,imhd->inhd",
        (raised / summed).astype(jnp.bfloat16),
        values,
        preferred_element_type=jnp.float32,
    )
    return (join_heads(context).astype(jnp.bfloat16), highest + jnp.log(summed))


def attend_back(query, keys, values, valid, log_total, context_grad):
    factor = 1.0 / math.sqrt(D // HEADS)
    upstream = context_grad.reshape(query.shape)
    weights = jnp.exp(masked_scores(query, keys, valid) - log_total)
    weight_grad = jnp.einsum(
        "inhd,imhd->ihnm", upstream, values, preferred_element_type=jnp.float32
    )
    score_grad = (
        weights * (weight_grad - jnp.sum(weight_grad * weights, -1, keepdims=True))
    ).astype(jnp.bfloat16)
    query_grad = (
        jnp.einsum("ihnm,imhd->inhd", score_grad, keys, preferred_element_type=jnp.float32) * factor
    ).astype(jnp.bfloat16)
    keys_grad = (
        jnp.einsum("ihnm,inhd->imhd", score_grad, query, preferred_element_type=jnp.float32)
        * factor
    ).astype(jnp.bfloat16)
    values_grad = jnp.einsum(
        "ihnm,inhd->imhd",
        weights.astype(jnp.bfloat16),
        upstream,
        preferred_element_type=jnp.float32,
    ).astype(jnp.bfloat16)
    return (join_heads(query_grad), join_heads(keys_grad), join_heads(values_grad))


def project_back(rows, query_grad, keys_grad, values_grad):
    stacked = jnp.stack([query_grad, keys_grad, values_grad])
    weight_grad = jnp.einsum("rd,jre->jde", rows, stacked, preferred_element_type=jnp.float32)
    bias_grad = jnp.stack(
        [jnp.sum(query_grad.astype(jnp.float32), 0), jnp.sum(values_grad.astype(jnp.float32), 0)]
    )
    return (weight_grad, bias_grad, stacked)


def gather_rows(language_rows, vision_rows):
    return (
        lax.all_gather(language_rows, "mp", axis=0, tiled=True),
        lax.all_gather(vision_rows, "mp", axis=0, tiled=True),
    )


def rows_of(language_part, vision_part):
    return (
        lax.all_to_all(language_part, "mp", split_axis=0, concat_axis=1, tiled=True),
        lax.all_to_all(vision_part, "mp", split_axis=0, concat_axis=1, tiled=True),
    )


def gather_grads(language_rows, vision_rows):
    return (
        lax.all_gather(language_rows, "mp", axis=0, tiled=True),
        lax.all_gather(vision_rows, "mp", axis=0, tiled=True),
    )


def grads_of(language_part, vision_part):
    return (
        lax.all_to_all(language_part, "mp", split_axis=1, concat_axis=2, tiled=True),
        lax.all_to_all(vision_part, "mp", split_axis=1, concat_axis=2, tiled=True),
    )


def matmul(left, right):
    return jnp.dot(left, right, preferred_element_type=jnp.float32)


def on_device(
    language_input,
    vision_input,
    word_lengths,
    region_counts,
    task_flags,
    language_cotangent,
    vision_cotangent,
    projection_weight,
    query_value_bias,
    output_weight,
    output_bias,
    expand_weight,
    expand_bias,
    contract_weight,
    contract_bias,
    norm_gain,
    norm_bias,
):
    item_count = word_lengths.shape[0]
    flag_total = lax.psum(jnp.sum(task_flags, 0), "dp")
    projection, out_weight, expand, contract = (
        lax.all_gather(projection_weight, "dp", axis=2, tiled=True),
        lax.all_gather(output_weight, "dp", axis=2, tiled=True),
        lax.all_gather(expand_weight, "dp", axis=1, tiled=True),
        lax.all_gather(contract_weight, "dp", axis=2, tiled=True),
    )
    projection_full, out_full, expand_full, contract_full = (
        lax.all_gather(projection, "mp", axis=3, tiled=True),
        lax.all_gather(out_weight, "mp", axis=1, tiled=True),
        lax.all_gather(expand, "mp", axis=2, tiled=True),
        lax.all_gather(contract, "mp", axis=1, tiled=True),
    )
    valid = [
        jnp.arange(WORDS, dtype=jnp.int32)[None, :] < word_lengths[:, None],
        jnp.arange(REGIONS, dtype=jnp.int32)[None, :] < region_counts[:, None],
    ]
    row_counts = [WORDS, REGIONS]
    inputs = [language_input.astype(jnp.float32), vision_input.astype(jnp.float32)]
    cross_rows = gather_rows(language_input, vision_input)
    cross_parts = [
        project(cross_rows[stream], projection[0], query_value_bias[0], item_count)
        for stream in range(2)
    ]
    cross_context = []
    cross_total = []
    for stream in range(2):
        other = 1 - stream
        context, log_total = attend(
            cross_parts[stream][0], cross_parts[other][1], cross_parts[other][2], valid[other]
        )
        cross_context.append(context)
        cross_total.append(log_total)
    moved = rows_of(cross_context[0], cross_context[1])
    branch = [matmul(moved[stream], out_full[0]) for stream in range(2)]
    first = [
        layer_norm(branch[stream] + output_bias[0] + inputs[stream], norm_gain[0], norm_bias[0])
        for stream in range(2)
    ]
    first_out = [first[stream][0].astype(jnp.bfloat16) for stream in range(2)]
    self_rows = gather_rows(first_out[0], first_out[1])
    self_parts = [
        project(self_rows[stream], projection[1 + stream], query_value_bias[1 + stream], item_count)
        for stream in range(2)
    ]
    self_context = []
    self_total = []
    for stream in range(2):
        context, log_total = attend(
            self_parts[stream][0], self_parts[stream][1], self_parts[stream][2], valid[stream]
        )
        self_context.append(context)
        self_total.append(log_total)
    moved = rows_of(self_context[0], self_context[1])
    branch = [matmul(moved[stream], out_full[1 + stream]) for stream in range(2)]
    second = [
        layer_norm(
            branch[stream] + output_bias[1 + stream] + first_out[stream].astype(jnp.float32),
            norm_gain[1 + stream],
            norm_bias[1 + stream],
        )
        for stream in range(2)
    ]
    second_out = [second[stream][0].astype(jnp.bfloat16) for stream in range(2)]
    feed_rows = gather_rows(second_out[0], second_out[1])
    before = [
        matmul(feed_rows[stream], expand[stream]) + expand_bias[stream] for stream in range(2)
    ]
    hidden = [
        jax.nn.gelu(before[stream], approximate=False).astype(jnp.bfloat16) for stream in range(2)
    ]
    moved = rows_of(hidden[0], hidden[1])
    branch = [matmul(moved[stream], contract_full[stream]) for stream in range(2)]
    third = [
        layer_norm(
            branch[stream] + contract_bias[stream] + second_out[stream].astype(jnp.float32),
            norm_gain[3 + stream],
            norm_bias[3 + stream],
        )
        for stream in range(2)
    ]
    language_out = third[0][0].astype(jnp.bfloat16)
    vision_out = third[1][0].astype(jnp.bfloat16)
    item_scale = task_flags.astype(jnp.float32) * (
        item_count * lax.axis_size("dp") / flag_total.astype(jnp.float32)
    )
    shard_index = lax.axis_index("mp")
    upstream = []
    for stream, cotangent in enumerate([language_cotangent, vision_cotangent]):
        per_row = jnp.repeat(
            item_scale[:, stream],
            row_counts[stream],
            total_repeat_length=item_count * row_counts[stream],
        )
        shard_rows = cotangent.shape[0]
        row_scale = lax.dynamic_slice_in_dim(per_row, shard_index * shard_rows, shard_rows)
        upstream.append(cotangent.astype(jnp.float32) * row_scale[:, None])
    third_back = [
        norm_back(upstream[stream], third[stream][1], third[stream][2], norm_gain[3 + stream])
        for stream in range(2)
    ]
    sent = gather_grads(
        third_back[0][0].astype(jnp.bfloat16), third_back[1][0].astype(jnp.bfloat16)
    )
    expand_local = []
    expand_bias_local = []
    contract_local = []
    before_grads = []
    for stream in range(2):
        hidden_grad = jnp.einsum(
            "rd,fd->rf", sent[stream], contract[stream], preferred_element_type=jnp.float32
        )
        contract_local.append(
            jnp.einsum(
                "rf,rd->fd", hidden[stream], sent[stream], preferred_element_type=jnp.float32
            )
        )
        unused, pull = jax.vjp(partial(jax.nn.gelu, approximate=False), before[stream])
        before_grad = pull(hidden_grad)[0].astype(jnp.bfloat16)
        expand_local.append(
            jnp.einsum(
                "rd,rf->df", feed_rows[stream], before_grad, preferred_element_type=jnp.float32
            )
        )
        expand_bias_local.append(jnp.sum(before_grad.astype(jnp.float32), 0))
        before_grads.append(before_grad[None])
    moved = grads_of(before_grads[0], before_grads[1])
    back = [
        jnp.einsum(
            "rf,df->rd", moved[stream][0], expand_full[stream], preferred_element_type=jnp.float32
        )
        for stream in range(2)
    ]
    second_grad = [third_back[stream][0] + back[stream] for stream in range(2)]
    second_back = [
        norm_back(second_grad[stream], second[stream][1], second[stream][2], norm_gain[1 + stream])
        for stream in range(2)
    ]
    sent = gather_grads(
        second_back[0][0].astype(jnp.bfloat16), second_back[1][0].astype(jnp.bfloat16)
    )
    self_weight = []
    self_bias = []
    self_out = []
    stacks = []
    for stream in range(2):
        context_grad = jnp.einsum(
            "rd,ed->re", sent[stream], out_weight[1 + stream], preferred_element_type=jnp.float32
        ).astype(jnp.bfloat16)
        self_out.append(
            jnp.einsum(
                "re,rd->ed", self_context[stream], sent[stream], preferred_element_type=jnp.float32
            )
        )
        grads = attend_back(
            self_parts[stream][0],
            self_parts[stream][1],
            self_parts[stream][2],
            valid[stream],
            self_total[stream],
            context_grad,
        )
        weight_part, bias_part, stacked = project_back(
            self_rows[stream], grads[0], grads[1], grads[2]
        )
        self_weight.append(weight_part)
        self_bias.append(bias_part)
        stacks.append(stacked)
    moved = grads_of(stacks[0], stacks[1])
    back = [
        jnp.einsum(
            "jre,jde->rd",
            moved[stream],
            projection_full[1 + stream],
            preferred_element_type=jnp.float32,
        )
        for stream in range(2)
    ]
    first_grad = [second_back[stream][0] + back[stream] for stream in range(2)]
    first_back = [
        norm_back(first_grad[stream], first[stream][1], first[stream][2], norm_gain[0])
        for stream in range(2)
    ]
    sent = gather_grads(
        first_back[0][0].astype(jnp.bfloat16), first_back[1][0].astype(jnp.bfloat16)
    )
    cross_out = jnp.einsum(
        "re,rd->ed", cross_context[0], sent[0], preferred_element_type=jnp.float32
    ) + jnp.einsum("re,rd->ed", cross_context[1], sent[1], preferred_element_type=jnp.float32)
    triples = [[None, None, None], [None, None, None]]
    for stream in range(2):
        other = 1 - stream
        context_grad = jnp.einsum(
            "rd,ed->re", sent[stream], out_weight[0], preferred_element_type=jnp.float32
        ).astype(jnp.bfloat16)
        grads = attend_back(
            cross_parts[stream][0],
            cross_parts[other][1],
            cross_parts[other][2],
            valid[other],
            cross_total[stream],
            context_grad,
        )
        triples[stream][0] = grads[0]
        triples[other][1] = grads[1]
        triples[other][2] = grads[2]
    results = [
        project_back(cross_rows[stream], triples[stream][0], triples[stream][1], triples[stream][2])
        for stream in range(2)
    ]
    cross_weight = results[0][0] + results[1][0]
    cross_bias = results[0][1] + results[1][1]
    moved = grads_of(results[0][2], results[1][2])
    back = [
        jnp.einsum(
            "jre,jde->rd", moved[stream], projection_full[0], preferred_element_type=jnp.float32
        )
        for stream in range(2)
    ]
    language_grad = first_back[0][0] + back[0]
    vision_grad = first_back[1][0] + back[1]
    projection_stack = jnp.stack([cross_weight, self_weight[0], self_weight[1]])
    output_stack = jnp.stack([cross_out, self_out[0], self_out[1]])
    projection_grad, output_weight_grad, expand_grad, contract_grad = (
        lax.psum_scatter(projection_stack, "dp", scatter_dimension=2, tiled=True),
        lax.psum_scatter(output_stack, "dp", scatter_dimension=2, tiled=True),
        lax.psum_scatter(jnp.stack(expand_local), "dp", scatter_dimension=1, tiled=True),
        lax.psum_scatter(jnp.stack(contract_local), "dp", scatter_dimension=2, tiled=True),
    )
    query_value_grad, expand_bias_grad = lax.psum(
        (jnp.stack([cross_bias, self_bias[0], self_bias[1]]), jnp.stack(expand_bias_local)), "dp"
    )
    output_bias_local = jnp.stack(
        [
            jnp.sum(first_back[0][0], 0) + jnp.sum(first_back[1][0], 0),
            jnp.sum(second_back[0][0], 0),
            jnp.sum(second_back[1][0], 0),
        ]
    )
    contract_bias_local = jnp.stack([jnp.sum(third_back[0][0], 0), jnp.sum(third_back[1][0], 0)])
    gain_local = jnp.stack(
        [
            first_back[0][1] + first_back[1][1],
            second_back[0][1],
            second_back[1][1],
            third_back[0][1],
            third_back[1][1],
        ]
    )
    shift_local = jnp.stack(
        [
            first_back[0][2] + first_back[1][2],
            second_back[0][2],
            second_back[1][2],
            third_back[0][2],
            third_back[1][2],
        ]
    )
    output_bias_grad, contract_bias_grad, norm_gain_grad, norm_bias_grad = lax.psum(
        (output_bias_local, contract_bias_local, gain_local, shift_local), ("dp", "mp")
    )
    return (
        language_out,
        vision_out,
        language_grad,
        vision_grad,
        projection_grad,
        query_value_grad,
        output_weight_grad,
        output_bias_grad,
        expand_grad,
        expand_bias_grad,
        contract_grad,
        contract_bias_grad,
        norm_gain_grad,
        norm_bias_grad,
    )


MESH = pl.DeviceIdType.MESH
BF = jnp.bfloat16
F32 = jnp.float32
SLOTS = 4
RL = SLOTS * WORDS
REGION_PAD = 40
RV = SLOTS * REGION_PAD
ROWS = RL + RV
SHARE = 96
HALF_PAIR = 2 * SHARE
LANG_HEAD = 16
VIS_HEAD = 32
LANG_TAIL = 32
VIS_TAIL = 64
N_AR = 48
NT = 3
TILE = 256
LANG = (0, RL)
V1 = (RL, RL + RV // 2)
V2 = (RL + RV // 2, ROWS)
VIS = (RL, ROWS)
BOTH = (0, ROWS)
CHAINS = (V1, V2, LANG)
SELF = {LANG: 1, V1: 2, V2: 2}
EXPAND = {LANG: 3, V1: 4, V2: 4}
CONTRACT = {LANG: 5, V1: 6, V2: 6}
PARTS = {w: (w, slice(0, 768)) for w in range(1, 7)} | {0: (0, slice(0, 384)), 7: (0, slice(384, 768))}
VMEM_LIMIT = 63 * 1024 * 1024


def dot_nn(left, right):
    return lax.dot_general(left, right, (((1,), (0,)), ((), ())), preferred_element_type=F32)


def dot_nt(left, right):
    return lax.dot_general(left, right, (((1,), (1,)), ((), ())), preferred_element_type=F32)


def dot_tn(left, right):
    return lax.dot_general(left, right, (((0,), (0,)), ((), ())), preferred_element_type=F32)


def head_mask(first_lane, dtype):
    lane = lax.broadcasted_iota(jnp.int32, (1, TILE), 1) - first_lane
    return [
        jnp.where((lane >= 64 * h) & (lane < 64 * h + 64), 1.0, 0.0).astype(dtype) for h in range(3)
    ]


def item_rows(shape, dim, first, size, pad):
    row = lax.broadcasted_iota(jnp.int32, shape, dim) + first
    item = sum(jnp.where(row >= pad * j, 1, 0) for j in range(1, SLOTS))
    return row - (pad - size) * item, row - pad * item < size


def rows_into_slab(shape, shift, count, size, pad):
    place, real = item_rows(shape, 0, 0, size, pad)
    column = lax.broadcasted_iota(jnp.int32, shape, 1)
    return jnp.where((column - place == shift) & real & (place < count), 1.0, 0.0)


def rows_from_slab(shape, shift, first, low, high, size, pad):
    place, real = item_rows(shape, 1, first, size, pad)
    row = lax.broadcasted_iota(jnp.int32, shape, 0)
    return jnp.where((place - row == shift) & real & (row >= low) & (row < high), 1.0, 0.0)


def layer_kernel(
    total_items,
    lang,
    vis,
    lcot,
    vcot,
    lengths,
    regions,
    flags,
    projection,
    query_value,
    out_weight,
    expand,
    expand_b,
    contract,
    out_bias,
    contract_b,
    gains,
    shifts,
    lang_out,
    vis_out,
    lang_grad,
    vis_grad,
    wgrad,
    vec_out,
    qb_out,
    W,
    G,
    RD,
    RX,
    R2,
    A,
    KV,
    RSB,
    STG,
    QVK,
    D,
    C,
    H,
    GP,
    PCL,
    PCV,
    PS,
    PART,
    PZ,
    NORM,
    RSTD,
    DZ,
    COT,
    SH,
    FLAG,
    QO,
    QB,
    QR,
    CA,
    CR,
    VG,
    QG,
    AVA,
    AVR,
    HL,
    HV,
    OUTS,
    TLO,
    TVO,
    TLG,
    TVG,
    ssem,
    rsem,
    wsem,
    wsem_z,
    gsem,
    gsem2,
):
    d = lax.axis_index("dp")
    z = lax.axis_index("mp")
    c = d % 2
    k = d // 2
    k_flip = [k + 1 - 2 * (k % 2), (k + 2) % 4, 3 - k]
    sib = (d + 1 - 2 * c, z)
    zp = (d, z + 1 - 2 * (z % 2))
    z2 = (z + 2) % 4
    up = (d, (z + 1) % 4)
    down = (d, (z + 3) % 4)
    plane = [(2 * kf + c, z) for kf in k_flip]
    far = (2 * k + 1, z2)

    pending = []
    counter = [0, 0]

    def remote(src, dst, send, recv, device):
        return pltpu.make_async_remote_copy(
            src_ref=src, dst_ref=dst, send_sem=send, recv_sem=recv, device_id=device, device_id_type=MESH
        )

    def send(src, dst, device, recv=None, keep=True):
        slot = counter[0]
        counter[0] += 1
        if recv is None:
            recv = rsem.at[counter[1]]
            counter[1] += 1
        copy = remote(src, dst, ssem.at[slot], recv, device)
        copy.start()
        if keep:
            pending.append(copy)
        return copy

    def wait_bytes(ref, sem):
        pltpu.make_async_copy(ref, ref, sem).wait()

    def arrived(name, *copies):
        with jax.named_scope("wait_" + name):
            for copy in copies:
                copy.wait_recv()

    barrier = pltpu.get_barrier_semaphore()
    peers = [sib, up, down, (d, z2), (d + 1 - 2 * c, z2)] + plane
    for peer in peers:
        pl.semaphore_signal(barrier, inc=1, device_id=peer, device_id_type=MESH)

    def weight_first(part):
        w, lanes = PARTS[part]
        row = pl.ds(pl.multiple_of(d * SHARE, 16), SHARE)
        slot = counter[0]
        counter[0] += 1
        share = SH.at[w] if w < 3 else (expand.at[w - 3] if w < 5 else contract.at[w - 5])
        share = share.at[:, lanes]
        target = W.at[w, row, lanes]
        near = remote(share, target, ssem.at[slot], wsem_z.at[part], sib)
        own = pltpu.make_async_copy(share, target, wsem_z.at[part])

        @pl.when(c == 1)
        def _():
            near.start()

        @pl.when(c == 0)
        def _():
            own.start()

        send(share, target, far, wsem_z.at[part])
        nears.append(near)

    def place(width, first):
        row = lax.broadcasted_iota(jnp.int32, (width, D_MODEL), 0)
        column = lax.broadcasted_iota(jnp.int32, (width, D_MODEL), 1)
        return jnp.where(column - row == first, 1.0, 0.0).astype(BF)

    def attention_share(b):
        SH[b] = (
            dot_nn(projection[b, 0], place(HALF_PAIR, 0))
            + dot_nn(projection[b, 2], place(HALF_PAIR, HALF_PAIR))
            + dot_nn(projection[b, 1], place(HALF_PAIR, 2 * HALF_PAIR))
            + dot_tn(out_weight[b], place(HALF_PAIR, 3 * HALF_PAIR))
        ).astype(BF)

    nears = []
    attention_share(0)

    n_items = lengths.shape[0]
    first_item = 3 * z + jnp.minimum(z, 1)
    KV[0] = jnp.full(KV.shape[1:], -1.0, F32)
    for row, source, size, pad, first_row in ((0, lengths, WORDS, WORDS, 0), (1, regions, REGIONS, REGION_PAD, RL)):
        lane = lax.broadcasted_iota(jnp.int32, (1, TILE), 1)
        owner = jnp.full((1, TILE), -1.0, F32)
        slab_row = lax.broadcasted_iota(jnp.int32, (SLOTS * pad, 1), 0)
        flag = jnp.zeros((SLOTS * pad, 1), F32)
        for j in range(SLOTS):
            item = jnp.minimum(first_item + j, n_items - 1)
            valid = (lane >= j * pad) & (lane < j * pad + source[item]) & (lane < j * pad + size)
            owner = jnp.where(valid, float(j), owner)
            inside = (slab_row >= j * pad) & (slab_row < (j + 1) * pad)
            flag = jnp.where(inside, flags[row, item].astype(F32), flag)
            if row == 1 and j % 2 == 1:
                pair = jnp.full((1, TILE), -1.0, F32)
                for i in (0, 1):
                    other = jnp.minimum(first_item + j - 1 + i, n_items - 1)
                    valid = (lane >= i * pad) & (lane < i * pad + source[other]) & (lane < i * pad + size)
                    pair = jnp.where(valid, float(j - 1 + i), pair)
                KV[0, 2 + j // 2 : 3 + j // 2] = pair
        KV[0, row : row + 1] = owner
        FLAG[first_row : first_row + SLOTS * pad] = flag
        count = flags[row, 0]
        for j in range(1, n_items):
            count = count + flags[row, j]
        CA[0, row : row + 1] = jnp.full((1, 128), count.astype(F32), F32)
    QO[...] = jnp.zeros_like(QO)
    for b in range(3):
        QO[b : b + 1, 0:HALF_PAIR] = query_value[b, 0:1]
        QO[b : b + 1, HALF_PAIR : 2 * HALF_PAIR] = query_value[b, 1:2]
    QO[3:5] = expand_b[...]

    pl.semaphore_wait(barrier, len(peers))
    heads = [
        send(lang.at[pl.ds(0, LANG_HEAD)], HL.at[0], down),
        send(vis.at[pl.ds(0, VIS_HEAD)], HV.at[0], down),
    ]
    weight_first(0)
    weight_first(7)
    heads_cot = [
        send(lcot.at[pl.ds(0, LANG_HEAD)], HL.at[1], down),
        send(vcot.at[pl.ds(0, VIS_HEAD)], HV.at[1], down),
    ]
    kv_sib = send(KV.at[0], KV.at[1], sib)
    kv_zp = send(KV.at[0], KV.at[2], zp)
    count_copies = [send(CA.at[0], CR.at[0], sib)]
    bias_swap = send(QO, QR, (d, z2))

    pair_rows = pl.ds(pl.multiple_of(k * HALF_PAIR, 16), HALF_PAIR)

    def rows_of_chip(chip, first=0, count=HALF_PAIR):
        return pl.ds(pl.multiple_of(chip * HALF_PAIR + first, 16), count)

    def weight_second(part):
        w, lanes = PARTS[part]
        block = W.at[w, pair_rows, lanes]
        wait_bytes(block, wsem_z.at[part])
        for j in range(2):
            send(block, block, plane[j], wsem.at[j, part])

    def weight_third(part):
        w, lanes = PARTS[part]
        for j in range(2):
            wait_bytes(W.at[w, pair_rows, lanes], wsem.at[j, part])
            half = W.at[w, rows_of_chip(k_flip[j], j * SHARE, SHARE), lanes]
            send(half, half, plane[1 - j], wsem.at[2, part])

    def weight_ready(part):
        w, lanes = PARTS[part]
        wait_bytes(W.at[w, pair_rows, lanes], wsem.at[2, part])

    off_l = jnp.where(z == 0, 0, 20 - 5 * z)
    off_v = jnp.where(z == 0, 0, 36 - 9 * z)
    n_l = jnp.where(z == 0, 4 * WORDS, 3 * WORDS)
    n_v = jnp.where(z == 0, 4 * REGIONS, 3 * REGIONS)
    own_l = lang.shape[0]
    own_v = vis.shape[0]
    def gather_start(p, stream):
        rows = pl.ds(stream[0], stream[1] - stream[0])
        return (
            p,
            rows,
            send(A.at[p, 0, rows], A.at[p, 1, rows], sib),
            send(A.at[p, 0, rows], A.at[p, 2, rows], zp),
        )

    def gather_forward(handle):
        p, rows, _, across = handle
        arrived("rows_z", across)
        return send(A.at[p, 2, rows], A.at[p, 3, rows], sib)

    def own_slab(index, source_l, source_v, copies, target):
        arrived("heads", *copies)
        for (r0, r1), size, pad, own, off, count, source, head, head_rows in (
            (VIS, REGIONS, REGION_PAD, own_v, off_v, n_v, source_v, HV, VIS_HEAD),
            (LANG, WORDS, WORDS, own_l, off_l, n_l, source_l, HL, LANG_HEAD),
        ):
            inside = rows_into_slab((r1 - r0, own), off, count, size, pad).astype(BF)
            beyond = rows_into_slab((r1 - r0, head_rows), off - own, count, size, pad).astype(BF)
            target[r0:r1] = (dot_nn(inside, source[...]) + dot_nn(beyond, head[index])).astype(BF)

    own_slab(0, lang, vis, heads, A.at[0, 0])
    rows_x = {stream: gather_start(0, stream) for stream in (VIS, LANG)}

    stage_used = {}

    def stage_free(index, stream):
        copy = stage_used.pop((index, stream), None)
        if copy is not None:
            copy.wait_send()

    def partial_nt(g, lhs_ref, stream, w, lanes):
        r0, r1 = stream
        rows = r1 - r0
        stage_free(g, stream)
        for n in range(NT):
            column = slice(n * TILE, (n + 1) * TILE)
            lhs = lhs_ref[2 * g : 2 * g + 2, r0:r1, :]
            lhs = lhs.reshape(2 * rows, lhs.shape[-1])
            out = dot_nt(lhs, W[w, column, lanes])
            target = PART if g == 0 else PZ
            target[r0:r1, column] = out[:rows]
            STG[g, r0:r1, column] = out[rows:].astype(BF)

    def stage_send(index, stream, device):
        rows = pl.ds(stream[0], stream[1] - stream[0])
        copy = send(STG.at[index, rows], RSB.at[index, rows], device, keep=False)
        stage_used[index, stream] = copy
        return copy

    def sums_near(stream):
        return stage_send(0, stream, sib)

    def sums_far(stream):
        return stage_send(1, stream, sib)

    def sums_z(stream, far):
        r0, r1 = stream
        arrived("sums_core", far)
        stage_free(2, stream)
        STG[2, r0:r1] = (PZ[r0:r1] + RSB[1, r0:r1].astype(F32)).astype(BF)
        return stage_send(2, stream, zp)

    def reduced(stream, *copies):
        r0, r1 = stream
        arrived("sums", *copies)
        return PART[r0:r1] + RSB[0, r0:r1].astype(F32) + RSB[2, r0:r1].astype(F32)

    mask_q = head_mask(0, BF)
    mask_c = head_mask(64, BF)
    mask_q32 = head_mask(0, F32)
    mask_c32 = head_mask(64, F32)
    factor = 1.0 / math.sqrt(D_HEAD)

    def attend_slab(QV, Cb, crossed, stream, s):
        def one(queries, keys_rows, kv_row, item_size, first_item_of, P):
            (q0, q1), (k0, k1) = queries, keys_rows
            nq, nk = q1 - q0, k1 - k0
            query = QV[s, q0:q1, 0:256]
            keys = QV[s, k0:k1, 384:640]
            values = QV[s, k0:k1, 128:384]
            spread = jnp.concatenate([query * mask_q[h] for h in range(3)], 0)
            scores = dot_nt(spread, keys) * factor
            row = lax.broadcasted_iota(jnp.int32, (nq, nk), 0)
            item = jnp.full((nq, nk), float(first_item_of), F32)
            for j in range(1, nq // item_size):
                item = item + jnp.where(row >= j * item_size, 1.0, 0.0)
            same = item == KV[s, kv_row : kv_row + 1, 0:nk]
            scores = jnp.where(same[None], scores.reshape(3, nq, nk), MASKED)
            raised = jnp.exp(scores - jnp.max(scores, -1, keepdims=True))
            weights = (raised / jnp.sum(raised, -1, keepdims=True)).astype(BF).reshape(3 * nq, nk)
            P[s] = weights
            context = dot_nn(weights, values).reshape(3, nq, TILE)
            Cb[s, q0:q1] = (
                context[0] * mask_c32[0] + context[1] * mask_c32[1] + context[2] * mask_c32[2]
            ).astype(BF)

        if stream == LANG:
            if crossed:
                one(LANG, VIS, 1, WORDS, 0, PCL)
            else:
                one(LANG, LANG, 0, WORDS, 0, PS.at[0])
        else:
            half = (V1, V2).index(stream)
            if crossed:
                one(stream, LANG, 0, REGION_PAD, 2 * half, PCV.at[half])
            else:
                one(stream, stream, 2 + half, REGION_PAD, 2 * half, PS.at[1 + half])

    def attend_back_slab(QV, crossed, stream, s):
        def one(queries, keys_rows, P):
            (q0, q1), (k0, k1) = queries, keys_rows
            nq = q1 - q0
            query = QV[s, q0:q1, 0:256]
            keys = QV[s, k0:k1, 384:640]
            values = QV[s, k0:k1, 128:384]
            spread = jnp.concatenate([query * mask_q[h] for h in range(3)], 0)
            upstream = D[s, q0:q1, 512:768]
            up_spread = jnp.concatenate([upstream * mask_c[h] for h in range(3)], 0)
            weights = P[s]
            weights32 = weights.astype(F32)
            weight_grad = dot_nt(up_spread, values)
            score_grad = (
                weights32
                * (weight_grad - jnp.sum(weight_grad * weights32, -1, keepdims=True))
            ).astype(BF)
            dq = dot_nn(score_grad, keys).reshape(3, nq, TILE)
            dq = (dq[0] * mask_q32[0] + dq[1] * mask_q32[1] + dq[2] * mask_q32[2]) * factor
            dk = dot_tn(score_grad, spread) * factor
            dv = dot_tn(weights, up_spread)
            return dq, dk, dv

        if crossed:
            half = RV // 2
            dq_l, dk_v, dv_v = one(LANG, VIS, PCL)
            dq_1, dk_1, dv_1 = one(V1, LANG, PCV.at[0])
            dq_2, dk_2, dv_2 = one(V2, LANG, PCV.at[1])
            results = {
                LANG: (dq_l, dk_1 + dk_2, dv_1 + dv_2),
                V1: (dq_1, dk_v[:half], dv_v[:half]),
                V2: (dq_2, dk_v[half:], dv_v[half:]),
            }
        else:
            results = {stream: one(stream, stream, PS.at[0 if stream == LANG else 1 + (V1, V2).index(stream)])}
        for (r0, r1), (dq, dk, dv) in results.items():
            D[s, r0:r1, 0:128] = dq[:, :128].astype(BF)
            D[s, r0:r1, 128:256] = (dq[:, 128:] + dv[:, :128]).astype(BF)
            D[s, r0:r1, 256:384] = dv[:, 128:].astype(BF)
            D[s, r0:r1, 384:640] = dk.astype(BF)
            D[s, r0:r1, 640:768] = jnp.zeros((r1 - r0, 128), BF)

    def forward_norm(value, index, gain_row, r0, r1):
        center = value - jnp.mean(value, -1, keepdims=True)
        scaled = lax.rsqrt(jnp.mean(center * center, -1, keepdims=True) + EPSILON)
        normed = center * scaled
        NORM[index, r0:r1] = normed
        RSTD[index, r0:r1] = scaled
        return normed * gains[gain_row : gain_row + 1] + shifts[gain_row : gain_row + 1]

    def backward_norm(upstream, index, gain_row, bias_row, r0, r1):
        normed = NORM[index, r0:r1]
        through = upstream * gains[gain_row : gain_row + 1]
        inner = (
            through
            - jnp.mean(through, -1, keepdims=True)
            - normed * jnp.mean(through * normed, -1, keepdims=True)
        )
        result = RSTD[index, r0:r1] * inner
        VG[5 + gain_row : 6 + gain_row] += jnp.sum(upstream * normed, 0, keepdims=True)
        VG[10 + gain_row : 11 + gain_row] += jnp.sum(upstream, 0, keepdims=True)
        VG[bias_row : bias_row + 1] += jnp.sum(result, 0, keepdims=True)
        return result

    def rows_of_group(p, g, stream):
        r0, r1 = stream
        return A[p, 2 * g : 2 * g + 2, r0:r1, :].reshape(2 * (r1 - r0), D_MODEL)

    def project(p, g, stream, w, QV):
        r0, r1 = stream
        for n in range(NT):
            column = slice(n * TILE, (n + 1) * TILE)
            mapped = dot_nn(rows_of_group(p, g, stream), W[w, :, column]) + QB[w : w + 1, column]
            QV[2 * g : 2 * g + 2, r0:r1, column] = mapped.astype(BF).reshape(2, r1 - r0, TILE)

    def attend(g, stream, b):
        for s in (2 * g, 2 * g + 1):
            attend_slab(QVK.at[b], C.at[b], b == 0, stream, s)

    def expand_rows(g, stream):
        r0, r1 = stream
        rows = r1 - r0
        w = EXPAND[stream]
        for n in range(NT):
            column = slice(n * TILE, (n + 1) * TILE)
            before = dot_nn(rows_of_group(2, g, stream), W[w, :, column]) + QB[w : w + 1, column]
            half = 0.5 * (1.0 + lax.erf(before * math.sqrt(0.5)))
            slope = half + before * jnp.exp(-0.5 * before * before) * (1.0 / math.sqrt(2.0 * math.pi))
            H[2 * g : 2 * g + 2, r0:r1, column] = (before * half).astype(BF).reshape(2, rows, TILE)
            GP[2 * g : 2 * g + 2, r0:r1, column] = slope.astype(BF).reshape(2, rows, TILE)

    def hidden_gradient(g, stream):
        r0, r1 = stream
        rows = r1 - r0
        for n in range(NT):
            column = slice(n * TILE, (n + 1) * TILE)
            up_hidden = dot_nn(rows_of_group(3, g, stream), W[CONTRACT[stream], :, column])
            slope = GP[2 * g : 2 * g + 2, r0:r1, column].reshape(2 * rows, TILE)
            D[2 * g : 2 * g + 2, r0:r1, column] = (
                (up_hidden * slope.astype(F32)).astype(BF).reshape(2, rows, TILE)
            )

    def context_gradient(p, g, stream, w):
        r0, r1 = stream
        upstream = dot_nn(rows_of_group(p, g, stream), W[w, :, 512:768])
        D[2 * g : 2 * g + 2, r0:r1, 512:768] = upstream.astype(BF).reshape(2, r1 - r0, TILE)

    def attend_gradient(g, stream, b):
        for s in (2 * g, 2 * g + 1):
            attend_back_slab(QVK.at[b], b == 0, stream, s)

    def all_rows(ref, r0, r1, lanes):
        value = ref[:, r0:r1, lanes]
        return value.reshape(SLOTS * (r1 - r0), value.shape[-1])

    def weight_grad(w, lhs_p, rhs_ref, r0, r1, lanes=slice(0, 768)):
        for m in range(NT):
            column = slice(m * TILE, (m + 1) * TILE)
            left = all_rows(A.at[lhs_p], r0, r1, column)
            G[w, column, lanes] = dot_tn(left, all_rows(rhs_ref, r0, r1, lanes)).astype(BF)

    def attention_weight_grad(w, x_p, b_p, Cb, r0, r1, middle=None):
        if middle is None:
            weight_grad(w, x_p, D, r0, r1, slice(0, 512))
        else:
            weight_grad(w, x_p, D, r0, r1, slice(0, 384))
            middle()
            weight_grad(w, x_p, D, r0, r1, slice(384, 512))
        for m in range(NT):
            column = slice(m * TILE, (m + 1) * TILE)
            G[w, column, 512:768] = (
                dot_tn(all_rows(A.at[x_p], r0, r1, column), all_rows(D, r0, r1, slice(512, 768)))
                + dot_tn(all_rows(A.at[b_p], r0, r1, column), all_rows(Cb, r0, r1, slice(0, 256)))
            ).astype(BF)

    def bias_grad(row, r0, r1):
        total = jnp.zeros((1, D_MODEL), F32)
        for s in range(SLOTS):
            total = total + jnp.sum(D[s, r0:r1].astype(F32), 0, keepdims=True)
        QG[row : row + 1] = total

    def grad_first(part):
        w, lanes = PARTS[part]
        for j in range(2):
            half = rows_of_chip(k_flip[2], (1 - j) * SHARE, SHARE)
            send(G.at[w, half, lanes], RD.at[j, w, :, lanes], plane[j], gsem.at[2, part])

    def grad_second(part):
        w, lanes = PARTS[part]
        wait_bytes(RD.at[:, w, :, lanes], gsem.at[2, part])
        for j in range(2):
            half = rows_of_chip(k_flip[1 - j], (1 - j) * SHARE, SHARE)
            G[w, half, lanes] = (G[w, half, lanes].astype(F32) + RD[j, w, :, lanes].astype(F32)).astype(BF)
        for j in range(2):
            send(G.at[w, rows_of_chip(k_flip[j]), lanes], RX.at[j, w, :, lanes], plane[j], gsem.at[j, part])

    grad_nears = []

    def grad_third(part):
        w, lanes = PARTS[part]
        for j in range(2):
            wait_bytes(RX.at[j, w, :, lanes], gsem.at[j, part])
        total = G[w, pair_rows, lanes].astype(F32)
        total = total + RX[0, w, :, lanes].astype(F32) + RX[1, w, :, lanes].astype(F32)
        G[w, pair_rows, lanes] = total.astype(BF)
        low = G.at[w, rows_of_chip(k, 0, SHARE), lanes]
        high = G.at[w, rows_of_chip(k, SHARE, SHARE), lanes]
        slot = counter[0]
        counter[0] += 2
        here, there = R2.at[0, w, :, lanes], R2.at[1, w, :, lanes]
        own = pltpu.make_async_copy(low, here, gsem2.at[part])
        near = remote(high, here, ssem.at[slot], gsem2.at[part], sib)
        far_low = remote(low, there, ssem.at[slot], gsem2.at[part], (2 * k, z2))
        far_high = remote(high, there, ssem.at[slot + 1], gsem2.at[part], (2 * k + 1, z2))

        @pl.when(c == 0)
        def _():
            own.start()
            near.start()

        @pl.when(c == 1)
        def _():
            far_low.start()
            far_high.start()

        grad_nears.append((near, far_low, far_high))

    def grad_last(part):
        w, lanes = PARTS[part]
        wait_bytes(R2.at[:, w, :, lanes], gsem2.at[part])
        wgrad[w, :, lanes] = R2[0, w, :, lanes].astype(F32) + R2[1, w, :, lanes].astype(F32)

    def count_step(stage, peer):
        count_copies[stage].wait_recv()
        CA[stage + 1] = CA[stage] + CR[stage]
        if peer is not None:
            count_copies.append(send(CA.at[stage + 1], CR.at[stage + 1], peer))

    VG[...] = jnp.zeros_like(VG)
    QG[...] = jnp.zeros_like(QG)
    weight_second(0)
    attention_share(2)
    weight_second(7)
    weight_first(2)
    attention_share(1)
    own_slab(1, lcot, vcot, heads_cot, COT)
    weight_third(0)
    weight_first(1)
    kv_sib.wait_recv()
    kv_zp.wait_recv()
    kv_far = send(KV.at[2], KV.at[3], sib)
    far_x = {stream: gather_forward(rows_x[stream]) for stream in (VIS, LANG)}
    bias_swap.wait_recv()
    QB[...] = jnp.where(c == 1, QR[...], QO[...])
    weight_third(7)
    kv_far.wait_recv()
    arrived("rows", rows_x[VIS][2], rows_x[LANG][2])
    weight_ready(0)
    weight_ready(7)

    near, far_sum, z_sum, rows, far_rows = {}, {}, {}, {}, {}
    out_lanes, all_lanes = slice(512, 768), slice(0, 768)

    def sums_near_after(stream, lhs, w, lanes):
        partial_nt(0, lhs, stream, w, lanes)
        near[stream] = sums_near(stream)

    def sums_far_after(stream, lhs, w, lanes):
        partial_nt(1, lhs, stream, w, lanes)
        far_sum[stream] = sums_far(stream)

    def sums_on(stream):
        z_sum[stream] = sums_z(stream, far_sum[stream])

    def total_of(stream):
        return reduced(stream, near[stream], z_sum[stream])

    def far_arrived(stream):
        arrived("rows", far_rows[stream])

    def near_arrived(stream):
        arrived("rows", rows[stream][2])

    def pass_on(stream):
        far_rows[stream] = gather_forward(rows[stream])

    project(0, 0, BOTH, 0, QVK.at[0])
    weight_second(2)
    weight_first(4)
    attend(0, V1, 0)
    sums_near_after(V1, C.at[0], 0, out_lanes)
    attend(0, V2, 0)
    sums_near_after(V2, C.at[0], 0, out_lanes)
    weight_second(1)
    weight_first(6)
    attend(0, LANG, 0)
    sums_near_after(LANG, C.at[0], 0, out_lanes)
    arrived("rows", far_x[VIS], far_x[LANG])
    project(0, 1, BOTH, 0, QVK.at[0])
    attend(1, V1, 0)
    sums_far_after(V1, C.at[0], 0, out_lanes)
    attend(1, V2, 0)
    sums_far_after(V2, C.at[0], 0, out_lanes)
    sums_on(V1)
    attend(1, LANG, 0)
    sums_far_after(LANG, C.at[0], 0, out_lanes)
    sums_on(V2)
    weight_third(2)
    sums_on(LANG)
    count_step(0, plane[0])
    weight_third(1)

    def first_norm(stream):
        r0, r1 = stream
        value = total_of(stream) + out_bias[0:1] + A[0, 0, r0:r1].astype(F32)
        A[1, 0, r0:r1] = forward_norm(value, 0, 0, r0, r1).astype(BF)
        rows[stream] = gather_start(1, stream)

    for stream in CHAINS:
        first_norm(stream)

    def self_rows(g, stream):
        project(1, g, stream, SELF[stream], QVK.at[1])
        attend(g, stream, 1)
        if g == 0:
            sums_near_after(stream, C.at[1], SELF[stream], out_lanes)
        else:
            sums_far_after(stream, C.at[1], SELF[stream], out_lanes)

    weight_second(4)
    weight_ready(2)
    near_arrived(V1)
    self_rows(0, V1)
    pass_on(V1)
    near_arrived(V2)
    self_rows(0, V2)
    pass_on(V2)
    weight_second(6)
    weight_first(3)
    weight_ready(1)
    near_arrived(LANG)
    self_rows(0, LANG)
    pass_on(LANG)
    far_arrived(V1)
    self_rows(1, V1)
    far_arrived(V2)
    self_rows(1, V2)
    sums_on(V1)
    weight_third(4)
    weight_first(5)
    far_arrived(LANG)
    self_rows(1, LANG)
    sums_on(V2)
    count_step(1, plane[1])
    sums_on(LANG)
    weight_third(6)

    def second_norm(stream):
        r0, r1 = stream
        n = 1 if stream == LANG else 2
        value = total_of(stream) + out_bias[n : n + 1] + A[1, 0, r0:r1].astype(F32)
        A[2, 0, r0:r1] = forward_norm(value, 1, n, r0, r1).astype(BF)
        rows[stream] = gather_start(2, stream)

    for stream in CHAINS:
        second_norm(stream)

    weight_second(3)
    weight_ready(4)
    near_arrived(V1)
    expand_rows(0, V1)
    pass_on(V1)
    near_arrived(V2)
    expand_rows(0, V2)
    pass_on(V2)
    weight_second(5)
    far_arrived(V1)
    expand_rows(1, V1)
    pass_on(LANG)
    weight_ready(6)
    sums_far_after(V1, H, 6, all_lanes)
    far_arrived(V2)
    expand_rows(1, V2)
    sums_on(V1)
    sums_far_after(V2, H, 6, all_lanes)
    sums_near_after(V1, H, 6, all_lanes)
    sums_on(V2)
    sums_near_after(V2, H, 6, all_lanes)
    weight_third(3)
    count_step(2, None)

    def last_norm(stream):
        r0, r1 = stream
        n = 0 if stream == LANG else 1
        value = total_of(stream) + contract_b[n : n + 1] + A[2, 0, r0:r1].astype(F32)
        OUTS[r0:r1] = forward_norm(value, 2, 3 + n, r0, r1).astype(BF)
        scale = total_items / CA[3, n : n + 1, 0:1]
        upstream = COT[r0:r1].astype(F32) * (FLAG[r0:r1] * scale)
        result = backward_norm(upstream, 2, 3 + n, 3 + n, r0, r1)
        DZ[r0:r1] = result
        A[3, 0, r0:r1] = result.astype(BF)
        rows[stream] = gather_start(3, stream)

    weight_third(5)
    last_norm(V1)
    weight_ready(3)
    near_arrived(LANG)
    far_arrived(LANG)
    expand_rows(0, LANG)
    last_norm(V2)
    expand_rows(1, LANG)
    weight_ready(5)
    sums_far_after(LANG, H, 5, all_lanes)
    sums_near_after(LANG, H, 5, all_lanes)
    sums_on(LANG)

    def feed_gradient(g, stream):
        hidden_gradient(g, stream)
        if g == 0:
            sums_near_after(stream, D, EXPAND[stream], all_lanes)
        else:
            sums_far_after(stream, D, EXPAND[stream], all_lanes)

    near_arrived(V1)
    feed_gradient(0, V1)
    pass_on(V1)
    near_arrived(V2)
    feed_gradient(0, V2)
    pass_on(V2)
    last_norm(LANG)
    far_arrived(V1)
    feed_gradient(1, V1)
    far_arrived(V2)
    weight_grad(6, 3, H, *VIS)
    grad_first(6)
    sums_on(V1)
    feed_gradient(1, V2)
    near_arrived(LANG)
    feed_gradient(0, LANG)
    pass_on(LANG)
    sums_on(V2)
    weight_grad(4, 2, D, *VIS)
    grad_first(4)

    def second_norm_back(stream):
        r0, r1 = stream
        n = 1 if stream == LANG else 2
        result = backward_norm(DZ[r0:r1] + total_of(stream), 1, n, n, r0, r1)
        DZ[r0:r1] = result
        A[4, 0, r0:r1] = result.astype(BF)
        rows[stream] = gather_start(4, stream)

    second_norm_back(V1)
    far_arrived(LANG)
    feed_gradient(1, LANG)
    grad_second(6)
    second_norm_back(V2)
    sums_on(LANG)
    weight_grad(5, 3, H, *LANG)
    grad_first(5)
    bias_grad(4, *VIS)
    tail_out = [
        send(OUTS.at[pl.ds(RL - LANG_TAIL, LANG_TAIL)], TLO, up),
        send(OUTS.at[pl.ds(ROWS - VIS_TAIL, VIS_TAIL)], TVO, up),
    ]
    grad_second(4)
    weight_grad(3, 2, D, *LANG)
    grad_first(3)
    bias_grad(3, *LANG)

    def self_gradient(g, stream):
        w = SELF[stream]
        context_gradient(4, g, stream, w)
        attend_gradient(g, stream, 1)
        if g == 0:
            sums_near_after(stream, D, w, all_lanes)
        else:
            sums_far_after(stream, D, w, all_lanes)

    near_arrived(V1)
    self_gradient(0, V1)
    pass_on(V1)
    second_norm_back(LANG)
    near_arrived(V2)
    self_gradient(0, V2)
    pass_on(V2)
    grad_second(5)
    grad_third(6)
    far_arrived(V1)
    self_gradient(1, V1)
    grad_second(3)
    far_arrived(V2)
    self_gradient(1, V2)
    sums_on(V1)
    near_arrived(LANG)
    self_gradient(0, LANG)
    pass_on(LANG)
    sums_on(V2)
    grad_third(4)
    attention_weight_grad(2, 1, 4, C.at[1], *VIS)
    grad_first(2)

    def first_norm_back(stream):
        r0, r1 = stream
        result = backward_norm(DZ[r0:r1] + total_of(stream), 0, 0, 0, r0, r1)
        DZ[r0:r1] = result
        A[5, 0, r0:r1] = result.astype(BF)
        rows[stream] = gather_start(5, stream)

    first_norm_back(V1)
    far_arrived(LANG)
    self_gradient(1, LANG)
    first_norm_back(V2)
    sums_on(LANG)
    bias_grad(2, *VIS)
    grad_third(5)
    attention_weight_grad(1, 1, 4, C.at[1], *LANG)
    grad_first(1)
    grad_second(2)
    bias_grad(1, *LANG)
    first_norm_back(LANG)

    for stream in CHAINS:
        near_arrived(stream)
        context_gradient(5, 0, stream, 0)
    attend_gradient(0, None, 0)
    for stream in CHAINS:
        pass_on(stream)
    for stream in CHAINS:
        sums_near_after(stream, D, 0, all_lanes)
    grad_second(1)
    grad_third(3)
    for stream in CHAINS:
        far_arrived(stream)
        context_gradient(5, 1, stream, 0)
    attend_gradient(1, None, 0)
    attention_weight_grad(0, 0, 5, C.at[0], *BOTH, middle=lambda: grad_first(0))
    grad_first(7)
    for stream in CHAINS:
        sums_far_after(stream, D, 0, all_lanes)
    for stream in CHAINS:
        sums_on(stream)
    grad_second(0)
    bias_grad(0, *BOTH)

    quarter = jnp.where(c == 0, z, z2)
    AVA[0, 0:16] = VG[...]
    for j in range(4):
        AVA[0, 16 + 8 * j : 24 + 8 * j] = jnp.where(quarter == j, QG[...], 0.0)
    vector_peers = [sib, plane[0], plane[1], zp, (d, z2)]
    vector_copies = [send(AVA.at[0], AVR.at[0], vector_peers[0])]

    def vector_step(stage):
        arrived("vectors", vector_copies[stage])
        AVA[stage + 1] = AVA[stage] + AVR[stage]
        if stage < 4:
            vector_copies.append(send(AVA.at[stage + 1], AVR.at[stage + 1], vector_peers[stage + 1]))

    grad_second(7)
    grad_third(2)
    vector_step(0)
    grad_third(1)
    vector_step(1)
    for w in (6, 4, 5, 3):
        grad_last(w)
    grad_third(0)
    vector_step(2)
    for stream in CHAINS:
        r0, r1 = stream
        DZ[r0:r1] = DZ[r0:r1] + total_of(stream)
    tail_grad = [
        send(DZ.at[pl.ds(RL - LANG_TAIL, LANG_TAIL)], TLG, up),
        send(DZ.at[pl.ds(ROWS - VIS_TAIL, VIS_TAIL)], TVG, up),
    ]
    grad_third(7)
    vector_step(3)
    for w in (2, 1):
        grad_last(w)
    vector_step(4)
    vec_out[...] = AVA[5, 0:16]
    qb_out[...] = AVA[5, pl.ds(pl.multiple_of(16 + 8 * z, 8), 8)]

    arrived("tails", *tail_out, *tail_grad)
    before_l = jnp.where(z == 1, 0, 25 - 5 * z)
    before_v = jnp.where(z == 1, 0, 45 - 9 * z)
    for (r0, r1), size, pad, own_rows, off, before, tail_rows, out_ref, grad_ref, t_out, t_grad in (
        (LANG, WORDS, WORDS, own_l, off_l, before_l, LANG_TAIL, lang_out, lang_grad, TLO, TLG),
        (VIS, REGIONS, REGION_PAD, own_v, off_v, before_v, VIS_TAIL, vis_out, vis_grad, TVO, TVG),
    ):
        from_own = rows_from_slab((own_rows, r1 - r0), -off, 0, off, own_rows, size, pad)
        from_tail = rows_from_slab(
            (own_rows, tail_rows), own_rows - before, r1 - r0 - tail_rows, 0, off, size, pad
        )
        out_ref[...] = (
            dot_nn(from_own.astype(BF), OUTS[r0:r1]) + dot_nn(from_tail.astype(BF), t_out[...])
        ).astype(BF)
        exact = lax.Precision.HIGHEST
        grad_ref[...] = jnp.dot(
            from_own, DZ[r0:r1], precision=exact, preferred_element_type=F32
        ) + jnp.dot(from_tail, t_grad[...], precision=exact, preferred_element_type=F32)

    grad_last(0)
    grad_last(7)

    for copy in pending:
        copy.wait_send()
    for index, stream in list(stage_used):
        stage_free(index, stream)

    @pl.when(c == 1)
    def _():
        for copy in nears:
            copy.wait_send()
        for _, far_low, far_high in grad_nears:
            far_low.wait_send()
            far_high.wait_send()

    @pl.when(c == 0)
    def _():
        for near, _, _ in grad_nears:
            near.wait_send()
    assert counter[0] <= ssem.shape[0] and counter[1] <= rsem.shape[0], counter


N_SEND = 240
N_RECV = 160


def fused_layer(total_items, *operands):
    own_l, own_v = operands[0].shape[0], operands[1].shape[0]
    vmem = pl.BlockSpec(memory_space=pltpu.VMEM)
    smem = pl.BlockSpec(memory_space=pltpu.SMEM)
    shapes = [
        ((own_l, D), BF),
        ((own_v, D), BF),
        ((own_l, D), F32),
        ((own_v, D), F32),
        ((7, SHARE, D), F32),
        ((16, D), F32),
        ((8, D), F32),
    ]
    scratch = [
        ((7, D, D), BF),
        ((7, D, D), BF),
        ((2, 7, SHARE, D), BF),
        ((2, 7, HALF_PAIR, D), BF),
        ((2, 7, SHARE, D), BF),
        ((6, SLOTS, ROWS, D), BF),
        ((SLOTS, 8, TILE), F32),
        ((3, ROWS, D), BF),
        ((3, ROWS, D), BF),
        ((2, SLOTS, ROWS, D), BF),
        ((SLOTS, ROWS, D), BF),
        ((2, SLOTS, ROWS, TILE), BF),
        ((SLOTS, ROWS, D), BF),
        ((SLOTS, ROWS, D), BF),
        ((SLOTS, 3 * RL, RV), BF),
        ((2, SLOTS, 3 * RL, RL), BF),
        ((3, SLOTS, 3 * RL, RL), BF),
        ((ROWS, D), F32),
        ((ROWS, D), F32),
        ((3, ROWS, D), F32),
        ((3, ROWS, 1), F32),
        ((ROWS, D), F32),
        ((ROWS, D), BF),
        ((3, SHARE, D), BF),
        ((ROWS, 1), F32),
        ((8, D), F32),
        ((8, D), F32),
        ((8, D), F32),
        ((4, 8, 128), F32),
        ((3, 8, 128), F32),
        ((16, D), F32),
        ((8, D), F32),
        ((6, N_AR, D), F32),
        ((5, N_AR, D), F32),
        ((2, LANG_HEAD, D), BF),
        ((2, VIS_HEAD, D), BF),
        ((ROWS, D), BF),
        ((LANG_TAIL, D), BF),
        ((VIS_TAIL, D), BF),
        ((LANG_TAIL, D), F32),
        ((VIS_TAIL, D), F32),
    ]
    dma = pltpu.SemaphoreType.DMA
    return pl.pallas_call(
        partial(layer_kernel, total_items),
        out_shape=[jax.ShapeDtypeStruct(s, t) for s, t in shapes],
        in_specs=[vmem] * 4 + [smem] * 3 + [vmem] * (len(operands) - 7),
        out_specs=[vmem] * len(shapes),
        scratch_shapes=[pltpu.VMEM(s, t) for s, t in scratch]
        + [dma((N_SEND,)), dma((N_RECV,)), dma((3, 8)), dma((8,)), dma((3, 8)), dma((8,))],
        compiler_params=pltpu.CompilerParams(
            collective_id=0, has_side_effects=True, vmem_limit_bytes=VMEM_LIMIT
        ),
    )(*operands)


def unpack_kernel(lo, vo, lg, vg, wgrad, vec, qb, *outs):
    (lo_out, vo_out, lg_out, vg_out, proj, qv, outw, outb, exp, expb, con, conb, gain, shift) = outs
    lo_out[...] = lo[...]
    vo_out[...] = vo[...]
    lg_out[...] = lg[...]
    vg_out[...] = vg[...]
    width = HALF_PAIR
    for b in range(3):
        for j, lane in enumerate((0, 2 * width, width)):
            proj[b, j] = wgrad[b, :, lane : lane + width]
        outw[b] = wgrad[b, :, 3 * width :].T
        for j in range(2):
            qv[b, j : j + 1] = qb[b : b + 1, j * width : (j + 1) * width]
    for stream in range(2):
        exp[stream] = wgrad[3 + stream]
        con[stream] = wgrad[5 + stream]
    expb[...] = qb[3:5]
    outb[...] = vec[0:3]
    conb[...] = vec[3:5]
    gain[...] = vec[5:10]
    shift[...] = vec[10:15]


def unpack(packed, shapes):
    vmem = pl.BlockSpec(memory_space=pltpu.VMEM)
    return pl.pallas_call(
        unpack_kernel,
        out_shape=shapes,
        in_specs=[vmem] * len(packed),
        out_specs=[vmem] * len(shapes),
        compiler_params=pltpu.CompilerParams(vmem_limit_bytes=VMEM_LIMIT),
    )(*packed)


def on_device_fused(
    language_input,
    vision_input,
    word_lengths,
    region_counts,
    task_flags,
    language_cotangent,
    vision_cotangent,
    projection_weight,
    query_value_bias,
    output_weight,
    output_bias,
    expand_weight,
    expand_bias,
    contract_weight,
    contract_bias,
    norm_gain,
    norm_bias,
):
    packed = fused_layer(
        float(word_lengths.shape[0] * lax.axis_size("dp")),
        language_input,
        vision_input,
        language_cotangent,
        vision_cotangent,
        word_lengths,
        region_counts,
        task_flags.T,
        projection_weight,
        query_value_bias,
        output_weight,
        expand_weight,
        expand_bias,
        contract_weight.transpose(0, 2, 1),
        output_bias,
        contract_bias,
        norm_gain,
        norm_bias,
    )
    like = [
        (language_input, BF),
        (vision_input, BF),
        (language_input, F32),
        (vision_input, F32),
        (projection_weight, F32),
        (query_value_bias, F32),
        (output_weight, F32),
        (output_bias, F32),
        (expand_weight, F32),
        (expand_bias, F32),
        (contract_weight.transpose(0, 2, 1), F32),
        (contract_bias, F32),
        (norm_gain, F32),
        (norm_bias, F32),
    ]
    outs = list(unpack(packed, [jax.ShapeDtypeStruct(a.shape, t) for a, t in like]))
    outs[10] = outs[10].transpose(0, 2, 1)
    return tuple(outs)


def solution(mesh):
    in_specs = (
        P(("dp", "mp"), None),
        P(("dp", "mp"), None),
        P("dp"),
        P("dp"),
        P("dp", None),
        P(("dp", "mp"), None),
        P(("dp", "mp"), None),
        P(None, None, "dp", "mp"),
        P(None, None, "mp"),
        P(None, "mp", "dp"),
        P(),
        P(None, "dp", "mp"),
        P(None, "mp"),
        P(None, "mp", "dp"),
        P(),
        P(),
        P(),
    )
    out_specs = (
        P(("dp", "mp"), None),
        P(("dp", "mp"), None),
        P(("dp", "mp"), None),
        P(("dp", "mp"), None),
        P(None, None, "dp", "mp"),
        P(None, None, "mp"),
        P(None, "mp", "dp"),
        P(),
        P(None, "dp", "mp"),
        P(None, "mp"),
        P(None, "mp", "dp"),
        P(),
        P(),
        P(),
    )
    fused = dict(mesh.shape) == {"dp": 8, "mp": 4}
    return jax.shard_map(
        on_device_fused if fused else on_device, mesh=mesh, in_specs=in_specs, out_specs=out_specs, check_vma=False
    )
```

```python
from functools import partial
import math

import jax
import jax.numpy as jnp
from jax import lax
from jax.experimental import pallas as pl
from jax.experimental.pallas import tpu as pltpu
from jax.sharding import PartitionSpec as P

D = 768
HEADS = 12
WORDS = 20
REGIONS = 36
D_MODEL = D
D_HEAD = D // HEADS

EPSILON = 1e-12
MASKED = -1e30


def layer_norm(summed, gain, shift):
    center = summed - jnp.mean(summed, -1, keepdims=True)
    scaled = lax.rsqrt(jnp.mean(center * center, -1, keepdims=True) + EPSILON)
    normed = center * scaled
    return (normed * gain + shift, normed, scaled)


def norm_back(upstream, normed, scaled, gain):
    through = upstream * gain
    inner = (
        through
        - jnp.mean(through, -1, keepdims=True)
        - normed * jnp.mean(through * normed, -1, keepdims=True)
    )
    return (scaled * inner, jnp.sum(upstream * normed, 0), jnp.sum(upstream, 0))


def split_heads(rows, item_count):
    head_size = D // HEADS
    return rows.reshape(
        item_count, rows.shape[0] // item_count, rows.shape[1] // head_size, head_size
    )


def join_heads(block):
    return block.reshape(block.shape[0] * block.shape[1], block.shape[2] * block.shape[3])


def project(rows, weight, bias, item_count):
    mapped = jnp.einsum("rd,jde->jre", rows, weight, preferred_element_type=jnp.float32)
    query = split_heads((mapped[0] + bias[0]).astype(jnp.bfloat16), item_count)
    keys = split_heads(mapped[1].astype(jnp.bfloat16), item_count)
    values = split_heads((mapped[2] + bias[1]).astype(jnp.bfloat16), item_count)
    return (query, keys, values)


def masked_scores(query, keys, valid):
    scores = jnp.einsum("inhd,imhd->ihnm", query, keys, preferred_element_type=jnp.float32) * (
        1.0 / math.sqrt(D // HEADS)
    )
    return jnp.where(valid[:, None, None, :], scores, MASKED)


def attend(query, keys, values, valid):
    scores = masked_scores(query, keys, valid)
    highest = jnp.max(scores, -1, keepdims=True)
    raised = jnp.exp(scores - highest)
    summed = jnp.sum(raised, -1, keepdims=True)
    context = jnp.einsum(
        "ihnm,imhd->inhd",
        (raised / summed).astype(jnp.bfloat16),
        values,
        preferred_element_type=jnp.float32,
    )
    return (join_heads(context).astype(jnp.bfloat16), highest + jnp.log(summed))


def attend_back(query, keys, values, valid, log_total, context_grad):
    factor = 1.0 / math.sqrt(D // HEADS)
    upstream = context_grad.reshape(query.shape)
    weights = jnp.exp(masked_scores(query, keys, valid) - log_total)
    weight_grad = jnp.einsum(
        "inhd,imhd->ihnm", upstream, values, preferred_element_type=jnp.float32
    )
    score_grad = (
        weights * (weight_grad - jnp.sum(weight_grad * weights, -1, keepdims=True))
    ).astype(jnp.bfloat16)
    query_grad = (
        jnp.einsum("ihnm,imhd->inhd", score_grad, keys, preferred_element_type=jnp.float32) * factor
    ).astype(jnp.bfloat16)
    keys_grad = (
        jnp.einsum("ihnm,inhd->imhd", score_grad, query, preferred_element_type=jnp.float32)
        * factor
    ).astype(jnp.bfloat16)
    values_grad = jnp.einsum(
        "ihnm,inhd->imhd",
        weights.astype(jnp.bfloat16),
        upstream,
        preferred_element_type=jnp.float32,
    ).astype(jnp.bfloat16)
    return (join_heads(query_grad), join_heads(keys_grad), join_heads(values_grad))


def project_back(rows, query_grad, keys_grad, values_grad):
    stacked = jnp.stack([query_grad, keys_grad, values_grad])
    weight_grad = jnp.einsum("rd,jre->jde", rows, stacked, preferred_element_type=jnp.float32)
    bias_grad = jnp.stack(
        [jnp.sum(query_grad.astype(jnp.float32), 0), jnp.sum(values_grad.astype(jnp.float32), 0)]
    )
    return (weight_grad, bias_grad, stacked)


def gather_rows(language_rows, vision_rows):
    return (
        lax.all_gather(language_rows, "mp", axis=0, tiled=True),
        lax.all_gather(vision_rows, "mp", axis=0, tiled=True),
    )


def rows_of(language_part, vision_part):
    return (
        lax.all_to_all(language_part, "mp", split_axis=0, concat_axis=1, tiled=True),
        lax.all_to_all(vision_part, "mp", split_axis=0, concat_axis=1, tiled=True),
    )


def gather_grads(language_rows, vision_rows):
    return (
        lax.all_gather(language_rows, "mp", axis=0, tiled=True),
        lax.all_gather(vision_rows, "mp", axis=0, tiled=True),
    )


def grads_of(language_part, vision_part):
    return (
        lax.all_to_all(language_part, "mp", split_axis=1, concat_axis=2, tiled=True),
        lax.all_to_all(vision_part, "mp", split_axis=1, concat_axis=2, tiled=True),
    )


def matmul(left, right):
    return jnp.dot(left, right, preferred_element_type=jnp.float32)


def on_device(
    language_input,
    vision_input,
    word_lengths,
    region_counts,
    task_flags,
    language_cotangent,
    vision_cotangent,
    projection_weight,
    query_value_bias,
    output_weight,
    output_bias,
    expand_weight,
    expand_bias,
    contract_weight,
    contract_bias,
    norm_gain,
    norm_bias,
):
    item_count = word_lengths.shape[0]
    flag_total = lax.psum(jnp.sum(task_flags, 0), "dp")
    projection, out_weight, expand, contract = (
        lax.all_gather(projection_weight, "dp", axis=2, tiled=True),
        lax.all_gather(output_weight, "dp", axis=2, tiled=True),
        lax.all_gather(expand_weight, "dp", axis=1, tiled=True),
        lax.all_gather(contract_weight, "dp", axis=2, tiled=True),
    )
    projection_full, out_full, expand_full, contract_full = (
        lax.all_gather(projection, "mp", axis=3, tiled=True),
        lax.all_gather(out_weight, "mp", axis=1, tiled=True),
        lax.all_gather(expand, "mp", axis=2, tiled=True),
        lax.all_gather(contract, "mp", axis=1, tiled=True),
    )
    valid = [
        jnp.arange(WORDS, dtype=jnp.int32)[None, :] < word_lengths[:, None],
        jnp.arange(REGIONS, dtype=jnp.int32)[None, :] < region_counts[:, None],
    ]
    row_counts = [WORDS, REGIONS]
    inputs = [language_input.astype(jnp.float32), vision_input.astype(jnp.float32)]
    cross_rows = gather_rows(language_input, vision_input)
    cross_parts = [
        project(cross_rows[stream], projection[0], query_value_bias[0], item_count)
        for stream in range(2)
    ]
    cross_context = []
    cross_total = []
    for stream in range(2):
        other = 1 - stream
        context, log_total = attend(
            cross_parts[stream][0], cross_parts[other][1], cross_parts[other][2], valid[other]
        )
        cross_context.append(context)
        cross_total.append(log_total)
    moved = rows_of(cross_context[0], cross_context[1])
    branch = [matmul(moved[stream], out_full[0]) for stream in range(2)]
    first = [
        layer_norm(branch[stream] + output_bias[0] + inputs[stream], norm_gain[0], norm_bias[0])
        for stream in range(2)
    ]
    first_out = [first[stream][0].astype(jnp.bfloat16) for stream in range(2)]
    self_rows = gather_rows(first_out[0], first_out[1])
    self_parts = [
        project(self_rows[stream], projection[1 + stream], query_value_bias[1 + stream], item_count)
        for stream in range(2)
    ]
    self_context = []
    self_total = []
    for stream in range(2):
        context, log_total = attend(
            self_parts[stream][0], self_parts[stream][1], self_parts[stream][2], valid[stream]
        )
        self_context.append(context)
        self_total.append(log_total)
    moved = rows_of(self_context[0], self_context[1])
    branch = [matmul(moved[stream], out_full[1 + stream]) for stream in range(2)]
    second = [
        layer_norm(
            branch[stream] + output_bias[1 + stream] + first_out[stream].astype(jnp.float32),
            norm_gain[1 + stream],
            norm_bias[1 + stream],
        )
        for stream in range(2)
    ]
    second_out = [second[stream][0].astype(jnp.bfloat16) for stream in range(2)]
    feed_rows = gather_rows(second_out[0], second_out[1])
    before = [
        matmul(feed_rows[stream], expand[stream]) + expand_bias[stream] for stream in range(2)
    ]
    hidden = [
        jax.nn.gelu(before[stream], approximate=False).astype(jnp.bfloat16) for stream in range(2)
    ]
    moved = rows_of(hidden[0], hidden[1])
    branch = [matmul(moved[stream], contract_full[stream]) for stream in range(2)]
    third = [
        layer_norm(
            branch[stream] + contract_bias[stream] + second_out[stream].astype(jnp.float32),
            norm_gain[3 + stream],
            norm_bias[3 + stream],
        )
        for stream in range(2)
    ]
    language_out = third[0][0].astype(jnp.bfloat16)
    vision_out = third[1][0].astype(jnp.bfloat16)
    item_scale = task_flags.astype(jnp.float32) * (
        item_count * lax.axis_size("dp") / flag_total.astype(jnp.float32)
    )
    shard_index = lax.axis_index("mp")
    upstream = []
    for stream, cotangent in enumerate([language_cotangent, vision_cotangent]):
        per_row = jnp.repeat(
            item_scale[:, stream],
            row_counts[stream],
            total_repeat_length=item_count * row_counts[stream],
        )
        shard_rows = cotangent.shape[0]
        row_scale = lax.dynamic_slice_in_dim(per_row, shard_index * shard_rows, shard_rows)
        upstream.append(cotangent.astype(jnp.float32) * row_scale[:, None])
    third_back = [
        norm_back(upstream[stream], third[stream][1], third[stream][2], norm_gain[3 + stream])
        for stream in range(2)
    ]
    sent = gather_grads(
        third_back[0][0].astype(jnp.bfloat16), third_back[1][0].astype(jnp.bfloat16)
    )
    expand_local = []
    expand_bias_local = []
    contract_local = []
    before_grads = []
    for stream in range(2):
        hidden_grad = jnp.einsum(
            "rd,fd->rf", sent[stream], contract[stream], preferred_element_type=jnp.float32
        )
        contract_local.append(
            jnp.einsum(
                "rf,rd->fd", hidden[stream], sent[stream], preferred_element_type=jnp.float32
            )
        )
        unused, pull = jax.vjp(partial(jax.nn.gelu, approximate=False), before[stream])
        before_grad = pull(hidden_grad)[0].astype(jnp.bfloat16)
        expand_local.append(
            jnp.einsum(
                "rd,rf->df", feed_rows[stream], before_grad, preferred_element_type=jnp.float32
            )
        )
        expand_bias_local.append(jnp.sum(before_grad.astype(jnp.float32), 0))
        before_grads.append(before_grad[None])
    moved = grads_of(before_grads[0], before_grads[1])
    back = [
        jnp.einsum(
            "rf,df->rd", moved[stream][0], expand_full[stream], preferred_element_type=jnp.float32
        )
        for stream in range(2)
    ]
    second_grad = [third_back[stream][0] + back[stream] for stream in range(2)]
    second_back = [
        norm_back(second_grad[stream], second[stream][1], second[stream][2], norm_gain[1 + stream])
        for stream in range(2)
    ]
    sent = gather_grads(
        second_back[0][0].astype(jnp.bfloat16), second_back[1][0].astype(jnp.bfloat16)
    )
    self_weight = []
    self_bias = []
    self_out = []
    stacks = []
    for stream in range(2):
        context_grad = jnp.einsum(
            "rd,ed->re", sent[stream], out_weight[1 + stream], preferred_element_type=jnp.float32
        ).astype(jnp.bfloat16)
        self_out.append(
            jnp.einsum(
                "re,rd->ed", self_context[stream], sent[stream], preferred_element_type=jnp.float32
            )
        )
        grads = attend_back(
            self_parts[stream][0],
            self_parts[stream][1],
            self_parts[stream][2],
            valid[stream],
            self_total[stream],
            context_grad,
        )
        weight_part, bias_part, stacked = project_back(
            self_rows[stream], grads[0], grads[1], grads[2]
        )
        self_weight.append(weight_part)
        self_bias.append(bias_part)
        stacks.append(stacked)
    moved = grads_of(stacks[0], stacks[1])
    back = [
        jnp.einsum(
            "jre,jde->rd",
            moved[stream],
            projection_full[1 + stream],
            preferred_element_type=jnp.float32,
        )
        for stream in range(2)
    ]
    first_grad = [second_back[stream][0] + back[stream] for stream in range(2)]
    first_back = [
        norm_back(first_grad[stream], first[stream][1], first[stream][2], norm_gain[0])
        for stream in range(2)
    ]
    sent = gather_grads(
        first_back[0][0].astype(jnp.bfloat16), first_back[1][0].astype(jnp.bfloat16)
    )
    cross_out = jnp.einsum(
        "re,rd->ed", cross_context[0], sent[0], preferred_element_type=jnp.float32
    ) + jnp.einsum("re,rd->ed", cross_context[1], sent[1], preferred_element_type=jnp.float32)
    triples = [[None, None, None], [None, None, None]]
    for stream in range(2):
        other = 1 - stream
        context_grad = jnp.einsum(
            "rd,ed->re", sent[stream], out_weight[0], preferred_element_type=jnp.float32
        ).astype(jnp.bfloat16)
        grads = attend_back(
            cross_parts[stream][0],
            cross_parts[other][1],
            cross_parts[other][2],
            valid[other],
            cross_total[stream],
            context_grad,
        )
        triples[stream][0] = grads[0]
        triples[other][1] = grads[1]
        triples[other][2] = grads[2]
    results = [
        project_back(cross_rows[stream], triples[stream][0], triples[stream][1], triples[stream][2])
        for stream in range(2)
    ]
    cross_weight = results[0][0] + results[1][0]
    cross_bias = results[0][1] + results[1][1]
    moved = grads_of(results[0][2], results[1][2])
    back = [
        jnp.einsum(
            "jre,jde->rd", moved[stream], projection_full[0], preferred_element_type=jnp.float32
        )
        for stream in range(2)
    ]
    language_grad = first_back[0][0] + back[0]
    vision_grad = first_back[1][0] + back[1]
    projection_stack = jnp.stack([cross_weight, self_weight[0], self_weight[1]])
    output_stack = jnp.stack([cross_out, self_out[0], self_out[1]])
    projection_grad, output_weight_grad, expand_grad, contract_grad = (
        lax.psum_scatter(projection_stack, "dp", scatter_dimension=2, tiled=True),
        lax.psum_scatter(output_stack, "dp", scatter_dimension=2, tiled=True),
        lax.psum_scatter(jnp.stack(expand_local), "dp", scatter_dimension=1, tiled=True),
        lax.psum_scatter(jnp.stack(contract_local), "dp", scatter_dimension=2, tiled=True),
    )
    query_value_grad, expand_bias_grad = lax.psum(
        (jnp.stack([cross_bias, self_bias[0], self_bias[1]]), jnp.stack(expand_bias_local)), "dp"
    )
    output_bias_local = jnp.stack(
        [
            jnp.sum(first_back[0][0], 0) + jnp.sum(first_back[1][0], 0),
            jnp.sum(second_back[0][0], 0),
            jnp.sum(second_back[1][0], 0),
        ]
    )
    contract_bias_local = jnp.stack([jnp.sum(third_back[0][0], 0), jnp.sum(third_back[1][0], 0)])
    gain_local = jnp.stack(
        [
            first_back[0][1] + first_back[1][1],
            second_back[0][1],
            second_back[1][1],
            third_back[0][1],
            third_back[1][1],
        ]
    )
    shift_local = jnp.stack(
        [
            first_back[0][2] + first_back[1][2],
            second_back[0][2],
            second_back[1][2],
            third_back[0][2],
            third_back[1][2],
        ]
    )
    output_bias_grad, contract_bias_grad, norm_gain_grad, norm_bias_grad = lax.psum(
        (output_bias_local, contract_bias_local, gain_local, shift_local), ("dp", "mp")
    )
    return (
        language_out,
        vision_out,
        language_grad,
        vision_grad,
        projection_grad,
        query_value_grad,
        output_weight_grad,
        output_bias_grad,
        expand_grad,
        expand_bias_grad,
        contract_grad,
        contract_bias_grad,
        norm_gain_grad,
        norm_bias_grad,
    )


MESH = pl.DeviceIdType.MESH
BF = jnp.bfloat16
F32 = jnp.float32
SLOTS = 4
RL = SLOTS * WORDS
REGION_PAD = 40
RV = SLOTS * REGION_PAD
ROWS = RL + RV
SHARE = 96
HALF_PAIR = 2 * SHARE
LANG_HEAD = 16
VIS_HEAD = 32
LANG_TAIL = 32
VIS_TAIL = 64
N_AR = 48
NT = 3
TILE = 256
LANG = (0, RL)
V1 = (RL, RL + RV // 2)
V2 = (RL + RV // 2, ROWS)
VIS = (RL, ROWS)
BOTH = (0, ROWS)
CHAINS = (V1, V2, LANG)
SELF = {LANG: 1, V1: 2, V2: 2}
EXPAND = {LANG: 3, V1: 4, V2: 4}
CONTRACT = {LANG: 5, V1: 6, V2: 6}
PARTS = {w: (w, slice(0, 768)) for w in range(1, 7)} | {0: (0, slice(0, 384)), 7: (0, slice(384, 768))}
VMEM_LIMIT = 63 * 1024 * 1024


def dot_nn(left, right):
    return lax.dot_general(left, right, (((1,), (0,)), ((), ())), preferred_element_type=F32)


def dot_nt(left, right):
    return lax.dot_general(left, right, (((1,), (1,)), ((), ())), preferred_element_type=F32)


def dot_tn(left, right):
    return lax.dot_general(left, right, (((0,), (0,)), ((), ())), preferred_element_type=F32)


def head_mask(first_lane, dtype):
    lane = lax.broadcasted_iota(jnp.int32, (1, TILE), 1) - first_lane
    return [
        jnp.where((lane >= 64 * h) & (lane < 64 * h + 64), 1.0, 0.0).astype(dtype) for h in range(3)
    ]


def item_rows(shape, dim, first, size, pad):
    row = lax.broadcasted_iota(jnp.int32, shape, dim) + first
    item = sum(jnp.where(row >= pad * j, 1, 0) for j in range(1, SLOTS))
    return row - (pad - size) * item, row - pad * item < size


def rows_into_slab(shape, shift, count, size, pad):
    place, real = item_rows(shape, 0, 0, size, pad)
    column = lax.broadcasted_iota(jnp.int32, shape, 1)
    return jnp.where((column - place == shift) & real & (place < count), 1.0, 0.0)


def rows_from_slab(shape, shift, first, low, high, size, pad):
    place, real = item_rows(shape, 1, first, size, pad)
    row = lax.broadcasted_iota(jnp.int32, shape, 0)
    return jnp.where((place - row == shift) & real & (row >= low) & (row < high), 1.0, 0.0)


def layer_kernel(
    total_items,
    lang,
    vis,
    lcot,
    vcot,
    lengths,
    regions,
    flags,
    projection,
    query_value,
    out_weight,
    expand,
    expand_b,
    contract,
    out_bias,
    contract_b,
    gains,
    shifts,
    lang_out,
    vis_out,
    lang_grad,
    vis_grad,
    wgrad,
    vec_out,
    qb_out,
    W,
    G,
    RD,
    RX,
    R2,
    A,
    KV,
    RSB,
    STG,
    QVK,
    D,
    C,
    H,
    GP,
    PCL,
    PCV,
    PS,
    PART,
    PZ,
    NORM,
    RSTD,
    DZ,
    COT,
    SH,
    FLAG,
    QO,
    QB,
    QR,
    CA,
    CR,
    VG,
    QG,
    AVA,
    AVR,
    HL,
    HV,
    OUTS,
    TLO,
    TVO,
    TLG,
    TVG,
    ssem,
    rsem,
    wsem,
    wsem_z,
    gsem,
    gsem2,
):
    d = lax.axis_index("dp")
    z = lax.axis_index("mp")
    c = d % 2
    k = d // 2
    k_flip = [k + 1 - 2 * (k % 2), (k + 2) % 4, 3 - k]
    sib = (d + 1 - 2 * c, z)
    zp = (d, z + 1 - 2 * (z % 2))
    z2 = (z + 2) % 4
    up = (d, (z + 1) % 4)
    down = (d, (z + 3) % 4)
    plane = [(2 * kf + c, z) for kf in k_flip]
    far = (2 * k + 1, z2)

    pending = []
    counter = [0, 0]

    def remote(src, dst, send, recv, device):
        return pltpu.make_async_remote_copy(
            src_ref=src, dst_ref=dst, send_sem=send, recv_sem=recv, device_id=device, device_id_type=MESH
        )

    def send(src, dst, device, recv=None, keep=True):
        slot = counter[0]
        counter[0] += 1
        if recv is None:
            recv = rsem.at[counter[1]]
            counter[1] += 1
        copy = remote(src, dst, ssem.at[slot], recv, device)
        copy.start()
        if keep:
            pending.append(copy)
        return copy

    def wait_bytes(ref, sem):
        pltpu.make_async_copy(ref, ref, sem).wait()

    def arrived(name, *copies):
        with jax.named_scope("wait_" + name):
            for copy in copies:
                copy.wait_recv()

    barrier = pltpu.get_barrier_semaphore()
    peers = [sib, up, down, (d, z2), (d + 1 - 2 * c, z2)] + plane
    for peer in peers:
        pl.semaphore_signal(barrier, inc=1, device_id=peer, device_id_type=MESH)

    def weight_first(part):
        w, lanes = PARTS[part]
        row = pl.ds(pl.multiple_of(d * SHARE, 16), SHARE)
        slot = counter[0]
        counter[0] += 1
        share = SH.at[w] if w < 3 else (expand.at[w - 3] if w < 5 else contract.at[w - 5])
        share = share.at[:, lanes]
        target = W.at[w, row, lanes]
        near = remote(share, target, ssem.at[slot], wsem_z.at[part], sib)
        own = pltpu.make_async_copy(share, target, wsem_z.at[part])

        @pl.when(c == 1)
        def _():
            near.start()

        @pl.when(c == 0)
        def _():
            own.start()

        send(share, target, far, wsem_z.at[part])
        nears.append(near)

    def place(width, first):
        row = lax.broadcasted_iota(jnp.int32, (width, D_MODEL), 0)
        column = lax.broadcasted_iota(jnp.int32, (width, D_MODEL), 1)
        return jnp.where(column - row == first, 1.0, 0.0).astype(BF)

    def attention_share(b):
        SH[b] = (
            dot_nn(projection[b, 0], place(HALF_PAIR, 0))
            + dot_nn(projection[b, 2], place(HALF_PAIR, HALF_PAIR))
            + dot_nn(projection[b, 1], place(HALF_PAIR, 2 * HALF_PAIR))
            + dot_tn(out_weight[b], place(HALF_PAIR, 3 * HALF_PAIR))
        ).astype(BF)

    nears = []
    attention_share(0)

    n_items = lengths.shape[0]
    first_item = 3 * z + jnp.minimum(z, 1)
    KV[0] = jnp.full(KV.shape[1:], -1.0, F32)
    for row, source, size, pad, first_row in ((0, lengths, WORDS, WORDS, 0), (1, regions, REGIONS, REGION_PAD, RL)):
        lane = lax.broadcasted_iota(jnp.int32, (1, TILE), 1)
        owner = jnp.full((1, TILE), -1.0, F32)
        slab_row = lax.broadcasted_iota(jnp.int32, (SLOTS * pad, 1), 0)
        flag = jnp.zeros((SLOTS * pad, 1), F32)
        for j in range(SLOTS):
            item = jnp.minimum(first_item + j, n_items - 1)
            valid = (lane >= j * pad) & (lane < j * pad + source[item]) & (lane < j * pad + size)
            owner = jnp.where(valid, float(j), owner)
            inside = (slab_row >= j * pad) & (slab_row < (j + 1) * pad)
            flag = jnp.where(inside, flags[row, item].astype(F32), flag)
            if row == 1 and j % 2 == 1:
                pair = jnp.full((1, TILE), -1.0, F32)
                for i in (0, 1):
                    other = jnp.minimum(first_item + j - 1 + i, n_items - 1)
                    valid = (lane >= i * pad) & (lane < i * pad + source[other]) & (lane < i * pad + size)
                    pair = jnp.where(valid, float(j - 1 + i), pair)
                KV[0, 2 + j // 2 : 3 + j // 2] = pair
        KV[0, row : row + 1] = owner
        FLAG[first_row : first_row + SLOTS * pad] = flag
        count = flags[row, 0]
        for j in range(1, n_items):
            count = count + flags[row, j]
        CA[0, row : row + 1] = jnp.full((1, 128), count.astype(F32), F32)
    QO[...] = jnp.zeros_like(QO)
    for b in range(3):
        QO[b : b + 1, 0:HALF_PAIR] = query_value[b, 0:1]
        QO[b : b + 1, HALF_PAIR : 2 * HALF_PAIR] = query_value[b, 1:2]
    QO[3:5] = expand_b[...]

    pl.semaphore_wait(barrier, len(peers))
    heads = [
        send(lang.at[pl.ds(0, LANG_HEAD)], HL.at[0], down),
        send(vis.at[pl.ds(0, VIS_HEAD)], HV.at[0], down),
    ]
    weight_first(0)
    weight_first(7)
    heads_cot = [
        send(lcot.at[pl.ds(0, LANG_HEAD)], HL.at[1], down),
        send(vcot.at[pl.ds(0, VIS_HEAD)], HV.at[1], down),
    ]
    kv_sib = send(KV.at[0], KV.at[1], sib)
    kv_zp = send(KV.at[0], KV.at[2], zp)
    count_copies = [send(CA.at[0], CR.at[0], sib)]
    bias_swap = send(QO, QR, (d, z2))

    pair_rows = pl.ds(pl.multiple_of(k * HALF_PAIR, 16), HALF_PAIR)

    def rows_of_chip(chip, first=0, count=HALF_PAIR):
        return pl.ds(pl.multiple_of(chip * HALF_PAIR + first, 16), count)

    def weight_second(part):
        w, lanes = PARTS[part]
        block = W.at[w, pair_rows, lanes]
        wait_bytes(block, wsem_z.at[part])
        for j in range(2):
            send(block, block, plane[j], wsem.at[j, part])

    def weight_third(part):
        w, lanes = PARTS[part]
        for j in range(2):
            wait_bytes(W.at[w, pair_rows, lanes], wsem.at[j, part])
            half = W.at[w, rows_of_chip(k_flip[j], j * SHARE, SHARE), lanes]
            send(half, half, plane[1 - j], wsem.at[2, part])

    def weight_ready(part):
        w, lanes = PARTS[part]
        wait_bytes(W.at[w, pair_rows, lanes], wsem.at[2, part])

    off_l = jnp.where(z == 0, 0, 20 - 5 * z)
    off_v = jnp.where(z == 0, 0, 36 - 9 * z)
    n_l = jnp.where(z == 0, 4 * WORDS, 3 * WORDS)
    n_v = jnp.where(z == 0, 4 * REGIONS, 3 * REGIONS)
    own_l = lang.shape[0]
    own_v = vis.shape[0]
    def gather_start(p, stream):
        rows = pl.ds(stream[0], stream[1] - stream[0])
        return (
            p,
            rows,
            send(A.at[p, 0, rows], A.at[p, 1, rows], sib),
            send(A.at[p, 0, rows], A.at[p, 2, rows], zp),
        )

    def gather_forward(handle):
        p, rows, _, across = handle
        arrived("rows_z", across)
        return send(A.at[p, 2, rows], A.at[p, 3, rows], sib)

    def own_slab(index, source_l, source_v, copies, target):
        arrived("heads", *copies)
        for (r0, r1), size, pad, own, off, count, source, head, head_rows in (
            (VIS, REGIONS, REGION_PAD, own_v, off_v, n_v, source_v, HV, VIS_HEAD),
            (LANG, WORDS, WORDS, own_l, off_l, n_l, source_l, HL, LANG_HEAD),
        ):
            inside = rows_into_slab((r1 - r0, own), off, count, size, pad).astype(BF)
            beyond = rows_into_slab((r1 - r0, head_rows), off - own, count, size, pad).astype(BF)
            target[r0:r1] = (dot_nn(inside, source[...]) + dot_nn(beyond, head[index])).astype(BF)

    own_slab(0, lang, vis, heads, A.at[0, 0])
    rows_x = {stream: gather_start(0, stream) for stream in (VIS, LANG)}

    def tiles(body):
        def step(n, carry):
            body(pl.ds(pl.multiple_of(n * TILE, TILE), TILE))
            return carry

        lax.fori_loop(0, NT, step, 0)

    def slabs(g, body):
        def step(s, carry):
            body(s)
            return carry

        lax.fori_loop(2 * g, 2 * g + 2, step, 0)

    stage_used = {}

    def stage_free(index, stream):
        copy = stage_used.pop((index, stream), None)
        if copy is not None:
            copy.wait_send()

    def partial_nt(g, lhs_ref, stream, w, lanes):
        r0, r1 = stream
        rows = r1 - r0
        stage_free(g, stream)
        def tile(column):
            lhs = lhs_ref[2 * g : 2 * g + 2, r0:r1, :]
            lhs = lhs.reshape(2 * rows, lhs.shape[-1])
            out = dot_nt(lhs, W[w, column, lanes])
            target = PART if g == 0 else PZ
            target[r0:r1, column] = out[:rows]
            STG[g, r0:r1, column] = out[rows:].astype(BF)

        tiles(tile)

    def stage_send(index, stream, device):
        rows = pl.ds(stream[0], stream[1] - stream[0])
        copy = send(STG.at[index, rows], RSB.at[index, rows], device, keep=False)
        stage_used[index, stream] = copy
        return copy

    def sums_near(stream):
        return stage_send(0, stream, sib)

    def sums_far(stream):
        return stage_send(1, stream, sib)

    def sums_z(stream, far):
        r0, r1 = stream
        arrived("sums_core", far)
        stage_free(2, stream)
        STG[2, r0:r1] = (PZ[r0:r1] + RSB[1, r0:r1].astype(F32)).astype(BF)
        return stage_send(2, stream, zp)

    def reduced(stream, *copies):
        r0, r1 = stream
        arrived("sums", *copies)
        return PART[r0:r1] + RSB[0, r0:r1].astype(F32) + RSB[2, r0:r1].astype(F32)

    mask_q = head_mask(0, BF)
    mask_c = head_mask(64, BF)
    mask_q32 = head_mask(0, F32)
    mask_c32 = head_mask(64, F32)
    factor = 1.0 / math.sqrt(D_HEAD)

    def attend_slab(QV, Cb, crossed, stream, s):
        def one(queries, keys_rows, kv_row, item_size, first_item_of, P):
            (q0, q1), (k0, k1) = queries, keys_rows
            nq, nk = q1 - q0, k1 - k0
            query = QV[s, q0:q1, 0:256]
            keys = QV[s, k0:k1, 384:640]
            values = QV[s, k0:k1, 128:384]
            spread = jnp.concatenate([query * mask_q[h] for h in range(3)], 0)
            scores = dot_nt(spread, keys) * factor
            row = lax.broadcasted_iota(jnp.int32, (nq, nk), 0)
            item = jnp.full((nq, nk), float(first_item_of), F32)
            for j in range(1, nq // item_size):
                item = item + jnp.where(row >= j * item_size, 1.0, 0.0)
            same = item == KV[s, kv_row : kv_row + 1, 0:nk]
            scores = jnp.where(same[None], scores.reshape(3, nq, nk), MASKED)
            raised = jnp.exp(scores - jnp.max(scores, -1, keepdims=True))
            weights = (raised / jnp.sum(raised, -1, keepdims=True)).astype(BF).reshape(3 * nq, nk)
            P[s] = weights
            context = dot_nn(weights, values).reshape(3, nq, TILE)
            Cb[s, q0:q1] = (
                context[0] * mask_c32[0] + context[1] * mask_c32[1] + context[2] * mask_c32[2]
            ).astype(BF)

        if stream == LANG:
            if crossed:
                one(LANG, VIS, 1, WORDS, 0, PCL)
            else:
                one(LANG, LANG, 0, WORDS, 0, PS.at[0])
        else:
            half = (V1, V2).index(stream)
            if crossed:
                one(stream, LANG, 0, REGION_PAD, 2 * half, PCV.at[half])
            else:
                one(stream, stream, 2 + half, REGION_PAD, 2 * half, PS.at[1 + half])

    def attend_back_slab(QV, crossed, stream, s):
        def one(queries, keys_rows, P):
            (q0, q1), (k0, k1) = queries, keys_rows
            nq = q1 - q0
            query = QV[s, q0:q1, 0:256]
            keys = QV[s, k0:k1, 384:640]
            values = QV[s, k0:k1, 128:384]
            spread = jnp.concatenate([query * mask_q[h] for h in range(3)], 0)
            upstream = D[s, q0:q1, 512:768]
            up_spread = jnp.concatenate([upstream * mask_c[h] for h in range(3)], 0)
            weights = P[s]
            weights32 = weights.astype(F32)
            weight_grad = dot_nt(up_spread, values)
            score_grad = (
                weights32
                * (weight_grad - jnp.sum(weight_grad * weights32, -1, keepdims=True))
            ).astype(BF)
            dq = dot_nn(score_grad, keys).reshape(3, nq, TILE)
            dq = (dq[0] * mask_q32[0] + dq[1] * mask_q32[1] + dq[2] * mask_q32[2]) * factor
            dk = dot_tn(score_grad, spread) * factor
            dv = dot_tn(weights, up_spread)
            return dq, dk, dv

        if crossed:
            half = RV // 2
            dq_l, dk_v, dv_v = one(LANG, VIS, PCL)
            dq_1, dk_1, dv_1 = one(V1, LANG, PCV.at[0])
            dq_2, dk_2, dv_2 = one(V2, LANG, PCV.at[1])
            results = {
                LANG: (dq_l, dk_1 + dk_2, dv_1 + dv_2),
                V1: (dq_1, dk_v[:half], dv_v[:half]),
                V2: (dq_2, dk_v[half:], dv_v[half:]),
            }
        else:
            results = {stream: one(stream, stream, PS.at[0 if stream == LANG else 1 + (V1, V2).index(stream)])}
        for (r0, r1), (dq, dk, dv) in results.items():
            D[s, r0:r1, 0:128] = dq[:, :128].astype(BF)
            D[s, r0:r1, 128:256] = (dq[:, 128:] + dv[:, :128]).astype(BF)
            D[s, r0:r1, 256:384] = dv[:, 128:].astype(BF)
            D[s, r0:r1, 384:640] = dk.astype(BF)
            D[s, r0:r1, 640:768] = jnp.zeros((r1 - r0, 128), BF)

    def forward_norm(value, index, gain_row, r0, r1):
        center = value - jnp.mean(value, -1, keepdims=True)
        scaled = lax.rsqrt(jnp.mean(center * center, -1, keepdims=True) + EPSILON)
        normed = center * scaled
        NORM[index, r0:r1] = normed
        RSTD[index, r0:r1] = scaled
        return normed * gains[gain_row : gain_row + 1] + shifts[gain_row : gain_row + 1]

    def backward_norm(upstream, index, gain_row, bias_row, r0, r1):
        normed = NORM[index, r0:r1]
        through = upstream * gains[gain_row : gain_row + 1]
        inner = (
            through
            - jnp.mean(through, -1, keepdims=True)
            - normed * jnp.mean(through * normed, -1, keepdims=True)
        )
        result = RSTD[index, r0:r1] * inner
        VG[5 + gain_row : 6 + gain_row] += jnp.sum(upstream * normed, 0, keepdims=True)
        VG[10 + gain_row : 11 + gain_row] += jnp.sum(upstream, 0, keepdims=True)
        VG[bias_row : bias_row + 1] += jnp.sum(result, 0, keepdims=True)
        return result

    def rows_of_group(p, g, stream):
        r0, r1 = stream
        return A[p, 2 * g : 2 * g + 2, r0:r1, :].reshape(2 * (r1 - r0), D_MODEL)

    def project(p, g, stream, w, QV):
        r0, r1 = stream
        def tile(column):
            mapped = dot_nn(rows_of_group(p, g, stream), W[w, :, column]) + QB[w : w + 1, column]
            QV[2 * g : 2 * g + 2, r0:r1, column] = mapped.astype(BF).reshape(2, r1 - r0, TILE)

        tiles(tile)

    def attend(g, stream, b):
        slabs(g, lambda s: attend_slab(QVK.at[b], C.at[b], b == 0, stream, s))

    def expand_rows(g, stream):
        r0, r1 = stream
        rows = r1 - r0
        w = EXPAND[stream]
        def tile(column):
            before = dot_nn(rows_of_group(2, g, stream), W[w, :, column]) + QB[w : w + 1, column]
            half = 0.5 * (1.0 + lax.erf(before * math.sqrt(0.5)))
            slope = half + before * jnp.exp(-0.5 * before * before) * (1.0 / math.sqrt(2.0 * math.pi))
            H[2 * g : 2 * g + 2, r0:r1, column] = (before * half).astype(BF).reshape(2, rows, TILE)
            GP[2 * g : 2 * g + 2, r0:r1, column] = slope.astype(BF).reshape(2, rows, TILE)

        tiles(tile)

    def hidden_gradient(g, stream):
        r0, r1 = stream
        rows = r1 - r0
        def tile(column):
            up_hidden = dot_nn(rows_of_group(3, g, stream), W[CONTRACT[stream], :, column])
            slope = GP[2 * g : 2 * g + 2, r0:r1, column].reshape(2 * rows, TILE)
            D[2 * g : 2 * g + 2, r0:r1, column] = (
                (up_hidden * slope.astype(F32)).astype(BF).reshape(2, rows, TILE)
            )

        tiles(tile)

    def context_gradient(p, g, stream, w):
        r0, r1 = stream
        upstream = dot_nn(rows_of_group(p, g, stream), W[w, :, 512:768])
        D[2 * g : 2 * g + 2, r0:r1, 512:768] = upstream.astype(BF).reshape(2, r1 - r0, TILE)

    def attend_gradient(g, stream, b):
        slabs(g, lambda s: attend_back_slab(QVK.at[b], b == 0, stream, s))

    def all_rows(ref, r0, r1, lanes):
        value = ref[:, r0:r1, lanes]
        return value.reshape(SLOTS * (r1 - r0), value.shape[-1])

    def weight_grad(w, lhs_p, rhs_ref, r0, r1, lanes=slice(0, 768)):
        def tile(column):
            left = all_rows(A.at[lhs_p], r0, r1, column)
            G[w, column, lanes] = dot_tn(left, all_rows(rhs_ref, r0, r1, lanes)).astype(BF)

        tiles(tile)

    def attention_weight_grad(w, x_p, b_p, Cb, r0, r1, middle=None):
        if middle is None:
            weight_grad(w, x_p, D, r0, r1, slice(0, 512))
        else:
            weight_grad(w, x_p, D, r0, r1, slice(0, 384))
            middle()
            weight_grad(w, x_p, D, r0, r1, slice(384, 512))
        def tile(column):
            G[w, column, 512:768] = (
                dot_tn(all_rows(A.at[x_p], r0, r1, column), all_rows(D, r0, r1, slice(512, 768)))
                + dot_tn(all_rows(A.at[b_p], r0, r1, column), all_rows(Cb, r0, r1, slice(0, 256)))
            ).astype(BF)

        tiles(tile)

    def bias_grad(row, r0, r1):
        total = jnp.zeros((1, D_MODEL), F32)
        for s in range(SLOTS):
            total = total + jnp.sum(D[s, r0:r1].astype(F32), 0, keepdims=True)
        QG[row : row + 1] = total

    def grad_first(part):
        w, lanes = PARTS[part]
        for j in range(2):
            half = rows_of_chip(k_flip[2], (1 - j) * SHARE, SHARE)
            send(G.at[w, half, lanes], RD.at[j, w, :, lanes], plane[j], gsem.at[2, part])

    def grad_second(part):
        w, lanes = PARTS[part]
        wait_bytes(RD.at[:, w, :, lanes], gsem.at[2, part])
        for j in range(2):
            half = rows_of_chip(k_flip[1 - j], (1 - j) * SHARE, SHARE)
            G[w, half, lanes] = (G[w, half, lanes].astype(F32) + RD[j, w, :, lanes].astype(F32)).astype(BF)
        for j in range(2):
            send(G.at[w, rows_of_chip(k_flip[j]), lanes], RX.at[j, w, :, lanes], plane[j], gsem.at[j, part])

    grad_nears = []

    def grad_third(part):
        w, lanes = PARTS[part]
        for j in range(2):
            wait_bytes(RX.at[j, w, :, lanes], gsem.at[j, part])
        total = G[w, pair_rows, lanes].astype(F32)
        total = total + RX[0, w, :, lanes].astype(F32) + RX[1, w, :, lanes].astype(F32)
        G[w, pair_rows, lanes] = total.astype(BF)
        low = G.at[w, rows_of_chip(k, 0, SHARE), lanes]
        high = G.at[w, rows_of_chip(k, SHARE, SHARE), lanes]
        slot = counter[0]
        counter[0] += 2
        here, there = R2.at[0, w, :, lanes], R2.at[1, w, :, lanes]
        own = pltpu.make_async_copy(low, here, gsem2.at[part])
        near = remote(high, here, ssem.at[slot], gsem2.at[part], sib)
        far_low = remote(low, there, ssem.at[slot], gsem2.at[part], (2 * k, z2))
        far_high = remote(high, there, ssem.at[slot + 1], gsem2.at[part], (2 * k + 1, z2))

        @pl.when(c == 0)
        def _():
            own.start()
            near.start()

        @pl.when(c == 1)
        def _():
            far_low.start()
            far_high.start()

        grad_nears.append((near, far_low, far_high))

    def grad_last(part):
        w, lanes = PARTS[part]
        wait_bytes(R2.at[:, w, :, lanes], gsem2.at[part])
        wgrad[w, :, lanes] = R2[0, w, :, lanes].astype(F32) + R2[1, w, :, lanes].astype(F32)

    def count_step(stage, peer):
        count_copies[stage].wait_recv()
        CA[stage + 1] = CA[stage] + CR[stage]
        if peer is not None:
            count_copies.append(send(CA.at[stage + 1], CR.at[stage + 1], peer))

    VG[...] = jnp.zeros_like(VG)
    QG[...] = jnp.zeros_like(QG)
    weight_second(0)
    attention_share(2)
    weight_second(7)
    weight_first(2)
    attention_share(1)
    own_slab(1, lcot, vcot, heads_cot, COT)
    weight_third(0)
    weight_first(1)
    kv_sib.wait_recv()
    kv_zp.wait_recv()
    kv_far = send(KV.at[2], KV.at[3], sib)
    far_x = {stream: gather_forward(rows_x[stream]) for stream in (VIS, LANG)}
    bias_swap.wait_recv()
    QB[...] = jnp.where(c == 1, QR[...], QO[...])
    weight_third(7)
    kv_far.wait_recv()
    arrived("rows", rows_x[VIS][2], rows_x[LANG][2])
    weight_ready(0)
    weight_ready(7)

    near, far_sum, z_sum, rows, far_rows = {}, {}, {}, {}, {}
    out_lanes, all_lanes = slice(512, 768), slice(0, 768)

    def sums_near_after(stream, lhs, w, lanes):
        partial_nt(0, lhs, stream, w, lanes)
        near[stream] = sums_near(stream)

    def sums_far_after(stream, lhs, w, lanes):
        partial_nt(1, lhs, stream, w, lanes)
        far_sum[stream] = sums_far(stream)

    def sums_on(stream):
        z_sum[stream] = sums_z(stream, far_sum[stream])

    def total_of(stream):
        return reduced(stream, near[stream], z_sum[stream])

    def far_arrived(stream):
        arrived("rows", far_rows[stream])

    def near_arrived(stream):
        arrived("rows", rows[stream][2])

    def pass_on(stream):
        far_rows[stream] = gather_forward(rows[stream])

    project(0, 0, BOTH, 0, QVK.at[0])
    weight_second(2)
    weight_first(4)
    attend(0, V1, 0)
    sums_near_after(V1, C.at[0], 0, out_lanes)
    attend(0, V2, 0)
    sums_near_after(V2, C.at[0], 0, out_lanes)
    weight_second(1)
    weight_first(6)
    attend(0, LANG, 0)
    sums_near_after(LANG, C.at[0], 0, out_lanes)
    arrived("rows", far_x[VIS], far_x[LANG])
    project(0, 1, BOTH, 0, QVK.at[0])
    attend(1, V1, 0)
    sums_far_after(V1, C.at[0], 0, out_lanes)
    attend(1, V2, 0)
    sums_far_after(V2, C.at[0], 0, out_lanes)
    sums_on(V1)
    attend(1, LANG, 0)
    sums_far_after(LANG, C.at[0], 0, out_lanes)
    sums_on(V2)
    weight_third(2)
    sums_on(LANG)
    count_step(0, plane[0])
    weight_third(1)

    def first_norm(stream):
        r0, r1 = stream
        value = total_of(stream) + out_bias[0:1] + A[0, 0, r0:r1].astype(F32)
        A[1, 0, r0:r1] = forward_norm(value, 0, 0, r0, r1).astype(BF)
        rows[stream] = gather_start(1, stream)

    for stream in CHAINS:
        first_norm(stream)

    def self_rows(g, stream):
        project(1, g, stream, SELF[stream], QVK.at[1])
        attend(g, stream, 1)
        if g == 0:
            sums_near_after(stream, C.at[1], SELF[stream], out_lanes)
        else:
            sums_far_after(stream, C.at[1], SELF[stream], out_lanes)

    weight_second(4)
    weight_ready(2)
    near_arrived(V1)
    self_rows(0, V1)
    pass_on(V1)
    near_arrived(V2)
    self_rows(0, V2)
    pass_on(V2)
    weight_second(6)
    weight_first(3)
    weight_ready(1)
    near_arrived(LANG)
    self_rows(0, LANG)
    pass_on(LANG)
    far_arrived(V1)
    self_rows(1, V1)
    far_arrived(V2)
    self_rows(1, V2)
    sums_on(V1)
    weight_third(4)
    weight_first(5)
    far_arrived(LANG)
    self_rows(1, LANG)
    sums_on(V2)
    count_step(1, plane[1])
    sums_on(LANG)
    weight_third(6)

    def second_norm(stream):
        r0, r1 = stream
        n = 1 if stream == LANG else 2
        value = total_of(stream) + out_bias[n : n + 1] + A[1, 0, r0:r1].astype(F32)
        A[2, 0, r0:r1] = forward_norm(value, 1, n, r0, r1).astype(BF)
        rows[stream] = gather_start(2, stream)

    for stream in CHAINS:
        second_norm(stream)

    weight_second(3)
    weight_ready(4)
    near_arrived(V1)
    expand_rows(0, V1)
    pass_on(V1)
    near_arrived(V2)
    expand_rows(0, V2)
    pass_on(V2)
    weight_second(5)
    far_arrived(V1)
    expand_rows(1, V1)
    pass_on(LANG)
    weight_ready(6)
    sums_far_after(V1, H, 6, all_lanes)
    far_arrived(V2)
    expand_rows(1, V2)
    sums_on(V1)
    sums_far_after(V2, H, 6, all_lanes)
    sums_near_after(V1, H, 6, all_lanes)
    sums_on(V2)
    sums_near_after(V2, H, 6, all_lanes)
    weight_third(3)
    count_step(2, None)

    def last_norm(stream):
        r0, r1 = stream
        n = 0 if stream == LANG else 1
        value = total_of(stream) + contract_b[n : n + 1] + A[2, 0, r0:r1].astype(F32)
        OUTS[r0:r1] = forward_norm(value, 2, 3 + n, r0, r1).astype(BF)
        scale = total_items / CA[3, n : n + 1, 0:1]
        upstream = COT[r0:r1].astype(F32) * (FLAG[r0:r1] * scale)
        result = backward_norm(upstream, 2, 3 + n, 3 + n, r0, r1)
        DZ[r0:r1] = result
        A[3, 0, r0:r1] = result.astype(BF)
        rows[stream] = gather_start(3, stream)

    weight_third(5)
    last_norm(V1)
    weight_ready(3)
    near_arrived(LANG)
    far_arrived(LANG)
    expand_rows(0, LANG)
    last_norm(V2)
    expand_rows(1, LANG)
    weight_ready(5)
    sums_far_after(LANG, H, 5, all_lanes)
    sums_near_after(LANG, H, 5, all_lanes)
    sums_on(LANG)

    def feed_gradient(g, stream):
        hidden_gradient(g, stream)
        if g == 0:
            sums_near_after(stream, D, EXPAND[stream], all_lanes)
        else:
            sums_far_after(stream, D, EXPAND[stream], all_lanes)

    near_arrived(V1)
    feed_gradient(0, V1)
    pass_on(V1)
    near_arrived(V2)
    feed_gradient(0, V2)
    pass_on(V2)
    last_norm(LANG)
    far_arrived(V1)
    feed_gradient(1, V1)
    far_arrived(V2)
    weight_grad(6, 3, H, *VIS)
    grad_first(6)
    sums_on(V1)
    feed_gradient(1, V2)
    near_arrived(LANG)
    feed_gradient(0, LANG)
    pass_on(LANG)
    sums_on(V2)
    weight_grad(4, 2, D, *VIS)
    grad_first(4)

    def second_norm_back(stream):
        r0, r1 = stream
        n = 1 if stream == LANG else 2
        result = backward_norm(DZ[r0:r1] + total_of(stream), 1, n, n, r0, r1)
        DZ[r0:r1] = result
        A[4, 0, r0:r1] = result.astype(BF)
        rows[stream] = gather_start(4, stream)

    second_norm_back(V1)
    far_arrived(LANG)
    feed_gradient(1, LANG)
    grad_second(6)
    second_norm_back(V2)
    sums_on(LANG)
    weight_grad(5, 3, H, *LANG)
    grad_first(5)
    bias_grad(4, *VIS)
    tail_out = [
        send(OUTS.at[pl.ds(RL - LANG_TAIL, LANG_TAIL)], TLO, up),
        send(OUTS.at[pl.ds(ROWS - VIS_TAIL, VIS_TAIL)], TVO, up),
    ]
    grad_second(4)
    weight_grad(3, 2, D, *LANG)
    grad_first(3)
    bias_grad(3, *LANG)

    def self_gradient(g, stream):
        w = SELF[stream]
        context_gradient(4, g, stream, w)
        attend_gradient(g, stream, 1)
        if g == 0:
            sums_near_after(stream, D, w, all_lanes)
        else:
            sums_far_after(stream, D, w, all_lanes)

    near_arrived(V1)
    self_gradient(0, V1)
    pass_on(V1)
    second_norm_back(LANG)
    near_arrived(V2)
    self_gradient(0, V2)
    pass_on(V2)
    grad_second(5)
    grad_third(6)
    far_arrived(V1)
    self_gradient(1, V1)
    grad_second(3)
    far_arrived(V2)
    self_gradient(1, V2)
    sums_on(V1)
    near_arrived(LANG)
    self_gradient(0, LANG)
    pass_on(LANG)
    sums_on(V2)
    grad_third(4)
    attention_weight_grad(2, 1, 4, C.at[1], *VIS)
    grad_first(2)

    def first_norm_back(stream):
        r0, r1 = stream
        result = backward_norm(DZ[r0:r1] + total_of(stream), 0, 0, 0, r0, r1)
        DZ[r0:r1] = result
        A[5, 0, r0:r1] = result.astype(BF)
        rows[stream] = gather_start(5, stream)

    first_norm_back(V1)
    far_arrived(LANG)
    self_gradient(1, LANG)
    first_norm_back(V2)
    sums_on(LANG)
    bias_grad(2, *VIS)
    grad_third(5)
    attention_weight_grad(1, 1, 4, C.at[1], *LANG)
    grad_first(1)
    grad_second(2)
    bias_grad(1, *LANG)
    first_norm_back(LANG)

    for stream in CHAINS:
        near_arrived(stream)
        context_gradient(5, 0, stream, 0)
    attend_gradient(0, None, 0)
    for stream in CHAINS:
        pass_on(stream)
    for stream in CHAINS:
        sums_near_after(stream, D, 0, all_lanes)
    grad_second(1)
    grad_third(3)
    for stream in CHAINS:
        far_arrived(stream)
        context_gradient(5, 1, stream, 0)
    attend_gradient(1, None, 0)
    attention_weight_grad(0, 0, 5, C.at[0], *BOTH, middle=lambda: grad_first(0))
    grad_first(7)
    for stream in CHAINS:
        sums_far_after(stream, D, 0, all_lanes)
    for stream in CHAINS:
        sums_on(stream)
    grad_second(0)
    bias_grad(0, *BOTH)

    quarter = jnp.where(c == 0, z, z2)
    AVA[0, 0:16] = VG[...]
    for j in range(4):
        AVA[0, 16 + 8 * j : 24 + 8 * j] = jnp.where(quarter == j, QG[...], 0.0)
    vector_peers = [sib, plane[0], plane[1], zp, (d, z2)]
    vector_copies = [send(AVA.at[0], AVR.at[0], vector_peers[0])]

    def vector_step(stage):
        arrived("vectors", vector_copies[stage])
        AVA[stage + 1] = AVA[stage] + AVR[stage]
        if stage < 4:
            vector_copies.append(send(AVA.at[stage + 1], AVR.at[stage + 1], vector_peers[stage + 1]))

    grad_second(7)
    grad_third(2)
    vector_step(0)
    grad_third(1)
    vector_step(1)
    for w in (6, 4, 5, 3):
        grad_last(w)
    grad_third(0)
    vector_step(2)
    for stream in CHAINS:
        r0, r1 = stream
        DZ[r0:r1] = DZ[r0:r1] + total_of(stream)
    tail_grad = [
        send(DZ.at[pl.ds(RL - LANG_TAIL, LANG_TAIL)], TLG, up),
        send(DZ.at[pl.ds(ROWS - VIS_TAIL, VIS_TAIL)], TVG, up),
    ]
    grad_third(7)
    vector_step(3)
    for w in (2, 1):
        grad_last(w)
    vector_step(4)
    vec_out[...] = AVA[5, 0:16]
    qb_out[...] = AVA[5, pl.ds(pl.multiple_of(16 + 8 * z, 8), 8)]

    arrived("tails", *tail_out, *tail_grad)
    before_l = jnp.where(z == 1, 0, 25 - 5 * z)
    before_v = jnp.where(z == 1, 0, 45 - 9 * z)
    for (r0, r1), size, pad, own_rows, off, before, tail_rows, out_ref, grad_ref, t_out, t_grad in (
        (LANG, WORDS, WORDS, own_l, off_l, before_l, LANG_TAIL, lang_out, lang_grad, TLO, TLG),
        (VIS, REGIONS, REGION_PAD, own_v, off_v, before_v, VIS_TAIL, vis_out, vis_grad, TVO, TVG),
    ):
        from_own = rows_from_slab((own_rows, r1 - r0), -off, 0, off, own_rows, size, pad)
        from_tail = rows_from_slab(
            (own_rows, tail_rows), own_rows - before, r1 - r0 - tail_rows, 0, off, size, pad
        )
        out_ref[...] = (
            dot_nn(from_own.astype(BF), OUTS[r0:r1]) + dot_nn(from_tail.astype(BF), t_out[...])
        ).astype(BF)
        exact = lax.Precision.HIGHEST
        grad_ref[...] = jnp.dot(
            from_own, DZ[r0:r1], precision=exact, preferred_element_type=F32
        ) + jnp.dot(from_tail, t_grad[...], precision=exact, preferred_element_type=F32)

    grad_last(0)
    grad_last(7)

    for copy in pending:
        copy.wait_send()
    for index, stream in list(stage_used):
        stage_free(index, stream)

    @pl.when(c == 1)
    def _():
        for copy in nears:
            copy.wait_send()
        for _, far_low, far_high in grad_nears:
            far_low.wait_send()
            far_high.wait_send()

    @pl.when(c == 0)
    def _():
        for near, _, _ in grad_nears:
            near.wait_send()
    assert counter[0] <= ssem.shape[0] and counter[1] <= rsem.shape[0], counter


N_SEND = 240
N_RECV = 160


def fused_layer(total_items, *operands):
    own_l, own_v = operands[0].shape[0], operands[1].shape[0]
    vmem = pl.BlockSpec(memory_space=pltpu.VMEM)
    smem = pl.BlockSpec(memory_space=pltpu.SMEM)
    shapes = [
        ((own_l, D), BF),
        ((own_v, D), BF),
        ((own_l, D), F32),
        ((own_v, D), F32),
        ((7, SHARE, D), F32),
        ((16, D), F32),
        ((8, D), F32),
    ]
    scratch = [
        ((7, D, D), BF),
        ((7, D, D), BF),
        ((2, 7, SHARE, D), BF),
        ((2, 7, HALF_PAIR, D), BF),
        ((2, 7, SHARE, D), BF),
        ((6, SLOTS, ROWS, D), BF),
        ((SLOTS, 8, TILE), F32),
        ((3, ROWS, D), BF),
        ((3, ROWS, D), BF),
        ((2, SLOTS, ROWS, D), BF),
        ((SLOTS, ROWS, D), BF),
        ((2, SLOTS, ROWS, TILE), BF),
        ((SLOTS, ROWS, D), BF),
        ((SLOTS, ROWS, D), BF),
        ((SLOTS, 3 * RL, RV), BF),
        ((2, SLOTS, 3 * RL, RL), BF),
        ((3, SLOTS, 3 * RL, RL), BF),
        ((ROWS, D), F32),
        ((ROWS, D), F32),
        ((3, ROWS, D), F32),
        ((3, ROWS, 1), F32),
        ((ROWS, D), F32),
        ((ROWS, D), BF),
        ((3, SHARE, D), BF),
        ((ROWS, 1), F32),
        ((8, D), F32),
        ((8, D), F32),
        ((8, D), F32),
        ((4, 8, 128), F32),
        ((3, 8, 128), F32),
        ((16, D), F32),
        ((8, D), F32),
        ((6, N_AR, D), F32),
        ((5, N_AR, D), F32),
        ((2, LANG_HEAD, D), BF),
        ((2, VIS_HEAD, D), BF),
        ((ROWS, D), BF),
        ((LANG_TAIL, D), BF),
        ((VIS_TAIL, D), BF),
        ((LANG_TAIL, D), F32),
        ((VIS_TAIL, D), F32),
    ]
    dma = pltpu.SemaphoreType.DMA
    return pl.pallas_call(
        partial(layer_kernel, total_items),
        out_shape=[jax.ShapeDtypeStruct(s, t) for s, t in shapes],
        in_specs=[vmem] * 4 + [smem] * 3 + [vmem] * (len(operands) - 7),
        out_specs=[vmem] * len(shapes),
        scratch_shapes=[pltpu.VMEM(s, t) for s, t in scratch]
        + [dma((N_SEND,)), dma((N_RECV,)), dma((3, 8)), dma((8,)), dma((3, 8)), dma((8,))],
        compiler_params=pltpu.CompilerParams(
            collective_id=0, has_side_effects=True, vmem_limit_bytes=VMEM_LIMIT
        ),
    )(*operands)


def unpack_kernel(lo, vo, lg, vg, wgrad, vec, qb, *outs):
    (lo_out, vo_out, lg_out, vg_out, proj, qv, outw, outb, exp, expb, con, conb, gain, shift) = outs
    lo_out[...] = lo[...]
    vo_out[...] = vo[...]
    lg_out[...] = lg[...]
    vg_out[...] = vg[...]
    width = HALF_PAIR
    for b in range(3):
        for j, lane in enumerate((0, 2 * width, width)):
            proj[b, j] = wgrad[b, :, lane : lane + width]
        outw[b] = wgrad[b, :, 3 * width :].T
        for j in range(2):
            qv[b, j : j + 1] = qb[b : b + 1, j * width : (j + 1) * width]
    for stream in range(2):
        exp[stream] = wgrad[3 + stream]
        con[stream] = wgrad[5 + stream]
    expb[...] = qb[3:5]
    outb[...] = vec[0:3]
    conb[...] = vec[3:5]
    gain[...] = vec[5:10]
    shift[...] = vec[10:15]


def unpack(packed, shapes):
    vmem = pl.BlockSpec(memory_space=pltpu.VMEM)
    return pl.pallas_call(
        unpack_kernel,
        out_shape=shapes,
        in_specs=[vmem] * len(packed),
        out_specs=[vmem] * len(shapes),
        compiler_params=pltpu.CompilerParams(vmem_limit_bytes=VMEM_LIMIT),
    )(*packed)


def on_device_fused(
    language_input,
    vision_input,
    word_lengths,
    region_counts,
    task_flags,
    language_cotangent,
    vision_cotangent,
    projection_weight,
    query_value_bias,
    output_weight,
    output_bias,
    expand_weight,
    expand_bias,
    contract_weight,
    contract_bias,
    norm_gain,
    norm_bias,
):
    packed = fused_layer(
        float(word_lengths.shape[0] * lax.axis_size("dp")),
        language_input,
        vision_input,
        language_cotangent,
        vision_cotangent,
        word_lengths,
        region_counts,
        task_flags.T,
        projection_weight,
        query_value_bias,
        output_weight,
        expand_weight,
        expand_bias,
        contract_weight.transpose(0, 2, 1),
        output_bias,
        contract_bias,
        norm_gain,
        norm_bias,
    )
    like = [
        (language_input, BF),
        (vision_input, BF),
        (language_input, F32),
        (vision_input, F32),
        (projection_weight, F32),
        (query_value_bias, F32),
        (output_weight, F32),
        (output_bias, F32),
        (expand_weight, F32),
        (expand_bias, F32),
        (contract_weight.transpose(0, 2, 1), F32),
        (contract_bias, F32),
        (norm_gain, F32),
        (norm_bias, F32),
    ]
    outs = list(unpack(packed, [jax.ShapeDtypeStruct(a.shape, t) for a, t in like]))
    outs[10] = outs[10].transpose(0, 2, 1)
    return tuple(outs)


def solution(mesh):
    in_specs = (
        P(("dp", "mp"), None),
        P(("dp", "mp"), None),
        P("dp"),
        P("dp"),
        P("dp", None),
        P(("dp", "mp"), None),
        P(("dp", "mp"), None),
        P(None, None, "dp", "mp"),
        P(None, None, "mp"),
        P(None, "mp", "dp"),
        P(),
        P(None, "dp", "mp"),
        P(None, "mp"),
        P(None, "mp", "dp"),
        P(),
        P(),
        P(),
    )
    out_specs = (
        P(("dp", "mp"), None),
        P(("dp", "mp"), None),
        P(("dp", "mp"), None),
        P(("dp", "mp"), None),
        P(None, None, "dp", "mp"),
        P(None, None, "mp"),
        P(None, "mp", "dp"),
        P(),
        P(None, "dp", "mp"),
        P(None, "mp"),
        P(None, "mp", "dp"),
        P(),
        P(),
        P(),
    )
    fused = dict(mesh.shape) == {"dp": 8, "mp": 4}
    return jax.shard_map(
        on_device_fused if fused else on_device, mesh=mesh, in_specs=in_specs, out_specs=out_specs, check_vma=False
    )
```

```python
from functools import partial
import math

import jax
import jax.numpy as jnp
from jax import lax
from jax.experimental import pallas as pl
from jax.experimental.pallas import tpu as pltpu
from jax.sharding import PartitionSpec as P

D = 768
HEADS = 12
WORDS = 20
REGIONS = 36
D_MODEL = D
D_HEAD = D // HEADS

EPSILON = 1e-12
MASKED = -1e30


def layer_norm(summed, gain, shift):
    center = summed - jnp.mean(summed, -1, keepdims=True)
    scaled = lax.rsqrt(jnp.mean(center * center, -1, keepdims=True) + EPSILON)
    normed = center * scaled
    return (normed * gain + shift, normed, scaled)


def norm_back(upstream, normed, scaled, gain):
    through = upstream * gain
    inner = (
        through
        - jnp.mean(through, -1, keepdims=True)
        - normed * jnp.mean(through * normed, -1, keepdims=True)
    )
    return (scaled * inner, jnp.sum(upstream * normed, 0), jnp.sum(upstream, 0))


def split_heads(rows, item_count):
    head_size = D // HEADS
    return rows.reshape(
        item_count, rows.shape[0] // item_count, rows.shape[1] // head_size, head_size
    )


def join_heads(block):
    return block.reshape(block.shape[0] * block.shape[1], block.shape[2] * block.shape[3])


def project(rows, weight, bias, item_count):
    mapped = jnp.einsum("rd,jde->jre", rows, weight, preferred_element_type=jnp.float32)
    query = split_heads((mapped[0] + bias[0]).astype(jnp.bfloat16), item_count)
    keys = split_heads(mapped[1].astype(jnp.bfloat16), item_count)
    values = split_heads((mapped[2] + bias[1]).astype(jnp.bfloat16), item_count)
    return (query, keys, values)


def masked_scores(query, keys, valid):
    scores = jnp.einsum("inhd,imhd->ihnm", query, keys, preferred_element_type=jnp.float32) * (
        1.0 / math.sqrt(D // HEADS)
    )
    return jnp.where(valid[:, None, None, :], scores, MASKED)


def attend(query, keys, values, valid):
    scores = masked_scores(query, keys, valid)
    highest = jnp.max(scores, -1, keepdims=True)
    raised = jnp.exp(scores - highest)
    summed = jnp.sum(raised, -1, keepdims=True)
    context = jnp.einsum(
        "ihnm,imhd->inhd",
        (raised / summed).astype(jnp.bfloat16),
        values,
        preferred_element_type=jnp.float32,
    )
    return (join_heads(context).astype(jnp.bfloat16), highest + jnp.log(summed))


def attend_back(query, keys, values, valid, log_total, context_grad):
    factor = 1.0 / math.sqrt(D // HEADS)
    upstream = context_grad.reshape(query.shape)
    weights = jnp.exp(masked_scores(query, keys, valid) - log_total)
    weight_grad = jnp.einsum(
        "inhd,imhd->ihnm", upstream, values, preferred_element_type=jnp.float32
    )
    score_grad = (
        weights * (weight_grad - jnp.sum(weight_grad * weights, -1, keepdims=True))
    ).astype(jnp.bfloat16)
    query_grad = (
        jnp.einsum("ihnm,imhd->inhd", score_grad, keys, preferred_element_type=jnp.float32) * factor
    ).astype(jnp.bfloat16)
    keys_grad = (
        jnp.einsum("ihnm,inhd->imhd", score_grad, query, preferred_element_type=jnp.float32)
        * factor
    ).astype(jnp.bfloat16)
    values_grad = jnp.einsum(
        "ihnm,inhd->imhd",
        weights.astype(jnp.bfloat16),
        upstream,
        preferred_element_type=jnp.float32,
    ).astype(jnp.bfloat16)
    return (join_heads(query_grad), join_heads(keys_grad), join_heads(values_grad))


def project_back(rows, query_grad, keys_grad, values_grad):
    stacked = jnp.stack([query_grad, keys_grad, values_grad])
    weight_grad = jnp.einsum("rd,jre->jde", rows, stacked, preferred_element_type=jnp.float32)
    bias_grad = jnp.stack(
        [jnp.sum(query_grad.astype(jnp.float32), 0), jnp.sum(values_grad.astype(jnp.float32), 0)]
    )
    return (weight_grad, bias_grad, stacked)


def gather_rows(language_rows, vision_rows):
    return (
        lax.all_gather(language_rows, "mp", axis=0, tiled=True),
        lax.all_gather(vision_rows, "mp", axis=0, tiled=True),
    )


def rows_of(language_part, vision_part):
    return (
        lax.all_to_all(language_part, "mp", split_axis=0, concat_axis=1, tiled=True),
        lax.all_to_all(vision_part, "mp", split_axis=0, concat_axis=1, tiled=True),
    )


def gather_grads(language_rows, vision_rows):
    return (
        lax.all_gather(language_rows, "mp", axis=0, tiled=True),
        lax.all_gather(vision_rows, "mp", axis=0, tiled=True),
    )


def grads_of(language_part, vision_part):
    return (
        lax.all_to_all(language_part, "mp", split_axis=1, concat_axis=2, tiled=True),
        lax.all_to_all(vision_part, "mp", split_axis=1, concat_axis=2, tiled=True),
    )


def matmul(left, right):
    return jnp.dot(left, right, preferred_element_type=jnp.float32)


def on_device(
    language_input,
    vision_input,
    word_lengths,
    region_counts,
    task_flags,
    language_cotangent,
    vision_cotangent,
    projection_weight,
    query_value_bias,
    output_weight,
    output_bias,
    expand_weight,
    expand_bias,
    contract_weight,
    contract_bias,
    norm_gain,
    norm_bias,
):
    item_count = word_lengths.shape[0]
    flag_total = lax.psum(jnp.sum(task_flags, 0), "dp")
    projection, out_weight, expand, contract = (
        lax.all_gather(projection_weight, "dp", axis=2, tiled=True),
        lax.all_gather(output_weight, "dp", axis=2, tiled=True),
        lax.all_gather(expand_weight, "dp", axis=1, tiled=True),
        lax.all_gather(contract_weight, "dp", axis=2, tiled=True),
    )
    projection_full, out_full, expand_full, contract_full = (
        lax.all_gather(projection, "mp", axis=3, tiled=True),
        lax.all_gather(out_weight, "mp", axis=1, tiled=True),
        lax.all_gather(expand, "mp", axis=2, tiled=True),
        lax.all_gather(contract, "mp", axis=1, tiled=True),
    )
    valid = [
        jnp.arange(WORDS, dtype=jnp.int32)[None, :] < word_lengths[:, None],
        jnp.arange(REGIONS, dtype=jnp.int32)[None, :] < region_counts[:, None],
    ]
    row_counts = [WORDS, REGIONS]
    inputs = [language_input.astype(jnp.float32), vision_input.astype(jnp.float32)]
    cross_rows = gather_rows(language_input, vision_input)
    cross_parts = [
        project(cross_rows[stream], projection[0], query_value_bias[0], item_count)
        for stream in range(2)
    ]
    cross_context = []
    cross_total = []
    for stream in range(2):
        other = 1 - stream
        context, log_total = attend(
            cross_parts[stream][0], cross_parts[other][1], cross_parts[other][2], valid[other]
        )
        cross_context.append(context)
        cross_total.append(log_total)
    moved = rows_of(cross_context[0], cross_context[1])
    branch = [matmul(moved[stream], out_full[0]) for stream in range(2)]
    first = [
        layer_norm(branch[stream] + output_bias[0] + inputs[stream], norm_gain[0], norm_bias[0])
        for stream in range(2)
    ]
    first_out = [first[stream][0].astype(jnp.bfloat16) for stream in range(2)]
    self_rows = gather_rows(first_out[0], first_out[1])
    self_parts = [
        project(self_rows[stream], projection[1 + stream], query_value_bias[1 + stream], item_count)
        for stream in range(2)
    ]
    self_context = []
    self_total = []
    for stream in range(2):
        context, log_total = attend(
            self_parts[stream][0], self_parts[stream][1], self_parts[stream][2], valid[stream]
        )
        self_context.append(context)
        self_total.append(log_total)
    moved = rows_of(self_context[0], self_context[1])
    branch = [matmul(moved[stream], out_full[1 + stream]) for stream in range(2)]
    second = [
        layer_norm(
            branch[stream] + output_bias[1 + stream] + first_out[stream].astype(jnp.float32),
            norm_gain[1 + stream],
            norm_bias[1 + stream],
        )
        for stream in range(2)
    ]
    second_out = [second[stream][0].astype(jnp.bfloat16) for stream in range(2)]
    feed_rows = gather_rows(second_out[0], second_out[1])
    before = [
        matmul(feed_rows[stream], expand[stream]) + expand_bias[stream] for stream in range(2)
    ]
    hidden = [
        jax.nn.gelu(before[stream], approximate=False).astype(jnp.bfloat16) for stream in range(2)
    ]
    moved = rows_of(hidden[0], hidden[1])
    branch = [matmul(moved[stream], contract_full[stream]) for stream in range(2)]
    third = [
        layer_norm(
            branch[stream] + contract_bias[stream] + second_out[stream].astype(jnp.float32),
            norm_gain[3 + stream],
            norm_bias[3 + stream],
        )
        for stream in range(2)
    ]
    language_out = third[0][0].astype(jnp.bfloat16)
    vision_out = third[1][0].astype(jnp.bfloat16)
    item_scale = task_flags.astype(jnp.float32) * (
        item_count * lax.axis_size("dp") / flag_total.astype(jnp.float32)
    )
    shard_index = lax.axis_index("mp")
    upstream = []
    for stream, cotangent in enumerate([language_cotangent, vision_cotangent]):
        per_row = jnp.repeat(
            item_scale[:, stream],
            row_counts[stream],
            total_repeat_length=item_count * row_counts[stream],
        )
        shard_rows = cotangent.shape[0]
        row_scale = lax.dynamic_slice_in_dim(per_row, shard_index * shard_rows, shard_rows)
        upstream.append(cotangent.astype(jnp.float32) * row_scale[:, None])
    third_back = [
        norm_back(upstream[stream], third[stream][1], third[stream][2], norm_gain[3 + stream])
        for stream in range(2)
    ]
    sent = gather_grads(
        third_back[0][0].astype(jnp.bfloat16), third_back[1][0].astype(jnp.bfloat16)
    )
    expand_local = []
    expand_bias_local = []
    contract_local = []
    before_grads = []
    for stream in range(2):
        hidden_grad = jnp.einsum(
            "rd,fd->rf", sent[stream], contract[stream], preferred_element_type=jnp.float32
        )
        contract_local.append(
            jnp.einsum(
                "rf,rd->fd", hidden[stream], sent[stream], preferred_element_type=jnp.float32
            )
        )
        unused, pull = jax.vjp(partial(jax.nn.gelu, approximate=False), before[stream])
        before_grad = pull(hidden_grad)[0].astype(jnp.bfloat16)
        expand_local.append(
            jnp.einsum(
                "rd,rf->df", feed_rows[stream], before_grad, preferred_element_type=jnp.float32
            )
        )
        expand_bias_local.append(jnp.sum(before_grad.astype(jnp.float32), 0))
        before_grads.append(before_grad[None])
    moved = grads_of(before_grads[0], before_grads[1])
    back = [
        jnp.einsum(
            "rf,df->rd", moved[stream][0], expand_full[stream], preferred_element_type=jnp.float32
        )
        for stream in range(2)
    ]
    second_grad = [third_back[stream][0] + back[stream] for stream in range(2)]
    second_back = [
        norm_back(second_grad[stream], second[stream][1], second[stream][2], norm_gain[1 + stream])
        for stream in range(2)
    ]
    sent = gather_grads(
        second_back[0][0].astype(jnp.bfloat16), second_back[1][0].astype(jnp.bfloat16)
    )
    self_weight = []
    self_bias = []
    self_out = []
    stacks = []
    for stream in range(2):
        context_grad = jnp.einsum(
            "rd,ed->re", sent[stream], out_weight[1 + stream], preferred_element_type=jnp.float32
        ).astype(jnp.bfloat16)
        self_out.append(
            jnp.einsum(
                "re,rd->ed", self_context[stream], sent[stream], preferred_element_type=jnp.float32
            )
        )
        grads = attend_back(
            self_parts[stream][0],
            self_parts[stream][1],
            self_parts[stream][2],
            valid[stream],
            self_total[stream],
            context_grad,
        )
        weight_part, bias_part, stacked = project_back(
            self_rows[stream], grads[0], grads[1], grads[2]
        )
        self_weight.append(weight_part)
        self_bias.append(bias_part)
        stacks.append(stacked)
    moved = grads_of(stacks[0], stacks[1])
    back = [
        jnp.einsum(
            "jre,jde->rd",
            moved[stream],
            projection_full[1 + stream],
            preferred_element_type=jnp.float32,
        )
        for stream in range(2)
    ]
    first_grad = [second_back[stream][0] + back[stream] for stream in range(2)]
    first_back = [
        norm_back(first_grad[stream], first[stream][1], first[stream][2], norm_gain[0])
        for stream in range(2)
    ]
    sent = gather_grads(
        first_back[0][0].astype(jnp.bfloat16), first_back[1][0].astype(jnp.bfloat16)
    )
    cross_out = jnp.einsum(
        "re,rd->ed", cross_context[0], sent[0], preferred_element_type=jnp.float32
    ) + jnp.einsum("re,rd->ed", cross_context[1], sent[1], preferred_element_type=jnp.float32)
    triples = [[None, None, None], [None, None, None]]
    for stream in range(2):
        other = 1 - stream
        context_grad = jnp.einsum(
            "rd,ed->re", sent[stream], out_weight[0], preferred_element_type=jnp.float32
        ).astype(jnp.bfloat16)
        grads = attend_back(
            cross_parts[stream][0],
            cross_parts[other][1],
            cross_parts[other][2],
            valid[other],
            cross_total[stream],
            context_grad,
        )
        triples[stream][0] = grads[0]
        triples[other][1] = grads[1]
        triples[other][2] = grads[2]
    results = [
        project_back(cross_rows[stream], triples[stream][0], triples[stream][1], triples[stream][2])
        for stream in range(2)
    ]
    cross_weight = results[0][0] + results[1][0]
    cross_bias = results[0][1] + results[1][1]
    moved = grads_of(results[0][2], results[1][2])
    back = [
        jnp.einsum(
            "jre,jde->rd", moved[stream], projection_full[0], preferred_element_type=jnp.float32
        )
        for stream in range(2)
    ]
    language_grad = first_back[0][0] + back[0]
    vision_grad = first_back[1][0] + back[1]
    projection_stack = jnp.stack([cross_weight, self_weight[0], self_weight[1]])
    output_stack = jnp.stack([cross_out, self_out[0], self_out[1]])
    projection_grad, output_weight_grad, expand_grad, contract_grad = (
        lax.psum_scatter(projection_stack, "dp", scatter_dimension=2, tiled=True),
        lax.psum_scatter(output_stack, "dp", scatter_dimension=2, tiled=True),
        lax.psum_scatter(jnp.stack(expand_local), "dp", scatter_dimension=1, tiled=True),
        lax.psum_scatter(jnp.stack(contract_local), "dp", scatter_dimension=2, tiled=True),
    )
    query_value_grad, expand_bias_grad = lax.psum(
        (jnp.stack([cross_bias, self_bias[0], self_bias[1]]), jnp.stack(expand_bias_local)), "dp"
    )
    output_bias_local = jnp.stack(
        [
            jnp.sum(first_back[0][0], 0) + jnp.sum(first_back[1][0], 0),
            jnp.sum(second_back[0][0], 0),
            jnp.sum(second_back[1][0], 0),
        ]
    )
    contract_bias_local = jnp.stack([jnp.sum(third_back[0][0], 0), jnp.sum(third_back[1][0], 0)])
    gain_local = jnp.stack(
        [
            first_back[0][1] + first_back[1][1],
            second_back[0][1],
            second_back[1][1],
            third_back[0][1],
            third_back[1][1],
        ]
    )
    shift_local = jnp.stack(
        [
            first_back[0][2] + first_back[1][2],
            second_back[0][2],
            second_back[1][2],
            third_back[0][2],
            third_back[1][2],
        ]
    )
    output_bias_grad, contract_bias_grad, norm_gain_grad, norm_bias_grad = lax.psum(
        (output_bias_local, contract_bias_local, gain_local, shift_local), ("dp", "mp")
    )
    return (
        language_out,
        vision_out,
        language_grad,
        vision_grad,
        projection_grad,
        query_value_grad,
        output_weight_grad,
        output_bias_grad,
        expand_grad,
        expand_bias_grad,
        contract_grad,
        contract_bias_grad,
        norm_gain_grad,
        norm_bias_grad,
    )


MESH = pl.DeviceIdType.MESH
BF = jnp.bfloat16
F32 = jnp.float32
SLOTS = 4
RL = SLOTS * WORDS
REGION_PAD = 40
RV = SLOTS * REGION_PAD
ROWS = RL + RV
SHARE = 96
HALF_PAIR = 2 * SHARE
LANG_HEAD = 16
VIS_HEAD = 32
LANG_TAIL = 32
VIS_TAIL = 64
N_AR = 48
NT = 3
TILE = 256
LANG = (0, RL)
V1 = (RL, RL + RV // 2)
V2 = (RL + RV // 2, ROWS)
VIS = (RL, ROWS)
BOTH = (0, ROWS)
CHAINS = (V1, V2, LANG)
SELF = {LANG: 1, V1: 2, V2: 2}
EXPAND = {LANG: 3, V1: 4, V2: 4}
CONTRACT = {LANG: 5, V1: 6, V2: 6}
PARTS = {w: (w, slice(0, 768)) for w in range(1, 7)} | {0: (0, slice(0, 384)), 7: (0, slice(384, 768))}
VMEM_LIMIT = 63 * 1024 * 1024


def dot_nn(left, right):
    return lax.dot_general(left, right, (((1,), (0,)), ((), ())), preferred_element_type=F32)


def dot_nt(left, right):
    return lax.dot_general(left, right, (((1,), (1,)), ((), ())), preferred_element_type=F32)


def dot_tn(left, right):
    return lax.dot_general(left, right, (((0,), (0,)), ((), ())), preferred_element_type=F32)


def head_mask(first_lane, dtype):
    lane = lax.broadcasted_iota(jnp.int32, (1, TILE), 1) - first_lane
    return [
        jnp.where((lane >= 64 * h) & (lane < 64 * h + 64), 1.0, 0.0).astype(dtype) for h in range(3)
    ]


def item_rows(shape, dim, first, size, pad):
    row = lax.broadcasted_iota(jnp.int32, shape, dim) + first
    item = sum(jnp.where(row >= pad * j, 1, 0) for j in range(1, SLOTS))
    return row - (pad - size) * item, row - pad * item < size


def rows_into_slab(shape, shift, count, size, pad):
    place, real = item_rows(shape, 0, 0, size, pad)
    column = lax.broadcasted_iota(jnp.int32, shape, 1)
    return jnp.where((column - place == shift) & real & (place < count), 1.0, 0.0)


def rows_from_slab(shape, shift, first, low, high, size, pad):
    place, real = item_rows(shape, 1, first, size, pad)
    row = lax.broadcasted_iota(jnp.int32, shape, 0)
    return jnp.where((place - row == shift) & real & (row >= low) & (row < high), 1.0, 0.0)


def layer_kernel(
    total_items,
    lang,
    vis,
    lcot,
    vcot,
    lengths,
    regions,
    flags,
    projection,
    query_value,
    out_weight,
    expand,
    expand_b,
    contract,
    out_bias,
    contract_b,
    gains,
    shifts,
    lang_out,
    vis_out,
    lang_grad,
    vis_grad,
    wgrad,
    vec_out,
    qb_out,
    W,
    G,
    RD,
    RX,
    R2,
    A,
    KV,
    RSB,
    STG,
    QVK,
    D,
    C,
    H,
    GP,
    PCL,
    PCV,
    PS,
    PART,
    PZ,
    NORM,
    RSTD,
    DZ,
    COT,
    SH,
    FLAG,
    QO,
    QB,
    QR,
    CA,
    CR,
    VG,
    QG,
    AVA,
    AVR,
    HL,
    HV,
    OUTS,
    TLO,
    TVO,
    TLG,
    TVG,
    ssem,
    rsem,
    wsem,
    wsem_z,
    gsem,
    gsem2,
):
    d = lax.axis_index("dp")
    z = lax.axis_index("mp")
    c = d % 2
    k = d // 2
    k_flip = [k + 1 - 2 * (k % 2), (k + 2) % 4, 3 - k]
    sib = (d + 1 - 2 * c, z)
    zp = (d, z + 1 - 2 * (z % 2))
    z2 = (z + 2) % 4
    up = (d, (z + 1) % 4)
    down = (d, (z + 3) % 4)
    plane = [(2 * kf + c, z) for kf in k_flip]
    far = (2 * k + 1, z2)

    pending = []
    counter = [0, 0]

    def remote(src, dst, send, recv, device):
        return pltpu.make_async_remote_copy(
            src_ref=src, dst_ref=dst, send_sem=send, recv_sem=recv, device_id=device, device_id_type=MESH
        )

    def send(src, dst, device, recv=None, keep=True):
        slot = counter[0]
        counter[0] += 1
        if recv is None:
            recv = rsem.at[counter[1]]
            counter[1] += 1
        copy = remote(src, dst, ssem.at[slot], recv, device)
        copy.start()
        if keep:
            pending.append(copy)
        return copy

    def wait_bytes(ref, sem):
        pltpu.make_async_copy(ref, ref, sem).wait()

    def arrived(name, *copies):
        with jax.named_scope("wait_" + name):
            for copy in copies:
                copy.wait_recv()

    barrier = pltpu.get_barrier_semaphore()
    peers = [sib, up, down, (d, z2), (d + 1 - 2 * c, z2)] + plane
    for peer in peers:
        pl.semaphore_signal(barrier, inc=1, device_id=peer, device_id_type=MESH)

    def weight_first(part):
        w, lanes = PARTS[part]
        row = pl.ds(pl.multiple_of(d * SHARE, 16), SHARE)
        slot = counter[0]
        counter[0] += 1
        share = SH.at[w] if w < 3 else (expand.at[w - 3] if w < 5 else contract.at[w - 5])
        share = share.at[:, lanes]
        target = W.at[w, row, lanes]
        near = remote(share, target, ssem.at[slot], wsem_z.at[part], sib)
        own = pltpu.make_async_copy(share, target, wsem_z.at[part])

        @pl.when(c == 1)
        def _():
            near.start()

        @pl.when(c == 0)
        def _():
            own.start()

        send(share, target, far, wsem_z.at[part])
        nears.append(near)

    def place(width, first):
        row = lax.broadcasted_iota(jnp.int32, (width, D_MODEL), 0)
        column = lax.broadcasted_iota(jnp.int32, (width, D_MODEL), 1)
        return jnp.where(column - row == first, 1.0, 0.0).astype(BF)

    def attention_share(b):
        SH[b] = (
            dot_nn(projection[b, 0], place(HALF_PAIR, 0))
            + dot_nn(projection[b, 2], place(HALF_PAIR, HALF_PAIR))
            + dot_nn(projection[b, 1], place(HALF_PAIR, 2 * HALF_PAIR))
            + dot_tn(out_weight[b], place(HALF_PAIR, 3 * HALF_PAIR))
        ).astype(BF)

    nears = []
    attention_share(0)

    n_items = lengths.shape[0]
    first_item = 3 * z + jnp.minimum(z, 1)
    KV[0] = jnp.full(KV.shape[1:], -1.0, F32)
    for row, source, size, pad, first_row in ((0, lengths, WORDS, WORDS, 0), (1, regions, REGIONS, REGION_PAD, RL)):
        lane = lax.broadcasted_iota(jnp.int32, (1, TILE), 1)
        owner = jnp.full((1, TILE), -1.0, F32)
        slab_row = lax.broadcasted_iota(jnp.int32, (SLOTS * pad, 1), 0)
        flag = jnp.zeros((SLOTS * pad, 1), F32)
        for j in range(SLOTS):
            item = jnp.minimum(first_item + j, n_items - 1)
            valid = (lane >= j * pad) & (lane < j * pad + source[item]) & (lane < j * pad + size)
            owner = jnp.where(valid, float(j), owner)
            inside = (slab_row >= j * pad) & (slab_row < (j + 1) * pad)
            flag = jnp.where(inside, flags[row, item].astype(F32), flag)
            if row == 1 and j % 2 == 1:
                pair = jnp.full((1, TILE), -1.0, F32)
                for i in (0, 1):
                    other = jnp.minimum(first_item + j - 1 + i, n_items - 1)
                    valid = (lane >= i * pad) & (lane < i * pad + source[other]) & (lane < i * pad + size)
                    pair = jnp.where(valid, float(j - 1 + i), pair)
                KV[0, 2 + j // 2 : 3 + j // 2] = pair
        KV[0, row : row + 1] = owner
        FLAG[first_row : first_row + SLOTS * pad] = flag
        count = flags[row, 0]
        for j in range(1, n_items):
            count = count + flags[row, j]
        CA[0, row : row + 1] = jnp.full((1, 128), count.astype(F32), F32)
    QO[...] = jnp.zeros_like(QO)
    for b in range(3):
        QO[b : b + 1, 0:HALF_PAIR] = query_value[b, 0:1]
        QO[b : b + 1, HALF_PAIR : 2 * HALF_PAIR] = query_value[b, 1:2]
    QO[3:5] = expand_b[...]

    pl.semaphore_wait(barrier, len(peers))
    heads = [
        send(lang.at[pl.ds(0, LANG_HEAD)], HL.at[0], down),
        send(vis.at[pl.ds(0, VIS_HEAD)], HV.at[0], down),
    ]
    weight_first(0)
    weight_first(7)
    heads_cot = [
        send(lcot.at[pl.ds(0, LANG_HEAD)], HL.at[1], down),
        send(vcot.at[pl.ds(0, VIS_HEAD)], HV.at[1], down),
    ]
    kv_sib = send(KV.at[0], KV.at[1], sib)
    kv_zp = send(KV.at[0], KV.at[2], zp)
    count_copies = [send(CA.at[0], CR.at[0], sib)]
    bias_swap = send(QO, QR, (d, z2))

    pair_rows = pl.ds(pl.multiple_of(k * HALF_PAIR, 16), HALF_PAIR)

    def rows_of_chip(chip, first=0, count=HALF_PAIR):
        return pl.ds(pl.multiple_of(chip * HALF_PAIR + first, 16), count)

    def weight_second(part):
        w, lanes = PARTS[part]
        block = W.at[w, pair_rows, lanes]
        wait_bytes(block, wsem_z.at[part])
        for j in range(2):
            send(block, block, plane[j], wsem.at[j, part])

    def weight_third(part):
        w, lanes = PARTS[part]
        for j in range(2):
            wait_bytes(W.at[w, pair_rows, lanes], wsem.at[j, part])
            half = W.at[w, rows_of_chip(k_flip[j], j * SHARE, SHARE), lanes]
            send(half, half, plane[1 - j], wsem.at[2, part])

    def weight_ready(part):
        w, lanes = PARTS[part]
        wait_bytes(W.at[w, pair_rows, lanes], wsem.at[2, part])

    off_l = jnp.where(z == 0, 0, 20 - 5 * z)
    off_v = jnp.where(z == 0, 0, 36 - 9 * z)
    n_l = jnp.where(z == 0, 4 * WORDS, 3 * WORDS)
    n_v = jnp.where(z == 0, 4 * REGIONS, 3 * REGIONS)
    own_l = lang.shape[0]
    own_v = vis.shape[0]
    def gather_start(p, stream):
        rows = pl.ds(stream[0], stream[1] - stream[0])
        return (
            p,
            rows,
            send(A.at[p, 0, rows], A.at[p, 1, rows], sib),
            send(A.at[p, 0, rows], A.at[p, 2, rows], zp),
        )

    def gather_forward(handle):
        p, rows, _, across = handle
        arrived("rows_z", across)
        return send(A.at[p, 2, rows], A.at[p, 3, rows], sib)

    def own_slab(index, source_l, source_v, copies, target):
        arrived("heads", *copies)
        for (r0, r1), size, pad, own, off, count, source, head, head_rows in (
            (VIS, REGIONS, REGION_PAD, own_v, off_v, n_v, source_v, HV, VIS_HEAD),
            (LANG, WORDS, WORDS, own_l, off_l, n_l, source_l, HL, LANG_HEAD),
        ):
            inside = rows_into_slab((r1 - r0, own), off, count, size, pad).astype(BF)
            beyond = rows_into_slab((r1 - r0, head_rows), off - own, count, size, pad).astype(BF)
            target[r0:r1] = (dot_nn(inside, source[...]) + dot_nn(beyond, head[index])).astype(BF)

    own_slab(0, lang, vis, heads, A.at[0, 0])
    rows_x = {stream: gather_start(0, stream) for stream in (VIS, LANG)}

    stage_used = {}

    def stage_free(index, stream):
        copy = stage_used.pop((index, stream), None)
        if copy is not None:
            copy.wait_send()

    def partial_nt(lhs_ref, stream, w, lanes):
        r0, r1 = stream
        rows = r1 - r0
        stage_free(0, stream)
        stage_free(1, stream)
        for n in range(NT):
            column = slice(n * TILE, (n + 1) * TILE)
            lhs = lhs_ref[:, r0:r1, :]
            lhs = lhs.reshape(SLOTS * rows, lhs.shape[-1])
            out = dot_nt(lhs, W[w, column, lanes])
            PART[r0:r1, column] = out[:rows]
            STG[0, r0:r1, column] = out[rows : 2 * rows].astype(BF)
            PZ[r0:r1, column] = out[2 * rows : 3 * rows]
            STG[1, r0:r1, column] = out[3 * rows :].astype(BF)

    def stage_send(index, stream, device):
        rows = pl.ds(stream[0], stream[1] - stream[0])
        copy = send(STG.at[index, rows], RSB.at[index, rows], device, keep=False)
        stage_used[index, stream] = copy
        return copy

    def sums_near(stream):
        return stage_send(0, stream, sib)

    def sums_far(stream):
        return stage_send(1, stream, sib)

    def sums_z(stream, far):
        r0, r1 = stream
        arrived("sums_core", far)
        stage_free(2, stream)
        STG[2, r0:r1] = (PZ[r0:r1] + RSB[1, r0:r1].astype(F32)).astype(BF)
        return stage_send(2, stream, zp)

    def reduced(stream, *copies):
        r0, r1 = stream
        arrived("sums", *copies)
        return PART[r0:r1] + RSB[0, r0:r1].astype(F32) + RSB[2, r0:r1].astype(F32)

    mask_q = head_mask(0, BF)
    mask_c = head_mask(64, BF)
    mask_q32 = head_mask(0, F32)
    mask_c32 = head_mask(64, F32)
    factor = 1.0 / math.sqrt(D_HEAD)

    def attend_slab(QV, Cb, crossed, stream, s):
        def one(queries, keys_rows, kv_row, item_size, first_item_of, P):
            (q0, q1), (k0, k1) = queries, keys_rows
            nq, nk = q1 - q0, k1 - k0
            query = QV[s, q0:q1, 0:256]
            keys = QV[s, k0:k1, 384:640]
            values = QV[s, k0:k1, 128:384]
            spread = jnp.concatenate([query * mask_q[h] for h in range(3)], 0)
            scores = dot_nt(spread, keys) * factor
            row = lax.broadcasted_iota(jnp.int32, (nq, nk), 0)
            item = jnp.full((nq, nk), float(first_item_of), F32)
            for j in range(1, nq // item_size):
                item = item + jnp.where(row >= j * item_size, 1.0, 0.0)
            same = item == KV[s, kv_row : kv_row + 1, 0:nk]
            scores = jnp.where(same[None], scores.reshape(3, nq, nk), MASKED)
            raised = jnp.exp(scores - jnp.max(scores, -1, keepdims=True))
            weights = (raised / jnp.sum(raised, -1, keepdims=True)).astype(BF).reshape(3 * nq, nk)
            P[s] = weights
            context = dot_nn(weights, values).reshape(3, nq, TILE)
            Cb[s, q0:q1] = (
                context[0] * mask_c32[0] + context[1] * mask_c32[1] + context[2] * mask_c32[2]
            ).astype(BF)

        if stream == LANG:
            if crossed:
                one(LANG, VIS, 1, WORDS, 0, PCL)
            else:
                one(LANG, LANG, 0, WORDS, 0, PS.at[0])
        else:
            half = (V1, V2).index(stream)
            if crossed:
                one(stream, LANG, 0, REGION_PAD, 2 * half, PCV.at[half])
            else:
                one(stream, stream, 2 + half, REGION_PAD, 2 * half, PS.at[1 + half])

    def attend_back_slab(QV, crossed, stream, s):
        def one(queries, keys_rows, P):
            (q0, q1), (k0, k1) = queries, keys_rows
            nq = q1 - q0
            query = QV[s, q0:q1, 0:256]
            keys = QV[s, k0:k1, 384:640]
            values = QV[s, k0:k1, 128:384]
            spread = jnp.concatenate([query * mask_q[h] for h in range(3)], 0)
            upstream = D[s, q0:q1, 512:768]
            up_spread = jnp.concatenate([upstream * mask_c[h] for h in range(3)], 0)
            weights = P[s]
            weights32 = weights.astype(F32)
            weight_grad = dot_nt(up_spread, values)
            score_grad = (
                weights32
                * (weight_grad - jnp.sum(weight_grad * weights32, -1, keepdims=True))
            ).astype(BF)
            dq = dot_nn(score_grad, keys).reshape(3, nq, TILE)
            dq = (dq[0] * mask_q32[0] + dq[1] * mask_q32[1] + dq[2] * mask_q32[2]) * factor
            dk = dot_tn(score_grad, spread) * factor
            dv = dot_tn(weights, up_spread)
            return dq, dk, dv

        if crossed:
            half = RV // 2
            dq_l, dk_v, dv_v = one(LANG, VIS, PCL)
            dq_1, dk_1, dv_1 = one(V1, LANG, PCV.at[0])
            dq_2, dk_2, dv_2 = one(V2, LANG, PCV.at[1])
            results = {
                LANG: (dq_l, dk_1 + dk_2, dv_1 + dv_2),
                V1: (dq_1, dk_v[:half], dv_v[:half]),
                V2: (dq_2, dk_v[half:], dv_v[half:]),
            }
        else:
            results = {stream: one(stream, stream, PS.at[0 if stream == LANG else 1 + (V1, V2).index(stream)])}
        for (r0, r1), (dq, dk, dv) in results.items():
            D[s, r0:r1, 0:128] = dq[:, :128].astype(BF)
            D[s, r0:r1, 128:256] = (dq[:, 128:] + dv[:, :128]).astype(BF)
            D[s, r0:r1, 256:384] = dv[:, 128:].astype(BF)
            D[s, r0:r1, 384:640] = dk.astype(BF)
            D[s, r0:r1, 640:768] = jnp.zeros((r1 - r0, 128), BF)

    def forward_norm(value, index, gain_row, r0, r1):
        center = value - jnp.mean(value, -1, keepdims=True)
        scaled = lax.rsqrt(jnp.mean(center * center, -1, keepdims=True) + EPSILON)
        normed = center * scaled
        NORM[index, r0:r1] = normed
        RSTD[index, r0:r1] = scaled
        return normed * gains[gain_row : gain_row + 1] + shifts[gain_row : gain_row + 1]

    def backward_norm(upstream, index, gain_row, bias_row, r0, r1):
        normed = NORM[index, r0:r1]
        through = upstream * gains[gain_row : gain_row + 1]
        inner = (
            through
            - jnp.mean(through, -1, keepdims=True)
            - normed * jnp.mean(through * normed, -1, keepdims=True)
        )
        result = RSTD[index, r0:r1] * inner
        VG[5 + gain_row : 6 + gain_row] += jnp.sum(upstream * normed, 0, keepdims=True)
        VG[10 + gain_row : 11 + gain_row] += jnp.sum(upstream, 0, keepdims=True)
        VG[bias_row : bias_row + 1] += jnp.sum(result, 0, keepdims=True)
        return result

    def rows_of(p, stream):
        r0, r1 = stream
        return A[p, :, r0:r1, :].reshape(SLOTS * (r1 - r0), D_MODEL)

    def tile_columns():
        return [slice(n * TILE, (n + 1) * TILE) for n in range(NT)]

    def project(stream, w):
        r0, r1 = stream
        for column in tile_columns():
            mapped = dot_nn(rows_of(1, stream), W[w, :, column]) + QB[w : w + 1, column]
            QVK[1, :, r0:r1, column] = mapped.astype(BF).reshape(SLOTS, r1 - r0, TILE)

    def project_cross(g):
        for column in tile_columns():
            rows = A[0, 2 * g : 2 * g + 2].reshape(2 * ROWS, D_MODEL)
            mapped = dot_nn(rows, W[0, :, column]) + QB[0:1, column]
            QVK[0, 2 * g : 2 * g + 2, :, column] = mapped.astype(BF).reshape(2, ROWS, TILE)

    def attend(stream, b):
        for s in range(SLOTS):
            attend_slab(QVK.at[b], C.at[b], b == 0, stream, s)

    def expand_rows(stream):
        r0, r1 = stream
        w = EXPAND[stream]
        for column in tile_columns():
            before = dot_nn(rows_of(2, stream), W[w, :, column]) + QB[w : w + 1, column]
            half = 0.5 * (1.0 + lax.erf(before * math.sqrt(0.5)))
            slope = half + before * jnp.exp(-0.5 * before * before) * (1.0 / math.sqrt(2.0 * math.pi))
            H[:, r0:r1, column] = (before * half).astype(BF).reshape(SLOTS, r1 - r0, TILE)
            GP[:, r0:r1, column] = slope.astype(BF).reshape(SLOTS, r1 - r0, TILE)

    def hidden_gradient(stream):
        r0, r1 = stream
        rows = SLOTS * (r1 - r0)
        for column in tile_columns():
            up_hidden = dot_nn(rows_of(3, stream), W[CONTRACT[stream], :, column])
            slope = GP[:, r0:r1, column].reshape(rows, TILE)
            D[:, r0:r1, column] = (up_hidden * slope.astype(F32)).astype(BF).reshape(SLOTS, r1 - r0, TILE)

    def context_gradient(p, stream, w):
        r0, r1 = stream
        upstream = dot_nn(rows_of(p, stream), W[w, :, 512:768])
        D[:, r0:r1, 512:768] = upstream.astype(BF).reshape(SLOTS, r1 - r0, TILE)

    def attend_gradient(stream, b):
        for s in range(SLOTS):
            attend_back_slab(QVK.at[b], b == 0, stream, s)

    def all_rows(ref, r0, r1, lanes):
        value = ref[:, r0:r1, lanes]
        return value.reshape(SLOTS * (r1 - r0), value.shape[-1])

    def weight_grad(w, lhs_p, rhs_ref, r0, r1, lanes=slice(0, 768)):
        for m in range(NT):
            column = slice(m * TILE, (m + 1) * TILE)
            left = all_rows(A.at[lhs_p], r0, r1, column)
            G[w, column, lanes] = dot_tn(left, all_rows(rhs_ref, r0, r1, lanes)).astype(BF)

    def attention_weight_grad(w, x_p, b_p, Cb, r0, r1, middle=None):
        if middle is None:
            weight_grad(w, x_p, D, r0, r1, slice(0, 512))
        else:
            weight_grad(w, x_p, D, r0, r1, slice(0, 384))
            middle()
            weight_grad(w, x_p, D, r0, r1, slice(384, 512))
        for m in range(NT):
            column = slice(m * TILE, (m + 1) * TILE)
            G[w, column, 512:768] = (
                dot_tn(all_rows(A.at[x_p], r0, r1, column), all_rows(D, r0, r1, slice(512, 768)))
                + dot_tn(all_rows(A.at[b_p], r0, r1, column), all_rows(Cb, r0, r1, slice(0, 256)))
            ).astype(BF)

    def bias_grad(row, r0, r1):
        total = jnp.zeros((1, D_MODEL), F32)
        for s in range(SLOTS):
            total = total + jnp.sum(D[s, r0:r1].astype(F32), 0, keepdims=True)
        QG[row : row + 1] = total

    def grad_first(part):
        w, lanes = PARTS[part]
        for j in range(2):
            half = rows_of_chip(k_flip[2], (1 - j) * SHARE, SHARE)
            send(G.at[w, half, lanes], RD.at[j, w, :, lanes], plane[j], gsem.at[2, part])

    def grad_second(part):
        w, lanes = PARTS[part]
        wait_bytes(RD.at[:, w, :, lanes], gsem.at[2, part])
        for j in range(2):
            half = rows_of_chip(k_flip[1 - j], (1 - j) * SHARE, SHARE)
            G[w, half, lanes] = (G[w, half, lanes].astype(F32) + RD[j, w, :, lanes].astype(F32)).astype(BF)
        for j in range(2):
            send(G.at[w, rows_of_chip(k_flip[j]), lanes], RX.at[j, w, :, lanes], plane[j], gsem.at[j, part])

    grad_nears = []

    def grad_third(part):
        w, lanes = PARTS[part]
        for j in range(2):
            wait_bytes(RX.at[j, w, :, lanes], gsem.at[j, part])
        total = G[w, pair_rows, lanes].astype(F32)
        total = total + RX[0, w, :, lanes].astype(F32) + RX[1, w, :, lanes].astype(F32)
        G[w, pair_rows, lanes] = total.astype(BF)
        low = G.at[w, rows_of_chip(k, 0, SHARE), lanes]
        high = G.at[w, rows_of_chip(k, SHARE, SHARE), lanes]
        slot = counter[0]
        counter[0] += 2
        here, there = R2.at[0, w, :, lanes], R2.at[1, w, :, lanes]
        own = pltpu.make_async_copy(low, here, gsem2.at[part])
        near = remote(high, here, ssem.at[slot], gsem2.at[part], sib)
        far_low = remote(low, there, ssem.at[slot], gsem2.at[part], (2 * k, z2))
        far_high = remote(high, there, ssem.at[slot + 1], gsem2.at[part], (2 * k + 1, z2))

        @pl.when(c == 0)
        def _():
            own.start()
            near.start()

        @pl.when(c == 1)
        def _():
            far_low.start()
            far_high.start()

        grad_nears.append((near, far_low, far_high))

    def grad_last(part):
        w, lanes = PARTS[part]
        wait_bytes(R2.at[:, w, :, lanes], gsem2.at[part])
        wgrad[w, :, lanes] = R2[0, w, :, lanes].astype(F32) + R2[1, w, :, lanes].astype(F32)

    def count_step(stage, peer):
        count_copies[stage].wait_recv()
        CA[stage + 1] = CA[stage] + CR[stage]
        if peer is not None:
            count_copies.append(send(CA.at[stage + 1], CR.at[stage + 1], peer))

    VG[...] = jnp.zeros_like(VG)
    QG[...] = jnp.zeros_like(QG)
    weight_second(0)
    attention_share(2)
    weight_second(7)
    weight_first(2)
    attention_share(1)
    own_slab(1, lcot, vcot, heads_cot, COT)
    weight_third(0)
    weight_first(1)
    kv_sib.wait_recv()
    kv_zp.wait_recv()
    kv_far = send(KV.at[2], KV.at[3], sib)
    far_x = {stream: gather_forward(rows_x[stream]) for stream in (VIS, LANG)}
    bias_swap.wait_recv()
    QB[...] = jnp.where(c == 1, QR[...], QO[...])
    weight_third(7)
    kv_far.wait_recv()
    arrived("rows", rows_x[VIS][2], rows_x[LANG][2], far_x[VIS], far_x[LANG])
    weight_second(2)
    weight_first(4)
    weight_second(1)
    weight_first(6)
    weight_ready(0)
    weight_ready(7)

    near, far_sum, z_sum, rows, far_rows = {}, {}, {}, {}, {}
    out_lanes, all_lanes = slice(512, 768), slice(0, 768)

    def sums_after(stream, lhs, w, lanes):
        partial_nt(lhs, stream, w, lanes)
        far_sum[stream] = sums_far(stream)
        near[stream] = sums_near(stream)

    def sums_on(stream):
        z_sum[stream] = sums_z(stream, far_sum[stream])

    def total_of(stream):
        return reduced(stream, near[stream], z_sum[stream])

    def all_arrived(stream):
        arrived("rows", rows[stream][2], far_rows[stream])

    def pass_on(stream):
        far_rows[stream] = gather_forward(rows[stream])

    project_cross(0)
    project_cross(1)
    weight_third(2)
    attend(V1, 0)
    sums_after(V1, C.at[0], 0, out_lanes)
    weight_second(4)
    attend(V2, 0)
    sums_after(V2, C.at[0], 0, out_lanes)
    sums_on(V1)
    weight_third(1)
    weight_first(3)
    attend(LANG, 0)
    sums_after(LANG, C.at[0], 0, out_lanes)
    sums_on(V2)
    weight_second(6)
    weight_first(5)
    sums_on(LANG)
    count_step(0, plane[0])
    weight_third(4)

    def first_norm(stream):
        r0, r1 = stream
        value = total_of(stream) + out_bias[0:1] + A[0, 0, r0:r1].astype(F32)
        A[1, 0, r0:r1] = forward_norm(value, 0, 0, r0, r1).astype(BF)
        rows[stream] = gather_start(1, stream)

    first_norm(V1)
    first_norm(V2)
    first_norm(LANG)

    def self_rows(stream, passed):
        w = SELF[stream]
        all_arrived(stream)
        project(stream, w)
        if passed is not None:
            pass_on(passed)
        attend(stream, 1)
        sums_after(stream, C.at[1], w, out_lanes)

    weight_third(6)
    weight_ready(2)
    pass_on(V1)
    self_rows(V1, V2)
    weight_second(3)
    self_rows(V2, LANG)
    sums_on(V1)
    weight_ready(1)
    self_rows(LANG, None)
    sums_on(V2)
    weight_second(5)
    weight_third(3)

    def second_norm(stream):
        r0, r1 = stream
        n = 1 if stream == LANG else 2
        value = total_of(stream) + out_bias[n : n + 1] + A[1, 0, r0:r1].astype(F32)
        A[2, 0, r0:r1] = forward_norm(value, 1, n, r0, r1).astype(BF)
        rows[stream] = gather_start(2, stream)

    second_norm(V1)
    sums_on(LANG)
    count_step(1, plane[1])
    second_norm(V2)
    pass_on(V1)
    weight_third(5)
    second_norm(LANG)

    def feed_rows(stream, passed, before_expand, before_contract):
        all_arrived(stream)
        weight_ready(before_expand) if before_expand is not None else None
        expand_rows(stream)
        if passed is not None:
            pass_on(passed)
        weight_ready(before_contract) if before_contract is not None else None
        sums_after(stream, H, CONTRACT[stream], all_lanes)

    feed_rows(V1, V2, 4, 6)
    feed_rows(V2, LANG, None, None)
    sums_on(V1)
    count_step(2, None)
    feed_rows(LANG, None, 3, 5)
    sums_on(V2)

    def last_norm(stream):
        r0, r1 = stream
        n = 0 if stream == LANG else 1
        value = total_of(stream) + contract_b[n : n + 1] + A[2, 0, r0:r1].astype(F32)
        OUTS[r0:r1] = forward_norm(value, 2, 3 + n, r0, r1).astype(BF)
        scale = total_items / CA[3, n : n + 1, 0:1]
        upstream = COT[r0:r1].astype(F32) * (FLAG[r0:r1] * scale)
        result = backward_norm(upstream, 2, 3 + n, 3 + n, r0, r1)
        DZ[r0:r1] = result
        A[3, 0, r0:r1] = result.astype(BF)
        rows[stream] = gather_start(3, stream)

    last_norm(V1)
    sums_on(LANG)
    last_norm(V2)
    pass_on(V1)
    last_norm(LANG)

    def feed_gradient(stream, passed):
        all_arrived(stream)
        hidden_gradient(stream)
        if passed is not None:
            pass_on(passed)
        sums_after(stream, D, EXPAND[stream], all_lanes)

    feed_gradient(V1, V2)
    feed_gradient(V2, LANG)
    sums_on(V1)
    weight_grad(6, 3, H, *VIS)
    grad_first(6)
    feed_gradient(LANG, None)
    sums_on(V2)
    weight_grad(4, 2, D, *VIS)
    grad_first(4)

    def second_norm_back(stream):
        r0, r1 = stream
        n = 1 if stream == LANG else 2
        result = backward_norm(DZ[r0:r1] + total_of(stream), 1, n, n, r0, r1)
        DZ[r0:r1] = result
        A[4, 0, r0:r1] = result.astype(BF)
        rows[stream] = gather_start(4, stream)

    second_norm_back(V1)
    sums_on(LANG)
    second_norm_back(V2)
    weight_grad(5, 3, H, *LANG)
    grad_first(5)
    pass_on(V1)
    grad_second(6)
    weight_grad(3, 2, D, *LANG)
    grad_first(3)
    second_norm_back(LANG)
    bias_grad(4, *VIS)
    bias_grad(3, *LANG)
    tail_out = [
        send(OUTS.at[pl.ds(RL - LANG_TAIL, LANG_TAIL)], TLO, up),
        send(OUTS.at[pl.ds(ROWS - VIS_TAIL, VIS_TAIL)], TVO, up),
    ]

    def self_gradient(stream, passed):
        w = SELF[stream]
        all_arrived(stream)
        context_gradient(4, stream, w)
        if passed is not None:
            pass_on(passed)
        attend_gradient(stream, 1)
        sums_after(stream, D, w, all_lanes)

    self_gradient(V1, V2)
    grad_second(4)
    self_gradient(V2, LANG)
    sums_on(V1)
    grad_third(6)
    grad_second(5)
    attention_weight_grad(2, 1, 4, C.at[1], *VIS)
    grad_first(2)
    self_gradient(LANG, None)
    sums_on(V2)
    grad_second(3)

    def first_norm_back(stream):
        r0, r1 = stream
        result = backward_norm(DZ[r0:r1] + total_of(stream), 0, 0, 0, r0, r1)
        DZ[r0:r1] = result
        A[5, 0, r0:r1] = result.astype(BF)
        rows[stream] = gather_start(5, stream)

    first_norm_back(V1)
    sums_on(LANG)
    grad_third(4)
    first_norm_back(V2)
    attention_weight_grad(1, 1, 4, C.at[1], *LANG)
    grad_first(1)
    pass_on(V1)
    first_norm_back(LANG)
    grad_third(5)
    grad_second(2)
    pass_on(V2)
    bias_grad(2, *VIS)
    bias_grad(1, *LANG)
    pass_on(LANG)

    for stream in CHAINS:
        all_arrived(stream)
        context_gradient(5, stream, 0)
    attend_gradient(None, 0)
    attention_weight_grad(0, 0, 5, C.at[0], *BOTH, middle=lambda: grad_first(0))
    grad_first(7)
    sums_after(V1, D, 0, all_lanes)
    grad_second(1)
    sums_after(V2, D, 0, all_lanes)
    sums_on(V1)
    grad_third(3)
    sums_after(LANG, D, 0, all_lanes)
    sums_on(V2)
    grad_second(0)
    sums_on(LANG)
    bias_grad(0, *BOTH)

    quarter = jnp.where(c == 0, z, z2)
    AVA[0, 0:16] = VG[...]
    for j in range(4):
        AVA[0, 16 + 8 * j : 24 + 8 * j] = jnp.where(quarter == j, QG[...], 0.0)
    vector_peers = [sib, plane[0], plane[1], zp, (d, z2)]
    vector_copies = [send(AVA.at[0], AVR.at[0], vector_peers[0])]

    def vector_step(stage):
        arrived("vectors", vector_copies[stage])
        AVA[stage + 1] = AVA[stage] + AVR[stage]
        if stage < 4:
            vector_copies.append(send(AVA.at[stage + 1], AVR.at[stage + 1], vector_peers[stage + 1]))

    grad_second(7)
    grad_third(2)
    vector_step(0)
    grad_third(1)
    vector_step(1)
    for w in (6, 4, 5, 3):
        grad_last(w)
    grad_third(0)
    vector_step(2)
    for stream in CHAINS:
        r0, r1 = stream
        DZ[r0:r1] = DZ[r0:r1] + total_of(stream)
    tail_grad = [
        send(DZ.at[pl.ds(RL - LANG_TAIL, LANG_TAIL)], TLG, up),
        send(DZ.at[pl.ds(ROWS - VIS_TAIL, VIS_TAIL)], TVG, up),
    ]
    grad_third(7)
    vector_step(3)
    for w in (2, 1):
        grad_last(w)
    vector_step(4)
    vec_out[...] = AVA[5, 0:16]
    qb_out[...] = AVA[5, pl.ds(pl.multiple_of(16 + 8 * z, 8), 8)]

    arrived("tails", *tail_out, *tail_grad)
    before_l = jnp.where(z == 1, 0, 25 - 5 * z)
    before_v = jnp.where(z == 1, 0, 45 - 9 * z)
    for (r0, r1), size, pad, own_rows, off, before, tail_rows, out_ref, grad_ref, t_out, t_grad in (
        (LANG, WORDS, WORDS, own_l, off_l, before_l, LANG_TAIL, lang_out, lang_grad, TLO, TLG),
        (VIS, REGIONS, REGION_PAD, own_v, off_v, before_v, VIS_TAIL, vis_out, vis_grad, TVO, TVG),
    ):
        from_own = rows_from_slab((own_rows, r1 - r0), -off, 0, off, own_rows, size, pad)
        from_tail = rows_from_slab(
            (own_rows, tail_rows), own_rows - before, r1 - r0 - tail_rows, 0, off, size, pad
        )
        out_ref[...] = (
            dot_nn(from_own.astype(BF), OUTS[r0:r1]) + dot_nn(from_tail.astype(BF), t_out[...])
        ).astype(BF)
        exact = lax.Precision.HIGHEST
        grad_ref[...] = jnp.dot(
            from_own, DZ[r0:r1], precision=exact, preferred_element_type=F32
        ) + jnp.dot(from_tail, t_grad[...], precision=exact, preferred_element_type=F32)

    grad_last(0)
    grad_last(7)

    for copy in pending:
        copy.wait_send()
    for index, stream in list(stage_used):
        stage_free(index, stream)

    @pl.when(c == 1)
    def _():
        for copy in nears:
            copy.wait_send()
        for _, far_low, far_high in grad_nears:
            far_low.wait_send()
            far_high.wait_send()

    @pl.when(c == 0)
    def _():
        for near, _, _ in grad_nears:
            near.wait_send()
    assert counter[0] <= ssem.shape[0] and counter[1] <= rsem.shape[0], counter


N_SEND = 240
N_RECV = 160


def fused_layer(total_items, *operands):
    own_l, own_v = operands[0].shape[0], operands[1].shape[0]
    vmem = pl.BlockSpec(memory_space=pltpu.VMEM)
    smem = pl.BlockSpec(memory_space=pltpu.SMEM)
    shapes = [
        ((own_l, D), BF),
        ((own_v, D), BF),
        ((own_l, D), F32),
        ((own_v, D), F32),
        ((7, SHARE, D), F32),
        ((16, D), F32),
        ((8, D), F32),
    ]
    scratch = [
        ((7, D, D), BF),
        ((7, D, D), BF),
        ((2, 7, SHARE, D), BF),
        ((2, 7, HALF_PAIR, D), BF),
        ((2, 7, SHARE, D), BF),
        ((6, SLOTS, ROWS, D), BF),
        ((SLOTS, 8, TILE), F32),
        ((3, ROWS, D), BF),
        ((3, ROWS, D), BF),
        ((2, SLOTS, ROWS, D), BF),
        ((SLOTS, ROWS, D), BF),
        ((2, SLOTS, ROWS, TILE), BF),
        ((SLOTS, ROWS, D), BF),
        ((SLOTS, ROWS, D), BF),
        ((SLOTS, 3 * RL, RV), BF),
        ((2, SLOTS, 3 * RL, RL), BF),
        ((3, SLOTS, 3 * RL, RL), BF),
        ((ROWS, D), F32),
        ((ROWS, D), F32),
        ((3, ROWS, D), F32),
        ((3, ROWS, 1), F32),
        ((ROWS, D), F32),
        ((ROWS, D), BF),
        ((3, SHARE, D), BF),
        ((ROWS, 1), F32),
        ((8, D), F32),
        ((8, D), F32),
        ((8, D), F32),
        ((4, 8, 128), F32),
        ((3, 8, 128), F32),
        ((16, D), F32),
        ((8, D), F32),
        ((6, N_AR, D), F32),
        ((5, N_AR, D), F32),
        ((2, LANG_HEAD, D), BF),
        ((2, VIS_HEAD, D), BF),
        ((ROWS, D), BF),
        ((LANG_TAIL, D), BF),
        ((VIS_TAIL, D), BF),
        ((LANG_TAIL, D), F32),
        ((VIS_TAIL, D), F32),
    ]
    dma = pltpu.SemaphoreType.DMA
    return pl.pallas_call(
        partial(layer_kernel, total_items),
        out_shape=[jax.ShapeDtypeStruct(s, t) for s, t in shapes],
        in_specs=[vmem] * 4 + [smem] * 3 + [vmem] * (len(operands) - 7),
        out_specs=[vmem] * len(shapes),
        scratch_shapes=[pltpu.VMEM(s, t) for s, t in scratch]
        + [dma((N_SEND,)), dma((N_RECV,)), dma((3, 8)), dma((8,)), dma((3, 8)), dma((8,))],
        compiler_params=pltpu.CompilerParams(
            collective_id=0, has_side_effects=True, vmem_limit_bytes=VMEM_LIMIT
        ),
    )(*operands)


def unpack_kernel(lo, vo, lg, vg, wgrad, vec, qb, *outs):
    (lo_out, vo_out, lg_out, vg_out, proj, qv, outw, outb, exp, expb, con, conb, gain, shift) = outs
    lo_out[...] = lo[...]
    vo_out[...] = vo[...]
    lg_out[...] = lg[...]
    vg_out[...] = vg[...]
    width = HALF_PAIR
    for b in range(3):
        for j, lane in enumerate((0, 2 * width, width)):
            proj[b, j] = wgrad[b, :, lane : lane + width]
        outw[b] = wgrad[b, :, 3 * width :].T
        for j in range(2):
            qv[b, j : j + 1] = qb[b : b + 1, j * width : (j + 1) * width]
    for stream in range(2):
        exp[stream] = wgrad[3 + stream]
        con[stream] = wgrad[5 + stream]
    expb[...] = qb[3:5]
    outb[...] = vec[0:3]
    conb[...] = vec[3:5]
    gain[...] = vec[5:10]
    shift[...] = vec[10:15]


def unpack(packed, shapes):
    vmem = pl.BlockSpec(memory_space=pltpu.VMEM)
    return pl.pallas_call(
        unpack_kernel,
        out_shape=shapes,
        in_specs=[vmem] * len(packed),
        out_specs=[vmem] * len(shapes),
        compiler_params=pltpu.CompilerParams(vmem_limit_bytes=VMEM_LIMIT),
    )(*packed)


def on_device_fused(
    language_input,
    vision_input,
    word_lengths,
    region_counts,
    task_flags,
    language_cotangent,
    vision_cotangent,
    projection_weight,
    query_value_bias,
    output_weight,
    output_bias,
    expand_weight,
    expand_bias,
    contract_weight,
    contract_bias,
    norm_gain,
    norm_bias,
):
    packed = fused_layer(
        float(word_lengths.shape[0] * lax.axis_size("dp")),
        language_input,
        vision_input,
        language_cotangent,
        vision_cotangent,
        word_lengths,
        region_counts,
        task_flags.T,
        projection_weight,
        query_value_bias,
        output_weight,
        expand_weight,
        expand_bias,
        contract_weight.transpose(0, 2, 1),
        output_bias,
        contract_bias,
        norm_gain,
        norm_bias,
    )
    like = [
        (language_input, BF),
        (vision_input, BF),
        (language_input, F32),
        (vision_input, F32),
        (projection_weight, F32),
        (query_value_bias, F32),
        (output_weight, F32),
        (output_bias, F32),
        (expand_weight, F32),
        (expand_bias, F32),
        (contract_weight.transpose(0, 2, 1), F32),
        (contract_bias, F32),
        (norm_gain, F32),
        (norm_bias, F32),
    ]
    outs = list(unpack(packed, [jax.ShapeDtypeStruct(a.shape, t) for a, t in like]))
    outs[10] = outs[10].transpose(0, 2, 1)
    return tuple(outs)


def solution(mesh):
    in_specs = (
        P(("dp", "mp"), None),
        P(("dp", "mp"), None),
        P("dp"),
        P("dp"),
        P("dp", None),
        P(("dp", "mp"), None),
        P(("dp", "mp"), None),
        P(None, None, "dp", "mp"),
        P(None, None, "mp"),
        P(None, "mp", "dp"),
        P(),
        P(None, "dp", "mp"),
        P(None, "mp"),
        P(None, "mp", "dp"),
        P(),
        P(),
        P(),
    )
    out_specs = (
        P(("dp", "mp"), None),
        P(("dp", "mp"), None),
        P(("dp", "mp"), None),
        P(("dp", "mp"), None),
        P(None, None, "dp", "mp"),
        P(None, None, "mp"),
        P(None, "mp", "dp"),
        P(),
        P(None, "dp", "mp"),
        P(None, "mp"),
        P(None, "mp", "dp"),
        P(),
        P(),
        P(),
    )
    fused = dict(mesh.shape) == {"dp": 8, "mp": 4}
    return jax.shard_map(
        on_device_fused if fused else on_device, mesh=mesh, in_specs=in_specs, out_specs=out_specs, check_vma=False
    )
```

```python
from functools import partial
import math

import jax
import jax.numpy as jnp
from jax import lax
from jax.experimental import pallas as pl
from jax.experimental.pallas import tpu as pltpu
from jax.sharding import PartitionSpec as P

D = 768
HEADS = 12
WORDS = 20
REGIONS = 36
D_MODEL = D
D_HEAD = D // HEADS

EPSILON = 1e-12
MASKED = -1e30


def layer_norm(summed, gain, shift):
    center = summed - jnp.mean(summed, -1, keepdims=True)
    scaled = lax.rsqrt(jnp.mean(center * center, -1, keepdims=True) + EPSILON)
    normed = center * scaled
    return (normed * gain + shift, normed, scaled)


def norm_back(upstream, normed, scaled, gain):
    through = upstream * gain
    inner = (
        through
        - jnp.mean(through, -1, keepdims=True)
        - normed * jnp.mean(through * normed, -1, keepdims=True)
    )
    return (scaled * inner, jnp.sum(upstream * normed, 0), jnp.sum(upstream, 0))


def split_heads(rows, item_count):
    head_size = D // HEADS
    return rows.reshape(
        item_count, rows.shape[0] // item_count, rows.shape[1] // head_size, head_size
    )


def join_heads(block):
    return block.reshape(block.shape[0] * block.shape[1], block.shape[2] * block.shape[3])


def project(rows, weight, bias, item_count):
    mapped = jnp.einsum("rd,jde->jre", rows, weight, preferred_element_type=jnp.float32)
    query = split_heads((mapped[0] + bias[0]).astype(jnp.bfloat16), item_count)
    keys = split_heads(mapped[1].astype(jnp.bfloat16), item_count)
    values = split_heads((mapped[2] + bias[1]).astype(jnp.bfloat16), item_count)
    return (query, keys, values)


def masked_scores(query, keys, valid):
    scores = jnp.einsum("inhd,imhd->ihnm", query, keys, preferred_element_type=jnp.float32) * (
        1.0 / math.sqrt(D // HEADS)
    )
    return jnp.where(valid[:, None, None, :], scores, MASKED)


def attend(query, keys, values, valid):
    scores = masked_scores(query, keys, valid)
    highest = jnp.max(scores, -1, keepdims=True)
    raised = jnp.exp(scores - highest)
    summed = jnp.sum(raised, -1, keepdims=True)
    context = jnp.einsum(
        "ihnm,imhd->inhd",
        (raised / summed).astype(jnp.bfloat16),
        values,
        preferred_element_type=jnp.float32,
    )
    return (join_heads(context).astype(jnp.bfloat16), highest + jnp.log(summed))


def attend_back(query, keys, values, valid, log_total, context_grad):
    factor = 1.0 / math.sqrt(D // HEADS)
    upstream = context_grad.reshape(query.shape)
    weights = jnp.exp(masked_scores(query, keys, valid) - log_total)
    weight_grad = jnp.einsum(
        "inhd,imhd->ihnm", upstream, values, preferred_element_type=jnp.float32
    )
    score_grad = (
        weights * (weight_grad - jnp.sum(weight_grad * weights, -1, keepdims=True))
    ).astype(jnp.bfloat16)
    query_grad = (
        jnp.einsum("ihnm,imhd->inhd", score_grad, keys, preferred_element_type=jnp.float32) * factor
    ).astype(jnp.bfloat16)
    keys_grad = (
        jnp.einsum("ihnm,inhd->imhd", score_grad, query, preferred_element_type=jnp.float32)
        * factor
    ).astype(jnp.bfloat16)
    values_grad = jnp.einsum(
        "ihnm,inhd->imhd",
        weights.astype(jnp.bfloat16),
        upstream,
        preferred_element_type=jnp.float32,
    ).astype(jnp.bfloat16)
    return (join_heads(query_grad), join_heads(keys_grad), join_heads(values_grad))


def project_back(rows, query_grad, keys_grad, values_grad):
    stacked = jnp.stack([query_grad, keys_grad, values_grad])
    weight_grad = jnp.einsum("rd,jre->jde", rows, stacked, preferred_element_type=jnp.float32)
    bias_grad = jnp.stack(
        [jnp.sum(query_grad.astype(jnp.float32), 0), jnp.sum(values_grad.astype(jnp.float32), 0)]
    )
    return (weight_grad, bias_grad, stacked)


def gather_rows(language_rows, vision_rows):
    return (
        lax.all_gather(language_rows, "mp", axis=0, tiled=True),
        lax.all_gather(vision_rows, "mp", axis=0, tiled=True),
    )


def rows_of(language_part, vision_part):
    return (
        lax.all_to_all(language_part, "mp", split_axis=0, concat_axis=1, tiled=True),
        lax.all_to_all(vision_part, "mp", split_axis=0, concat_axis=1, tiled=True),
    )


def gather_grads(language_rows, vision_rows):
    return (
        lax.all_gather(language_rows, "mp", axis=0, tiled=True),
        lax.all_gather(vision_rows, "mp", axis=0, tiled=True),
    )


def grads_of(language_part, vision_part):
    return (
        lax.all_to_all(language_part, "mp", split_axis=1, concat_axis=2, tiled=True),
        lax.all_to_all(vision_part, "mp", split_axis=1, concat_axis=2, tiled=True),
    )


def matmul(left, right):
    return jnp.dot(left, right, preferred_element_type=jnp.float32)


def on_device(
    language_input,
    vision_input,
    word_lengths,
    region_counts,
    task_flags,
    language_cotangent,
    vision_cotangent,
    projection_weight,
    query_value_bias,
    output_weight,
    output_bias,
    expand_weight,
    expand_bias,
    contract_weight,
    contract_bias,
    norm_gain,
    norm_bias,
):
    item_count = word_lengths.shape[0]
    flag_total = lax.psum(jnp.sum(task_flags, 0), "dp")
    projection, out_weight, expand, contract = (
        lax.all_gather(projection_weight, "dp", axis=2, tiled=True),
        lax.all_gather(output_weight, "dp", axis=2, tiled=True),
        lax.all_gather(expand_weight, "dp", axis=1, tiled=True),
        lax.all_gather(contract_weight, "dp", axis=2, tiled=True),
    )
    projection_full, out_full, expand_full, contract_full = (
        lax.all_gather(projection, "mp", axis=3, tiled=True),
        lax.all_gather(out_weight, "mp", axis=1, tiled=True),
        lax.all_gather(expand, "mp", axis=2, tiled=True),
        lax.all_gather(contract, "mp", axis=1, tiled=True),
    )
    valid = [
        jnp.arange(WORDS, dtype=jnp.int32)[None, :] < word_lengths[:, None],
        jnp.arange(REGIONS, dtype=jnp.int32)[None, :] < region_counts[:, None],
    ]
    row_counts = [WORDS, REGIONS]
    inputs = [language_input.astype(jnp.float32), vision_input.astype(jnp.float32)]
    cross_rows = gather_rows(language_input, vision_input)
    cross_parts = [
        project(cross_rows[stream], projection[0], query_value_bias[0], item_count)
        for stream in range(2)
    ]
    cross_context = []
    cross_total = []
    for stream in range(2):
        other = 1 - stream
        context, log_total = attend(
            cross_parts[stream][0], cross_parts[other][1], cross_parts[other][2], valid[other]
        )
        cross_context.append(context)
        cross_total.append(log_total)
    moved = rows_of(cross_context[0], cross_context[1])
    branch = [matmul(moved[stream], out_full[0]) for stream in range(2)]
    first = [
        layer_norm(branch[stream] + output_bias[0] + inputs[stream], norm_gain[0], norm_bias[0])
        for stream in range(2)
    ]
    first_out = [first[stream][0].astype(jnp.bfloat16) for stream in range(2)]
    self_rows = gather_rows(first_out[0], first_out[1])
    self_parts = [
        project(self_rows[stream], projection[1 + stream], query_value_bias[1 + stream], item_count)
        for stream in range(2)
    ]
    self_context = []
    self_total = []
    for stream in range(2):
        context, log_total = attend(
            self_parts[stream][0], self_parts[stream][1], self_parts[stream][2], valid[stream]
        )
        self_context.append(context)
        self_total.append(log_total)
    moved = rows_of(self_context[0], self_context[1])
    branch = [matmul(moved[stream], out_full[1 + stream]) for stream in range(2)]
    second = [
        layer_norm(
            branch[stream] + output_bias[1 + stream] + first_out[stream].astype(jnp.float32),
            norm_gain[1 + stream],
            norm_bias[1 + stream],
        )
        for stream in range(2)
    ]
    second_out = [second[stream][0].astype(jnp.bfloat16) for stream in range(2)]
    feed_rows = gather_rows(second_out[0], second_out[1])
    before = [
        matmul(feed_rows[stream], expand[stream]) + expand_bias[stream] for stream in range(2)
    ]
    hidden = [
        jax.nn.gelu(before[stream], approximate=False).astype(jnp.bfloat16) for stream in range(2)
    ]
    moved = rows_of(hidden[0], hidden[1])
    branch = [matmul(moved[stream], contract_full[stream]) for stream in range(2)]
    third = [
        layer_norm(
            branch[stream] + contract_bias[stream] + second_out[stream].astype(jnp.float32),
            norm_gain[3 + stream],
            norm_bias[3 + stream],
        )
        for stream in range(2)
    ]
    language_out = third[0][0].astype(jnp.bfloat16)
    vision_out = third[1][0].astype(jnp.bfloat16)
    item_scale = task_flags.astype(jnp.float32) * (
        item_count * lax.axis_size("dp") / flag_total.astype(jnp.float32)
    )
    shard_index = lax.axis_index("mp")
    upstream = []
    for stream, cotangent in enumerate([language_cotangent, vision_cotangent]):
        per_row = jnp.repeat(
            item_scale[:, stream],
            row_counts[stream],
            total_repeat_length=item_count * row_counts[stream],
        )
        shard_rows = cotangent.shape[0]
        row_scale = lax.dynamic_slice_in_dim(per_row, shard_index * shard_rows, shard_rows)
        upstream.append(cotangent.astype(jnp.float32) * row_scale[:, None])
    third_back = [
        norm_back(upstream[stream], third[stream][1], third[stream][2], norm_gain[3 + stream])
        for stream in range(2)
    ]
    sent = gather_grads(
        third_back[0][0].astype(jnp.bfloat16), third_back[1][0].astype(jnp.bfloat16)
    )
    expand_local = []
    expand_bias_local = []
    contract_local = []
    before_grads = []
    for stream in range(2):
        hidden_grad = jnp.einsum(
            "rd,fd->rf", sent[stream], contract[stream], preferred_element_type=jnp.float32
        )
        contract_local.append(
            jnp.einsum(
                "rf,rd->fd", hidden[stream], sent[stream], preferred_element_type=jnp.float32
            )
        )
        unused, pull = jax.vjp(partial(jax.nn.gelu, approximate=False), before[stream])
        before_grad = pull(hidden_grad)[0].astype(jnp.bfloat16)
        expand_local.append(
            jnp.einsum(
                "rd,rf->df", feed_rows[stream], before_grad, preferred_element_type=jnp.float32
            )
        )
        expand_bias_local.append(jnp.sum(before_grad.astype(jnp.float32), 0))
        before_grads.append(before_grad[None])
    moved = grads_of(before_grads[0], before_grads[1])
    back = [
        jnp.einsum(
            "rf,df->rd", moved[stream][0], expand_full[stream], preferred_element_type=jnp.float32
        )
        for stream in range(2)
    ]
    second_grad = [third_back[stream][0] + back[stream] for stream in range(2)]
    second_back = [
        norm_back(second_grad[stream], second[stream][1], second[stream][2], norm_gain[1 + stream])
        for stream in range(2)
    ]
    sent = gather_grads(
        second_back[0][0].astype(jnp.bfloat16), second_back[1][0].astype(jnp.bfloat16)
    )
    self_weight = []
    self_bias = []
    self_out = []
    stacks = []
    for stream in range(2):
        context_grad = jnp.einsum(
            "rd,ed->re", sent[stream], out_weight[1 + stream], preferred_element_type=jnp.float32
        ).astype(jnp.bfloat16)
        self_out.append(
            jnp.einsum(
                "re,rd->ed", self_context[stream], sent[stream], preferred_element_type=jnp.float32
            )
        )
        grads = attend_back(
            self_parts[stream][0],
            self_parts[stream][1],
            self_parts[stream][2],
            valid[stream],
            self_total[stream],
            context_grad,
        )
        weight_part, bias_part, stacked = project_back(
            self_rows[stream], grads[0], grads[1], grads[2]
        )
        self_weight.append(weight_part)
        self_bias.append(bias_part)
        stacks.append(stacked)
    moved = grads_of(stacks[0], stacks[1])
    back = [
        jnp.einsum(
            "jre,jde->rd",
            moved[stream],
            projection_full[1 + stream],
            preferred_element_type=jnp.float32,
        )
        for stream in range(2)
    ]
    first_grad = [second_back[stream][0] + back[stream] for stream in range(2)]
    first_back = [
        norm_back(first_grad[stream], first[stream][1], first[stream][2], norm_gain[0])
        for stream in range(2)
    ]
    sent = gather_grads(
        first_back[0][0].astype(jnp.bfloat16), first_back[1][0].astype(jnp.bfloat16)
    )
    cross_out = jnp.einsum(
        "re,rd->ed", cross_context[0], sent[0], preferred_element_type=jnp.float32
    ) + jnp.einsum("re,rd->ed", cross_context[1], sent[1], preferred_element_type=jnp.float32)
    triples = [[None, None, None], [None, None, None]]
    for stream in range(2):
        other = 1 - stream
        context_grad = jnp.einsum(
            "rd,ed->re", sent[stream], out_weight[0], preferred_element_type=jnp.float32
        ).astype(jnp.bfloat16)
        grads = attend_back(
            cross_parts[stream][0],
            cross_parts[other][1],
            cross_parts[other][2],
            valid[other],
            cross_total[stream],
            context_grad,
        )
        triples[stream][0] = grads[0]
        triples[other][1] = grads[1]
        triples[other][2] = grads[2]
    results = [
        project_back(cross_rows[stream], triples[stream][0], triples[stream][1], triples[stream][2])
        for stream in range(2)
    ]
    cross_weight = results[0][0] + results[1][0]
    cross_bias = results[0][1] + results[1][1]
    moved = grads_of(results[0][2], results[1][2])
    back = [
        jnp.einsum(
            "jre,jde->rd", moved[stream], projection_full[0], preferred_element_type=jnp.float32
        )
        for stream in range(2)
    ]
    language_grad = first_back[0][0] + back[0]
    vision_grad = first_back[1][0] + back[1]
    projection_stack = jnp.stack([cross_weight, self_weight[0], self_weight[1]])
    output_stack = jnp.stack([cross_out, self_out[0], self_out[1]])
    projection_grad, output_weight_grad, expand_grad, contract_grad = (
        lax.psum_scatter(projection_stack, "dp", scatter_dimension=2, tiled=True),
        lax.psum_scatter(output_stack, "dp", scatter_dimension=2, tiled=True),
        lax.psum_scatter(jnp.stack(expand_local), "dp", scatter_dimension=1, tiled=True),
        lax.psum_scatter(jnp.stack(contract_local), "dp", scatter_dimension=2, tiled=True),
    )
    query_value_grad, expand_bias_grad = lax.psum(
        (jnp.stack([cross_bias, self_bias[0], self_bias[1]]), jnp.stack(expand_bias_local)), "dp"
    )
    output_bias_local = jnp.stack(
        [
            jnp.sum(first_back[0][0], 0) + jnp.sum(first_back[1][0], 0),
            jnp.sum(second_back[0][0], 0),
            jnp.sum(second_back[1][0], 0),
        ]
    )
    contract_bias_local = jnp.stack([jnp.sum(third_back[0][0], 0), jnp.sum(third_back[1][0], 0)])
    gain_local = jnp.stack(
        [
            first_back[0][1] + first_back[1][1],
            second_back[0][1],
            second_back[1][1],
            third_back[0][1],
            third_back[1][1],
        ]
    )
    shift_local = jnp.stack(
        [
            first_back[0][2] + first_back[1][2],
            second_back[0][2],
            second_back[1][2],
            third_back[0][2],
            third_back[1][2],
        ]
    )
    output_bias_grad, contract_bias_grad, norm_gain_grad, norm_bias_grad = lax.psum(
        (output_bias_local, contract_bias_local, gain_local, shift_local), ("dp", "mp")
    )
    return (
        language_out,
        vision_out,
        language_grad,
        vision_grad,
        projection_grad,
        query_value_grad,
        output_weight_grad,
        output_bias_grad,
        expand_grad,
        expand_bias_grad,
        contract_grad,
        contract_bias_grad,
        norm_gain_grad,
        norm_bias_grad,
    )


MESH = pl.DeviceIdType.MESH
BF = jnp.bfloat16
F32 = jnp.float32
SLOTS = 4
RL = SLOTS * WORDS
REGION_PAD = 40
RV = SLOTS * REGION_PAD
ROWS = RL + RV
SHARE = 96
HALF_PAIR = 2 * SHARE
LANG_HEAD = 16
VIS_HEAD = 32
LANG_TAIL = 32
VIS_TAIL = 64
N_AR = 48
NT = 3
TILE = 256
LANG = (0, RL)
V1 = (RL, RL + RV // 2)
V2 = (RL + RV // 2, ROWS)
VIS = (RL, ROWS)
BOTH = (0, ROWS)
CHAINS = (V1, V2, LANG)
SELF = {LANG: 1, V1: 2, V2: 2}
EXPAND = {LANG: 3, V1: 4, V2: 4}
CONTRACT = {LANG: 5, V1: 6, V2: 6}
PARTS = {w: (w, slice(0, 768)) for w in range(1, 7)} | {0: (0, slice(0, 384)), 7: (0, slice(384, 768))}
VMEM_LIMIT = 63 * 1024 * 1024


def dot_nn(left, right):
    return lax.dot_general(left, right, (((1,), (0,)), ((), ())), preferred_element_type=F32)


def dot_nt(left, right):
    return lax.dot_general(left, right, (((1,), (1,)), ((), ())), preferred_element_type=F32)


def dot_tn(left, right):
    return lax.dot_general(left, right, (((0,), (0,)), ((), ())), preferred_element_type=F32)


def head_mask(first_lane, dtype):
    lane = lax.broadcasted_iota(jnp.int32, (1, TILE), 1) - first_lane
    return [
        jnp.where((lane >= 64 * h) & (lane < 64 * h + 64), 1.0, 0.0).astype(dtype) for h in range(3)
    ]


def item_rows(shape, dim, first, size, pad):
    row = lax.broadcasted_iota(jnp.int32, shape, dim) + first
    item = sum(jnp.where(row >= pad * j, 1, 0) for j in range(1, SLOTS))
    return row - (pad - size) * item, row - pad * item < size


def rows_into_slab(shape, shift, count, size, pad):
    place, real = item_rows(shape, 0, 0, size, pad)
    column = lax.broadcasted_iota(jnp.int32, shape, 1)
    return jnp.where((column - place == shift) & real & (place < count), 1.0, 0.0)


def rows_from_slab(shape, shift, first, low, high, size, pad):
    place, real = item_rows(shape, 1, first, size, pad)
    row = lax.broadcasted_iota(jnp.int32, shape, 0)
    return jnp.where((place - row == shift) & real & (row >= low) & (row < high), 1.0, 0.0)


def layer_kernel(
    total_items,
    lang,
    vis,
    lcot,
    vcot,
    lengths,
    regions,
    flags,
    projection,
    query_value,
    out_weight,
    expand,
    expand_b,
    contract,
    out_bias,
    contract_b,
    gains,
    shifts,
    lang_out,
    vis_out,
    lang_grad,
    vis_grad,
    wgrad,
    vec_out,
    qb_out,
    W,
    G,
    RD,
    RX,
    R2,
    A,
    KV,
    RSB,
    STG,
    QVK,
    D,
    C,
    H,
    GP,
    PCL,
    PCV,
    PS,
    PART,
    PZ,
    NORM,
    RSTD,
    DZ,
    COT,
    SH,
    FLAG,
    QO,
    QB,
    QR,
    CA,
    CR,
    VG,
    QG,
    AVA,
    AVR,
    HL,
    HV,
    OUTS,
    TLO,
    TVO,
    TLG,
    TVG,
    ssem,
    rsem,
    wsem,
    wsem_z,
    gsem,
    gsem2,
):
    d = lax.axis_index("dp")
    z = lax.axis_index("mp")
    c = d % 2
    k = d // 2
    k_flip = [k + 1 - 2 * (k % 2), (k + 2) % 4, 3 - k]
    sib = (d + 1 - 2 * c, z)
    zp = (d, z + 1 - 2 * (z % 2))
    z2 = (z + 2) % 4
    up = (d, (z + 1) % 4)
    down = (d, (z + 3) % 4)
    plane = [(2 * kf + c, z) for kf in k_flip]
    far = (2 * k + 1, z2)

    pending = []
    counter = [0, 0]

    def remote(src, dst, send, recv, device):
        return pltpu.make_async_remote_copy(
            src_ref=src, dst_ref=dst, send_sem=send, recv_sem=recv, device_id=device, device_id_type=MESH
        )

    def send(src, dst, device, recv=None, keep=True):
        slot = counter[0]
        counter[0] += 1
        if recv is None:
            recv = rsem.at[counter[1]]
            counter[1] += 1
        copy = remote(src, dst, ssem.at[slot], recv, device)
        copy.start()
        if keep:
            pending.append(copy)
        return copy

    def wait_bytes(ref, sem):
        pltpu.make_async_copy(ref, ref, sem).wait()

    def arrived(name, *copies):
        with jax.named_scope("wait_" + name):
            for copy in copies:
                copy.wait_recv()

    barrier = pltpu.get_barrier_semaphore()
    peers = [sib, up, down, (d, z2), (d + 1 - 2 * c, z2)] + plane
    for peer in peers:
        pl.semaphore_signal(barrier, inc=1, device_id=peer, device_id_type=MESH)

    def weight_first(part):
        w, lanes = PARTS[part]
        row = pl.ds(pl.multiple_of(d * SHARE, 16), SHARE)
        slot = counter[0]
        counter[0] += 1
        share = SH.at[w] if w < 3 else (expand.at[w - 3] if w < 5 else contract.at[w - 5])
        share = share.at[:, lanes]
        target = W.at[w, row, lanes]
        near = remote(share, target, ssem.at[slot], wsem_z.at[part], sib)
        own = pltpu.make_async_copy(share, target, wsem_z.at[part])

        @pl.when(c == 1)
        def _():
            near.start()

        @pl.when(c == 0)
        def _():
            own.start()

        send(share, target, far, wsem_z.at[part])
        nears.append(near)

    def place(width, first):
        row = lax.broadcasted_iota(jnp.int32, (width, D_MODEL), 0)
        column = lax.broadcasted_iota(jnp.int32, (width, D_MODEL), 1)
        return jnp.where(column - row == first, 1.0, 0.0).astype(BF)

    def attention_share(b):
        SH[b] = (
            dot_nn(projection[b, 0], place(HALF_PAIR, 0))
            + dot_nn(projection[b, 2], place(HALF_PAIR, HALF_PAIR))
            + dot_nn(projection[b, 1], place(HALF_PAIR, 2 * HALF_PAIR))
            + dot_tn(out_weight[b], place(HALF_PAIR, 3 * HALF_PAIR))
        ).astype(BF)

    nears = []
    attention_share(0)

    n_items = lengths.shape[0]
    first_item = 3 * z + jnp.minimum(z, 1)
    KV[0] = jnp.full(KV.shape[1:], -1.0, F32)
    for row, source, size, pad, first_row in ((0, lengths, WORDS, WORDS, 0), (1, regions, REGIONS, REGION_PAD, RL)):
        lane = lax.broadcasted_iota(jnp.int32, (1, TILE), 1)
        owner = jnp.full((1, TILE), -1.0, F32)
        slab_row = lax.broadcasted_iota(jnp.int32, (SLOTS * pad, 1), 0)
        flag = jnp.zeros((SLOTS * pad, 1), F32)
        for j in range(SLOTS):
            item = jnp.minimum(first_item + j, n_items - 1)
            valid = (lane >= j * pad) & (lane < j * pad + source[item]) & (lane < j * pad + size)
            owner = jnp.where(valid, float(j), owner)
            inside = (slab_row >= j * pad) & (slab_row < (j + 1) * pad)
            flag = jnp.where(inside, flags[row, item].astype(F32), flag)
            if row == 1 and j % 2 == 1:
                pair = jnp.full((1, TILE), -1.0, F32)
                for i in (0, 1):
                    other = jnp.minimum(first_item + j - 1 + i, n_items - 1)
                    valid = (lane >= i * pad) & (lane < i * pad + source[other]) & (lane < i * pad + size)
                    pair = jnp.where(valid, float(j - 1 + i), pair)
                KV[0, 2 + j // 2 : 3 + j // 2] = pair
        KV[0, row : row + 1] = owner
        FLAG[first_row : first_row + SLOTS * pad] = flag
        count = flags[row, 0]
        for j in range(1, n_items):
            count = count + flags[row, j]
        CA[0, row : row + 1] = jnp.full((1, 128), count.astype(F32), F32)
    QO[...] = jnp.zeros_like(QO)
    for b in range(3):
        QO[b : b + 1, 0:HALF_PAIR] = query_value[b, 0:1]
        QO[b : b + 1, HALF_PAIR : 2 * HALF_PAIR] = query_value[b, 1:2]
    QO[3:5] = expand_b[...]

    pl.semaphore_wait(barrier, len(peers))
    heads = [
        send(lang.at[pl.ds(0, LANG_HEAD)], HL.at[0], down),
        send(vis.at[pl.ds(0, VIS_HEAD)], HV.at[0], down),
    ]
    weight_first(0)
    weight_first(7)
    heads_cot = [
        send(lcot.at[pl.ds(0, LANG_HEAD)], HL.at[1], down),
        send(vcot.at[pl.ds(0, VIS_HEAD)], HV.at[1], down),
    ]
    kv_sib = send(KV.at[0], KV.at[1], sib)
    kv_zp = send(KV.at[0], KV.at[2], zp)
    count_copies = [send(CA.at[0], CR.at[0], sib)]
    bias_swap = send(QO, QR, (d, z2))

    pair_rows = pl.ds(pl.multiple_of(k * HALF_PAIR, 16), HALF_PAIR)

    def rows_of_chip(chip, first=0, count=HALF_PAIR):
        return pl.ds(pl.multiple_of(chip * HALF_PAIR + first, 16), count)

    def weight_second(part):
        w, lanes = PARTS[part]
        block = W.at[w, pair_rows, lanes]
        wait_bytes(block, wsem_z.at[part])
        for j in range(2):
            send(block, block, plane[j], wsem.at[j, part])

    def weight_third(part):
        w, lanes = PARTS[part]
        for j in range(2):
            wait_bytes(W.at[w, pair_rows, lanes], wsem.at[j, part])
            half = W.at[w, rows_of_chip(k_flip[j], j * SHARE, SHARE), lanes]
            send(half, half, plane[1 - j], wsem.at[2, part])

    def weight_ready(part):
        w, lanes = PARTS[part]
        wait_bytes(W.at[w, pair_rows, lanes], wsem.at[2, part])

    off_l = jnp.where(z == 0, 0, 20 - 5 * z)
    off_v = jnp.where(z == 0, 0, 36 - 9 * z)
    n_l = jnp.where(z == 0, 4 * WORDS, 3 * WORDS)
    n_v = jnp.where(z == 0, 4 * REGIONS, 3 * REGIONS)
    own_l = lang.shape[0]
    own_v = vis.shape[0]
    def gather_start(p, stream):
        rows = pl.ds(stream[0], stream[1] - stream[0])
        return (
            p,
            rows,
            send(A.at[p, 0, rows], A.at[p, 1, rows], sib),
            send(A.at[p, 0, rows], A.at[p, 2, rows], zp),
        )

    def gather_forward(handle):
        p, rows, _, across = handle
        arrived("rows_z", across)
        return send(A.at[p, 2, rows], A.at[p, 3, rows], sib)

    def own_slab(index, source_l, source_v, copies, target):
        arrived("heads", *copies)
        for (r0, r1), size, pad, own, off, count, source, head, head_rows in (
            (VIS, REGIONS, REGION_PAD, own_v, off_v, n_v, source_v, HV, VIS_HEAD),
            (LANG, WORDS, WORDS, own_l, off_l, n_l, source_l, HL, LANG_HEAD),
        ):
            inside = rows_into_slab((r1 - r0, own), off, count, size, pad).astype(BF)
            beyond = rows_into_slab((r1 - r0, head_rows), off - own, count, size, pad).astype(BF)
            target[r0:r1] = (dot_nn(inside, source[...]) + dot_nn(beyond, head[index])).astype(BF)

    own_slab(0, lang, vis, heads, A.at[0, 0])
    rows_x = {stream: gather_start(0, stream) for stream in (VIS, LANG)}

    stage_used = {}

    def stage_free(index, stream):
        copy = stage_used.pop((index, stream), None)
        if copy is not None:
            copy.wait_send()

    def partial_nt(lhs_ref, stream, w, lanes):
        r0, r1 = stream
        rows = r1 - r0
        stage_free(0, stream)
        stage_free(1, stream)
        for n in range(NT):
            column = slice(n * TILE, (n + 1) * TILE)
            lhs = lhs_ref[:, r0:r1, :]
            lhs = lhs.reshape(SLOTS * rows, lhs.shape[-1])
            out = dot_nt(lhs, W[w, column, lanes])
            PART[r0:r1, column] = out[:rows]
            STG[0, r0:r1, column] = out[rows : 2 * rows].astype(BF)
            PZ[r0:r1, column] = out[2 * rows : 3 * rows]
            STG[1, r0:r1, column] = out[3 * rows :].astype(BF)

    def stage_send(index, stream, device):
        rows = pl.ds(stream[0], stream[1] - stream[0])
        copy = send(STG.at[index, rows], RSB.at[index, rows], device, keep=False)
        stage_used[index, stream] = copy
        return copy

    def sums_near(stream):
        return stage_send(0, stream, sib)

    def sums_far(stream):
        return stage_send(1, stream, sib)

    def sums_z(stream, far):
        r0, r1 = stream
        arrived("sums_core", far)
        stage_free(2, stream)
        STG[2, r0:r1] = (PZ[r0:r1] + RSB[1, r0:r1].astype(F32)).astype(BF)
        return stage_send(2, stream, zp)

    def reduced(stream, *copies):
        r0, r1 = stream
        arrived("sums", *copies)
        return PART[r0:r1] + RSB[0, r0:r1].astype(F32) + RSB[2, r0:r1].astype(F32)

    mask_q = head_mask(0, BF)
    mask_c = head_mask(64, BF)
    mask_q32 = head_mask(0, F32)
    mask_c32 = head_mask(64, F32)
    factor = 1.0 / math.sqrt(D_HEAD)

    def attend_slab(QV, Cb, crossed, stream, s):
        def one(queries, keys_rows, kv_row, item_size, first_item_of, P):
            (q0, q1), (k0, k1) = queries, keys_rows
            nq, nk = q1 - q0, k1 - k0
            query = QV[s, q0:q1, 0:256]
            keys = QV[s, k0:k1, 384:640]
            values = QV[s, k0:k1, 128:384]
            spread = jnp.concatenate([query * mask_q[h] for h in range(3)], 0)
            scores = dot_nt(spread, keys) * factor
            row = lax.broadcasted_iota(jnp.int32, (nq, nk), 0)
            item = jnp.full((nq, nk), float(first_item_of), F32)
            for j in range(1, nq // item_size):
                item = item + jnp.where(row >= j * item_size, 1.0, 0.0)
            same = item == KV[s, kv_row : kv_row + 1, 0:nk]
            scores = jnp.where(same[None], scores.reshape(3, nq, nk), MASKED)
            raised = jnp.exp(scores - jnp.max(scores, -1, keepdims=True))
            weights = (raised / jnp.sum(raised, -1, keepdims=True)).astype(BF).reshape(3 * nq, nk)
            P[s] = weights
            context = dot_nn(weights, values).reshape(3, nq, TILE)
            Cb[s, q0:q1] = (
                context[0] * mask_c32[0] + context[1] * mask_c32[1] + context[2] * mask_c32[2]
            ).astype(BF)

        if stream == LANG:
            if crossed:
                one(LANG, VIS, 1, WORDS, 0, PCL)
            else:
                one(LANG, LANG, 0, WORDS, 0, PS.at[0])
        else:
            half = (V1, V2).index(stream)
            if crossed:
                one(stream, LANG, 0, REGION_PAD, 2 * half, PCV.at[half])
            else:
                one(stream, stream, 2 + half, REGION_PAD, 2 * half, PS.at[1 + half])

    def attend_back_slab(QV, crossed, stream, s):
        def one(queries, keys_rows, P):
            (q0, q1), (k0, k1) = queries, keys_rows
            nq = q1 - q0
            query = QV[s, q0:q1, 0:256]
            keys = QV[s, k0:k1, 384:640]
            values = QV[s, k0:k1, 128:384]
            spread = jnp.concatenate([query * mask_q[h] for h in range(3)], 0)
            upstream = D[s, q0:q1, 512:768]
            up_spread = jnp.concatenate([upstream * mask_c[h] for h in range(3)], 0)
            weights = P[s]
            weights32 = weights.astype(F32)
            weight_grad = dot_nt(up_spread, values)
            score_grad = (
                weights32
                * (weight_grad - jnp.sum(weight_grad * weights32, -1, keepdims=True))
            ).astype(BF)
            dq = dot_nn(score_grad, keys).reshape(3, nq, TILE)
            dq = (dq[0] * mask_q32[0] + dq[1] * mask_q32[1] + dq[2] * mask_q32[2]) * factor
            dk = dot_tn(score_grad, spread) * factor
            dv = dot_tn(weights, up_spread)
            return dq, dk, dv

        if crossed:
            half = RV // 2
            dq_l, dk_v, dv_v = one(LANG, VIS, PCL)
            dq_1, dk_1, dv_1 = one(V1, LANG, PCV.at[0])
            dq_2, dk_2, dv_2 = one(V2, LANG, PCV.at[1])
            results = {
                LANG: (dq_l, dk_1 + dk_2, dv_1 + dv_2),
                V1: (dq_1, dk_v[:half], dv_v[:half]),
                V2: (dq_2, dk_v[half:], dv_v[half:]),
            }
        else:
            results = {stream: one(stream, stream, PS.at[0 if stream == LANG else 1 + (V1, V2).index(stream)])}
        for (r0, r1), (dq, dk, dv) in results.items():
            D[s, r0:r1, 0:128] = dq[:, :128].astype(BF)
            D[s, r0:r1, 128:256] = (dq[:, 128:] + dv[:, :128]).astype(BF)
            D[s, r0:r1, 256:384] = dv[:, 128:].astype(BF)
            D[s, r0:r1, 384:640] = dk.astype(BF)
            D[s, r0:r1, 640:768] = jnp.zeros((r1 - r0, 128), BF)

    def forward_norm(value, index, gain_row, r0, r1):
        center = value - jnp.mean(value, -1, keepdims=True)
        scaled = lax.rsqrt(jnp.mean(center * center, -1, keepdims=True) + EPSILON)
        normed = center * scaled
        NORM[index, r0:r1] = normed
        RSTD[index, r0:r1] = scaled
        return normed * gains[gain_row : gain_row + 1] + shifts[gain_row : gain_row + 1]

    def backward_norm(upstream, index, gain_row, bias_row, r0, r1):
        normed = NORM[index, r0:r1]
        through = upstream * gains[gain_row : gain_row + 1]
        inner = (
            through
            - jnp.mean(through, -1, keepdims=True)
            - normed * jnp.mean(through * normed, -1, keepdims=True)
        )
        result = RSTD[index, r0:r1] * inner
        VG[5 + gain_row : 6 + gain_row] += jnp.sum(upstream * normed, 0, keepdims=True)
        VG[10 + gain_row : 11 + gain_row] += jnp.sum(upstream, 0, keepdims=True)
        VG[bias_row : bias_row + 1] += jnp.sum(result, 0, keepdims=True)
        return result

    def rows_of(p, stream):
        r0, r1 = stream
        return A[p, :, r0:r1, :].reshape(SLOTS * (r1 - r0), D_MODEL)

    def tile_columns():
        return [slice(n * TILE, (n + 1) * TILE) for n in range(NT)]

    def project(stream, w):
        r0, r1 = stream
        for column in tile_columns():
            mapped = dot_nn(rows_of(1, stream), W[w, :, column]) + QB[w : w + 1, column]
            QVK[1, :, r0:r1, column] = mapped.astype(BF).reshape(SLOTS, r1 - r0, TILE)

    def project_cross(g):
        for column in tile_columns():
            rows = A[0, 2 * g : 2 * g + 2].reshape(2 * ROWS, D_MODEL)
            mapped = dot_nn(rows, W[0, :, column]) + QB[0:1, column]
            QVK[0, 2 * g : 2 * g + 2, :, column] = mapped.astype(BF).reshape(2, ROWS, TILE)

    def attend(stream, b):
        for s in range(SLOTS):
            attend_slab(QVK.at[b], C.at[b], b == 0, stream, s)

    def expand_rows(stream):
        r0, r1 = stream
        w = EXPAND[stream]
        for column in tile_columns():
            before = dot_nn(rows_of(2, stream), W[w, :, column]) + QB[w : w + 1, column]
            half = 0.5 * (1.0 + lax.erf(before * math.sqrt(0.5)))
            slope = half + before * jnp.exp(-0.5 * before * before) * (1.0 / math.sqrt(2.0 * math.pi))
            H[:, r0:r1, column] = (before * half).astype(BF).reshape(SLOTS, r1 - r0, TILE)
            GP[:, r0:r1, column] = slope.astype(BF).reshape(SLOTS, r1 - r0, TILE)

    def hidden_gradient(stream):
        r0, r1 = stream
        rows = SLOTS * (r1 - r0)
        for column in tile_columns():
            up_hidden = dot_nn(rows_of(3, stream), W[CONTRACT[stream], :, column])
            slope = GP[:, r0:r1, column].reshape(rows, TILE)
            D[:, r0:r1, column] = (up_hidden * slope.astype(F32)).astype(BF).reshape(SLOTS, r1 - r0, TILE)

    def context_gradient(p, stream, w):
        r0, r1 = stream
        upstream = dot_nn(rows_of(p, stream), W[w, :, 512:768])
        D[:, r0:r1, 512:768] = upstream.astype(BF).reshape(SLOTS, r1 - r0, TILE)

    def attend_gradient(stream, b):
        for s in range(SLOTS):
            attend_back_slab(QVK.at[b], b == 0, stream, s)

    def all_rows(ref, r0, r1, lanes):
        value = ref[:, r0:r1, lanes]
        return value.reshape(SLOTS * (r1 - r0), value.shape[-1])

    def weight_grad(w, lhs_p, rhs_ref, r0, r1, lanes=slice(0, 768)):
        for m in range(NT):
            column = slice(m * TILE, (m + 1) * TILE)
            left = all_rows(A.at[lhs_p], r0, r1, column)
            G[w, column, lanes] = dot_tn(left, all_rows(rhs_ref, r0, r1, lanes)).astype(BF)

    def attention_weight_grad(w, x_p, b_p, Cb, r0, r1, middle=None):
        if middle is None:
            weight_grad(w, x_p, D, r0, r1, slice(0, 512))
        else:
            weight_grad(w, x_p, D, r0, r1, slice(0, 384))
            middle()
            weight_grad(w, x_p, D, r0, r1, slice(384, 512))
        for m in range(NT):
            column = slice(m * TILE, (m + 1) * TILE)
            G[w, column, 512:768] = (
                dot_tn(all_rows(A.at[x_p], r0, r1, column), all_rows(D, r0, r1, slice(512, 768)))
                + dot_tn(all_rows(A.at[b_p], r0, r1, column), all_rows(Cb, r0, r1, slice(0, 256)))
            ).astype(BF)

    def bias_grad(row, r0, r1):
        total = jnp.zeros((1, D_MODEL), F32)
        for s in range(SLOTS):
            total = total + jnp.sum(D[s, r0:r1].astype(F32), 0, keepdims=True)
        QG[row : row + 1] = total

    def grad_first(part):
        w, lanes = PARTS[part]
        for j in range(2):
            half = rows_of_chip(k_flip[2], (1 - j) * SHARE, SHARE)
            send(G.at[w, half, lanes], RD.at[j, w, :, lanes], plane[j], gsem.at[2, part])

    def grad_second(part):
        w, lanes = PARTS[part]
        wait_bytes(RD.at[:, w, :, lanes], gsem.at[2, part])
        for j in range(2):
            half = rows_of_chip(k_flip[1 - j], (1 - j) * SHARE, SHARE)
            G[w, half, lanes] = (G[w, half, lanes].astype(F32) + RD[j, w, :, lanes].astype(F32)).astype(BF)
        for j in range(2):
            send(G.at[w, rows_of_chip(k_flip[j]), lanes], RX.at[j, w, :, lanes], plane[j], gsem.at[j, part])

    grad_nears = []

    def grad_third(part):
        w, lanes = PARTS[part]
        for j in range(2):
            wait_bytes(RX.at[j, w, :, lanes], gsem.at[j, part])
        total = G[w, pair_rows, lanes].astype(F32)
        total = total + RX[0, w, :, lanes].astype(F32) + RX[1, w, :, lanes].astype(F32)
        G[w, pair_rows, lanes] = total.astype(BF)
        low = G.at[w, rows_of_chip(k, 0, SHARE), lanes]
        high = G.at[w, rows_of_chip(k, SHARE, SHARE), lanes]
        slot = counter[0]
        counter[0] += 2
        here, there = R2.at[0, w, :, lanes], R2.at[1, w, :, lanes]
        own = pltpu.make_async_copy(low, here, gsem2.at[part])
        near = remote(high, here, ssem.at[slot], gsem2.at[part], sib)
        far_low = remote(low, there, ssem.at[slot], gsem2.at[part], (2 * k, z2))
        far_high = remote(high, there, ssem.at[slot + 1], gsem2.at[part], (2 * k + 1, z2))

        @pl.when(c == 0)
        def _():
            own.start()
            near.start()

        @pl.when(c == 1)
        def _():
            far_low.start()
            far_high.start()

        grad_nears.append((near, far_low, far_high))

    def grad_last(part):
        w, lanes = PARTS[part]
        wait_bytes(R2.at[:, w, :, lanes], gsem2.at[part])
        wgrad[w, :, lanes] = R2[0, w, :, lanes].astype(F32) + R2[1, w, :, lanes].astype(F32)

    def count_step(stage, peer):
        count_copies[stage].wait_recv()
        CA[stage + 1] = CA[stage] + CR[stage]
        if peer is not None:
            count_copies.append(send(CA.at[stage + 1], CR.at[stage + 1], peer))

    VG[...] = jnp.zeros_like(VG)
    QG[...] = jnp.zeros_like(QG)
    weight_second(0)
    attention_share(2)
    weight_second(7)
    weight_first(2)
    attention_share(1)
    weight_third(0)
    far_x = {stream: gather_forward(rows_x[stream]) for stream in (VIS, LANG)}
    weight_third(7)
    weight_second(2)
    weight_first(1)
    kv_sib.wait_recv()
    kv_zp.wait_recv()
    kv_far = send(KV.at[2], KV.at[3], sib)
    bias_swap.wait_recv()
    QB[...] = jnp.where(c == 1, QR[...], QO[...])
    own_slab(1, lcot, vcot, heads_cot, COT)
    kv_far.wait_recv()
    arrived("rows", rows_x[VIS][2], rows_x[LANG][2], far_x[VIS], far_x[LANG])
    weight_ready(0)
    weight_ready(7)

    near, far_sum, z_sum, rows, far_rows = {}, {}, {}, {}, {}
    out_lanes, all_lanes = slice(512, 768), slice(0, 768)

    def sums_after(stream, lhs, w, lanes):
        partial_nt(lhs, stream, w, lanes)
        far_sum[stream] = sums_far(stream)
        near[stream] = sums_near(stream)

    def sums_on(stream):
        z_sum[stream] = sums_z(stream, far_sum[stream])

    def total_of(stream):
        return reduced(stream, near[stream], z_sum[stream])

    def all_arrived(stream):
        arrived("rows", rows[stream][2], far_rows[stream])

    def pass_on(stream):
        far_rows[stream] = gather_forward(rows[stream])

    def weight_step(third, second, first=None):
        weight_third(third)
        if second is not None:
            weight_second(second)
        if first is not None:
            weight_first(first)

    project_cross(0)
    weight_step(2, 1, 4)
    project_cross(1)
    attend(V1, 0)
    sums_after(V1, C.at[0], 0, out_lanes)
    attend(V2, 0)
    sums_after(V2, C.at[0], 0, out_lanes)
    sums_on(V1)
    attend(LANG, 0)
    sums_after(LANG, C.at[0], 0, out_lanes)
    sums_on(V2)
    weight_step(1, 4, 6)
    sums_on(LANG)
    count_step(0, plane[0])

    def first_norm(stream):
        r0, r1 = stream
        value = total_of(stream) + out_bias[0:1] + A[0, 0, r0:r1].astype(F32)
        A[1, 0, r0:r1] = forward_norm(value, 0, 0, r0, r1).astype(BF)
        rows[stream] = gather_start(1, stream)

    first_norm(V1)
    first_norm(V2)
    first_norm(LANG)

    def self_rows(stream, passed):
        w = SELF[stream]
        all_arrived(stream)
        project(stream, w)
        if passed is not None:
            pass_on(passed)
        attend(stream, 1)
        sums_after(stream, C.at[1], w, out_lanes)

    pass_on(V1)
    weight_ready(2)
    self_rows(V1, V2)
    weight_step(4, 6, 3)
    self_rows(V2, LANG)
    sums_on(V1)
    weight_ready(1)
    self_rows(LANG, None)
    sums_on(V2)

    def second_norm(stream):
        r0, r1 = stream
        n = 1 if stream == LANG else 2
        value = total_of(stream) + out_bias[n : n + 1] + A[1, 0, r0:r1].astype(F32)
        A[2, 0, r0:r1] = forward_norm(value, 1, n, r0, r1).astype(BF)
        rows[stream] = gather_start(2, stream)

    second_norm(V1)
    sums_on(LANG)
    count_step(1, plane[1])
    weight_step(6, 3, 5)
    second_norm(V2)
    pass_on(V1)
    second_norm(LANG)

    def last_norm(stream):
        r0, r1 = stream
        n = 0 if stream == LANG else 1
        value = total_of(stream) + contract_b[n : n + 1] + A[2, 0, r0:r1].astype(F32)
        OUTS[r0:r1] = forward_norm(value, 2, 3 + n, r0, r1).astype(BF)
        scale = total_items / CA[3, n : n + 1, 0:1]
        upstream = COT[r0:r1].astype(F32) * (FLAG[r0:r1] * scale)
        result = backward_norm(upstream, 2, 3 + n, 3 + n, r0, r1)
        DZ[r0:r1] = result
        A[3, 0, r0:r1] = result.astype(BF)
        rows[stream] = gather_start(3, stream)

    weight_ready(4)
    all_arrived(V1)
    expand_rows(V1)
    pass_on(V2)
    all_arrived(V2)
    expand_rows(V2)
    pass_on(LANG)
    weight_step(3, 5)
    weight_ready(6)
    sums_after(V1, H, 6, all_lanes)
    sums_after(V2, H, 6, all_lanes)
    sums_on(V1)
    count_step(2, None)
    weight_ready(3)
    all_arrived(LANG)
    expand_rows(LANG)
    sums_on(V2)
    last_norm(V1)
    weight_step(5, None)
    last_norm(V2)
    pass_on(V1)
    all_arrived(V1)
    hidden_gradient(V1)
    sums_after(V1, D, 4, all_lanes)
    pass_on(V2)
    weight_ready(5)
    sums_after(LANG, H, 5, all_lanes)
    all_arrived(V2)
    hidden_gradient(V2)
    weight_grad(6, 3, H, *VIS)
    grad_first(6)
    sums_on(LANG)
    sums_on(V1)
    sums_after(V2, D, 4, all_lanes)
    weight_grad(4, 2, D, *VIS)
    grad_second(6)
    grad_first(4)
    sums_on(V2)
    last_norm(LANG)

    def second_norm_back(stream):
        r0, r1 = stream
        n = 1 if stream == LANG else 2
        result = backward_norm(DZ[r0:r1] + total_of(stream), 1, n, n, r0, r1)
        DZ[r0:r1] = result
        A[4, 0, r0:r1] = result.astype(BF)
        rows[stream] = gather_start(4, stream)

    second_norm_back(V1)
    bias_grad(4, *VIS)
    pass_on(LANG)
    second_norm_back(V2)
    all_arrived(LANG)
    hidden_gradient(LANG)
    sums_after(LANG, D, 3, all_lanes)
    pass_on(V1)
    weight_grad(5, 3, H, *LANG)
    grad_third(6)
    grad_second(4)
    grad_first(5)
    sums_on(LANG)

    def self_gradient(stream, passed):
        w = SELF[stream]
        all_arrived(stream)
        context_gradient(4, stream, w)
        if passed is not None:
            pass_on(passed)
        attend_gradient(stream, 1)
        sums_after(stream, D, w, all_lanes)

    weight_grad(3, 2, D, *LANG)
    bias_grad(3, *LANG)
    self_gradient(V1, V2)
    second_norm_back(LANG)
    grad_third(4)
    grad_second(5)
    grad_first(3)
    self_gradient(V2, LANG)
    sums_on(V1)
    attention_weight_grad(2, 1, 4, C.at[1], *VIS)
    grad_third(5)
    grad_second(3)
    grad_first(2)
    sums_on(V2)
    self_gradient(LANG, None)
    tail_out = [
        send(OUTS.at[pl.ds(RL - LANG_TAIL, LANG_TAIL)], TLO, up),
        send(OUTS.at[pl.ds(ROWS - VIS_TAIL, VIS_TAIL)], TVO, up),
    ]

    def first_norm_back(stream):
        r0, r1 = stream
        result = backward_norm(DZ[r0:r1] + total_of(stream), 0, 0, 0, r0, r1)
        DZ[r0:r1] = result
        A[5, 0, r0:r1] = result.astype(BF)
        rows[stream] = gather_start(5, stream)

    first_norm_back(V1)
    sums_on(LANG)
    first_norm_back(V2)
    attention_weight_grad(1, 1, 4, C.at[1], *LANG)
    grad_third(3)
    grad_second(2)
    grad_first(1)
    pass_on(V1)
    first_norm_back(LANG)
    bias_grad(2, *VIS)
    pass_on(V2)
    bias_grad(1, *LANG)
    pass_on(LANG)

    for stream in CHAINS:
        all_arrived(stream)
        context_gradient(5, stream, 0)
    attend_gradient(None, 0)
    grad_third(2)
    grad_second(1)
    attention_weight_grad(0, 0, 5, C.at[0], *BOTH, middle=lambda: grad_first(0))
    grad_first(7)
    sums_after(V1, D, 0, all_lanes)
    sums_after(V2, D, 0, all_lanes)
    grad_second(0)
    sums_on(V1)
    sums_after(LANG, D, 0, all_lanes)
    sums_on(V2)
    grad_second(7)
    sums_on(LANG)
    bias_grad(0, *BOTH)

    quarter = jnp.where(c == 0, z, z2)
    AVA[0, 0:16] = VG[...]
    for j in range(4):
        AVA[0, 16 + 8 * j : 24 + 8 * j] = jnp.where(quarter == j, QG[...], 0.0)
    vector_peers = [sib, plane[0], plane[1], zp, (d, z2)]
    vector_copies = [send(AVA.at[0], AVR.at[0], vector_peers[0])]

    def vector_step(stage):
        arrived("vectors", vector_copies[stage])
        AVA[stage + 1] = AVA[stage] + AVR[stage]
        if stage < 4:
            vector_copies.append(send(AVA.at[stage + 1], AVR.at[stage + 1], vector_peers[stage + 1]))

    grad_third(1)
    vector_step(0)
    grad_last(6)
    grad_last(4)
    vector_step(1)
    grad_last(5)
    grad_last(3)
    grad_third(0)
    vector_step(2)
    for stream in CHAINS:
        r0, r1 = stream
        DZ[r0:r1] = DZ[r0:r1] + total_of(stream)
    tail_grad = [
        send(DZ.at[pl.ds(RL - LANG_TAIL, LANG_TAIL)], TLG, up),
        send(DZ.at[pl.ds(ROWS - VIS_TAIL, VIS_TAIL)], TVG, up),
    ]
    grad_third(7)
    vector_step(3)
    for w in (2, 1):
        grad_last(w)
    vector_step(4)
    vec_out[...] = AVA[5, 0:16]
    qb_out[...] = AVA[5, pl.ds(pl.multiple_of(16 + 8 * z, 8), 8)]

    arrived("tails", *tail_out, *tail_grad)
    before_l = jnp.where(z == 1, 0, 25 - 5 * z)
    before_v = jnp.where(z == 1, 0, 45 - 9 * z)
    for (r0, r1), size, pad, own_rows, off, before, tail_rows, out_ref, grad_ref, t_out, t_grad in (
        (LANG, WORDS, WORDS, own_l, off_l, before_l, LANG_TAIL, lang_out, lang_grad, TLO, TLG),
        (VIS, REGIONS, REGION_PAD, own_v, off_v, before_v, VIS_TAIL, vis_out, vis_grad, TVO, TVG),
    ):
        from_own = rows_from_slab((own_rows, r1 - r0), -off, 0, off, own_rows, size, pad)
        from_tail = rows_from_slab(
            (own_rows, tail_rows), own_rows - before, r1 - r0 - tail_rows, 0, off, size, pad
        )
        out_ref[...] = (
            dot_nn(from_own.astype(BF), OUTS[r0:r1]) + dot_nn(from_tail.astype(BF), t_out[...])
        ).astype(BF)
        exact = lax.Precision.HIGHEST
        grad_ref[...] = jnp.dot(
            from_own, DZ[r0:r1], precision=exact, preferred_element_type=F32
        ) + jnp.dot(from_tail, t_grad[...], precision=exact, preferred_element_type=F32)

    grad_last(0)
    grad_last(7)

    for copy in pending:
        copy.wait_send()
    for index, stream in list(stage_used):
        stage_free(index, stream)

    @pl.when(c == 1)
    def _():
        for copy in nears:
            copy.wait_send()
        for _, far_low, far_high in grad_nears:
            far_low.wait_send()
            far_high.wait_send()

    @pl.when(c == 0)
    def _():
        for near, _, _ in grad_nears:
            near.wait_send()
    assert counter[0] <= ssem.shape[0] and counter[1] <= rsem.shape[0], counter


N_SEND = 240
N_RECV = 160


def fused_layer(total_items, *operands):
    own_l, own_v = operands[0].shape[0], operands[1].shape[0]
    vmem = pl.BlockSpec(memory_space=pltpu.VMEM)
    smem = pl.BlockSpec(memory_space=pltpu.SMEM)
    shapes = [
        ((own_l, D), BF),
        ((own_v, D), BF),
        ((own_l, D), F32),
        ((own_v, D), F32),
        ((7, SHARE, D), F32),
        ((16, D), F32),
        ((8, D), F32),
    ]
    scratch = [
        ((7, D, D), BF),
        ((7, D, D), BF),
        ((2, 7, SHARE, D), BF),
        ((2, 7, HALF_PAIR, D), BF),
        ((2, 7, SHARE, D), BF),
        ((6, SLOTS, ROWS, D), BF),
        ((SLOTS, 8, TILE), F32),
        ((3, ROWS, D), BF),
        ((3, ROWS, D), BF),
        ((2, SLOTS, ROWS, D), BF),
        ((SLOTS, ROWS, D), BF),
        ((2, SLOTS, ROWS, TILE), BF),
        ((SLOTS, ROWS, D), BF),
        ((SLOTS, ROWS, D), BF),
        ((SLOTS, 3 * RL, RV), BF),
        ((2, SLOTS, 3 * RL, RL), BF),
        ((3, SLOTS, 3 * RL, RL), BF),
        ((ROWS, D), F32),
        ((ROWS, D), F32),
        ((3, ROWS, D), F32),
        ((3, ROWS, 1), F32),
        ((ROWS, D), F32),
        ((ROWS, D), BF),
        ((3, SHARE, D), BF),
        ((ROWS, 1), F32),
        ((8, D), F32),
        ((8, D), F32),
        ((8, D), F32),
        ((4, 8, 128), F32),
        ((3, 8, 128), F32),
        ((16, D), F32),
        ((8, D), F32),
        ((6, N_AR, D), F32),
        ((5, N_AR, D), F32),
        ((2, LANG_HEAD, D), BF),
        ((2, VIS_HEAD, D), BF),
        ((ROWS, D), BF),
        ((LANG_TAIL, D), BF),
        ((VIS_TAIL, D), BF),
        ((LANG_TAIL, D), F32),
        ((VIS_TAIL, D), F32),
    ]
    dma = pltpu.SemaphoreType.DMA
    return pl.pallas_call(
        partial(layer_kernel, total_items),
        out_shape=[jax.ShapeDtypeStruct(s, t) for s, t in shapes],
        in_specs=[vmem] * 4 + [smem] * 3 + [vmem] * (len(operands) - 7),
        out_specs=[vmem] * len(shapes),
        scratch_shapes=[pltpu.VMEM(s, t) for s, t in scratch]
        + [dma((N_SEND,)), dma((N_RECV,)), dma((3, 8)), dma((8,)), dma((3, 8)), dma((8,))],
        compiler_params=pltpu.CompilerParams(
            collective_id=0, has_side_effects=True, vmem_limit_bytes=VMEM_LIMIT
        ),
    )(*operands)


def unpack_kernel(lo, vo, lg, vg, wgrad, vec, qb, *outs):
    (lo_out, vo_out, lg_out, vg_out, proj, qv, outw, outb, exp, expb, con, conb, gain, shift) = outs
    lo_out[...] = lo[...]
    vo_out[...] = vo[...]
    lg_out[...] = lg[...]
    vg_out[...] = vg[...]
    width = HALF_PAIR
    for b in range(3):
        for j, lane in enumerate((0, 2 * width, width)):
            proj[b, j] = wgrad[b, :, lane : lane + width]
        outw[b] = wgrad[b, :, 3 * width :].T
        for j in range(2):
            qv[b, j : j + 1] = qb[b : b + 1, j * width : (j + 1) * width]
    for stream in range(2):
        exp[stream] = wgrad[3 + stream]
        con[stream] = wgrad[5 + stream]
    expb[...] = qb[3:5]
    outb[...] = vec[0:3]
    conb[...] = vec[3:5]
    gain[...] = vec[5:10]
    shift[...] = vec[10:15]


def unpack(packed, shapes):
    vmem = pl.BlockSpec(memory_space=pltpu.VMEM)
    return pl.pallas_call(
        unpack_kernel,
        out_shape=shapes,
        in_specs=[vmem] * len(packed),
        out_specs=[vmem] * len(shapes),
        compiler_params=pltpu.CompilerParams(vmem_limit_bytes=VMEM_LIMIT),
    )(*packed)


def on_device_fused(
    language_input,
    vision_input,
    word_lengths,
    region_counts,
    task_flags,
    language_cotangent,
    vision_cotangent,
    projection_weight,
    query_value_bias,
    output_weight,
    output_bias,
    expand_weight,
    expand_bias,
    contract_weight,
    contract_bias,
    norm_gain,
    norm_bias,
):
    packed = fused_layer(
        float(word_lengths.shape[0] * lax.axis_size("dp")),
        language_input,
        vision_input,
        language_cotangent,
        vision_cotangent,
        word_lengths,
        region_counts,
        task_flags.T,
        projection_weight,
        query_value_bias,
        output_weight,
        expand_weight,
        expand_bias,
        contract_weight.transpose(0, 2, 1),
        output_bias,
        contract_bias,
        norm_gain,
        norm_bias,
    )
    like = [
        (language_input, BF),
        (vision_input, BF),
        (language_input, F32),
        (vision_input, F32),
        (projection_weight, F32),
        (query_value_bias, F32),
        (output_weight, F32),
        (output_bias, F32),
        (expand_weight, F32),
        (expand_bias, F32),
        (contract_weight.transpose(0, 2, 1), F32),
        (contract_bias, F32),
        (norm_gain, F32),
        (norm_bias, F32),
    ]
    outs = list(unpack(packed, [jax.ShapeDtypeStruct(a.shape, t) for a, t in like]))
    outs[10] = outs[10].transpose(0, 2, 1)
    return tuple(outs)


def solution(mesh):
    in_specs = (
        P(("dp", "mp"), None),
        P(("dp", "mp"), None),
        P("dp"),
        P("dp"),
        P("dp", None),
        P(("dp", "mp"), None),
        P(("dp", "mp"), None),
        P(None, None, "dp", "mp"),
        P(None, None, "mp"),
        P(None, "mp", "dp"),
        P(),
        P(None, "dp", "mp"),
        P(None, "mp"),
        P(None, "mp", "dp"),
        P(),
        P(),
        P(),
    )
    out_specs = (
        P(("dp", "mp"), None),
        P(("dp", "mp"), None),
        P(("dp", "mp"), None),
        P(("dp", "mp"), None),
        P(None, None, "dp", "mp"),
        P(None, None, "mp"),
        P(None, "mp", "dp"),
        P(),
        P(None, "dp", "mp"),
        P(None, "mp"),
        P(None, "mp", "dp"),
        P(),
        P(),
        P(),
    )
    fused = dict(mesh.shape) == {"dp": 8, "mp": 4}
    return jax.shard_map(
        on_device_fused if fused else on_device, mesh=mesh, in_specs=in_specs, out_specs=out_specs, check_vma=False
    )
```

```python
from functools import partial
import math

import jax
import jax.numpy as jnp
from jax import lax
from jax.experimental import pallas as pl
from jax.experimental.pallas import tpu as pltpu
from jax.sharding import PartitionSpec as P

D = 768
HEADS = 12
WORDS = 20
REGIONS = 36
D_MODEL = D
D_HEAD = D // HEADS

EPSILON = 1e-12
MASKED = -1e30


def layer_norm(summed, gain, shift):
    center = summed - jnp.mean(summed, -1, keepdims=True)
    scaled = lax.rsqrt(jnp.mean(center * center, -1, keepdims=True) + EPSILON)
    normed = center * scaled
    return (normed * gain + shift, normed, scaled)


def norm_back(upstream, normed, scaled, gain):
    through = upstream * gain
    inner = (
        through
        - jnp.mean(through, -1, keepdims=True)
        - normed * jnp.mean(through * normed, -1, keepdims=True)
    )
    return (scaled * inner, jnp.sum(upstream * normed, 0), jnp.sum(upstream, 0))


def split_heads(rows, item_count):
    head_size = D // HEADS
    return rows.reshape(
        item_count, rows.shape[0] // item_count, rows.shape[1] // head_size, head_size
    )


def join_heads(block):
    return block.reshape(block.shape[0] * block.shape[1], block.shape[2] * block.shape[3])


def project(rows, weight, bias, item_count):
    mapped = jnp.einsum("rd,jde->jre", rows, weight, preferred_element_type=jnp.float32)
    query = split_heads((mapped[0] + bias[0]).astype(jnp.bfloat16), item_count)
    keys = split_heads(mapped[1].astype(jnp.bfloat16), item_count)
    values = split_heads((mapped[2] + bias[1]).astype(jnp.bfloat16), item_count)
    return (query, keys, values)


def masked_scores(query, keys, valid):
    scores = jnp.einsum("inhd,imhd->ihnm", query, keys, preferred_element_type=jnp.float32) * (
        1.0 / math.sqrt(D // HEADS)
    )
    return jnp.where(valid[:, None, None, :], scores, MASKED)


def attend(query, keys, values, valid):
    scores = masked_scores(query, keys, valid)
    highest = jnp.max(scores, -1, keepdims=True)
    raised = jnp.exp(scores - highest)
    summed = jnp.sum(raised, -1, keepdims=True)
    context = jnp.einsum(
        "ihnm,imhd->inhd",
        (raised / summed).astype(jnp.bfloat16),
        values,
        preferred_element_type=jnp.float32,
    )
    return (join_heads(context).astype(jnp.bfloat16), highest + jnp.log(summed))


def attend_back(query, keys, values, valid, log_total, context_grad):
    factor = 1.0 / math.sqrt(D // HEADS)
    upstream = context_grad.reshape(query.shape)
    weights = jnp.exp(masked_scores(query, keys, valid) - log_total)
    weight_grad = jnp.einsum(
        "inhd,imhd->ihnm", upstream, values, preferred_element_type=jnp.float32
    )
    score_grad = (
        weights * (weight_grad - jnp.sum(weight_grad * weights, -1, keepdims=True))
    ).astype(jnp.bfloat16)
    query_grad = (
        jnp.einsum("ihnm,imhd->inhd", score_grad, keys, preferred_element_type=jnp.float32) * factor
    ).astype(jnp.bfloat16)
    keys_grad = (
        jnp.einsum("ihnm,inhd->imhd", score_grad, query, preferred_element_type=jnp.float32)
        * factor
    ).astype(jnp.bfloat16)
    values_grad = jnp.einsum(
        "ihnm,inhd->imhd",
        weights.astype(jnp.bfloat16),
        upstream,
        preferred_element_type=jnp.float32,
    ).astype(jnp.bfloat16)
    return (join_heads(query_grad), join_heads(keys_grad), join_heads(values_grad))


def project_back(rows, query_grad, keys_grad, values_grad):
    stacked = jnp.stack([query_grad, keys_grad, values_grad])
    weight_grad = jnp.einsum("rd,jre->jde", rows, stacked, preferred_element_type=jnp.float32)
    bias_grad = jnp.stack(
        [jnp.sum(query_grad.astype(jnp.float32), 0), jnp.sum(values_grad.astype(jnp.float32), 0)]
    )
    return (weight_grad, bias_grad, stacked)


def gather_rows(language_rows, vision_rows):
    return (
        lax.all_gather(language_rows, "mp", axis=0, tiled=True),
        lax.all_gather(vision_rows, "mp", axis=0, tiled=True),
    )


def rows_of(language_part, vision_part):
    return (
        lax.all_to_all(language_part, "mp", split_axis=0, concat_axis=1, tiled=True),
        lax.all_to_all(vision_part, "mp", split_axis=0, concat_axis=1, tiled=True),
    )


def gather_grads(language_rows, vision_rows):
    return (
        lax.all_gather(language_rows, "mp", axis=0, tiled=True),
        lax.all_gather(vision_rows, "mp", axis=0, tiled=True),
    )


def grads_of(language_part, vision_part):
    return (
        lax.all_to_all(language_part, "mp", split_axis=1, concat_axis=2, tiled=True),
        lax.all_to_all(vision_part, "mp", split_axis=1, concat_axis=2, tiled=True),
    )


def matmul(left, right):
    return jnp.dot(left, right, preferred_element_type=jnp.float32)


def on_device(
    language_input,
    vision_input,
    word_lengths,
    region_counts,
    task_flags,
    language_cotangent,
    vision_cotangent,
    projection_weight,
    query_value_bias,
    output_weight,
    output_bias,
    expand_weight,
    expand_bias,
    contract_weight,
    contract_bias,
    norm_gain,
    norm_bias,
):
    item_count = word_lengths.shape[0]
    flag_total = lax.psum(jnp.sum(task_flags, 0), "dp")
    projection, out_weight, expand, contract = (
        lax.all_gather(projection_weight, "dp", axis=2, tiled=True),
        lax.all_gather(output_weight, "dp", axis=2, tiled=True),
        lax.all_gather(expand_weight, "dp", axis=1, tiled=True),
        lax.all_gather(contract_weight, "dp", axis=2, tiled=True),
    )
    projection_full, out_full, expand_full, contract_full = (
        lax.all_gather(projection, "mp", axis=3, tiled=True),
        lax.all_gather(out_weight, "mp", axis=1, tiled=True),
        lax.all_gather(expand, "mp", axis=2, tiled=True),
        lax.all_gather(contract, "mp", axis=1, tiled=True),
    )
    valid = [
        jnp.arange(WORDS, dtype=jnp.int32)[None, :] < word_lengths[:, None],
        jnp.arange(REGIONS, dtype=jnp.int32)[None, :] < region_counts[:, None],
    ]
    row_counts = [WORDS, REGIONS]
    inputs = [language_input.astype(jnp.float32), vision_input.astype(jnp.float32)]
    cross_rows = gather_rows(language_input, vision_input)
    cross_parts = [
        project(cross_rows[stream], projection[0], query_value_bias[0], item_count)
        for stream in range(2)
    ]
    cross_context = []
    cross_total = []
    for stream in range(2):
        other = 1 - stream
        context, log_total = attend(
            cross_parts[stream][0], cross_parts[other][1], cross_parts[other][2], valid[other]
        )
        cross_context.append(context)
        cross_total.append(log_total)
    moved = rows_of(cross_context[0], cross_context[1])
    branch = [matmul(moved[stream], out_full[0]) for stream in range(2)]
    first = [
        layer_norm(branch[stream] + output_bias[0] + inputs[stream], norm_gain[0], norm_bias[0])
        for stream in range(2)
    ]
    first_out = [first[stream][0].astype(jnp.bfloat16) for stream in range(2)]
    self_rows = gather_rows(first_out[0], first_out[1])
    self_parts = [
        project(self_rows[stream], projection[1 + stream], query_value_bias[1 + stream], item_count)
        for stream in range(2)
    ]
    self_context = []
    self_total = []
    for stream in range(2):
        context, log_total = attend(
            self_parts[stream][0], self_parts[stream][1], self_parts[stream][2], valid[stream]
        )
        self_context.append(context)
        self_total.append(log_total)
    moved = rows_of(self_context[0], self_context[1])
    branch = [matmul(moved[stream], out_full[1 + stream]) for stream in range(2)]
    second = [
        layer_norm(
            branch[stream] + output_bias[1 + stream] + first_out[stream].astype(jnp.float32),
            norm_gain[1 + stream],
            norm_bias[1 + stream],
        )
        for stream in range(2)
    ]
    second_out = [second[stream][0].astype(jnp.bfloat16) for stream in range(2)]
    feed_rows = gather_rows(second_out[0], second_out[1])
    before = [
        matmul(feed_rows[stream], expand[stream]) + expand_bias[stream] for stream in range(2)
    ]
    hidden = [
        jax.nn.gelu(before[stream], approximate=False).astype(jnp.bfloat16) for stream in range(2)
    ]
    moved = rows_of(hidden[0], hidden[1])
    branch = [matmul(moved[stream], contract_full[stream]) for stream in range(2)]
    third = [
        layer_norm(
            branch[stream] + contract_bias[stream] + second_out[stream].astype(jnp.float32),
            norm_gain[3 + stream],
            norm_bias[3 + stream],
        )
        for stream in range(2)
    ]
    language_out = third[0][0].astype(jnp.bfloat16)
    vision_out = third[1][0].astype(jnp.bfloat16)
    item_scale = task_flags.astype(jnp.float32) * (
        item_count * lax.axis_size("dp") / flag_total.astype(jnp.float32)
    )
    shard_index = lax.axis_index("mp")
    upstream = []
    for stream, cotangent in enumerate([language_cotangent, vision_cotangent]):
        per_row = jnp.repeat(
            item_scale[:, stream],
            row_counts[stream],
            total_repeat_length=item_count * row_counts[stream],
        )
        shard_rows = cotangent.shape[0]
        row_scale = lax.dynamic_slice_in_dim(per_row, shard_index * shard_rows, shard_rows)
        upstream.append(cotangent.astype(jnp.float32) * row_scale[:, None])
    third_back = [
        norm_back(upstream[stream], third[stream][1], third[stream][2], norm_gain[3 + stream])
        for stream in range(2)
    ]
    sent = gather_grads(
        third_back[0][0].astype(jnp.bfloat16), third_back[1][0].astype(jnp.bfloat16)
    )
    expand_local = []
    expand_bias_local = []
    contract_local = []
    before_grads = []
    for stream in range(2):
        hidden_grad = jnp.einsum(
            "rd,fd->rf", sent[stream], contract[stream], preferred_element_type=jnp.float32
        )
        contract_local.append(
            jnp.einsum(
                "rf,rd->fd", hidden[stream], sent[stream], preferred_element_type=jnp.float32
            )
        )
        unused, pull = jax.vjp(partial(jax.nn.gelu, approximate=False), before[stream])
        before_grad = pull(hidden_grad)[0].astype(jnp.bfloat16)
        expand_local.append(
            jnp.einsum(
                "rd,rf->df", feed_rows[stream], before_grad, preferred_element_type=jnp.float32
            )
        )
        expand_bias_local.append(jnp.sum(before_grad.astype(jnp.float32), 0))
        before_grads.append(before_grad[None])
    moved = grads_of(before_grads[0], before_grads[1])
    back = [
        jnp.einsum(
            "rf,df->rd", moved[stream][0], expand_full[stream], preferred_element_type=jnp.float32
        )
        for stream in range(2)
    ]
    second_grad = [third_back[stream][0] + back[stream] for stream in range(2)]
    second_back = [
        norm_back(second_grad[stream], second[stream][1], second[stream][2], norm_gain[1 + stream])
        for stream in range(2)
    ]
    sent = gather_grads(
        second_back[0][0].astype(jnp.bfloat16), second_back[1][0].astype(jnp.bfloat16)
    )
    self_weight = []
    self_bias = []
    self_out = []
    stacks = []
    for stream in range(2):
        context_grad = jnp.einsum(
            "rd,ed->re", sent[stream], out_weight[1 + stream], preferred_element_type=jnp.float32
        ).astype(jnp.bfloat16)
        self_out.append(
            jnp.einsum(
                "re,rd->ed", self_context[stream], sent[stream], preferred_element_type=jnp.float32
            )
        )
        grads = attend_back(
            self_parts[stream][0],
            self_parts[stream][1],
            self_parts[stream][2],
            valid[stream],
            self_total[stream],
            context_grad,
        )
        weight_part, bias_part, stacked = project_back(
            self_rows[stream], grads[0], grads[1], grads[2]
        )
        self_weight.append(weight_part)
        self_bias.append(bias_part)
        stacks.append(stacked)
    moved = grads_of(stacks[0], stacks[1])
    back = [
        jnp.einsum(
            "jre,jde->rd",
            moved[stream],
            projection_full[1 + stream],
            preferred_element_type=jnp.float32,
        )
        for stream in range(2)
    ]
    first_grad = [second_back[stream][0] + back[stream] for stream in range(2)]
    first_back = [
        norm_back(first_grad[stream], first[stream][1], first[stream][2], norm_gain[0])
        for stream in range(2)
    ]
    sent = gather_grads(
        first_back[0][0].astype(jnp.bfloat16), first_back[1][0].astype(jnp.bfloat16)
    )
    cross_out = jnp.einsum(
        "re,rd->ed", cross_context[0], sent[0], preferred_element_type=jnp.float32
    ) + jnp.einsum("re,rd->ed", cross_context[1], sent[1], preferred_element_type=jnp.float32)
    triples = [[None, None, None], [None, None, None]]
    for stream in range(2):
        other = 1 - stream
        context_grad = jnp.einsum(
            "rd,ed->re", sent[stream], out_weight[0], preferred_element_type=jnp.float32
        ).astype(jnp.bfloat16)
        grads = attend_back(
            cross_parts[stream][0],
            cross_parts[other][1],
            cross_parts[other][2],
            valid[other],
            cross_total[stream],
            context_grad,
        )
        triples[stream][0] = grads[0]
        triples[other][1] = grads[1]
        triples[other][2] = grads[2]
    results = [
        project_back(cross_rows[stream], triples[stream][0], triples[stream][1], triples[stream][2])
        for stream in range(2)
    ]
    cross_weight = results[0][0] + results[1][0]
    cross_bias = results[0][1] + results[1][1]
    moved = grads_of(results[0][2], results[1][2])
    back = [
        jnp.einsum(
            "jre,jde->rd", moved[stream], projection_full[0], preferred_element_type=jnp.float32
        )
        for stream in range(2)
    ]
    language_grad = first_back[0][0] + back[0]
    vision_grad = first_back[1][0] + back[1]
    projection_stack = jnp.stack([cross_weight, self_weight[0], self_weight[1]])
    output_stack = jnp.stack([cross_out, self_out[0], self_out[1]])
    projection_grad, output_weight_grad, expand_grad, contract_grad = (
        lax.psum_scatter(projection_stack, "dp", scatter_dimension=2, tiled=True),
        lax.psum_scatter(output_stack, "dp", scatter_dimension=2, tiled=True),
        lax.psum_scatter(jnp.stack(expand_local), "dp", scatter_dimension=1, tiled=True),
        lax.psum_scatter(jnp.stack(contract_local), "dp", scatter_dimension=2, tiled=True),
    )
    query_value_grad, expand_bias_grad = lax.psum(
        (jnp.stack([cross_bias, self_bias[0], self_bias[1]]), jnp.stack(expand_bias_local)), "dp"
    )
    output_bias_local = jnp.stack(
        [
            jnp.sum(first_back[0][0], 0) + jnp.sum(first_back[1][0], 0),
            jnp.sum(second_back[0][0], 0),
            jnp.sum(second_back[1][0], 0),
        ]
    )
    contract_bias_local = jnp.stack([jnp.sum(third_back[0][0], 0), jnp.sum(third_back[1][0], 0)])
    gain_local = jnp.stack(
        [
            first_back[0][1] + first_back[1][1],
            second_back[0][1],
            second_back[1][1],
            third_back[0][1],
            third_back[1][1],
        ]
    )
    shift_local = jnp.stack(
        [
            first_back[0][2] + first_back[1][2],
            second_back[0][2],
            second_back[1][2],
            third_back[0][2],
            third_back[1][2],
        ]
    )
    output_bias_grad, contract_bias_grad, norm_gain_grad, norm_bias_grad = lax.psum(
        (output_bias_local, contract_bias_local, gain_local, shift_local), ("dp", "mp")
    )
    return (
        language_out,
        vision_out,
        language_grad,
        vision_grad,
        projection_grad,
        query_value_grad,
        output_weight_grad,
        output_bias_grad,
        expand_grad,
        expand_bias_grad,
        contract_grad,
        contract_bias_grad,
        norm_gain_grad,
        norm_bias_grad,
    )


MESH = pl.DeviceIdType.MESH
BF = jnp.bfloat16
F32 = jnp.float32
SLOTS = 4
RL = SLOTS * WORDS
REGION_PAD = 40
RV = SLOTS * REGION_PAD
ROWS = RL + RV
SHARE = 96
HALF_PAIR = 2 * SHARE
LANG_HEAD = 16
VIS_HEAD = 32
LANG_TAIL = 32
VIS_TAIL = 64
N_AR = 32
NT = 3
TILE = 256
LANG = (0, RL)
V1 = (RL, RL + RV // 2)
V2 = (RL + RV // 2, ROWS)
VIS = (RL, ROWS)
BOTH = (0, ROWS)
CHAINS = (V1, V2, LANG)
TRIM = {V1: V1[1], V2: V2[0] + 48, LANG: LANG[0] + 64}
SELF = {LANG: 1, V1: 2, V2: 2}
EXPAND = {LANG: 3, V1: 4, V2: 4}
CONTRACT = {LANG: 5, V1: 6, V2: 6}
PARTS = {w: (w, slice(0, 768)) for w in range(1, 7)} | {0: (0, slice(0, 384)), 7: (0, slice(384, 768))}
VMEM_LIMIT = 63 * 1024 * 1024


def dot_nn(left, right):
    return lax.dot_general(left, right, (((1,), (0,)), ((), ())), preferred_element_type=F32)


def dot_nt(left, right):
    return lax.dot_general(left, right, (((1,), (1,)), ((), ())), preferred_element_type=F32)


def dot_tn(left, right):
    return lax.dot_general(left, right, (((0,), (0,)), ((), ())), preferred_element_type=F32)


def head_mask(first_lane, dtype):
    lane = lax.broadcasted_iota(jnp.int32, (1, TILE), 1) - first_lane
    return [
        jnp.where((lane >= 64 * h) & (lane < 64 * h + 64), 1.0, 0.0).astype(dtype) for h in range(3)
    ]


def item_rows(shape, dim, first, size, pad):
    row = lax.broadcasted_iota(jnp.int32, shape, dim) + first
    item = sum(jnp.where(row >= pad * j, 1, 0) for j in range(1, SLOTS))
    return row - (pad - size) * item, row - pad * item < size


def rows_into_slab(shape, shift, count, size, pad):
    place, real = item_rows(shape, 0, 0, size, pad)
    column = lax.broadcasted_iota(jnp.int32, shape, 1)
    return jnp.where((column - place == shift) & real & (place < count), 1.0, 0.0)


def rows_from_slab(shape, shift, first, low, high, size, pad):
    place, real = item_rows(shape, 1, first, size, pad)
    row = lax.broadcasted_iota(jnp.int32, shape, 0)
    return jnp.where((place - row == shift) & real & (row >= low) & (row < high), 1.0, 0.0)


def layer_kernel(
    total_items,
    lang,
    vis,
    lcot,
    vcot,
    lengths,
    regions,
    flags,
    projection,
    query_value,
    out_weight,
    expand,
    expand_b,
    contract,
    out_bias,
    contract_b,
    gains,
    shifts,
    lang_out,
    vis_out,
    lang_grad,
    vis_grad,
    wgrad,
    vec_out,
    qb_out,
    W,
    G,
    RD,
    RX,
    R2,
    A,
    KV,
    RSB,
    STG,
    QVK,
    D,
    C,
    H,
    GP,
    PCL,
    PCV,
    PS,
    PART,
    PZ,
    NORM,
    RSTD,
    DZ,
    COT,
    SH,
    FLAG,
    QO,
    QB,
    QR,
    CA,
    CR,
    VG,
    QG,
    AVA,
    AVR,
    LVA,
    LVR,
    HL,
    HV,
    OUTS,
    TLO,
    TVO,
    TLG,
    TVG,
    ssem,
    rsem,
    wsem,
    wsem_z,
    gsem,
    gsem2,
):
    d = lax.axis_index("dp")
    z = lax.axis_index("mp")
    c = d % 2
    k = d // 2
    k_flip = [k + 1 - 2 * (k % 2), (k + 2) % 4, 3 - k]
    sib = (d + 1 - 2 * c, z)
    zp = (d, z + 1 - 2 * (z % 2))
    z2 = (z + 2) % 4
    up = (d, (z + 1) % 4)
    down = (d, (z + 3) % 4)
    plane = [(2 * kf + c, z) for kf in k_flip]
    far = (2 * k + 1, z2)

    pending, pending_z = [], []
    counter = [0, 0]

    def remote(src, dst, send, recv, device):
        return pltpu.make_async_remote_copy(
            src_ref=src, dst_ref=dst, send_sem=send, recv_sem=recv, device_id=device, device_id_type=MESH
        )

    def send(src, dst, device, recv=None, keep=True):
        slot = counter[0]
        counter[0] += 1
        if recv is None:
            recv = rsem.at[counter[1]]
            counter[1] += 1
        copy = remote(src, dst, ssem.at[slot], recv, device)
        copy.start()
        if keep:
            pending.append(copy)
        return copy

    def wait_bytes(ref, sem):
        pltpu.make_async_copy(ref, ref, sem).wait()

    def arrived(name, *copies):
        with jax.named_scope("wait_" + name):
            for copy in copies:
                copy.wait_recv()

    barrier = pltpu.get_barrier_semaphore()
    peers = [sib, up, down, (d, z2), (d + 1 - 2 * c, z2)] + plane
    for peer in peers:
        pl.semaphore_signal(barrier, inc=1, device_id=peer, device_id_type=MESH)

    def weight_first(part):
        w, lanes = PARTS[part]
        row = pl.ds(pl.multiple_of(d * SHARE, 16), SHARE)
        slot = counter[0]
        counter[0] += 1
        share = SH.at[w] if w < 3 else (expand.at[w - 3] if w < 5 else contract.at[w - 5])
        share = share.at[:, lanes]
        target = W.at[w, row, lanes]
        near = remote(share, target, ssem.at[slot], wsem_z.at[part], sib)
        own = pltpu.make_async_copy(share, target, wsem_z.at[part])

        @pl.when(c == 1)
        def _():
            near.start()

        @pl.when(c == 0)
        def _():
            own.start()

        send(share, target, far, wsem_z.at[part])
        nears.append(near)

    def place(width, first):
        row = lax.broadcasted_iota(jnp.int32, (width, D_MODEL), 0)
        column = lax.broadcasted_iota(jnp.int32, (width, D_MODEL), 1)
        return jnp.where(column - row == first, 1.0, 0.0).astype(BF)

    def attention_share(b):
        SH[b] = (
            dot_nn(projection[b, 0], place(HALF_PAIR, 0))
            + dot_nn(projection[b, 2], place(HALF_PAIR, HALF_PAIR))
            + dot_nn(projection[b, 1], place(HALF_PAIR, 2 * HALF_PAIR))
            + dot_tn(out_weight[b], place(HALF_PAIR, 3 * HALF_PAIR))
        ).astype(BF)

    nears = []
    attention_share(0)

    n_items = lengths.shape[0]
    first_item = 3 * z + jnp.minimum(z, 1)
    KV[0] = jnp.full(KV.shape[1:], -1.0, F32)
    for row, source, size, pad, first_row in ((0, lengths, WORDS, WORDS, 0), (1, regions, REGIONS, REGION_PAD, RL)):
        lane = lax.broadcasted_iota(jnp.int32, (1, TILE), 1)
        owner = jnp.full((1, TILE), -1.0, F32)
        slab_row = lax.broadcasted_iota(jnp.int32, (SLOTS * pad, 1), 0)
        flag = jnp.zeros((SLOTS * pad, 1), F32)
        for j in range(SLOTS):
            item = jnp.minimum(first_item + j, n_items - 1)
            valid = (lane >= j * pad) & (lane < j * pad + source[item]) & (lane < j * pad + size)
            owner = jnp.where(valid, float(j), owner)
            inside = (slab_row >= j * pad) & (slab_row < (j + 1) * pad)
            flag = jnp.where(inside, flags[row, item].astype(F32), flag)
            if row == 1 and j % 2 == 1:
                pair = jnp.full((1, TILE), -1.0, F32)
                for i in (0, 1):
                    other = jnp.minimum(first_item + j - 1 + i, n_items - 1)
                    valid = (lane >= i * pad) & (lane < i * pad + source[other]) & (lane < i * pad + size)
                    pair = jnp.where(valid, float(j - 1 + i), pair)
                KV[0, 2 + j // 2 : 3 + j // 2] = pair
        KV[0, row : row + 1] = owner
        FLAG[first_row : first_row + SLOTS * pad] = flag
        count = flags[row, 0]
        for j in range(1, n_items):
            count = count + flags[row, j]
        CA[0, row : row + 1] = jnp.full((1, 128), count.astype(F32), F32)
    QO[...] = jnp.zeros_like(QO)
    for b in range(3):
        QO[b : b + 1, 0:HALF_PAIR] = query_value[b, 0:1]
        QO[b : b + 1, HALF_PAIR : 2 * HALF_PAIR] = query_value[b, 1:2]
    QO[3:5] = expand_b[...]

    for first, last in ((TRIM[LANG], LANG[1]), (TRIM[V2], V2[1])):
        A[:, 2, first:last] = jnp.zeros((6, last - first, D_MODEL), BF)
        RSB[2, first:last] = jnp.zeros((last - first, D_MODEL), BF)
    VG[...] = jnp.zeros_like(VG)
    QG[...] = jnp.zeros_like(QG)
    pl.semaphore_wait(barrier, len(peers))

    pair_rows = pl.ds(pl.multiple_of(k * HALF_PAIR, 16), HALF_PAIR)

    def rows_of_chip(chip, first=0, count=HALF_PAIR):
        return pl.ds(pl.multiple_of(chip * HALF_PAIR + first, 16), count)

    def weight_second(part):
        w, lanes = PARTS[part]
        block = W.at[w, pair_rows, lanes]
        wait_bytes(block, wsem_z.at[part])
        for j in range(2):
            send(block, block, plane[j], wsem.at[j, part])

    def weight_third(part):
        w, lanes = PARTS[part]
        for j in range(2):
            wait_bytes(W.at[w, pair_rows, lanes], wsem.at[j, part])
            half = W.at[w, rows_of_chip(k_flip[j], j * SHARE, SHARE), lanes]
            send(half, half, plane[1 - j], wsem.at[2, part])

    def weight_ready(part):
        w, lanes = PARTS[part]
        wait_bytes(W.at[w, pair_rows, lanes], wsem.at[2, part])

    off_l = jnp.where(z == 0, 0, 20 - 5 * z)
    off_v = jnp.where(z == 0, 0, 36 - 9 * z)
    n_l = jnp.where(z == 0, 4 * WORDS, 3 * WORDS)
    n_v = jnp.where(z == 0, 4 * REGIONS, 3 * REGIONS)
    own_l = lang.shape[0]
    own_v = vis.shape[0]
    def start_z(source, target, stream, device, big):
        slot, recv = counter[0], rsem.at[counter[1]]
        counter[0] += 1
        counter[1] += 1
        copies = []
        for last in (stream[1], TRIM[stream]):
            rows = pl.ds(stream[0], last - stream[0])
            copies.append(remote(source.at[rows], target.at[rows], ssem.at[slot], recv, device))
        if TRIM[stream] == stream[1]:
            copies[0].start()
            return copies[0].wait_send, copies[0].wait_recv

        @pl.when(big)
        def _():
            copies[0].start()

        @pl.when(jnp.logical_not(big))
        def _():
            copies[1].start()

        def finish(condition, full, cut):
            def wait():
                @pl.when(condition)
                def _():
                    full()

                @pl.when(jnp.logical_not(condition))
                def _():
                    cut()

            return wait

        other = z == (1 if big is own_big else 0)
        return (
            finish(big, copies[0].wait_send, copies[1].wait_send),
            finish(other, copies[0].wait_recv, copies[1].wait_recv),
        )

    own_big, mate_big = z == 0, z == 1
    rows, near_rows, far_rows, near, far_sum, z_sum, handles = {}, {}, {}, {}, {}, {}, {}
    out_lanes, all_lanes = slice(512, 768), slice(0, 768)

    def gather_start(p, stream):
        part = pl.ds(stream[0], stream[1] - stream[0])
        near_rows[stream] = send(A.at[p, 0, part], A.at[p, 1, part], sib)
        sent, arrives = start_z(A.at[p, 0], A.at[p, 2], stream, zp, own_big)
        pending_z.append(sent)
        rows[stream] = (p, part, arrives)

    def pass_on(stream):
        p, part, arrives = rows[stream]
        arrives()
        far_rows[stream] = send(A.at[p, 2, part], A.at[p, 3, part], sib)

    def all_arrived(stream):
        near_rows[stream].wait_recv()
        far_rows[stream].wait_recv()

    def own_slab(index, source_l, source_v, copies, target):
        arrived("heads", *copies)
        for (r0, r1), size, pad, own, off, count, source, head, head_rows in (
            (VIS, REGIONS, REGION_PAD, own_v, off_v, n_v, source_v, HV, VIS_HEAD),
            (LANG, WORDS, WORDS, own_l, off_l, n_l, source_l, HL, LANG_HEAD),
        ):
            inside = rows_into_slab((r1 - r0, own), off, count, size, pad).astype(BF)
            beyond = rows_into_slab((r1 - r0, head_rows), off - own, count, size, pad).astype(BF)
            target[r0:r1] = (dot_nn(inside, source[...]) + dot_nn(beyond, head[index])).astype(BF)

    stage_used = {}

    def stage_free(index, stream):
        sent = stage_used.pop((index, stream), None)
        if sent is not None:
            sent()

    def partial_nt(lhs_ref, stream, w, lanes):
        r0, r1 = stream
        rows = r1 - r0
        stage_free(0, stream)
        stage_free(1, stream)
        for n in range(NT):
            column = slice(n * TILE, (n + 1) * TILE)
            lhs = lhs_ref[:, r0:r1, :]
            lhs = lhs.reshape(SLOTS * rows, lhs.shape[-1])
            out = dot_nt(lhs, W[w, column, lanes])
            PART[r0:r1, column] = out[:rows]
            STG[0, r0:r1, column] = out[rows : 2 * rows].astype(BF)
            PZ[r0:r1, column] = out[2 * rows : 3 * rows]
            STG[1, r0:r1, column] = out[3 * rows :].astype(BF)

    def stage_send(index, stream, device):
        rows = pl.ds(stream[0], stream[1] - stream[0])
        copy = send(STG.at[index, rows], RSB.at[index, rows], device, keep=False)
        stage_used[index, stream] = copy.wait_send
        return copy

    def sums_after(stream, lhs, w, lanes):
        partial_nt(lhs, stream, w, lanes)
        far_sum[stream] = stage_send(1, stream, sib)
        near[stream] = stage_send(0, stream, sib)

    def sums_on(stream):
        r0, r1 = stream
        far_sum[stream].wait_recv()
        stage_free(2, stream)
        STG[2, r0:r1] = (PZ[r0:r1] + RSB[1, r0:r1].astype(F32)).astype(BF)
        sent, z_sum[stream] = start_z(STG.at[2], RSB.at[2], stream, zp, mate_big)
        stage_used[2, stream] = sent

    def total_of(stream):
        r0, r1 = stream
        near[stream].wait_recv()
        z_sum[stream]()
        return PART[r0:r1] + RSB[0, r0:r1].astype(F32) + RSB[2, r0:r1].astype(F32)

    mask_q = head_mask(0, BF)
    mask_c = head_mask(64, BF)
    mask_q32 = head_mask(0, F32)
    mask_c32 = head_mask(64, F32)
    factor = 1.0 / math.sqrt(D_HEAD)

    def attend_slab(QV, Cb, crossed, stream, s):
        def one(queries, keys_rows, kv_row, item_size, first_item_of, P):
            (q0, q1), (k0, k1) = queries, keys_rows
            nq, nk = q1 - q0, k1 - k0
            query = QV[s, q0:q1, 0:256]
            keys = QV[s, k0:k1, 384:640]
            values = QV[s, k0:k1, 128:384]
            spread = jnp.concatenate([query * mask_q[h] for h in range(3)], 0)
            scores = dot_nt(spread, keys) * factor
            row = lax.broadcasted_iota(jnp.int32, (nq, nk), 0)
            item = jnp.full((nq, nk), float(first_item_of), F32)
            for j in range(1, nq // item_size):
                item = item + jnp.where(row >= j * item_size, 1.0, 0.0)
            same = item == KV[s, kv_row : kv_row + 1, 0:nk]
            scores = jnp.where(same[None], scores.reshape(3, nq, nk), MASKED)
            raised = jnp.exp(scores - jnp.max(scores, -1, keepdims=True))
            weights = (raised / jnp.sum(raised, -1, keepdims=True)).astype(BF).reshape(3 * nq, nk)
            P[s] = weights
            context = dot_nn(weights, values).reshape(3, nq, TILE)
            Cb[s, q0:q1] = (
                context[0] * mask_c32[0] + context[1] * mask_c32[1] + context[2] * mask_c32[2]
            ).astype(BF)

        if stream == LANG:
            if crossed:
                one(LANG, VIS, 1, WORDS, 0, PCL)
            else:
                one(LANG, LANG, 0, WORDS, 0, PS.at[0])
        else:
            half = (V1, V2).index(stream)
            if crossed:
                one(stream, LANG, 0, REGION_PAD, 2 * half, PCV.at[half])
            else:
                one(stream, stream, 2 + half, REGION_PAD, 2 * half, PS.at[1 + half])

    def attend_back_slab(QV, crossed, stream, s):
        def one(queries, keys_rows, P):
            (q0, q1), (k0, k1) = queries, keys_rows
            nq = q1 - q0
            query = QV[s, q0:q1, 0:256]
            keys = QV[s, k0:k1, 384:640]
            values = QV[s, k0:k1, 128:384]
            spread = jnp.concatenate([query * mask_q[h] for h in range(3)], 0)
            upstream = D[s, q0:q1, 512:768]
            up_spread = jnp.concatenate([upstream * mask_c[h] for h in range(3)], 0)
            weights = P[s]
            weights32 = weights.astype(F32)
            weight_grad = dot_nt(up_spread, values)
            score_grad = (
                weights32
                * (weight_grad - jnp.sum(weight_grad * weights32, -1, keepdims=True))
            ).astype(BF)
            dq = dot_nn(score_grad, keys).reshape(3, nq, TILE)
            dq = (dq[0] * mask_q32[0] + dq[1] * mask_q32[1] + dq[2] * mask_q32[2]) * factor
            dk = dot_tn(score_grad, spread) * factor
            dv = dot_tn(weights, up_spread)
            return dq, dk, dv

        if crossed:
            half = RV // 2
            dq_l, dk_v, dv_v = one(LANG, VIS, PCL)
            dq_1, dk_1, dv_1 = one(V1, LANG, PCV.at[0])
            dq_2, dk_2, dv_2 = one(V2, LANG, PCV.at[1])
            results = {
                LANG: (dq_l, dk_1 + dk_2, dv_1 + dv_2),
                V1: (dq_1, dk_v[:half], dv_v[:half]),
                V2: (dq_2, dk_v[half:], dv_v[half:]),
            }
        else:
            results = {stream: one(stream, stream, PS.at[0 if stream == LANG else 1 + (V1, V2).index(stream)])}
        for (r0, r1), (dq, dk, dv) in results.items():
            D[s, r0:r1, 0:128] = dq[:, :128].astype(BF)
            D[s, r0:r1, 128:256] = (dq[:, 128:] + dv[:, :128]).astype(BF)
            D[s, r0:r1, 256:384] = dv[:, 128:].astype(BF)
            D[s, r0:r1, 384:640] = dk.astype(BF)
            D[s, r0:r1, 640:768] = jnp.zeros((r1 - r0, 128), BF)

    def forward_norm(value, index, gain_row, r0, r1):
        center = value - jnp.mean(value, -1, keepdims=True)
        scaled = lax.rsqrt(jnp.mean(center * center, -1, keepdims=True) + EPSILON)
        normed = center * scaled
        NORM[index, r0:r1] = normed
        RSTD[index, r0:r1] = scaled
        return normed * gains[gain_row : gain_row + 1] + shifts[gain_row : gain_row + 1]

    def backward_norm(upstream, index, gain_row, bias_row, r0, r1):
        normed = NORM[index, r0:r1]
        through = upstream * gains[gain_row : gain_row + 1]
        inner = (
            through
            - jnp.mean(through, -1, keepdims=True)
            - normed * jnp.mean(through * normed, -1, keepdims=True)
        )
        result = RSTD[index, r0:r1] * inner
        VG[5 + gain_row : 6 + gain_row] += jnp.sum(upstream * normed, 0, keepdims=True)
        VG[10 + gain_row : 11 + gain_row] += jnp.sum(upstream, 0, keepdims=True)
        VG[bias_row : bias_row + 1] += jnp.sum(result, 0, keepdims=True)
        return result

    def rows_of(p, stream):
        r0, r1 = stream
        return A[p, :, r0:r1, :].reshape(SLOTS * (r1 - r0), D_MODEL)

    def tile_columns():
        return [slice(n * TILE, (n + 1) * TILE) for n in range(NT)]

    def project(stream, w):
        r0, r1 = stream
        for column in tile_columns():
            mapped = dot_nn(rows_of(1, stream), W[w, :, column]) + QB[w : w + 1, column]
            QVK[1, :, r0:r1, column] = mapped.astype(BF).reshape(SLOTS, r1 - r0, TILE)

    def project_cross(g):
        for column in tile_columns():
            rows = A[0, 2 * g : 2 * g + 2].reshape(2 * ROWS, D_MODEL)
            mapped = dot_nn(rows, W[0, :, column]) + QB[0:1, column]
            QVK[0, 2 * g : 2 * g + 2, :, column] = mapped.astype(BF).reshape(2, ROWS, TILE)

    def attend(stream, b):
        for s in range(SLOTS):
            attend_slab(QVK.at[b], C.at[b], b == 0, stream, s)

    def expand_rows(stream):
        r0, r1 = stream
        w = EXPAND[stream]
        for column in tile_columns():
            before = dot_nn(rows_of(2, stream), W[w, :, column]) + QB[w : w + 1, column]
            half = 0.5 * (1.0 + lax.erf(before * math.sqrt(0.5)))
            slope = half + before * jnp.exp(-0.5 * before * before) * (1.0 / math.sqrt(2.0 * math.pi))
            H[:, r0:r1, column] = (before * half).astype(BF).reshape(SLOTS, r1 - r0, TILE)
            GP[:, r0:r1, column] = slope.astype(BF).reshape(SLOTS, r1 - r0, TILE)

    def hidden_gradient(stream):
        r0, r1 = stream
        rows = SLOTS * (r1 - r0)
        for column in tile_columns():
            up_hidden = dot_nn(rows_of(3, stream), W[CONTRACT[stream], :, column])
            slope = GP[:, r0:r1, column].reshape(rows, TILE)
            D[:, r0:r1, column] = (up_hidden * slope.astype(F32)).astype(BF).reshape(SLOTS, r1 - r0, TILE)

    def context_gradient(p, stream, w):
        r0, r1 = stream
        upstream = dot_nn(rows_of(p, stream), W[w, :, 512:768])
        D[:, r0:r1, 512:768] = upstream.astype(BF).reshape(SLOTS, r1 - r0, TILE)

    def attend_gradient(stream, b):
        for s in range(SLOTS):
            attend_back_slab(QVK.at[b], b == 0, stream, s)

    def all_rows(ref, r0, r1, lanes):
        value = ref[:, r0:r1, lanes]
        return value.reshape(SLOTS * (r1 - r0), value.shape[-1])

    def weight_grad(w, lhs_p, rhs_ref, r0, r1, lanes=slice(0, 768)):
        for m in range(NT):
            column = slice(m * TILE, (m + 1) * TILE)
            left = all_rows(A.at[lhs_p], r0, r1, column)
            G[w, column, lanes] = dot_tn(left, all_rows(rhs_ref, r0, r1, lanes)).astype(BF)

    def attention_weight_grad(w, x_p, b_p, Cb, r0, r1, middle=None):
        if middle is None:
            weight_grad(w, x_p, D, r0, r1, slice(0, 512))
        else:
            weight_grad(w, x_p, D, r0, r1, slice(0, 384))
            middle()
            weight_grad(w, x_p, D, r0, r1, slice(384, 512))
        for m in range(NT):
            column = slice(m * TILE, (m + 1) * TILE)
            G[w, column, 512:768] = (
                dot_tn(all_rows(A.at[x_p], r0, r1, column), all_rows(D, r0, r1, slice(512, 768)))
                + dot_tn(all_rows(A.at[b_p], r0, r1, column), all_rows(Cb, r0, r1, slice(0, 256)))
            ).astype(BF)

    def bias_grad(row, r0, r1):
        total = jnp.zeros((1, D_MODEL), F32)
        for s in range(SLOTS):
            total = total + jnp.sum(D[s, r0:r1].astype(F32), 0, keepdims=True)
        QG[row : row + 1] = total

    def grad_first(part):
        w, lanes = PARTS[part]
        for j in range(2):
            half = rows_of_chip(k_flip[2], (1 - j) * SHARE, SHARE)
            send(G.at[w, half, lanes], RD.at[j, w, :, lanes], plane[j], gsem.at[2, part])

    def grad_second(part):
        w, lanes = PARTS[part]
        wait_bytes(RD.at[:, w, :, lanes], gsem.at[2, part])
        for j in range(2):
            half = rows_of_chip(k_flip[1 - j], (1 - j) * SHARE, SHARE)
            G[w, half, lanes] = (G[w, half, lanes].astype(F32) + RD[j, w, :, lanes].astype(F32)).astype(BF)
        for j in range(2):
            send(G.at[w, rows_of_chip(k_flip[j]), lanes], RX.at[j, w, :, lanes], plane[j], gsem.at[j, part])

    grad_nears = []

    def grad_third(part):
        w, lanes = PARTS[part]
        for j in range(2):
            wait_bytes(RX.at[j, w, :, lanes], gsem.at[j, part])
        total = G[w, pair_rows, lanes].astype(F32)
        total = total + RX[0, w, :, lanes].astype(F32) + RX[1, w, :, lanes].astype(F32)
        G[w, pair_rows, lanes] = total.astype(BF)
        low = G.at[w, rows_of_chip(k, 0, SHARE), lanes]
        high = G.at[w, rows_of_chip(k, SHARE, SHARE), lanes]
        slot = counter[0]
        counter[0] += 2
        here, there = R2.at[0, w, :, lanes], R2.at[1, w, :, lanes]
        own = pltpu.make_async_copy(low, here, gsem2.at[part])
        near = remote(high, here, ssem.at[slot], gsem2.at[part], sib)
        far_low = remote(low, there, ssem.at[slot], gsem2.at[part], (2 * k, z2))
        far_high = remote(high, there, ssem.at[slot + 1], gsem2.at[part], (2 * k + 1, z2))

        @pl.when(c == 0)
        def _():
            own.start()
            near.start()

        @pl.when(c == 1)
        def _():
            far_low.start()
            far_high.start()

        grad_nears.append((near, far_low, far_high))

    def grad_last(part):
        w, lanes = PARTS[part]
        wait_bytes(R2.at[:, w, :, lanes], gsem2.at[part])
        wgrad[w, :, lanes] = R2[0, w, :, lanes].astype(F32) + R2[1, w, :, lanes].astype(F32)

    def count_step(stage, peer):
        count_copies[stage].wait_recv()
        CA[stage + 1] = CA[stage] + CR[stage]
        if peer is not None:
            count_copies.append(send(CA.at[stage + 1], CR.at[stage + 1], peer))

    VG[...] = jnp.zeros_like(VG)
    QG[...] = jnp.zeros_like(QG)
    def send_heads(index, source_l, source_v):
        handles["heads", index] = (
            send(source_l.at[pl.ds(0, LANG_HEAD)], HL.at[index], down),
            send(source_v.at[pl.ds(0, VIS_HEAD)], HV.at[index], down),
        )

    def send_small():
        handles["kv"] = (send(KV.at[0], KV.at[1], sib), send(KV.at[0], KV.at[2], zp))
        handles["count"] = [send(CA.at[0], CR.at[0], sib)]
        handles["bias"] = send(QO, QR, (d, z2))

    def pass_keys():
        for copy in handles["kv"]:
            copy.wait_recv()
        handles["kv_far"] = send(KV.at[2], KV.at[3], sib)

    def take_small():
        handles["bias"].wait_recv()
        QB[...] = jnp.where(c == 1, QR[...], QO[...])
        handles["kv_far"].wait_recv()

    def count_step(stage, peer):
        handles["count"][stage].wait_recv()
        CA[stage + 1] = CA[stage] + CR[stage]
        if peer is not None:
            handles["count"].append(send(CA.at[stage + 1], CR.at[stage + 1], peer))

    def first_norm(stream):
        r0, r1 = stream
        value = total_of(stream) + out_bias[0:1] + A[0, 0, r0:r1].astype(F32)
        A[1, 0, r0:r1] = forward_norm(value, 0, 0, r0, r1).astype(BF)
        gather_start(1, stream)

    def second_norm(stream):
        r0, r1 = stream
        n = 1 if stream == LANG else 2
        value = total_of(stream) + out_bias[n : n + 1] + A[1, 0, r0:r1].astype(F32)
        A[2, 0, r0:r1] = forward_norm(value, 1, n, r0, r1).astype(BF)
        gather_start(2, stream)

    def last_norm(stream):
        r0, r1 = stream
        n = 0 if stream == LANG else 1
        value = total_of(stream) + contract_b[n : n + 1] + A[2, 0, r0:r1].astype(F32)
        OUTS[r0:r1] = forward_norm(value, 2, 3 + n, r0, r1).astype(BF)
        scale = total_items / CA[3, n : n + 1, 0:1]
        upstream = COT[r0:r1].astype(F32) * (FLAG[r0:r1] * scale)
        result = backward_norm(upstream, 2, 3 + n, 3 + n, r0, r1)
        DZ[r0:r1] = result
        A[3, 0, r0:r1] = result.astype(BF)
        gather_start(3, stream)

    def second_norm_back(stream):
        r0, r1 = stream
        n = 1 if stream == LANG else 2
        result = backward_norm(DZ[r0:r1] + total_of(stream), 1, n, n, r0, r1)
        DZ[r0:r1] = result
        A[4, 0, r0:r1] = result.astype(BF)
        gather_start(4, stream)

    def first_norm_back(stream):
        r0, r1 = stream
        result = backward_norm(DZ[r0:r1] + total_of(stream), 0, 0, 0, r0, r1)
        DZ[r0:r1] = result
        A[5, 0, r0:r1] = result.astype(BF)
        gather_start(5, stream)

    def final_sum(stream):
        r0, r1 = stream
        DZ[r0:r1] = DZ[r0:r1] + total_of(stream)

    quarter = jnp.where(c == 0, z, z2)
    vector_peers = [sib, plane[0], plane[1], zp, (d, z2)]
    vector_copies, late_copies = [], []

    def vector_start():
        AVA[0, 0:16] = VG[...]
        for j in range(4):
            AVA[0, 16 + 4 * j : 20 + 4 * j] = jnp.where(quarter == j, QG[1:5], 0.0)
        vector_copies.append(send(AVA.at[0], AVR.at[0], vector_peers[0]))

    def vector_step(stage):
        vector_copies[stage].wait_recv()
        AVA[stage + 1] = AVA[stage] + AVR[stage]
        if stage < 4:
            vector_copies.append(send(AVA.at[stage + 1], AVR.at[stage + 1], vector_peers[stage + 1]))

    def late_start():
        for j in range(4):
            LVA[0, j : j + 1] = jnp.where(quarter == j, QG[0:1], 0.0)
        LVA[0, 4:8] = jnp.zeros((4, D_MODEL), F32)
        late_copies.append(send(LVA.at[0], LVR.at[0], vector_peers[0]))

    def late_step(stage):
        late_copies[stage].wait_recv()
        LVA[stage + 1] = LVA[stage] + LVR[stage]
        if stage < 4:
            late_copies.append(send(LVA.at[stage + 1], LVR.at[stage + 1], vector_peers[stage + 1]))

    def vectors_out():
        vec_out[...] = AVA[5, 0:16]
        for j in range(4):

            @pl.when(z == j)
            def _(j=j):
                qb_out[0:1] = LVA[5, j : j + 1]
                qb_out[1:5] = AVA[5, 16 + 4 * j : 20 + 4 * j]

    def send_tail(name, source, target_l, target_v):
        handles[name] = (
            send(source.at[pl.ds(RL - LANG_TAIL, LANG_TAIL)], target_l, up),
            send(source.at[pl.ds(ROWS - VIS_TAIL, VIS_TAIL)], target_v, up),
        )

    def place_rows():
        for name in ("outs", "grads"):
            for copy in handles[name]:
                copy.wait_recv()
        before_l = jnp.where(z == 1, 0, 25 - 5 * z)
        before_v = jnp.where(z == 1, 0, 45 - 9 * z)
        for (r0, r1), size, pad, own_rows, off, before, tail_rows, out_ref, grad_ref, t_out, t_grad in (
            (LANG, WORDS, WORDS, own_l, off_l, before_l, LANG_TAIL, lang_out, lang_grad, TLO, TLG),
            (VIS, REGIONS, REGION_PAD, own_v, off_v, before_v, VIS_TAIL, vis_out, vis_grad, TVO, TVG),
        ):
            from_own = rows_from_slab((own_rows, r1 - r0), -off, 0, off, own_rows, size, pad)
            from_tail = rows_from_slab(
                (own_rows, tail_rows), own_rows - before, r1 - r0 - tail_rows, 0, off, size, pad
            )
            out_ref[...] = (
                dot_nn(from_own.astype(BF), OUTS[r0:r1]) + dot_nn(from_tail.astype(BF), t_out[...])
            ).astype(BF)
            exact = lax.Precision.HIGHEST
            grad_ref[...] = jnp.dot(
                from_own, DZ[r0:r1], precision=exact, preferred_element_type=F32
            ) + jnp.dot(from_tail, t_grad[...], precision=exact, preferred_element_type=F32)


    weight_first(0)
    weight_second(0)
    send_heads(0, lang, vis)
    weight_first(7)
    send_heads(1, lcot, vcot)
    weight_third(0)
    send_small()
    own_slab(0, lang, vis, handles["heads", 0], A.at[0, 0])
    gather_start(0, V1)
    gather_start(0, V2)
    gather_start(0, LANG)
    attention_share(2)
    weight_first(2)
    attention_share(1)
    weight_second(7)
    pass_on(V2)
    pass_on(V1)
    weight_third(7)
    weight_first(1)
    pass_keys()
    own_slab(1, lcot, vcot, handles["heads", 1], COT)
    pass_on(LANG)
    weight_second(2)
    all_arrived(V2)
    all_arrived(LANG)
    weight_ready(0)
    take_small()
    all_arrived(V1)
    weight_first(4)
    weight_ready(7)
    project_cross(0)
    weight_second(1)
    weight_first(6)
    project_cross(1)
    weight_third(2)
    attend(V1, 0)
    sums_after(V1, C.at[0], 0, out_lanes)
    weight_second(4)
    attend(V2, 0)
    sums_on(V1)
    weight_first(3)
    attend(LANG, 0)
    sums_after(LANG, C.at[0], 0, out_lanes)
    sums_after(V2, C.at[0], 0, out_lanes)
    sums_on(V2)
    weight_third(1)
    count_step(0, plane[0])
    weight_third(4)
    sums_on(LANG)
    weight_second(6)
    weight_first(5)
    first_norm(V1)
    first_norm(V2)
    first_norm(LANG)
    weight_third(6)
    pass_on(V1)
    pass_on(V2)
    all_arrived(V1)
    weight_ready(2)
    project(V1, 2)
    attend(V1, 1)
    sums_after(V1, C.at[1], 2, out_lanes)
    all_arrived(V2)
    weight_second(3)
    project(V2, 2)
    attend(V2, 1)
    pass_on(LANG)
    sums_after(V2, C.at[1], 2, out_lanes)
    sums_on(V1)
    weight_ready(1)
    all_arrived(LANG)
    project(LANG, 1)
    sums_on(V2)
    attend(LANG, 1)
    sums_after(LANG, C.at[1], 1, out_lanes)
    weight_second(5)
    weight_third(3)
    second_norm(V1)
    weight_ready(4)
    sums_on(LANG)
    second_norm(LANG)
    second_norm(V2)
    count_step(1, plane[1])
    pass_on(V1)
    all_arrived(V1)
    count_step(2, None)
    expand_rows(V1)
    pass_on(V2)
    pass_on(LANG)
    weight_ready(6)
    weight_third(5)
    sums_after(V1, H, 6, all_lanes)
    all_arrived(V2)
    expand_rows(V2)
    weight_ready(5)
    sums_after(V2, H, 6, all_lanes)
    sums_on(V1)
    all_arrived(LANG)
    sums_on(V2)
    weight_ready(3)
    expand_rows(LANG)
    last_norm(V1)
    sums_after(LANG, H, 5, all_lanes)
    sums_on(LANG)
    pass_on(V1)
    last_norm(V2)
    last_norm(LANG)
    all_arrived(V1)
    hidden_gradient(V1)
    pass_on(V2)
    sums_after(V1, D, 4, all_lanes)
    all_arrived(V2)
    hidden_gradient(V2)
    sums_after(V2, D, 4, all_lanes)
    sums_on(V1)
    pass_on(LANG)
    weight_grad(6, 3, H, *VIS)
    grad_first(6)
    all_arrived(LANG)
    hidden_gradient(LANG)
    sums_after(LANG, D, 3, all_lanes)
    sums_on(V2)
    weight_grad(4, 2, D, *VIS)
    grad_first(4)
    second_norm_back(V1)
    weight_grad(5, 3, H, *LANG)
    grad_first(5)
    second_norm_back(V2)
    sums_on(LANG)
    pass_on(V1)
    grad_second(6)
    bias_grad(4, *VIS)
    weight_grad(3, 2, D, *LANG)
    grad_first(3)
    all_arrived(V1)
    send_tail("outs", OUTS, TLO, TVO)
    context_gradient(4, V1, 2)
    second_norm_back(LANG)
    attend_gradient(V1, 1)
    sums_after(V1, D, 2, all_lanes)
    bias_grad(3, *LANG)
    pass_on(V2)
    grad_second(4)
    all_arrived(V2)
    pass_on(LANG)
    context_gradient(4, V2, 2)
    sums_on(V1)
    attend_gradient(V2, 1)
    sums_after(V2, D, 2, all_lanes)
    grad_third(6)
    all_arrived(LANG)
    context_gradient(4, LANG, 1)
    sums_on(V2)
    grad_second(5)
    attend_gradient(LANG, 1)
    sums_after(LANG, D, 1, all_lanes)
    attention_weight_grad(2, 1, 4, C.at[1], *VIS)
    grad_first(2)
    sums_on(LANG)
    first_norm_back(V1)
    first_norm_back(V2)
    grad_second(3)
    attention_weight_grad(1, 1, 4, C.at[1], *LANG)
    first_norm_back(LANG)
    bias_grad(1, *LANG)
    grad_third(5)
    pass_on(V2)
    grad_first(1)
    grad_third(4)
    bias_grad(2, *VIS)
    pass_on(LANG)
    all_arrived(V2)
    vector_start()
    pass_on(V1)
    all_arrived(LANG)
    all_arrived(V1)
    context_gradient(5, LANG, 0)
    context_gradient(5, V1, 0)
    grad_second(2)
    vector_step(0)
    context_gradient(5, V2, 0)
    attend_gradient(None, 0)
    sums_after(V1, D, 0, all_lanes)
    bias_grad(0, *BOTH)
    vector_step(1)
    sums_on(V1)
    grad_third(3)
    grad_second(1)
    attention_weight_grad(0, 0, 5, C.at[0], *BOTH, middle=lambda: grad_first(0))
    grad_first(7)
    vector_step(2)
    grad_third(2)
    final_sum(V1)
    grad_second(0)
    sums_after(LANG, D, 0, all_lanes)
    sums_on(LANG)
    vector_step(3)
    grad_last(5)
    late_start()
    sums_after(V2, D, 0, all_lanes)
    grad_third(0)
    grad_second(7)
    grad_last(6)
    grad_last(4)
    sums_on(V2)
    final_sum(LANG)
    grad_third(1)
    late_step(0)
    grad_last(3)
    vector_step(4)
    grad_last(2)
    final_sum(V2)
    send_tail("grads", DZ, TLG, TVG)
    late_step(1)
    late_step(2)
    late_step(3)
    late_step(4)
    grad_last(0)
    grad_last(1)
    vectors_out()
    grad_third(7)
    place_rows()
    grad_last(7)

    for copy in pending:
        copy.wait_send()
    for sent in pending_z:
        sent()
    for index, stream in list(stage_used):
        stage_free(index, stream)

    @pl.when(c == 1)
    def _():
        for copy in nears:
            copy.wait_send()
        for _, far_low, far_high in grad_nears:
            far_low.wait_send()
            far_high.wait_send()

    @pl.when(c == 0)
    def _():
        for near, _, _ in grad_nears:
            near.wait_send()
    assert counter[0] <= ssem.shape[0] and counter[1] <= rsem.shape[0], counter


N_SEND = 240
N_RECV = 160


def fused_layer(total_items, *operands):
    own_l, own_v = operands[0].shape[0], operands[1].shape[0]
    vmem = pl.BlockSpec(memory_space=pltpu.VMEM)
    smem = pl.BlockSpec(memory_space=pltpu.SMEM)
    shapes = [
        ((own_l, D), BF),
        ((own_v, D), BF),
        ((own_l, D), F32),
        ((own_v, D), F32),
        ((7, SHARE, D), F32),
        ((16, D), F32),
        ((8, D), F32),
    ]
    scratch = [
        ((7, D, D), BF),
        ((7, D, D), BF),
        ((2, 7, SHARE, D), BF),
        ((2, 7, HALF_PAIR, D), BF),
        ((2, 7, SHARE, D), BF),
        ((6, SLOTS, ROWS, D), BF),
        ((SLOTS, 8, TILE), F32),
        ((3, ROWS, D), BF),
        ((3, ROWS, D), BF),
        ((2, SLOTS, ROWS, D), BF),
        ((SLOTS, ROWS, D), BF),
        ((2, SLOTS, ROWS, TILE), BF),
        ((SLOTS, ROWS, D), BF),
        ((SLOTS, ROWS, D), BF),
        ((SLOTS, 3 * RL, RV), BF),
        ((2, SLOTS, 3 * RL, RL), BF),
        ((3, SLOTS, 3 * RL, RL), BF),
        ((ROWS, D), F32),
        ((ROWS, D), F32),
        ((3, ROWS, D), F32),
        ((3, ROWS, 1), F32),
        ((ROWS, D), F32),
        ((ROWS, D), BF),
        ((3, SHARE, D), BF),
        ((ROWS, 1), F32),
        ((8, D), F32),
        ((8, D), F32),
        ((8, D), F32),
        ((4, 8, 128), F32),
        ((3, 8, 128), F32),
        ((16, D), F32),
        ((8, D), F32),
        ((6, N_AR, D), F32),
        ((5, N_AR, D), F32),
        ((6, 8, D), F32),
        ((5, 8, D), F32),
        ((2, LANG_HEAD, D), BF),
        ((2, VIS_HEAD, D), BF),
        ((ROWS, D), BF),
        ((LANG_TAIL, D), BF),
        ((VIS_TAIL, D), BF),
        ((LANG_TAIL, D), F32),
        ((VIS_TAIL, D), F32),
    ]
    dma = pltpu.SemaphoreType.DMA
    return pl.pallas_call(
        partial(layer_kernel, total_items),
        out_shape=[jax.ShapeDtypeStruct(s, t) for s, t in shapes],
        in_specs=[vmem] * 4 + [smem] * 3 + [vmem] * (len(operands) - 7),
        out_specs=[vmem] * len(shapes),
        scratch_shapes=[pltpu.VMEM(s, t) for s, t in scratch]
        + [dma((N_SEND,)), dma((N_RECV,)), dma((3, 8)), dma((8,)), dma((3, 8)), dma((8,))],
        compiler_params=pltpu.CompilerParams(
            collective_id=0, has_side_effects=True, vmem_limit_bytes=VMEM_LIMIT
        ),
    )(*operands)


def unpack_kernel(lo, vo, lg, vg, wgrad, vec, qb, *outs):
    (lo_out, vo_out, lg_out, vg_out, proj, qv, outw, outb, exp, expb, con, conb, gain, shift) = outs
    lo_out[...] = lo[...]
    vo_out[...] = vo[...]
    lg_out[...] = lg[...]
    vg_out[...] = vg[...]
    width = HALF_PAIR
    for b in range(3):
        for j, lane in enumerate((0, 2 * width, width)):
            proj[b, j] = wgrad[b, :, lane : lane + width]
        outw[b] = wgrad[b, :, 3 * width :].T
        for j in range(2):
            qv[b, j : j + 1] = qb[b : b + 1, j * width : (j + 1) * width]
    for stream in range(2):
        exp[stream] = wgrad[3 + stream]
        con[stream] = wgrad[5 + stream]
    expb[...] = qb[3:5]
    outb[...] = vec[0:3]
    conb[...] = vec[3:5]
    gain[...] = vec[5:10]
    shift[...] = vec[10:15]


def unpack(packed, shapes):
    vmem = pl.BlockSpec(memory_space=pltpu.VMEM)
    return pl.pallas_call(
        unpack_kernel,
        out_shape=shapes,
        in_specs=[vmem] * len(packed),
        out_specs=[vmem] * len(shapes),
        compiler_params=pltpu.CompilerParams(vmem_limit_bytes=VMEM_LIMIT),
    )(*packed)


def on_device_fused(
    language_input,
    vision_input,
    word_lengths,
    region_counts,
    task_flags,
    language_cotangent,
    vision_cotangent,
    projection_weight,
    query_value_bias,
    output_weight,
    output_bias,
    expand_weight,
    expand_bias,
    contract_weight,
    contract_bias,
    norm_gain,
    norm_bias,
):
    packed = fused_layer(
        float(word_lengths.shape[0] * lax.axis_size("dp")),
        language_input,
        vision_input,
        language_cotangent,
        vision_cotangent,
        word_lengths,
        region_counts,
        task_flags.T,
        projection_weight,
        query_value_bias,
        output_weight,
        expand_weight,
        expand_bias,
        contract_weight.transpose(0, 2, 1),
        output_bias,
        contract_bias,
        norm_gain,
        norm_bias,
    )
    like = [
        (language_input, BF),
        (vision_input, BF),
        (language_input, F32),
        (vision_input, F32),
        (projection_weight, F32),
        (query_value_bias, F32),
        (output_weight, F32),
        (output_bias, F32),
        (expand_weight, F32),
        (expand_bias, F32),
        (contract_weight.transpose(0, 2, 1), F32),
        (contract_bias, F32),
        (norm_gain, F32),
        (norm_bias, F32),
    ]
    outs = list(unpack(packed, [jax.ShapeDtypeStruct(a.shape, t) for a, t in like]))
    outs[10] = outs[10].transpose(0, 2, 1)
    return tuple(outs)


def solution(mesh):
    in_specs = (
        P(("dp", "mp"), None),
        P(("dp", "mp"), None),
        P("dp"),
        P("dp"),
        P("dp", None),
        P(("dp", "mp"), None),
        P(("dp", "mp"), None),
        P(None, None, "dp", "mp"),
        P(None, None, "mp"),
        P(None, "mp", "dp"),
        P(),
        P(None, "dp", "mp"),
        P(None, "mp"),
        P(None, "mp", "dp"),
        P(),
        P(),
        P(),
    )
    out_specs = (
        P(("dp", "mp"), None),
        P(("dp", "mp"), None),
        P(("dp", "mp"), None),
        P(("dp", "mp"), None),
        P(None, None, "dp", "mp"),
        P(None, None, "mp"),
        P(None, "mp", "dp"),
        P(),
        P(None, "dp", "mp"),
        P(None, "mp"),
        P(None, "mp", "dp"),
        P(),
        P(),
        P(),
    )
    fused = dict(mesh.shape) == {"dp": 8, "mp": 4}
    return jax.shard_map(
        on_device_fused if fused else on_device, mesh=mesh, in_specs=in_specs, out_specs=out_specs, check_vma=False
    )
```

```python
from functools import partial
import math

import jax
import jax.numpy as jnp
from jax import lax
from jax.experimental import pallas as pl
from jax.experimental.pallas import tpu as pltpu
from jax.sharding import PartitionSpec as P

D = 768
HEADS = 12
WORDS = 20
REGIONS = 36
D_MODEL = D
D_HEAD = D // HEADS

EPSILON = 1e-12
MASKED = -1e30


def layer_norm(summed, gain, shift):
    center = summed - jnp.mean(summed, -1, keepdims=True)
    scaled = lax.rsqrt(jnp.mean(center * center, -1, keepdims=True) + EPSILON)
    normed = center * scaled
    return (normed * gain + shift, normed, scaled)


def norm_back(upstream, normed, scaled, gain):
    through = upstream * gain
    inner = (
        through
        - jnp.mean(through, -1, keepdims=True)
        - normed * jnp.mean(through * normed, -1, keepdims=True)
    )
    return (scaled * inner, jnp.sum(upstream * normed, 0), jnp.sum(upstream, 0))


def split_heads(rows, item_count):
    head_size = D // HEADS
    return rows.reshape(
        item_count, rows.shape[0] // item_count, rows.shape[1] // head_size, head_size
    )


def join_heads(block):
    return block.reshape(block.shape[0] * block.shape[1], block.shape[2] * block.shape[3])


def project(rows, weight, bias, item_count):
    mapped = jnp.einsum("rd,jde->jre", rows, weight, preferred_element_type=jnp.float32)
    query = split_heads((mapped[0] + bias[0]).astype(jnp.bfloat16), item_count)
    keys = split_heads(mapped[1].astype(jnp.bfloat16), item_count)
    values = split_heads((mapped[2] + bias[1]).astype(jnp.bfloat16), item_count)
    return (query, keys, values)


def masked_scores(query, keys, valid):
    scores = jnp.einsum("inhd,imhd->ihnm", query, keys, preferred_element_type=jnp.float32) * (
        1.0 / math.sqrt(D // HEADS)
    )
    return jnp.where(valid[:, None, None, :], scores, MASKED)


def attend(query, keys, values, valid):
    scores = masked_scores(query, keys, valid)
    highest = jnp.max(scores, -1, keepdims=True)
    raised = jnp.exp(scores - highest)
    summed = jnp.sum(raised, -1, keepdims=True)
    context = jnp.einsum(
        "ihnm,imhd->inhd",
        (raised / summed).astype(jnp.bfloat16),
        values,
        preferred_element_type=jnp.float32,
    )
    return (join_heads(context).astype(jnp.bfloat16), highest + jnp.log(summed))


def attend_back(query, keys, values, valid, log_total, context_grad):
    factor = 1.0 / math.sqrt(D // HEADS)
    upstream = context_grad.reshape(query.shape)
    weights = jnp.exp(masked_scores(query, keys, valid) - log_total)
    weight_grad = jnp.einsum(
        "inhd,imhd->ihnm", upstream, values, preferred_element_type=jnp.float32
    )
    score_grad = (
        weights * (weight_grad - jnp.sum(weight_grad * weights, -1, keepdims=True))
    ).astype(jnp.bfloat16)
    query_grad = (
        jnp.einsum("ihnm,imhd->inhd", score_grad, keys, preferred_element_type=jnp.float32) * factor
    ).astype(jnp.bfloat16)
    keys_grad = (
        jnp.einsum("ihnm,inhd->imhd", score_grad, query, preferred_element_type=jnp.float32)
        * factor
    ).astype(jnp.bfloat16)
    values_grad = jnp.einsum(
        "ihnm,inhd->imhd",
        weights.astype(jnp.bfloat16),
        upstream,
        preferred_element_type=jnp.float32,
    ).astype(jnp.bfloat16)
    return (join_heads(query_grad), join_heads(keys_grad), join_heads(values_grad))


def project_back(rows, query_grad, keys_grad, values_grad):
    stacked = jnp.stack([query_grad, keys_grad, values_grad])
    weight_grad = jnp.einsum("rd,jre->jde", rows, stacked, preferred_element_type=jnp.float32)
    bias_grad = jnp.stack(
        [jnp.sum(query_grad.astype(jnp.float32), 0), jnp.sum(values_grad.astype(jnp.float32), 0)]
    )
    return (weight_grad, bias_grad, stacked)


def gather_rows(language_rows, vision_rows):
    return (
        lax.all_gather(language_rows, "mp", axis=0, tiled=True),
        lax.all_gather(vision_rows, "mp", axis=0, tiled=True),
    )


def rows_of(language_part, vision_part):
    return (
        lax.all_to_all(language_part, "mp", split_axis=0, concat_axis=1, tiled=True),
        lax.all_to_all(vision_part, "mp", split_axis=0, concat_axis=1, tiled=True),
    )


def gather_grads(language_rows, vision_rows):
    return (
        lax.all_gather(language_rows, "mp", axis=0, tiled=True),
        lax.all_gather(vision_rows, "mp", axis=0, tiled=True),
    )


def grads_of(language_part, vision_part):
    return (
        lax.all_to_all(language_part, "mp", split_axis=1, concat_axis=2, tiled=True),
        lax.all_to_all(vision_part, "mp", split_axis=1, concat_axis=2, tiled=True),
    )


def matmul(left, right):
    return jnp.dot(left, right, preferred_element_type=jnp.float32)


def on_device(
    language_input,
    vision_input,
    word_lengths,
    region_counts,
    task_flags,
    language_cotangent,
    vision_cotangent,
    projection_weight,
    query_value_bias,
    output_weight,
    output_bias,
    expand_weight,
    expand_bias,
    contract_weight,
    contract_bias,
    norm_gain,
    norm_bias,
):
    item_count = word_lengths.shape[0]
    flag_total = lax.psum(jnp.sum(task_flags, 0), "dp")
    projection, out_weight, expand, contract = (
        lax.all_gather(projection_weight, "dp", axis=2, tiled=True),
        lax.all_gather(output_weight, "dp", axis=2, tiled=True),
        lax.all_gather(expand_weight, "dp", axis=1, tiled=True),
        lax.all_gather(contract_weight, "dp", axis=2, tiled=True),
    )
    projection_full, out_full, expand_full, contract_full = (
        lax.all_gather(projection, "mp", axis=3, tiled=True),
        lax.all_gather(out_weight, "mp", axis=1, tiled=True),
        lax.all_gather(expand, "mp", axis=2, tiled=True),
        lax.all_gather(contract, "mp", axis=1, tiled=True),
    )
    valid = [
        jnp.arange(WORDS, dtype=jnp.int32)[None, :] < word_lengths[:, None],
        jnp.arange(REGIONS, dtype=jnp.int32)[None, :] < region_counts[:, None],
    ]
    row_counts = [WORDS, REGIONS]
    inputs = [language_input.astype(jnp.float32), vision_input.astype(jnp.float32)]
    cross_rows = gather_rows(language_input, vision_input)
    cross_parts = [
        project(cross_rows[stream], projection[0], query_value_bias[0], item_count)
        for stream in range(2)
    ]
    cross_context = []
    cross_total = []
    for stream in range(2):
        other = 1 - stream
        context, log_total = attend(
            cross_parts[stream][0], cross_parts[other][1], cross_parts[other][2], valid[other]
        )
        cross_context.append(context)
        cross_total.append(log_total)
    moved = rows_of(cross_context[0], cross_context[1])
    branch = [matmul(moved[stream], out_full[0]) for stream in range(2)]
    first = [
        layer_norm(branch[stream] + output_bias[0] + inputs[stream], norm_gain[0], norm_bias[0])
        for stream in range(2)
    ]
    first_out = [first[stream][0].astype(jnp.bfloat16) for stream in range(2)]
    self_rows = gather_rows(first_out[0], first_out[1])
    self_parts = [
        project(self_rows[stream], projection[1 + stream], query_value_bias[1 + stream], item_count)
        for stream in range(2)
    ]
    self_context = []
    self_total = []
    for stream in range(2):
        context, log_total = attend(
            self_parts[stream][0], self_parts[stream][1], self_parts[stream][2], valid[stream]
        )
        self_context.append(context)
        self_total.append(log_total)
    moved = rows_of(self_context[0], self_context[1])
    branch = [matmul(moved[stream], out_full[1 + stream]) for stream in range(2)]
    second = [
        layer_norm(
            branch[stream] + output_bias[1 + stream] + first_out[stream].astype(jnp.float32),
            norm_gain[1 + stream],
            norm_bias[1 + stream],
        )
        for stream in range(2)
    ]
    second_out = [second[stream][0].astype(jnp.bfloat16) for stream in range(2)]
    feed_rows = gather_rows(second_out[0], second_out[1])
    before = [
        matmul(feed_rows[stream], expand[stream]) + expand_bias[stream] for stream in range(2)
    ]
    hidden = [
        jax.nn.gelu(before[stream], approximate=False).astype(jnp.bfloat16) for stream in range(2)
    ]
    moved = rows_of(hidden[0], hidden[1])
    branch = [matmul(moved[stream], contract_full[stream]) for stream in range(2)]
    third = [
        layer_norm(
            branch[stream] + contract_bias[stream] + second_out[stream].astype(jnp.float32),
            norm_gain[3 + stream],
            norm_bias[3 + stream],
        )
        for stream in range(2)
    ]
    language_out = third[0][0].astype(jnp.bfloat16)
    vision_out = third[1][0].astype(jnp.bfloat16)
    item_scale = task_flags.astype(jnp.float32) * (
        item_count * lax.axis_size("dp") / flag_total.astype(jnp.float32)
    )
    shard_index = lax.axis_index("mp")
    upstream = []
    for stream, cotangent in enumerate([language_cotangent, vision_cotangent]):
        per_row = jnp.repeat(
            item_scale[:, stream],
            row_counts[stream],
            total_repeat_length=item_count * row_counts[stream],
        )
        shard_rows = cotangent.shape[0]
        row_scale = lax.dynamic_slice_in_dim(per_row, shard_index * shard_rows, shard_rows)
        upstream.append(cotangent.astype(jnp.float32) * row_scale[:, None])
    third_back = [
        norm_back(upstream[stream], third[stream][1], third[stream][2], norm_gain[3 + stream])
        for stream in range(2)
    ]
    sent = gather_grads(
        third_back[0][0].astype(jnp.bfloat16), third_back[1][0].astype(jnp.bfloat16)
    )
    expand_local = []
    expand_bias_local = []
    contract_local = []
    before_grads = []
    for stream in range(2):
        hidden_grad = jnp.einsum(
            "rd,fd->rf", sent[stream], contract[stream], preferred_element_type=jnp.float32
        )
        contract_local.append(
            jnp.einsum(
                "rf,rd->fd", hidden[stream], sent[stream], preferred_element_type=jnp.float32
            )
        )
        unused, pull = jax.vjp(partial(jax.nn.gelu, approximate=False), before[stream])
        before_grad = pull(hidden_grad)[0].astype(jnp.bfloat16)
        expand_local.append(
            jnp.einsum(
                "rd,rf->df", feed_rows[stream], before_grad, preferred_element_type=jnp.float32
            )
        )
        expand_bias_local.append(jnp.sum(before_grad.astype(jnp.float32), 0))
        before_grads.append(before_grad[None])
    moved = grads_of(before_grads[0], before_grads[1])
    back = [
        jnp.einsum(
            "rf,df->rd", moved[stream][0], expand_full[stream], preferred_element_type=jnp.float32
        )
        for stream in range(2)
    ]
    second_grad = [third_back[stream][0] + back[stream] for stream in range(2)]
    second_back = [
        norm_back(second_grad[stream], second[stream][1], second[stream][2], norm_gain[1 + stream])
        for stream in range(2)
    ]
    sent = gather_grads(
        second_back[0][0].astype(jnp.bfloat16), second_back[1][0].astype(jnp.bfloat16)
    )
    self_weight = []
    self_bias = []
    self_out = []
    stacks = []
    for stream in range(2):
        context_grad = jnp.einsum(
            "rd,ed->re", sent[stream], out_weight[1 + stream], preferred_element_type=jnp.float32
        ).astype(jnp.bfloat16)
        self_out.append(
            jnp.einsum(
                "re,rd->ed", self_context[stream], sent[stream], preferred_element_type=jnp.float32
            )
        )
        grads = attend_back(
            self_parts[stream][0],
            self_parts[stream][1],
            self_parts[stream][2],
            valid[stream],
            self_total[stream],
            context_grad,
        )
        weight_part, bias_part, stacked = project_back(
            self_rows[stream], grads[0], grads[1], grads[2]
        )
        self_weight.append(weight_part)
        self_bias.append(bias_part)
        stacks.append(stacked)
    moved = grads_of(stacks[0], stacks[1])
    back = [
        jnp.einsum(
            "jre,jde->rd",
            moved[stream],
            projection_full[1 + stream],
            preferred_element_type=jnp.float32,
        )
        for stream in range(2)
    ]
    first_grad = [second_back[stream][0] + back[stream] for stream in range(2)]
    first_back = [
        norm_back(first_grad[stream], first[stream][1], first[stream][2], norm_gain[0])
        for stream in range(2)
    ]
    sent = gather_grads(
        first_back[0][0].astype(jnp.bfloat16), first_back[1][0].astype(jnp.bfloat16)
    )
    cross_out = jnp.einsum(
        "re,rd->ed", cross_context[0], sent[0], preferred_element_type=jnp.float32
    ) + jnp.einsum("re,rd->ed", cross_context[1], sent[1], preferred_element_type=jnp.float32)
    triples = [[None, None, None], [None, None, None]]
    for stream in range(2):
        other = 1 - stream
        context_grad = jnp.einsum(
            "rd,ed->re", sent[stream], out_weight[0], preferred_element_type=jnp.float32
        ).astype(jnp.bfloat16)
        grads = attend_back(
            cross_parts[stream][0],
            cross_parts[other][1],
            cross_parts[other][2],
            valid[other],
            cross_total[stream],
            context_grad,
        )
        triples[stream][0] = grads[0]
        triples[other][1] = grads[1]
        triples[other][2] = grads[2]
    results = [
        project_back(cross_rows[stream], triples[stream][0], triples[stream][1], triples[stream][2])
        for stream in range(2)
    ]
    cross_weight = results[0][0] + results[1][0]
    cross_bias = results[0][1] + results[1][1]
    moved = grads_of(results[0][2], results[1][2])
    back = [
        jnp.einsum(
            "jre,jde->rd", moved[stream], projection_full[0], preferred_element_type=jnp.float32
        )
        for stream in range(2)
    ]
    language_grad = first_back[0][0] + back[0]
    vision_grad = first_back[1][0] + back[1]
    projection_stack = jnp.stack([cross_weight, self_weight[0], self_weight[1]])
    output_stack = jnp.stack([cross_out, self_out[0], self_out[1]])
    projection_grad, output_weight_grad, expand_grad, contract_grad = (
        lax.psum_scatter(projection_stack, "dp", scatter_dimension=2, tiled=True),
        lax.psum_scatter(output_stack, "dp", scatter_dimension=2, tiled=True),
        lax.psum_scatter(jnp.stack(expand_local), "dp", scatter_dimension=1, tiled=True),
        lax.psum_scatter(jnp.stack(contract_local), "dp", scatter_dimension=2, tiled=True),
    )
    query_value_grad, expand_bias_grad = lax.psum(
        (jnp.stack([cross_bias, self_bias[0], self_bias[1]]), jnp.stack(expand_bias_local)), "dp"
    )
    output_bias_local = jnp.stack(
        [
            jnp.sum(first_back[0][0], 0) + jnp.sum(first_back[1][0], 0),
            jnp.sum(second_back[0][0], 0),
            jnp.sum(second_back[1][0], 0),
        ]
    )
    contract_bias_local = jnp.stack([jnp.sum(third_back[0][0], 0), jnp.sum(third_back[1][0], 0)])
    gain_local = jnp.stack(
        [
            first_back[0][1] + first_back[1][1],
            second_back[0][1],
            second_back[1][1],
            third_back[0][1],
            third_back[1][1],
        ]
    )
    shift_local = jnp.stack(
        [
            first_back[0][2] + first_back[1][2],
            second_back[0][2],
            second_back[1][2],
            third_back[0][2],
            third_back[1][2],
        ]
    )
    output_bias_grad, contract_bias_grad, norm_gain_grad, norm_bias_grad = lax.psum(
        (output_bias_local, contract_bias_local, gain_local, shift_local), ("dp", "mp")
    )
    return (
        language_out,
        vision_out,
        language_grad,
        vision_grad,
        projection_grad,
        query_value_grad,
        output_weight_grad,
        output_bias_grad,
        expand_grad,
        expand_bias_grad,
        contract_grad,
        contract_bias_grad,
        norm_gain_grad,
        norm_bias_grad,
    )


MESH = pl.DeviceIdType.MESH
BF = jnp.bfloat16
F32 = jnp.float32
SLOTS = 4
RL = SLOTS * WORDS
REGION_PAD = 40
RV = SLOTS * REGION_PAD
ROWS = RL + RV
SHARE = 96
HALF_PAIR = 2 * SHARE
LANG_HEAD = 16
VIS_HEAD = 32
LANG_TAIL = 32
VIS_TAIL = 64
N_AR = 32
NT = 3
TILE = 256
LANG = (0, RL)
V1 = (RL, RL + RV // 2)
V2 = (RL + RV // 2, ROWS)
VIS = (RL, ROWS)
BOTH = (0, ROWS)
CHAINS = (V1, V2, LANG)
TRIM = {V1: V1[1], V2: V2[0] + 48, LANG: LANG[0] + 64}
SELF = {LANG: 1, V1: 2, V2: 2}
EXPAND = {LANG: 3, V1: 4, V2: 4}
CONTRACT = {LANG: 5, V1: 6, V2: 6}
PARTS = {w: (w, slice(0, 768)) for w in range(1, 7)} | {0: (0, slice(0, 384)), 7: (0, slice(384, 768))}
VMEM_LIMIT = 63 * 1024 * 1024


def dot_nn(left, right):
    return lax.dot_general(left, right, (((1,), (0,)), ((), ())), preferred_element_type=F32)


def dot_nt(left, right):
    return lax.dot_general(left, right, (((1,), (1,)), ((), ())), preferred_element_type=F32)


def dot_tn(left, right):
    return lax.dot_general(left, right, (((0,), (0,)), ((), ())), preferred_element_type=F32)


def head_mask(first_lane, dtype):
    lane = lax.broadcasted_iota(jnp.int32, (1, TILE), 1) - first_lane
    return [
        jnp.where((lane >= 64 * h) & (lane < 64 * h + 64), 1.0, 0.0).astype(dtype) for h in range(3)
    ]


def item_rows(shape, dim, first, size, pad):
    row = lax.broadcasted_iota(jnp.int32, shape, dim) + first
    item = sum(jnp.where(row >= pad * j, 1, 0) for j in range(1, SLOTS))
    return row - (pad - size) * item, row - pad * item < size


def rows_into_slab(shape, shift, count, size, pad):
    place, real = item_rows(shape, 0, 0, size, pad)
    column = lax.broadcasted_iota(jnp.int32, shape, 1)
    return jnp.where((column - place == shift) & real & (place < count), 1.0, 0.0)


def rows_from_slab(shape, shift, first, low, high, size, pad):
    place, real = item_rows(shape, 1, first, size, pad)
    row = lax.broadcasted_iota(jnp.int32, shape, 0)
    return jnp.where((place - row == shift) & real & (row >= low) & (row < high), 1.0, 0.0)


def layer_kernel(
    total_items,
    lang,
    vis,
    lcot,
    vcot,
    lengths,
    regions,
    flags,
    projection,
    query_value,
    out_weight,
    expand,
    expand_b,
    contract,
    out_bias,
    contract_b,
    gains,
    shifts,
    lang_out,
    vis_out,
    lang_grad,
    vis_grad,
    wgrad,
    vec_out,
    qb_out,
    W,
    G,
    RD,
    RX,
    R2,
    A,
    KV,
    RSB,
    STG,
    QVK,
    D,
    C,
    H,
    GP,
    PCL,
    PCV,
    PS,
    PART,
    PZ,
    NORM,
    RSTD,
    DZ,
    COT,
    SH,
    FLAG,
    QO,
    QB,
    QR,
    CA,
    CR,
    VG,
    QG,
    AVA,
    AVR,
    LVA,
    LVR,
    HL,
    HV,
    OUTS,
    TLO,
    TVO,
    TLG,
    TVG,
    ssem,
    rsem,
    wsem,
    wsem_z,
    gsem,
    gsem2,
):
    d = lax.axis_index("dp")
    z = lax.axis_index("mp")
    c = d % 2
    k = d // 2
    k_flip = [k + 1 - 2 * (k % 2), (k + 2) % 4, 3 - k]
    sib = (d + 1 - 2 * c, z)
    zp = (d, z + 1 - 2 * (z % 2))
    z2 = (z + 2) % 4
    up = (d, (z + 1) % 4)
    down = (d, (z + 3) % 4)
    plane = [(2 * kf + c, z) for kf in k_flip]
    far = (2 * k + 1, z2)

    pending, pending_z = [], []
    counter = [0, 0]

    def remote(src, dst, send, recv, device):
        return pltpu.make_async_remote_copy(
            src_ref=src, dst_ref=dst, send_sem=send, recv_sem=recv, device_id=device, device_id_type=MESH
        )

    groups = {}

    def send(src, dst, device, recv=None, keep=True, group=None):
        if group is None:
            slot = counter[0]
            counter[0] += 1
        else:
            if group not in groups:
                groups[group] = counter[0]
                counter[0] += 1
            slot, keep = groups[group], False
        if recv is None:
            recv = rsem.at[counter[1]]
            counter[1] += 1
        copy = remote(src, dst, ssem.at[slot], recv, device)
        copy.start()
        if keep:
            pending.append(copy)
        return copy

    def wait_bytes(ref, sem):
        pltpu.make_async_copy(ref, ref, sem).wait()

    def arrived(name, *copies):
        with jax.named_scope("wait_" + name):
            for copy in copies:
                copy.wait_recv()

    barrier = pltpu.get_barrier_semaphore()
    peers = [sib, up, down, (d, z2), (d + 1 - 2 * c, z2)] + plane
    for peer in peers:
        pl.semaphore_signal(barrier, inc=1, device_id=peer, device_id_type=MESH)

    def weight_first(part):
        w, lanes = PARTS[part]
        row = pl.ds(pl.multiple_of(d * SHARE, 16), SHARE)
        slot = counter[0]
        counter[0] += 1
        share = SH.at[w] if w < 3 else (expand.at[w - 3] if w < 5 else contract.at[w - 5])
        share = share.at[:, lanes]
        target = W.at[w, row, lanes]
        near = remote(share, target, ssem.at[slot], wsem_z.at[part], sib)
        own = pltpu.make_async_copy(share, target, wsem_z.at[part])

        @pl.when(c == 1)
        def _():
            near.start()

        @pl.when(c == 0)
        def _():
            own.start()

        send(share, target, far, wsem_z.at[part])
        nears.append(near)

    def place(width, first):
        row = lax.broadcasted_iota(jnp.int32, (width, D_MODEL), 0)
        column = lax.broadcasted_iota(jnp.int32, (width, D_MODEL), 1)
        return jnp.where(column - row == first, 1.0, 0.0).astype(BF)

    def attention_share(b):
        SH[b] = (
            dot_nn(projection[b, 0], place(HALF_PAIR, 0))
            + dot_nn(projection[b, 2], place(HALF_PAIR, HALF_PAIR))
            + dot_nn(projection[b, 1], place(HALF_PAIR, 2 * HALF_PAIR))
            + dot_tn(out_weight[b], place(HALF_PAIR, 3 * HALF_PAIR))
        ).astype(BF)

    nears = []
    attention_share(0)

    n_items = lengths.shape[0]
    first_item = 3 * z + jnp.minimum(z, 1)
    KV[0] = jnp.full(KV.shape[1:], -1.0, F32)
    for row, source, size, pad, first_row in ((0, lengths, WORDS, WORDS, 0), (1, regions, REGIONS, REGION_PAD, RL)):
        lane = lax.broadcasted_iota(jnp.int32, (1, TILE), 1)
        owner = jnp.full((1, TILE), -1.0, F32)
        slab_row = lax.broadcasted_iota(jnp.int32, (SLOTS * pad, 1), 0)
        flag = jnp.zeros((SLOTS * pad, 1), F32)
        for j in range(SLOTS):
            item = jnp.minimum(first_item + j, n_items - 1)
            valid = (lane >= j * pad) & (lane < j * pad + source[item]) & (lane < j * pad + size)
            owner = jnp.where(valid, float(j), owner)
            inside = (slab_row >= j * pad) & (slab_row < (j + 1) * pad)
            flag = jnp.where(inside, flags[row, item].astype(F32), flag)
            if row == 1 and j % 2 == 1:
                pair = jnp.full((1, TILE), -1.0, F32)
                for i in (0, 1):
                    other = jnp.minimum(first_item + j - 1 + i, n_items - 1)
                    valid = (lane >= i * pad) & (lane < i * pad + source[other]) & (lane < i * pad + size)
                    pair = jnp.where(valid, float(j - 1 + i), pair)
                KV[0, 2 + j // 2 : 3 + j // 2] = pair
        KV[0, row : row + 1] = owner
        FLAG[first_row : first_row + SLOTS * pad] = flag
        count = flags[row, 0]
        for j in range(1, n_items):
            count = count + flags[row, j]
        CA[0, row : row + 1] = jnp.full((1, 128), count.astype(F32), F32)
    QO[...] = jnp.zeros_like(QO)
    for b in range(3):
        QO[b : b + 1, 0:HALF_PAIR] = query_value[b, 0:1]
        QO[b : b + 1, HALF_PAIR : 2 * HALF_PAIR] = query_value[b, 1:2]
    QO[3:5] = expand_b[...]

    for first, last in ((TRIM[LANG], LANG[1]), (TRIM[V2], V2[1])):
        A[:, 2, first:last] = jnp.zeros((6, last - first, D_MODEL), BF)
        RSB[2, first:last] = jnp.zeros((last - first, D_MODEL), BF)
    VG[...] = jnp.zeros_like(VG)
    QG[...] = jnp.zeros_like(QG)
    pl.semaphore_wait(barrier, len(peers))

    pair_rows = pl.ds(pl.multiple_of(k * HALF_PAIR, 16), HALF_PAIR)

    def rows_of_chip(chip, first=0, count=HALF_PAIR):
        return pl.ds(pl.multiple_of(chip * HALF_PAIR + first, 16), count)

    def weight_second(part):
        w, lanes = PARTS[part]
        block = W.at[w, pair_rows, lanes]
        wait_bytes(block, wsem_z.at[part])
        for j in range(2):
            send(block, block, plane[j], wsem.at[j, part], group=("w", part))

    def weight_third(part):
        w, lanes = PARTS[part]
        for j in range(2):
            wait_bytes(W.at[w, pair_rows, lanes], wsem.at[j, part])
            half = W.at[w, rows_of_chip(k_flip[j], j * SHARE, SHARE), lanes]
            send(half, half, plane[1 - j], wsem.at[2, part], group=("w", part))

    def weight_ready(part):
        w, lanes = PARTS[part]
        wait_bytes(W.at[w, pair_rows, lanes], wsem.at[2, part])

    off_l = jnp.where(z == 0, 0, 20 - 5 * z)
    off_v = jnp.where(z == 0, 0, 36 - 9 * z)
    n_l = jnp.where(z == 0, 4 * WORDS, 3 * WORDS)
    n_v = jnp.where(z == 0, 4 * REGIONS, 3 * REGIONS)
    own_l = lang.shape[0]
    own_v = vis.shape[0]
    def start_z(source, target, stream, device, big):
        slot, recv = counter[0], rsem.at[counter[1]]
        counter[0] += 1
        counter[1] += 1
        copies = []
        for last in (stream[1], TRIM[stream]):
            rows = pl.ds(stream[0], last - stream[0])
            copies.append(remote(source.at[rows], target.at[rows], ssem.at[slot], recv, device))
        if TRIM[stream] == stream[1]:
            copies[0].start()
            return copies[0].wait_send, copies[0].wait_recv

        @pl.when(big)
        def _():
            copies[0].start()

        @pl.when(jnp.logical_not(big))
        def _():
            copies[1].start()

        def finish(condition, full, cut):
            def wait():
                @pl.when(condition)
                def _():
                    full()

                @pl.when(jnp.logical_not(condition))
                def _():
                    cut()

            return wait

        other = z == (1 if big is own_big else 0)
        return (
            finish(big, copies[0].wait_send, copies[1].wait_send),
            finish(other, copies[0].wait_recv, copies[1].wait_recv),
        )

    own_big, mate_big = z == 0, z == 1
    rows, near_rows, far_rows, near, far_sum, z_sum, handles = {}, {}, {}, {}, {}, {}, {}
    out_lanes, all_lanes = slice(512, 768), slice(0, 768)

    def gather_start(p, stream):
        part = pl.ds(stream[0], stream[1] - stream[0])
        near_rows[stream] = send(A.at[p, 0, part], A.at[p, 1, part], sib, group=("near", p))
        sent, arrives = start_z(A.at[p, 0], A.at[p, 2], stream, zp, own_big)
        pending_z.append(sent)
        rows[stream] = (p, part, arrives)

    def pass_on(stream):
        p, part, arrives = rows[stream]
        arrives()
        far_rows[stream] = send(A.at[p, 2, part], A.at[p, 3, part], sib, group=("far", p))

    def all_arrived(stream):
        near_rows[stream].wait_recv()
        far_rows[stream].wait_recv()

    def own_slab(index, source_l, source_v, copies, target):
        arrived("heads", *copies)
        for (r0, r1), size, pad, own, off, count, source, head, head_rows in (
            (VIS, REGIONS, REGION_PAD, own_v, off_v, n_v, source_v, HV, VIS_HEAD),
            (LANG, WORDS, WORDS, own_l, off_l, n_l, source_l, HL, LANG_HEAD),
        ):
            inside = rows_into_slab((r1 - r0, own), off, count, size, pad).astype(BF)
            beyond = rows_into_slab((r1 - r0, head_rows), off - own, count, size, pad).astype(BF)
            target[r0:r1] = (dot_nn(inside, source[...]) + dot_nn(beyond, head[index])).astype(BF)

    stage_used = {}

    def stage_free(index, stream):
        sent = stage_used.pop((index, stream), None)
        if sent is not None:
            sent()

    def partial_nt(lhs_ref, stream, w, lanes):
        r0, r1 = stream
        rows = r1 - r0
        stage_free(0, stream)
        for n in range(NT):
            column = slice(n * TILE, (n + 1) * TILE)
            lhs = lhs_ref[:, r0:r1, :]
            lhs = lhs.reshape(SLOTS * rows, lhs.shape[-1])
            out = dot_nt(lhs, W[w, column, lanes])
            PART[r0:r1, column] = out[:rows]
            STG[0, r0:r1, column] = out[rows : 2 * rows].astype(BF)
            PZ[r0:r1, column] = out[2 * rows : 3 * rows]
            STG[1, r0:r1, column] = out[3 * rows :].astype(BF)

    def sums_after(stream, lhs, w, lanes):
        partial_nt(lhs, stream, w, lanes)
        part = pl.ds(stream[0], stream[1] - stream[0])
        copy = send(STG.at[pl.ds(0, 2), part], RSB.at[pl.ds(0, 2), part], sib, keep=False)
        stage_used[0, stream] = copy.wait_send
        far_sum[stream] = copy

    def sums_on(stream):
        r0, r1 = stream
        far_sum[stream].wait_recv()
        stage_free(2, stream)
        STG[2, r0:r1] = (PZ[r0:r1] + RSB[1, r0:r1].astype(F32)).astype(BF)
        sent, z_sum[stream] = start_z(STG.at[2], RSB.at[2], stream, zp, mate_big)
        stage_used[2, stream] = sent

    def total_of(stream):
        r0, r1 = stream
        z_sum[stream]()
        return PART[r0:r1] + RSB[0, r0:r1].astype(F32) + RSB[2, r0:r1].astype(F32)

    mask_q = head_mask(0, BF)
    mask_c = head_mask(64, BF)
    mask_q32 = head_mask(0, F32)
    mask_c32 = head_mask(64, F32)
    factor = 1.0 / math.sqrt(D_HEAD)

    def attend_slab(QV, Cb, crossed, stream, s):
        def one(queries, keys_rows, kv_row, item_size, first_item_of, P):
            (q0, q1), (k0, k1) = queries, keys_rows
            nq, nk = q1 - q0, k1 - k0
            query = QV[s, q0:q1, 0:256]
            keys = QV[s, k0:k1, 384:640]
            values = QV[s, k0:k1, 128:384]
            spread = jnp.concatenate([query * mask_q[h] for h in range(3)], 0)
            scores = dot_nt(spread, keys) * factor
            row = lax.broadcasted_iota(jnp.int32, (nq, nk), 0)
            item = jnp.full((nq, nk), float(first_item_of), F32)
            for j in range(1, nq // item_size):
                item = item + jnp.where(row >= j * item_size, 1.0, 0.0)
            same = item == KV[s, kv_row : kv_row + 1, 0:nk]
            scores = jnp.where(same[None], scores.reshape(3, nq, nk), MASKED)
            raised = jnp.exp(scores - jnp.max(scores, -1, keepdims=True))
            weights = (raised / jnp.sum(raised, -1, keepdims=True)).astype(BF).reshape(3 * nq, nk)
            P[s] = weights
            context = dot_nn(weights, values).reshape(3, nq, TILE)
            Cb[s, q0:q1] = (
                context[0] * mask_c32[0] + context[1] * mask_c32[1] + context[2] * mask_c32[2]
            ).astype(BF)

        if stream == LANG:
            if crossed:
                one(LANG, VIS, 1, WORDS, 0, PCL)
            else:
                one(LANG, LANG, 0, WORDS, 0, PS.at[0])
        else:
            half = (V1, V2).index(stream)
            if crossed:
                one(stream, LANG, 0, REGION_PAD, 2 * half, PCV.at[half])
            else:
                one(stream, stream, 2 + half, REGION_PAD, 2 * half, PS.at[1 + half])

    def attend_back_slab(QV, crossed, stream, s):
        def one(queries, keys_rows, P):
            (q0, q1), (k0, k1) = queries, keys_rows
            nq = q1 - q0
            query = QV[s, q0:q1, 0:256]
            keys = QV[s, k0:k1, 384:640]
            values = QV[s, k0:k1, 128:384]
            spread = jnp.concatenate([query * mask_q[h] for h in range(3)], 0)
            upstream = D[s, q0:q1, 512:768]
            up_spread = jnp.concatenate([upstream * mask_c[h] for h in range(3)], 0)
            weights = P[s]
            weights32 = weights.astype(F32)
            weight_grad = dot_nt(up_spread, values)
            score_grad = (
                weights32
                * (weight_grad - jnp.sum(weight_grad * weights32, -1, keepdims=True))
            ).astype(BF)
            dq = dot_nn(score_grad, keys).reshape(3, nq, TILE)
            dq = (dq[0] * mask_q32[0] + dq[1] * mask_q32[1] + dq[2] * mask_q32[2]) * factor
            dk = dot_tn(score_grad, spread) * factor
            dv = dot_tn(weights, up_spread)
            return dq, dk, dv

        if crossed:
            half = RV // 2
            dq_l, dk_v, dv_v = one(LANG, VIS, PCL)
            dq_1, dk_1, dv_1 = one(V1, LANG, PCV.at[0])
            dq_2, dk_2, dv_2 = one(V2, LANG, PCV.at[1])
            results = {
                LANG: (dq_l, dk_1 + dk_2, dv_1 + dv_2),
                V1: (dq_1, dk_v[:half], dv_v[:half]),
                V2: (dq_2, dk_v[half:], dv_v[half:]),
            }
        else:
            results = {stream: one(stream, stream, PS.at[0 if stream == LANG else 1 + (V1, V2).index(stream)])}
        for (r0, r1), (dq, dk, dv) in results.items():
            D[s, r0:r1, 0:128] = dq[:, :128].astype(BF)
            D[s, r0:r1, 128:256] = (dq[:, 128:] + dv[:, :128]).astype(BF)
            D[s, r0:r1, 256:384] = dv[:, 128:].astype(BF)
            D[s, r0:r1, 384:640] = dk.astype(BF)
            D[s, r0:r1, 640:768] = jnp.zeros((r1 - r0, 128), BF)

    def forward_norm(value, index, gain_row, r0, r1):
        center = value - jnp.mean(value, -1, keepdims=True)
        scaled = lax.rsqrt(jnp.mean(center * center, -1, keepdims=True) + EPSILON)
        normed = center * scaled
        NORM[index, r0:r1] = normed
        RSTD[index, r0:r1] = scaled
        return normed * gains[gain_row : gain_row + 1] + shifts[gain_row : gain_row + 1]

    def backward_norm(upstream, index, gain_row, bias_row, r0, r1):
        normed = NORM[index, r0:r1]
        through = upstream * gains[gain_row : gain_row + 1]
        inner = (
            through
            - jnp.mean(through, -1, keepdims=True)
            - normed * jnp.mean(through * normed, -1, keepdims=True)
        )
        result = RSTD[index, r0:r1] * inner
        VG[5 + gain_row : 6 + gain_row] += jnp.sum(upstream * normed, 0, keepdims=True)
        VG[10 + gain_row : 11 + gain_row] += jnp.sum(upstream, 0, keepdims=True)
        VG[bias_row : bias_row + 1] += jnp.sum(result, 0, keepdims=True)
        return result

    def rows_of(p, stream):
        r0, r1 = stream
        return A[p, :, r0:r1, :].reshape(SLOTS * (r1 - r0), D_MODEL)

    def tile_columns():
        return [slice(n * TILE, (n + 1) * TILE) for n in range(NT)]

    def project(stream, w):
        r0, r1 = stream
        for column in tile_columns():
            mapped = dot_nn(rows_of(1, stream), W[w, :, column]) + QB[w : w + 1, column]
            QVK[1, :, r0:r1, column] = mapped.astype(BF).reshape(SLOTS, r1 - r0, TILE)

    def project_cross(g):
        for column in tile_columns():
            rows = A[0, 2 * g : 2 * g + 2].reshape(2 * ROWS, D_MODEL)
            mapped = dot_nn(rows, W[0, :, column]) + QB[0:1, column]
            QVK[0, 2 * g : 2 * g + 2, :, column] = mapped.astype(BF).reshape(2, ROWS, TILE)

    def attend(stream, b):
        for s in range(SLOTS):
            attend_slab(QVK.at[b], C.at[b], b == 0, stream, s)

    def expand_rows(stream):
        r0, r1 = stream
        w = EXPAND[stream]
        for column in tile_columns():
            before = dot_nn(rows_of(2, stream), W[w, :, column]) + QB[w : w + 1, column]
            half = 0.5 * (1.0 + lax.erf(before * math.sqrt(0.5)))
            slope = half + before * jnp.exp(-0.5 * before * before) * (1.0 / math.sqrt(2.0 * math.pi))
            H[:, r0:r1, column] = (before * half).astype(BF).reshape(SLOTS, r1 - r0, TILE)
            GP[:, r0:r1, column] = slope.astype(BF).reshape(SLOTS, r1 - r0, TILE)

    def hidden_gradient(stream):
        r0, r1 = stream
        rows = SLOTS * (r1 - r0)
        for column in tile_columns():
            up_hidden = dot_nn(rows_of(3, stream), W[CONTRACT[stream], :, column])
            slope = GP[:, r0:r1, column].reshape(rows, TILE)
            D[:, r0:r1, column] = (up_hidden * slope.astype(F32)).astype(BF).reshape(SLOTS, r1 - r0, TILE)

    def context_gradient(p, stream, w):
        r0, r1 = stream
        upstream = dot_nn(rows_of(p, stream), W[w, :, 512:768])
        D[:, r0:r1, 512:768] = upstream.astype(BF).reshape(SLOTS, r1 - r0, TILE)

    def attend_gradient(stream, b):
        for s in range(SLOTS):
            attend_back_slab(QVK.at[b], b == 0, stream, s)

    def all_rows(ref, r0, r1, lanes):
        value = ref[:, r0:r1, lanes]
        return value.reshape(SLOTS * (r1 - r0), value.shape[-1])

    def weight_grad(w, lhs_p, rhs_ref, r0, r1, lanes=slice(0, 768)):
        for m in range(NT):
            column = slice(m * TILE, (m + 1) * TILE)
            left = all_rows(A.at[lhs_p], r0, r1, column)
            G[w, column, lanes] = dot_tn(left, all_rows(rhs_ref, r0, r1, lanes)).astype(BF)

    def attention_weight_grad(w, x_p, b_p, Cb, r0, r1, middle=None):
        if middle is None:
            weight_grad(w, x_p, D, r0, r1, slice(0, 512))
        else:
            weight_grad(w, x_p, D, r0, r1, slice(0, 384))
            middle()
            weight_grad(w, x_p, D, r0, r1, slice(384, 512))
        for m in range(NT):
            column = slice(m * TILE, (m + 1) * TILE)
            G[w, column, 512:768] = (
                dot_tn(all_rows(A.at[x_p], r0, r1, column), all_rows(D, r0, r1, slice(512, 768)))
                + dot_tn(all_rows(A.at[b_p], r0, r1, column), all_rows(Cb, r0, r1, slice(0, 256)))
            ).astype(BF)

    def bias_grad(row, r0, r1):
        total = jnp.zeros((1, D_MODEL), F32)
        for s in range(SLOTS):
            total = total + jnp.sum(D[s, r0:r1].astype(F32), 0, keepdims=True)
        QG[row : row + 1] = total

    def grad_first(part):
        w, lanes = PARTS[part]
        for j in range(2):
            half = rows_of_chip(k_flip[2], (1 - j) * SHARE, SHARE)
            send(G.at[w, half, lanes], RD.at[j, w, :, lanes], plane[j], gsem.at[2, part], group=("g", part))

    def grad_second(part):
        w, lanes = PARTS[part]
        wait_bytes(RD.at[:, w, :, lanes], gsem.at[2, part])
        for j in range(2):
            half = rows_of_chip(k_flip[1 - j], (1 - j) * SHARE, SHARE)
            G[w, half, lanes] = (G[w, half, lanes].astype(F32) + RD[j, w, :, lanes].astype(F32)).astype(BF)
        for j in range(2):
            rows_j = G.at[w, rows_of_chip(k_flip[j]), lanes]
            send(rows_j, RX.at[j, w, :, lanes], plane[j], gsem.at[j, part], group=("g", part))

    grad_nears = []

    def grad_third(part):
        w, lanes = PARTS[part]
        for j in range(2):
            wait_bytes(RX.at[j, w, :, lanes], gsem.at[j, part])
        total = G[w, pair_rows, lanes].astype(F32)
        total = total + RX[0, w, :, lanes].astype(F32) + RX[1, w, :, lanes].astype(F32)
        G[w, pair_rows, lanes] = total.astype(BF)
        low = G.at[w, rows_of_chip(k, 0, SHARE), lanes]
        high = G.at[w, rows_of_chip(k, SHARE, SHARE), lanes]
        slot = counter[0]
        counter[0] += 2
        here, there = R2.at[0, w, :, lanes], R2.at[1, w, :, lanes]
        own = pltpu.make_async_copy(low, here, gsem2.at[part])
        near = remote(high, here, ssem.at[slot], gsem2.at[part], sib)
        far_low = remote(low, there, ssem.at[slot], gsem2.at[part], (2 * k, z2))
        far_high = remote(high, there, ssem.at[slot + 1], gsem2.at[part], (2 * k + 1, z2))

        @pl.when(c == 0)
        def _():
            own.start()
            near.start()

        @pl.when(c == 1)
        def _():
            far_low.start()
            far_high.start()

        grad_nears.append((near, far_low, far_high))

    def grad_last(part):
        w, lanes = PARTS[part]
        wait_bytes(R2.at[:, w, :, lanes], gsem2.at[part])
        wgrad[w, :, lanes] = R2[0, w, :, lanes].astype(F32) + R2[1, w, :, lanes].astype(F32)

    def count_step(stage, peer):
        count_copies[stage].wait_recv()
        CA[stage + 1] = CA[stage] + CR[stage]
        if peer is not None:
            count_copies.append(send(CA.at[stage + 1], CR.at[stage + 1], peer))

    VG[...] = jnp.zeros_like(VG)
    QG[...] = jnp.zeros_like(QG)
    def send_heads(index, source_l, source_v):
        handles["heads", index] = (
            send(source_l.at[pl.ds(0, LANG_HEAD)], HL.at[index], down),
            send(source_v.at[pl.ds(0, VIS_HEAD)], HV.at[index], down),
        )

    def send_small():
        handles["kv"] = (send(KV.at[0], KV.at[1], sib), send(KV.at[0], KV.at[2], zp))
        handles["count"] = [send(CA.at[0], CR.at[0], sib)]
        handles["bias"] = send(QO, QR, (d, z2))

    def pass_keys():
        for copy in handles["kv"]:
            copy.wait_recv()
        handles["kv_far"] = send(KV.at[2], KV.at[3], sib)

    def take_small():
        handles["bias"].wait_recv()
        QB[...] = jnp.where(c == 1, QR[...], QO[...])
        handles["kv_far"].wait_recv()

    def count_step(stage, peer):
        handles["count"][stage].wait_recv()
        CA[stage + 1] = CA[stage] + CR[stage]
        if peer is not None:
            handles["count"].append(send(CA.at[stage + 1], CR.at[stage + 1], peer))

    def first_norm(stream):
        r0, r1 = stream
        value = total_of(stream) + out_bias[0:1] + A[0, 0, r0:r1].astype(F32)
        A[1, 0, r0:r1] = forward_norm(value, 0, 0, r0, r1).astype(BF)
        gather_start(1, stream)

    def second_norm(stream):
        r0, r1 = stream
        n = 1 if stream == LANG else 2
        value = total_of(stream) + out_bias[n : n + 1] + A[1, 0, r0:r1].astype(F32)
        A[2, 0, r0:r1] = forward_norm(value, 1, n, r0, r1).astype(BF)
        gather_start(2, stream)

    def last_norm(stream):
        r0, r1 = stream
        n = 0 if stream == LANG else 1
        value = total_of(stream) + contract_b[n : n + 1] + A[2, 0, r0:r1].astype(F32)
        OUTS[r0:r1] = forward_norm(value, 2, 3 + n, r0, r1).astype(BF)
        scale = total_items / CA[3, n : n + 1, 0:1]
        upstream = COT[r0:r1].astype(F32) * (FLAG[r0:r1] * scale)
        result = backward_norm(upstream, 2, 3 + n, 3 + n, r0, r1)
        DZ[r0:r1] = result
        A[3, 0, r0:r1] = result.astype(BF)
        gather_start(3, stream)

    def second_norm_back(stream):
        r0, r1 = stream
        n = 1 if stream == LANG else 2
        result = backward_norm(DZ[r0:r1] + total_of(stream), 1, n, n, r0, r1)
        DZ[r0:r1] = result
        A[4, 0, r0:r1] = result.astype(BF)
        gather_start(4, stream)

    def first_norm_back(stream):
        r0, r1 = stream
        result = backward_norm(DZ[r0:r1] + total_of(stream), 0, 0, 0, r0, r1)
        DZ[r0:r1] = result
        A[5, 0, r0:r1] = result.astype(BF)
        gather_start(5, stream)

    def final_sum(stream):
        r0, r1 = stream
        DZ[r0:r1] = DZ[r0:r1] + total_of(stream)

    quarter = jnp.where(c == 0, z, z2)
    vector_peers = [sib, plane[0], plane[1], zp, (d, z2)]
    vector_copies, late_copies = [], []

    def vector_start():
        AVA[0, 0:16] = VG[...]
        for j in range(4):
            AVA[0, 16 + 4 * j : 20 + 4 * j] = jnp.where(quarter == j, QG[1:5], 0.0)
        vector_copies.append(send(AVA.at[0], AVR.at[0], vector_peers[0]))

    def vector_step(stage):
        vector_copies[stage].wait_recv()
        AVA[stage + 1] = AVA[stage] + AVR[stage]
        if stage < 4:
            vector_copies.append(send(AVA.at[stage + 1], AVR.at[stage + 1], vector_peers[stage + 1]))

    def late_start():
        for j in range(4):
            LVA[0, j : j + 1] = jnp.where(quarter == j, QG[0:1], 0.0)
        LVA[0, 4:8] = jnp.zeros((4, D_MODEL), F32)
        late_copies.append(send(LVA.at[0], LVR.at[0], vector_peers[0]))

    def late_step(stage):
        late_copies[stage].wait_recv()
        LVA[stage + 1] = LVA[stage] + LVR[stage]
        if stage < 4:
            late_copies.append(send(LVA.at[stage + 1], LVR.at[stage + 1], vector_peers[stage + 1]))

    def vectors_out():
        vec_out[...] = AVA[5, 0:16]
        for j in range(4):

            @pl.when(z == j)
            def _(j=j):
                qb_out[0:1] = LVA[5, j : j + 1]
                qb_out[1:5] = AVA[5, 16 + 4 * j : 20 + 4 * j]

    def send_tail(name, source, target_l, target_v):
        handles[name] = (
            send(source.at[pl.ds(RL - LANG_TAIL, LANG_TAIL)], target_l, up),
            send(source.at[pl.ds(ROWS - VIS_TAIL, VIS_TAIL)], target_v, up),
        )

    def place_rows():
        for name in ("outs", "grads"):
            for copy in handles[name]:
                copy.wait_recv()
        before_l = jnp.where(z == 1, 0, 25 - 5 * z)
        before_v = jnp.where(z == 1, 0, 45 - 9 * z)
        for (r0, r1), size, pad, own_rows, off, before, tail_rows, out_ref, grad_ref, t_out, t_grad in (
            (LANG, WORDS, WORDS, own_l, off_l, before_l, LANG_TAIL, lang_out, lang_grad, TLO, TLG),
            (VIS, REGIONS, REGION_PAD, own_v, off_v, before_v, VIS_TAIL, vis_out, vis_grad, TVO, TVG),
        ):
            from_own = rows_from_slab((own_rows, r1 - r0), -off, 0, off, own_rows, size, pad)
            from_tail = rows_from_slab(
                (own_rows, tail_rows), own_rows - before, r1 - r0 - tail_rows, 0, off, size, pad
            )
            out_ref[...] = (
                dot_nn(from_own.astype(BF), OUTS[r0:r1]) + dot_nn(from_tail.astype(BF), t_out[...])
            ).astype(BF)
            exact = lax.Precision.HIGHEST
            grad_ref[...] = jnp.dot(
                from_own, DZ[r0:r1], precision=exact, preferred_element_type=F32
            ) + jnp.dot(from_tail, t_grad[...], precision=exact, preferred_element_type=F32)


    weight_first(0)
    weight_second(0)
    send_heads(0, lang, vis)
    weight_first(7)
    weight_third(0)
    send_heads(1, lcot, vcot)
    own_slab(0, lang, vis, handles["heads", 0], A.at[0, 0])
    gather_start(0, V1)
    gather_start(0, V2)
    attention_share(2)
    weight_ready(0)
    weight_first(2)
    send_small()
    gather_start(0, LANG)
    weight_second(7)
    attention_share(1)
    pass_on(V2)
    pass_on(V1)
    weight_third(7)
    weight_first(1)
    pass_keys()
    weight_second(2)
    pass_on(LANG)
    all_arrived(V1)
    all_arrived(V2)
    own_slab(1, lcot, vcot, handles["heads", 1], COT)
    weight_ready(7)
    weight_first(4)
    take_small()
    all_arrived(LANG)
    project_cross(0)
    weight_second(1)
    project_cross(1)
    weight_third(2)
    weight_first(6)
    attend(V1, 0)
    sums_after(V1, C.at[0], 0, out_lanes)
    weight_second(4)
    attend(V2, 0)
    sums_after(V2, C.at[0], 0, out_lanes)
    weight_first(3)
    sums_on(V1)
    attend(LANG, 0)
    sums_after(LANG, C.at[0], 0, out_lanes)
    sums_on(V2)
    count_step(0, plane[0])
    weight_third(1)
    sums_on(LANG)
    weight_third(4)
    weight_first(5)
    weight_second(6)
    first_norm(V1)
    first_norm(V2)
    pass_on(V1)
    weight_ready(2)
    pass_on(V2)
    first_norm(LANG)
    all_arrived(V1)
    project(V1, 2)
    attend(V1, 1)
    sums_after(V1, C.at[1], 2, out_lanes)
    weight_second(3)
    all_arrived(V2)
    project(V2, 2)
    attend(V2, 1)
    weight_ready(1)
    pass_on(LANG)
    sums_after(V2, C.at[1], 2, out_lanes)
    weight_third(6)
    sums_on(V1)
    weight_ready(4)
    all_arrived(LANG)
    project(LANG, 1)
    attend(LANG, 1)
    sums_after(LANG, C.at[1], 1, out_lanes)
    sums_on(V2)
    weight_second(5)
    sums_on(LANG)
    weight_third(3)
    second_norm(V1)
    second_norm(LANG)
    second_norm(V2)
    count_step(1, plane[1])
    pass_on(V1)
    all_arrived(V1)
    weight_ready(6)
    expand_rows(V1)
    pass_on(V2)
    sums_after(V1, H, 6, all_lanes)
    pass_on(LANG)
    weight_third(5)
    weight_ready(3)
    all_arrived(V2)
    expand_rows(V2)
    sums_after(V2, H, 6, all_lanes)
    count_step(2, None)
    all_arrived(LANG)
    sums_on(V1)
    expand_rows(LANG)
    weight_ready(5)
    sums_on(V2)
    last_norm(V1)
    sums_after(LANG, H, 5, all_lanes)
    sums_on(LANG)
    pass_on(V1)
    last_norm(V2)
    last_norm(LANG)
    all_arrived(V1)
    hidden_gradient(V1)
    pass_on(V2)
    sums_after(V1, D, 4, all_lanes)
    all_arrived(V2)
    hidden_gradient(V2)
    sums_after(V2, D, 4, all_lanes)
    pass_on(LANG)
    weight_grad(4, 2, D, *VIS)
    sums_on(V1)
    weight_grad(6, 3, H, *VIS)
    grad_first(6)
    sums_on(V2)
    all_arrived(LANG)
    hidden_gradient(LANG)
    grad_first(4)
    sums_after(LANG, D, 3, all_lanes)
    second_norm_back(V1)
    weight_grad(5, 3, H, *LANG)
    grad_first(5)
    second_norm_back(V2)
    sums_on(LANG)
    bias_grad(4, *VIS)
    pass_on(V1)
    grad_second(6)
    all_arrived(V1)
    send_tail("outs", OUTS, TLO, TVO)
    context_gradient(4, V1, 2)
    weight_grad(3, 2, D, *LANG)
    grad_first(3)
    bias_grad(3, *LANG)
    second_norm_back(LANG)
    pass_on(V2)
    attend_gradient(V1, 1)
    sums_after(V1, D, 2, all_lanes)
    grad_second(4)
    all_arrived(V2)
    context_gradient(4, V2, 2)
    attend_gradient(V2, 1)
    pass_on(LANG)
    sums_on(V1)
    sums_after(V2, D, 2, all_lanes)
    all_arrived(LANG)
    context_gradient(4, LANG, 1)
    attend_gradient(LANG, 1)
    grad_third(6)
    grad_second(5)
    sums_on(V2)
    sums_after(LANG, D, 1, all_lanes)
    bias_grad(1, *LANG)
    sums_on(LANG)
    attention_weight_grad(1, 1, 4, C.at[1], *LANG)
    first_norm_back(V1)
    first_norm_back(V2)
    grad_second(3)
    attention_weight_grad(2, 1, 4, C.at[1], *VIS)
    grad_first(2)
    first_norm_back(LANG)
    bias_grad(2, *VIS)
    pass_on(V1)
    grad_third(4)
    pass_on(V2)
    grad_first(1)
    grad_third(5)
    pass_on(LANG)
    all_arrived(V2)
    all_arrived(V1)
    context_gradient(5, V1, 0)
    context_gradient(5, V2, 0)
    vector_start()
    grad_second(2)
    vector_step(0)
    all_arrived(LANG)
    context_gradient(5, LANG, 0)
    grad_third(3)
    attend_gradient(None, 0)
    sums_after(V1, D, 0, all_lanes)
    vector_step(1)
    attention_weight_grad(0, 0, 5, C.at[0], *BOTH, middle=lambda: grad_first(0))
    grad_first(7)
    vector_step(2)
    grad_third(2)
    grad_second(0)
    grad_second(1)
    sums_after(LANG, D, 0, all_lanes)
    grad_last(4)
    sums_on(V1)
    grad_last(6)
    vector_step(3)
    sums_on(LANG)
    grad_last(5)
    bias_grad(0, *BOTH)
    late_start()
    grad_third(0)
    sums_after(V2, D, 0, all_lanes)
    sums_on(V2)
    final_sum(V1)
    grad_third(1)
    grad_second(7)
    final_sum(LANG)
    late_step(0)
    grad_last(2)
    final_sum(V2)
    send_tail("grads", DZ, TLG, TVG)
    vector_step(4)
    late_step(1)
    late_step(2)
    late_step(3)
    grad_last(1)
    grad_last(0)
    grad_last(3)
    late_step(4)
    vectors_out()
    grad_third(7)
    place_rows()
    grad_last(7)

    for copy in pending:
        copy.wait_send()
    for (name, index), slot in groups.items():
        if name in ("w", "g"):
            w, lanes = PARTS[index]
            wait_bytes(W.at[w, pl.ds(0, 3 * HALF_PAIR), lanes], ssem.at[slot])
        else:
            wait_bytes(A.at[index, 0], ssem.at[slot])
    for sent in pending_z:
        sent()
    for index, stream in list(stage_used):
        stage_free(index, stream)

    @pl.when(c == 1)
    def _():
        for copy in nears:
            copy.wait_send()
        for _, far_low, far_high in grad_nears:
            far_low.wait_send()
            far_high.wait_send()

    @pl.when(c == 0)
    def _():
        for near, _, _ in grad_nears:
            near.wait_send()
    assert counter[0] <= ssem.shape[0] and counter[1] <= rsem.shape[0], counter


N_SEND = 240
N_RECV = 160


def fused_layer(total_items, *operands):
    own_l, own_v = operands[0].shape[0], operands[1].shape[0]
    vmem = pl.BlockSpec(memory_space=pltpu.VMEM)
    smem = pl.BlockSpec(memory_space=pltpu.SMEM)
    shapes = [
        ((own_l, D), BF),
        ((own_v, D), BF),
        ((own_l, D), F32),
        ((own_v, D), F32),
        ((7, SHARE, D), F32),
        ((16, D), F32),
        ((8, D), F32),
    ]
    scratch = [
        ((7, D, D), BF),
        ((7, D, D), BF),
        ((2, 7, SHARE, D), BF),
        ((2, 7, HALF_PAIR, D), BF),
        ((2, 7, SHARE, D), BF),
        ((6, SLOTS, ROWS, D), BF),
        ((SLOTS, 8, TILE), F32),
        ((3, ROWS, D), BF),
        ((3, ROWS, D), BF),
        ((2, SLOTS, ROWS, D), BF),
        ((SLOTS, ROWS, D), BF),
        ((2, SLOTS, ROWS, TILE), BF),
        ((SLOTS, ROWS, D), BF),
        ((SLOTS, ROWS, D), BF),
        ((SLOTS, 3 * RL, RV), BF),
        ((2, SLOTS, 3 * RL, RL), BF),
        ((3, SLOTS, 3 * RL, RL), BF),
        ((ROWS, D), F32),
        ((ROWS, D), F32),
        ((3, ROWS, D), F32),
        ((3, ROWS, 1), F32),
        ((ROWS, D), F32),
        ((ROWS, D), BF),
        ((3, SHARE, D), BF),
        ((ROWS, 1), F32),
        ((8, D), F32),
        ((8, D), F32),
        ((8, D), F32),
        ((4, 8, 128), F32),
        ((3, 8, 128), F32),
        ((16, D), F32),
        ((8, D), F32),
        ((6, N_AR, D), F32),
        ((5, N_AR, D), F32),
        ((6, 8, D), F32),
        ((5, 8, D), F32),
        ((2, LANG_HEAD, D), BF),
        ((2, VIS_HEAD, D), BF),
        ((ROWS, D), BF),
        ((LANG_TAIL, D), BF),
        ((VIS_TAIL, D), BF),
        ((LANG_TAIL, D), F32),
        ((VIS_TAIL, D), F32),
    ]
    dma = pltpu.SemaphoreType.DMA
    return pl.pallas_call(
        partial(layer_kernel, total_items),
        out_shape=[jax.ShapeDtypeStruct(s, t) for s, t in shapes],
        in_specs=[vmem] * 4 + [smem] * 3 + [vmem] * (len(operands) - 7),
        out_specs=[vmem] * len(shapes),
        scratch_shapes=[pltpu.VMEM(s, t) for s, t in scratch]
        + [dma((N_SEND,)), dma((N_RECV,)), dma((3, 8)), dma((8,)), dma((3, 8)), dma((8,))],
        compiler_params=pltpu.CompilerParams(
            collective_id=0, has_side_effects=True, vmem_limit_bytes=VMEM_LIMIT
        ),
    )(*operands)


def unpack_kernel(lo, vo, lg, vg, wgrad, vec, qb, *outs):
    (lo_out, vo_out, lg_out, vg_out, proj, qv, outw, outb, exp, expb, con, conb, gain, shift) = outs
    lo_out[...] = lo[...]
    vo_out[...] = vo[...]
    lg_out[...] = lg[...]
    vg_out[...] = vg[...]
    width = HALF_PAIR
    for b in range(3):
        for j, lane in enumerate((0, 2 * width, width)):
            proj[b, j] = wgrad[b, :, lane : lane + width]
        outw[b] = wgrad[b, :, 3 * width :].T
        for j in range(2):
            qv[b, j : j + 1] = qb[b : b + 1, j * width : (j + 1) * width]
    for stream in range(2):
        exp[stream] = wgrad[3 + stream]
        con[stream] = wgrad[5 + stream]
    expb[...] = qb[3:5]
    outb[...] = vec[0:3]
    conb[...] = vec[3:5]
    gain[...] = vec[5:10]
    shift[...] = vec[10:15]


def unpack(packed, shapes):
    vmem = pl.BlockSpec(memory_space=pltpu.VMEM)
    return pl.pallas_call(
        unpack_kernel,
        out_shape=shapes,
        in_specs=[vmem] * len(packed),
        out_specs=[vmem] * len(shapes),
        compiler_params=pltpu.CompilerParams(vmem_limit_bytes=VMEM_LIMIT),
    )(*packed)


def on_device_fused(
    language_input,
    vision_input,
    word_lengths,
    region_counts,
    task_flags,
    language_cotangent,
    vision_cotangent,
    projection_weight,
    query_value_bias,
    output_weight,
    output_bias,
    expand_weight,
    expand_bias,
    contract_weight,
    contract_bias,
    norm_gain,
    norm_bias,
):
    packed = fused_layer(
        float(word_lengths.shape[0] * lax.axis_size("dp")),
        language_input,
        vision_input,
        language_cotangent,
        vision_cotangent,
        word_lengths,
        region_counts,
        task_flags.T,
        projection_weight,
        query_value_bias,
        output_weight,
        expand_weight,
        expand_bias,
        contract_weight.transpose(0, 2, 1),
        output_bias,
        contract_bias,
        norm_gain,
        norm_bias,
    )
    like = [
        (language_input, BF),
        (vision_input, BF),
        (language_input, F32),
        (vision_input, F32),
        (projection_weight, F32),
        (query_value_bias, F32),
        (output_weight, F32),
        (output_bias, F32),
        (expand_weight, F32),
        (expand_bias, F32),
        (contract_weight.transpose(0, 2, 1), F32),
        (contract_bias, F32),
        (norm_gain, F32),
        (norm_bias, F32),
    ]
    outs = list(unpack(packed, [jax.ShapeDtypeStruct(a.shape, t) for a, t in like]))
    outs[10] = outs[10].transpose(0, 2, 1)
    return tuple(outs)


def solution(mesh):
    in_specs = (
        P(("dp", "mp"), None),
        P(("dp", "mp"), None),
        P("dp"),
        P("dp"),
        P("dp", None),
        P(("dp", "mp"), None),
        P(("dp", "mp"), None),
        P(None, None, "dp", "mp"),
        P(None, None, "mp"),
        P(None, "mp", "dp"),
        P(),
        P(None, "dp", "mp"),
        P(None, "mp"),
        P(None, "mp", "dp"),
        P(),
        P(),
        P(),
    )
    out_specs = (
        P(("dp", "mp"), None),
        P(("dp", "mp"), None),
        P(("dp", "mp"), None),
        P(("dp", "mp"), None),
        P(None, None, "dp", "mp"),
        P(None, None, "mp"),
        P(None, "mp", "dp"),
        P(),
        P(None, "dp", "mp"),
        P(None, "mp"),
        P(None, "mp", "dp"),
        P(),
        P(),
        P(),
    )
    fused = dict(mesh.shape) == {"dp": 8, "mp": 4}
    return jax.shard_map(
        on_device_fused if fused else on_device, mesh=mesh, in_specs=in_specs, out_specs=out_specs, check_vma=False
    )
```

```python
from functools import partial
import math
from types import SimpleNamespace

import jax
import jax.numpy as jnp
from jax import lax
from jax.experimental import pallas as pl
from jax.experimental.pallas import tpu as pltpu
from jax.sharding import PartitionSpec as P

D = 768
HEADS = 12
WORDS = 20
REGIONS = 36
D_MODEL = D
D_HEAD = D // HEADS

EPSILON = 1e-12
MASKED = -1e30


def layer_norm(summed, gain, shift):
    center = summed - jnp.mean(summed, -1, keepdims=True)
    scaled = lax.rsqrt(jnp.mean(center * center, -1, keepdims=True) + EPSILON)
    normed = center * scaled
    return (normed * gain + shift, normed, scaled)


def norm_back(upstream, normed, scaled, gain):
    through = upstream * gain
    inner = (
        through
        - jnp.mean(through, -1, keepdims=True)
        - normed * jnp.mean(through * normed, -1, keepdims=True)
    )
    return (scaled * inner, jnp.sum(upstream * normed, 0), jnp.sum(upstream, 0))


def split_heads(rows, item_count):
    head_size = D // HEADS
    return rows.reshape(
        item_count, rows.shape[0] // item_count, rows.shape[1] // head_size, head_size
    )


def join_heads(block):
    return block.reshape(block.shape[0] * block.shape[1], block.shape[2] * block.shape[3])


def project(rows, weight, bias, item_count):
    mapped = jnp.einsum("rd,jde->jre", rows, weight, preferred_element_type=jnp.float32)
    query = split_heads((mapped[0] + bias[0]).astype(jnp.bfloat16), item_count)
    keys = split_heads(mapped[1].astype(jnp.bfloat16), item_count)
    values = split_heads((mapped[2] + bias[1]).astype(jnp.bfloat16), item_count)
    return (query, keys, values)


def masked_scores(query, keys, valid):
    scores = jnp.einsum("inhd,imhd->ihnm", query, keys, preferred_element_type=jnp.float32) * (
        1.0 / math.sqrt(D // HEADS)
    )
    return jnp.where(valid[:, None, None, :], scores, MASKED)


def attend(query, keys, values, valid):
    scores = masked_scores(query, keys, valid)
    highest = jnp.max(scores, -1, keepdims=True)
    raised = jnp.exp(scores - highest)
    summed = jnp.sum(raised, -1, keepdims=True)
    context = jnp.einsum(
        "ihnm,imhd->inhd",
        (raised / summed).astype(jnp.bfloat16),
        values,
        preferred_element_type=jnp.float32,
    )
    return (join_heads(context).astype(jnp.bfloat16), highest + jnp.log(summed))


def attend_back(query, keys, values, valid, log_total, context_grad):
    factor = 1.0 / math.sqrt(D // HEADS)
    upstream = context_grad.reshape(query.shape)
    weights = jnp.exp(masked_scores(query, keys, valid) - log_total)
    weight_grad = jnp.einsum(
        "inhd,imhd->ihnm", upstream, values, preferred_element_type=jnp.float32
    )
    score_grad = (
        weights * (weight_grad - jnp.sum(weight_grad * weights, -1, keepdims=True))
    ).astype(jnp.bfloat16)
    query_grad = (
        jnp.einsum("ihnm,imhd->inhd", score_grad, keys, preferred_element_type=jnp.float32) * factor
    ).astype(jnp.bfloat16)
    keys_grad = (
        jnp.einsum("ihnm,inhd->imhd", score_grad, query, preferred_element_type=jnp.float32)
        * factor
    ).astype(jnp.bfloat16)
    values_grad = jnp.einsum(
        "ihnm,inhd->imhd",
        weights.astype(jnp.bfloat16),
        upstream,
        preferred_element_type=jnp.float32,
    ).astype(jnp.bfloat16)
    return (join_heads(query_grad), join_heads(keys_grad), join_heads(values_grad))


def project_back(rows, query_grad, keys_grad, values_grad):
    stacked = jnp.stack([query_grad, keys_grad, values_grad])
    weight_grad = jnp.einsum("rd,jre->jde", rows, stacked, preferred_element_type=jnp.float32)
    bias_grad = jnp.stack(
        [jnp.sum(query_grad.astype(jnp.float32), 0), jnp.sum(values_grad.astype(jnp.float32), 0)]
    )
    return (weight_grad, bias_grad, stacked)


def gather_rows(language_rows, vision_rows):
    return (
        lax.all_gather(language_rows, "mp", axis=0, tiled=True),
        lax.all_gather(vision_rows, "mp", axis=0, tiled=True),
    )


def rows_of(language_part, vision_part):
    return (
        lax.all_to_all(language_part, "mp", split_axis=0, concat_axis=1, tiled=True),
        lax.all_to_all(vision_part, "mp", split_axis=0, concat_axis=1, tiled=True),
    )


def gather_grads(language_rows, vision_rows):
    return (
        lax.all_gather(language_rows, "mp", axis=0, tiled=True),
        lax.all_gather(vision_rows, "mp", axis=0, tiled=True),
    )


def grads_of(language_part, vision_part):
    return (
        lax.all_to_all(language_part, "mp", split_axis=1, concat_axis=2, tiled=True),
        lax.all_to_all(vision_part, "mp", split_axis=1, concat_axis=2, tiled=True),
    )


def matmul(left, right):
    return jnp.dot(left, right, preferred_element_type=jnp.float32)


def on_device(
    language_input,
    vision_input,
    word_lengths,
    region_counts,
    task_flags,
    language_cotangent,
    vision_cotangent,
    projection_weight,
    query_value_bias,
    output_weight,
    output_bias,
    expand_weight,
    expand_bias,
    contract_weight,
    contract_bias,
    norm_gain,
    norm_bias,
):
    item_count = word_lengths.shape[0]
    flag_total = lax.psum(jnp.sum(task_flags, 0), "dp")
    projection, out_weight, expand, contract = (
        lax.all_gather(projection_weight, "dp", axis=2, tiled=True),
        lax.all_gather(output_weight, "dp", axis=2, tiled=True),
        lax.all_gather(expand_weight, "dp", axis=1, tiled=True),
        lax.all_gather(contract_weight, "dp", axis=2, tiled=True),
    )
    projection_full, out_full, expand_full, contract_full = (
        lax.all_gather(projection, "mp", axis=3, tiled=True),
        lax.all_gather(out_weight, "mp", axis=1, tiled=True),
        lax.all_gather(expand, "mp", axis=2, tiled=True),
        lax.all_gather(contract, "mp", axis=1, tiled=True),
    )
    valid = [
        jnp.arange(WORDS, dtype=jnp.int32)[None, :] < word_lengths[:, None],
        jnp.arange(REGIONS, dtype=jnp.int32)[None, :] < region_counts[:, None],
    ]
    row_counts = [WORDS, REGIONS]
    inputs = [language_input.astype(jnp.float32), vision_input.astype(jnp.float32)]
    cross_rows = gather_rows(language_input, vision_input)
    cross_parts = [
        project(cross_rows[stream], projection[0], query_value_bias[0], item_count)
        for stream in range(2)
    ]
    cross_context = []
    cross_total = []
    for stream in range(2):
        other = 1 - stream
        context, log_total = attend(
            cross_parts[stream][0], cross_parts[other][1], cross_parts[other][2], valid[other]
        )
        cross_context.append(context)
        cross_total.append(log_total)
    moved = rows_of(cross_context[0], cross_context[1])
    branch = [matmul(moved[stream], out_full[0]) for stream in range(2)]
    first = [
        layer_norm(branch[stream] + output_bias[0] + inputs[stream], norm_gain[0], norm_bias[0])
        for stream in range(2)
    ]
    first_out = [first[stream][0].astype(jnp.bfloat16) for stream in range(2)]
    self_rows = gather_rows(first_out[0], first_out[1])
    self_parts = [
        project(self_rows[stream], projection[1 + stream], query_value_bias[1 + stream], item_count)
        for stream in range(2)
    ]
    self_context = []
    self_total = []
    for stream in range(2):
        context, log_total = attend(
            self_parts[stream][0], self_parts[stream][1], self_parts[stream][2], valid[stream]
        )
        self_context.append(context)
        self_total.append(log_total)
    moved = rows_of(self_context[0], self_context[1])
    branch = [matmul(moved[stream], out_full[1 + stream]) for stream in range(2)]
    second = [
        layer_norm(
            branch[stream] + output_bias[1 + stream] + first_out[stream].astype(jnp.float32),
            norm_gain[1 + stream],
            norm_bias[1 + stream],
        )
        for stream in range(2)
    ]
    second_out = [second[stream][0].astype(jnp.bfloat16) for stream in range(2)]
    feed_rows = gather_rows(second_out[0], second_out[1])
    before = [
        matmul(feed_rows[stream], expand[stream]) + expand_bias[stream] for stream in range(2)
    ]
    hidden = [
        jax.nn.gelu(before[stream], approximate=False).astype(jnp.bfloat16) for stream in range(2)
    ]
    moved = rows_of(hidden[0], hidden[1])
    branch = [matmul(moved[stream], contract_full[stream]) for stream in range(2)]
    third = [
        layer_norm(
            branch[stream] + contract_bias[stream] + second_out[stream].astype(jnp.float32),
            norm_gain[3 + stream],
            norm_bias[3 + stream],
        )
        for stream in range(2)
    ]
    language_out = third[0][0].astype(jnp.bfloat16)
    vision_out = third[1][0].astype(jnp.bfloat16)
    item_scale = task_flags.astype(jnp.float32) * (
        item_count * lax.axis_size("dp") / flag_total.astype(jnp.float32)
    )
    shard_index = lax.axis_index("mp")
    upstream = []
    for stream, cotangent in enumerate([language_cotangent, vision_cotangent]):
        per_row = jnp.repeat(
            item_scale[:, stream],
            row_counts[stream],
            total_repeat_length=item_count * row_counts[stream],
        )
        shard_rows = cotangent.shape[0]
        row_scale = lax.dynamic_slice_in_dim(per_row, shard_index * shard_rows, shard_rows)
        upstream.append(cotangent.astype(jnp.float32) * row_scale[:, None])
    third_back = [
        norm_back(upstream[stream], third[stream][1], third[stream][2], norm_gain[3 + stream])
        for stream in range(2)
    ]
    sent = gather_grads(
        third_back[0][0].astype(jnp.bfloat16), third_back[1][0].astype(jnp.bfloat16)
    )
    expand_local = []
    expand_bias_local = []
    contract_local = []
    before_grads = []
    for stream in range(2):
        hidden_grad = jnp.einsum(
            "rd,fd->rf", sent[stream], contract[stream], preferred_element_type=jnp.float32
        )
        contract_local.append(
            jnp.einsum(
                "rf,rd->fd", hidden[stream], sent[stream], preferred_element_type=jnp.float32
            )
        )
        unused, pull = jax.vjp(partial(jax.nn.gelu, approximate=False), before[stream])
        before_grad = pull(hidden_grad)[0].astype(jnp.bfloat16)
        expand_local.append(
            jnp.einsum(
                "rd,rf->df", feed_rows[stream], before_grad, preferred_element_type=jnp.float32
            )
        )
        expand_bias_local.append(jnp.sum(before_grad.astype(jnp.float32), 0))
        before_grads.append(before_grad[None])
    moved = grads_of(before_grads[0], before_grads[1])
    back = [
        jnp.einsum(
            "rf,df->rd", moved[stream][0], expand_full[stream], preferred_element_type=jnp.float32
        )
        for stream in range(2)
    ]
    second_grad = [third_back[stream][0] + back[stream] for stream in range(2)]
    second_back = [
        norm_back(second_grad[stream], second[stream][1], second[stream][2], norm_gain[1 + stream])
        for stream in range(2)
    ]
    sent = gather_grads(
        second_back[0][0].astype(jnp.bfloat16), second_back[1][0].astype(jnp.bfloat16)
    )
    self_weight = []
    self_bias = []
    self_out = []
    stacks = []
    for stream in range(2):
        context_grad = jnp.einsum(
            "rd,ed->re", sent[stream], out_weight[1 + stream], preferred_element_type=jnp.float32
        ).astype(jnp.bfloat16)
        self_out.append(
            jnp.einsum(
                "re,rd->ed", self_context[stream], sent[stream], preferred_element_type=jnp.float32
            )
        )
        grads = attend_back(
            self_parts[stream][0],
            self_parts[stream][1],
            self_parts[stream][2],
            valid[stream],
            self_total[stream],
            context_grad,
        )
        weight_part, bias_part, stacked = project_back(
            self_rows[stream], grads[0], grads[1], grads[2]
        )
        self_weight.append(weight_part)
        self_bias.append(bias_part)
        stacks.append(stacked)
    moved = grads_of(stacks[0], stacks[1])
    back = [
        jnp.einsum(
            "jre,jde->rd",
            moved[stream],
            projection_full[1 + stream],
            preferred_element_type=jnp.float32,
        )
        for stream in range(2)
    ]
    first_grad = [second_back[stream][0] + back[stream] for stream in range(2)]
    first_back = [
        norm_back(first_grad[stream], first[stream][1], first[stream][2], norm_gain[0])
        for stream in range(2)
    ]
    sent = gather_grads(
        first_back[0][0].astype(jnp.bfloat16), first_back[1][0].astype(jnp.bfloat16)
    )
    cross_out = jnp.einsum(
        "re,rd->ed", cross_context[0], sent[0], preferred_element_type=jnp.float32
    ) + jnp.einsum("re,rd->ed", cross_context[1], sent[1], preferred_element_type=jnp.float32)
    triples = [[None, None, None], [None, None, None]]
    for stream in range(2):
        other = 1 - stream
        context_grad = jnp.einsum(
            "rd,ed->re", sent[stream], out_weight[0], preferred_element_type=jnp.float32
        ).astype(jnp.bfloat16)
        grads = attend_back(
            cross_parts[stream][0],
            cross_parts[other][1],
            cross_parts[other][2],
            valid[other],
            cross_total[stream],
            context_grad,
        )
        triples[stream][0] = grads[0]
        triples[other][1] = grads[1]
        triples[other][2] = grads[2]
    results = [
        project_back(cross_rows[stream], triples[stream][0], triples[stream][1], triples[stream][2])
        for stream in range(2)
    ]
    cross_weight = results[0][0] + results[1][0]
    cross_bias = results[0][1] + results[1][1]
    moved = grads_of(results[0][2], results[1][2])
    back = [
        jnp.einsum(
            "jre,jde->rd", moved[stream], projection_full[0], preferred_element_type=jnp.float32
        )
        for stream in range(2)
    ]
    language_grad = first_back[0][0] + back[0]
    vision_grad = first_back[1][0] + back[1]
    projection_stack = jnp.stack([cross_weight, self_weight[0], self_weight[1]])
    output_stack = jnp.stack([cross_out, self_out[0], self_out[1]])
    projection_grad, output_weight_grad, expand_grad, contract_grad = (
        lax.psum_scatter(projection_stack, "dp", scatter_dimension=2, tiled=True),
        lax.psum_scatter(output_stack, "dp", scatter_dimension=2, tiled=True),
        lax.psum_scatter(jnp.stack(expand_local), "dp", scatter_dimension=1, tiled=True),
        lax.psum_scatter(jnp.stack(contract_local), "dp", scatter_dimension=2, tiled=True),
    )
    query_value_grad, expand_bias_grad = lax.psum(
        (jnp.stack([cross_bias, self_bias[0], self_bias[1]]), jnp.stack(expand_bias_local)), "dp"
    )
    output_bias_local = jnp.stack(
        [
            jnp.sum(first_back[0][0], 0) + jnp.sum(first_back[1][0], 0),
            jnp.sum(second_back[0][0], 0),
            jnp.sum(second_back[1][0], 0),
        ]
    )
    contract_bias_local = jnp.stack([jnp.sum(third_back[0][0], 0), jnp.sum(third_back[1][0], 0)])
    gain_local = jnp.stack(
        [
            first_back[0][1] + first_back[1][1],
            second_back[0][1],
            second_back[1][1],
            third_back[0][1],
            third_back[1][1],
        ]
    )
    shift_local = jnp.stack(
        [
            first_back[0][2] + first_back[1][2],
            second_back[0][2],
            second_back[1][2],
            third_back[0][2],
            third_back[1][2],
        ]
    )
    output_bias_grad, contract_bias_grad, norm_gain_grad, norm_bias_grad = lax.psum(
        (output_bias_local, contract_bias_local, gain_local, shift_local), ("dp", "mp")
    )
    return (
        language_out,
        vision_out,
        language_grad,
        vision_grad,
        projection_grad,
        query_value_grad,
        output_weight_grad,
        output_bias_grad,
        expand_grad,
        expand_bias_grad,
        contract_grad,
        contract_bias_grad,
        norm_gain_grad,
        norm_bias_grad,
    )


MESH = pl.DeviceIdType.MESH
BF = jnp.bfloat16
F32 = jnp.float32
SLOTS = 4
RL = SLOTS * WORDS
RV = SLOTS * REGIONS
ROWS = RL + RV
SHARE = 96
HALF_PAIR = 2 * SHARE
LANG_HEAD = 16
VIS_HEAD = 32
LANG_TAIL = 32
VIS_TAIL = 64
N_AR = 32
NT = 3
TILE = 256
LANG = (0, RL)
VIS = (RL, ROWS)
BOTH = (0, ROWS)
SELF = {LANG: 1, VIS: 2}
EXPAND = {LANG: 3, VIS: 4}
CONTRACT = {LANG: 5, VIS: 6}
TRIM = {LANG: LANG[0] + 64, VIS: VIS[0] + 112}
VMEM_LIMIT = 63 * 1024 * 1024


def dot_nn(left, right):
    return lax.dot_general(left, right, (((1,), (0,)), ((), ())), preferred_element_type=F32)


def dot_nt(left, right):
    return lax.dot_general(left, right, (((1,), (1,)), ((), ())), preferred_element_type=F32)


def dot_tn(left, right):
    return lax.dot_general(left, right, (((0,), (0,)), ((), ())), preferred_element_type=F32)


def head_mask(first_lane, dtype):
    lane = lax.broadcasted_iota(jnp.int32, (1, TILE), 1) - first_lane
    return [
        jnp.where((lane >= 64 * h) & (lane < 64 * h + 64), 1.0, 0.0).astype(dtype) for h in range(3)
    ]


def select_rows(shape, shift, low, high):
    row = lax.broadcasted_iota(jnp.int32, shape, 0)
    column = lax.broadcasted_iota(jnp.int32, shape, 1)
    return jnp.where((column - row == shift) & (row >= low) & (row < high), 1.0, 0.0)


def layer_kernel(
    total_items,
    lang,
    vis,
    lcot,
    vcot,
    lengths,
    regions,
    flags,
    projection,
    query_value,
    out_weight,
    expand,
    expand_b,
    contract,
    out_bias,
    contract_b,
    gains,
    shifts,
    lang_out,
    vis_out,
    lang_grad,
    vis_grad,
    wgrad,
    vec_out,
    qb_out,
    W,
    G,
    RD,
    RX,
    R2,
    A,
    KV,
    RSB,
    STG,
    QVK,
    D,
    C,
    H,
    GP,
    PCL,
    PCV,
    PSL,
    PSV,
    PART,
    PZ,
    NORM,
    RSTD,
    DZ,
    COT,
    SH,
    FLAG,
    QO,
    QB,
    QR,
    CA,
    CR,
    VG,
    QG,
    AVA,
    AVR,
    LVA,
    LVR,
    HL,
    HV,
    OUTS,
    TLO,
    TVO,
    TLG,
    TVG,
    ssem,
    rsem,
    wsem,
    wsem_z,
    gsem,
    gsem2,
    lsem,
):
    d = lax.axis_index("dp")
    z = lax.axis_index("mp")
    c = d % 2
    k = d // 2
    k_flip = [k + 1 - 2 * (k % 2), (k + 2) % 4, 3 - k]
    sib = (d + 1 - 2 * c, z)
    zp = (d, z + 1 - 2 * (z % 2))
    z2 = (z + 2) % 4
    up = (d, (z + 1) % 4)
    down = (d, (z + 3) % 4)
    plane = [(2 * kf + c, z) for kf in k_flip]
    far = (2 * k + 1, z2)

    pending = []
    counter = [0, 0]

    def remote(src, dst, send, recv, device):
        return pltpu.make_async_remote_copy(
            src_ref=src, dst_ref=dst, send_sem=send, recv_sem=recv, device_id=device, device_id_type=MESH
        )

    def send(src, dst, device, recv=None, keep=True):
        slot = counter[0]
        counter[0] += 1
        if recv is None:
            recv = rsem.at[counter[1]]
            counter[1] += 1
        copy = remote(src, dst, ssem.at[slot], recv, device)
        copy.start()
        if keep:
            pending.append(copy)
        return copy

    own_big, mate_big = z == 0, z == 1

    def either(condition, full, cut):
        def wait():
            @pl.when(condition)
            def _():
                full()

            @pl.when(jnp.logical_not(condition))
            def _():
                cut()

        return wait

    def send_z(source, target, stream, big, keep=True):
        slot, recv = counter[0], rsem.at[counter[1]]
        counter[0] += 1
        counter[1] += 1
        full, cut = [
            remote(
                source.at[pl.ds(stream[0], last - stream[0])],
                target.at[pl.ds(stream[0], last - stream[0])],
                ssem.at[slot],
                recv,
                zp,
            )
            for last in (stream[1], TRIM[stream])
        ]
        either(big, full.start, cut.start)()
        other = mate_big if big is own_big else own_big
        copy = SimpleNamespace(
            wait_send=either(big, full.wait_send, cut.wait_send),
            wait_recv=either(other, full.wait_recv, cut.wait_recv),
        )
        if keep:
            pending.append(copy)
        return copy

    def wait_bytes(ref, sem):
        pltpu.make_async_copy(ref, ref, sem).wait()

    def arrived(name, *copies):
        with jax.named_scope("wait_" + name):
            for copy in copies:
                copy.wait_recv()

    barrier = pltpu.get_barrier_semaphore()
    peers = [sib, up, down, (d, z2), (d + 1 - 2 * c, z2)] + plane
    for stream in (LANG, VIS):
        first, last = TRIM[stream], stream[1]
        A[:, 2, first:last] = jnp.zeros((6, last - first, D_MODEL), BF)
        RSB[2, first:last] = jnp.zeros((last - first, D_MODEL), BF)
    with jax.named_scope("barrier"):
        for peer in peers:
            pl.semaphore_signal(barrier, inc=1, device_id=peer, device_id_type=MESH)
        pl.semaphore_wait(barrier, len(peers))

    def weight_first(w):
        row = pl.ds(pl.multiple_of(d * SHARE, 16), SHARE)
        slot = counter[0]
        counter[0] += 1
        share = SH.at[w] if w < 3 else (expand.at[w - 3] if w < 5 else contract.at[w - 5])
        near = remote(share, W.at[w, row], ssem.at[slot], wsem_z.at[w], sib)
        own = pltpu.make_async_copy(share, W.at[w, row], wsem_z.at[w])

        @pl.when(c == 1)
        def _():
            near.start()

        @pl.when(c == 0)
        def _():
            own.start()

        send(share, W.at[w, row], far, wsem_z.at[w])
        return near

    def place(width, first):
        row = lax.broadcasted_iota(jnp.int32, (width, D_MODEL), 0)
        column = lax.broadcasted_iota(jnp.int32, (width, D_MODEL), 1)
        return jnp.where(column - row == first, 1.0, 0.0).astype(BF)

    @jax.named_scope("share")
    def attention_share(b):
        SH[b] = (
            dot_nn(projection[b, 0], place(HALF_PAIR, 0))
            + dot_nn(projection[b, 2], place(HALF_PAIR, HALF_PAIR))
            + dot_nn(projection[b, 1], place(HALF_PAIR, 2 * HALF_PAIR))
            + dot_tn(out_weight[b], place(HALF_PAIR, 3 * HALF_PAIR))
        ).astype(BF)

    nears = []
    heads = [
        send(lang.at[pl.ds(0, LANG_HEAD)], HL.at[0], down),
        send(vis.at[pl.ds(0, VIS_HEAD)], HV.at[0], down),
        send(lcot.at[pl.ds(0, LANG_HEAD)], HL.at[1], down),
        send(vcot.at[pl.ds(0, VIS_HEAD)], HV.at[1], down),
    ]
    attention_share(0)
    nears.append(weight_first(0))

    n_items = lengths.shape[0]
    first_item = 3 * z + jnp.minimum(z, 1)
    KV[0] = jnp.full(KV.shape[1:], -1.0, F32)
    for row, source, size in ((0, lengths, WORDS), (1, regions, REGIONS)):
        lane = lax.broadcasted_iota(jnp.int32, (1, TILE), 1)
        owner = jnp.full((1, TILE), -1.0, F32)
        slab_row = lax.broadcasted_iota(jnp.int32, (SLOTS * size, 1), 0)
        flag = jnp.zeros((SLOTS * size, 1), F32)
        for j in range(SLOTS):
            item = jnp.minimum(first_item + j, n_items - 1)
            valid = (lane >= j * size) & (lane < j * size + source[item]) & (lane < (j + 1) * size)
            owner = jnp.where(valid, float(j), owner)
            inside = (slab_row >= j * size) & (slab_row < (j + 1) * size)
            flag = jnp.where(inside, flags[row, item].astype(F32), flag)
        KV[0, row : row + 1] = owner
        FLAG[row * RL : row * RL + SLOTS * size] = flag
        count = flags[row, 0]
        for j in range(1, n_items):
            count = count + flags[row, j]
        CA[0, row : row + 1] = jnp.full((1, 128), count.astype(F32), F32)
    kv_sib = send(KV.at[0], KV.at[1], sib)
    kv_zp = send(KV.at[0], KV.at[2], zp)
    count_copies = [send(CA.at[0], CR.at[0], sib)]
    QO[...] = jnp.zeros_like(QO)
    for b in range(3):
        QO[b : b + 1, 0:HALF_PAIR] = query_value[b, 0:1]
        QO[b : b + 1, HALF_PAIR : 2 * HALF_PAIR] = query_value[b, 1:2]
    QO[3:5] = expand_b[...]
    bias_swap = send(QO, QR, (d, z2))

    pair_rows = pl.ds(pl.multiple_of(k * HALF_PAIR, 16), HALF_PAIR)

    def rows_of_chip(chip, first=0, count=HALF_PAIR):
        return pl.ds(pl.multiple_of(chip * HALF_PAIR + first, 16), count)

    def weight_second(w):
        wait_bytes(W.at[w, pair_rows], wsem_z.at[w])
        for j in range(2):
            send(W.at[w, pair_rows], W.at[w, pair_rows], plane[j], wsem.at[j, w])

    def weight_third(w):
        for j in range(2):
            wait_bytes(W.at[w, pair_rows], wsem.at[j, w])
            half = rows_of_chip(k_flip[j], j * SHARE, SHARE)
            send(W.at[w, half], W.at[w, half], plane[1 - j], wsem.at[2, w])

    def weight_ready(w):
        wait_bytes(W.at[w, pair_rows], wsem.at[2, w])

    off_l = jnp.where(z == 0, 0, 20 - 5 * z)
    off_v = jnp.where(z == 0, 0, 36 - 9 * z)
    n_l = jnp.where(z == 0, 4 * WORDS, 3 * WORDS)
    n_v = jnp.where(z == 0, 4 * REGIONS, 3 * REGIONS)
    own_l = lang.shape[0]
    own_v = vis.shape[0]
    arrived("heads", *heads)

    def gather_start(p, stream):
        rows = pl.ds(stream[0], stream[1] - stream[0])
        return (
            p,
            rows,
            send(A.at[p, 0, rows], A.at[p, 1, rows], sib),
            send_z(A.at[p, 0], A.at[p, 2], stream, own_big),
        )

    def gather_forward(handle):
        p, rows, _, across = handle
        arrived("rows_z", across)
        return send(A.at[p, 2, rows], A.at[p, 3, rows], sib)

    for index, (source_l, source_v) in enumerate([(lang, vis), (lcot, vcot)]):
        slab_l = dot_nn(select_rows((RL, own_l), off_l, 0, n_l).astype(BF), source_l[...]) + dot_nn(
            select_rows((RL, LANG_HEAD), off_l - own_l, 0, n_l).astype(BF), HL[index]
        )
        slab_v = dot_nn(select_rows((RV, own_v), off_v, 0, n_v).astype(BF), source_v[...]) + dot_nn(
            select_rows((RV, VIS_HEAD), off_v - own_v, 0, n_v).astype(BF), HV[index]
        )
        if index == 0:
            A[0, 0, 0:RL] = slab_l.astype(BF)
            A[0, 0, RL:ROWS] = slab_v.astype(BF)
            rows_x = {stream: gather_start(0, stream) for stream in (VIS, LANG)}
        else:
            COT[0:RL] = slab_l.astype(BF)
            COT[RL:ROWS] = slab_v.astype(BF)

    stage_used = {}

    def stage_free(index, stream):
        copy = stage_used.pop((index, stream), None)
        if copy is not None:
            copy.wait_send()

    def partial_nt(g, lhs_ref, stream, w, lanes):
        r0, r1 = stream
        rows = r1 - r0
        stage_free(g, stream)
        for n in range(NT):
            column = slice(n * TILE, (n + 1) * TILE)
            lhs = lhs_ref[2 * g : 2 * g + 2, r0:r1, :]
            lhs = lhs.reshape(2 * rows, lhs.shape[-1])
            out = dot_nt(lhs, W[w, column, lanes])
            target = PART if g == 0 else PZ
            target[r0:r1, column] = out[:rows]
            STG[g, r0:r1, column] = out[rows:].astype(BF)

    def stage_send(index, stream, device):
        rows = pl.ds(stream[0], stream[1] - stream[0])
        copy = send(STG.at[index, rows], RSB.at[index, rows], device, keep=False)
        stage_used[index, stream] = copy
        return copy

    def sums_near(stream):
        return stage_send(0, stream, sib)

    def sums_far(stream):
        return stage_send(1, stream, sib)

    def sums_z(stream, far):
        r0, r1 = stream
        arrived("sums_core", far)
        stage_free(2, stream)
        STG[2, r0:r1] = (PZ[r0:r1] + RSB[1, r0:r1].astype(F32)).astype(BF)
        stage_used[2, stream] = send_z(STG.at[2], RSB.at[2], stream, mate_big, keep=False)
        return stage_used[2, stream]

    def reduced(stream, *copies):
        r0, r1 = stream
        arrived("sums", *copies)
        return PART[r0:r1] + RSB[0, r0:r1].astype(F32) + RSB[2, r0:r1].astype(F32)

    mask_q = head_mask(0, BF)
    mask_c = head_mask(64, BF)
    mask_q32 = head_mask(0, F32)
    mask_c32 = head_mask(64, F32)
    factor = 1.0 / math.sqrt(D_HEAD)

    def attend_slab(QV, Cb, PL, PV, crossed, stream, s):
        def one(q0, q1, k0, k1, words_keys, P):
            nq, nk = q1 - q0, k1 - k0
            query = QV[s, q0:q1, 0:256]
            keys = QV[s, k0:k1, 384:640]
            values = QV[s, k0:k1, 128:384]
            query_size = WORDS if q0 == 0 else REGIONS
            spread = jnp.concatenate([query * mask_q[h] for h in range(3)], 0)
            scores = dot_nt(spread, keys) * factor
            row = lax.broadcasted_iota(jnp.int32, (nq, nk), 0)
            item = jnp.zeros((nq, nk), F32)
            for j in range(1, SLOTS):
                item = item + jnp.where(row >= j * query_size, 1.0, 0.0)
            column = KV[s, 0:1, 0:nk] if words_keys else KV[s, 1:2, 0:nk]
            same = item == column
            scores = jnp.where(same[None], scores.reshape(3, nq, nk), MASKED)
            raised = jnp.exp(scores - jnp.max(scores, -1, keepdims=True))
            weights = (raised / jnp.sum(raised, -1, keepdims=True)).astype(BF).reshape(3 * nq, nk)
            P[s] = weights
            context = dot_nn(weights, values).reshape(3, nq, TILE)
            Cb[s, q0:q1] = (
                context[0] * mask_c32[0] + context[1] * mask_c32[1] + context[2] * mask_c32[2]
            ).astype(BF)

        if stream == LANG:
            if crossed:
                one(0, RL, RL, ROWS, False, PL)
            else:
                one(0, RL, 0, RL, True, PL)
        elif crossed:
            one(RL, ROWS, 0, RL, True, PV)
        else:
            one(RL, ROWS, RL, ROWS, False, PV)

    def attend_back_slab(QV, PL, PV, crossed, streams, s):
        def one(q0, q1, k0, k1, P):
            nq, nk = q1 - q0, k1 - k0
            query = QV[s, q0:q1, 0:256]
            keys = QV[s, k0:k1, 384:640]
            values = QV[s, k0:k1, 128:384]
            spread = jnp.concatenate([query * mask_q[h] for h in range(3)], 0)
            upstream = D[s, q0:q1, 512:768]
            up_spread = jnp.concatenate([upstream * mask_c[h] for h in range(3)], 0)
            weights = P[s]
            weights32 = weights.astype(F32)
            weight_grad = dot_nt(up_spread, values)
            score_grad = (
                weights32
                * (weight_grad - jnp.sum(weight_grad * weights32, -1, keepdims=True))
            ).astype(BF)
            dq = dot_nn(score_grad, keys).reshape(3, nq, TILE)
            dq = (dq[0] * mask_q32[0] + dq[1] * mask_q32[1] + dq[2] * mask_q32[2]) * factor
            dk = dot_tn(score_grad, spread) * factor
            dv = dot_tn(weights, up_spread)
            return dq, dk, dv

        if crossed:
            dq_l, dk_v, dv_v = one(0, RL, RL, ROWS, PL)
            dq_v, dk_l, dv_l = one(RL, ROWS, 0, RL, PV)
            results = {LANG: (dq_l, dk_l, dv_l), VIS: (dq_v, dk_v, dv_v)}
        else:
            results = {stream: one(*stream, *stream, PL if stream == LANG else PV) for stream in streams}
        for (r0, r1), (dq, dk, dv) in results.items():
            D[s, r0:r1, 0:128] = dq[:, :128].astype(BF)
            D[s, r0:r1, 128:256] = (dq[:, 128:] + dv[:, :128]).astype(BF)
            D[s, r0:r1, 256:384] = dv[:, 128:].astype(BF)
            D[s, r0:r1, 384:640] = dk.astype(BF)
            D[s, r0:r1, 640:768] = jnp.zeros((r1 - r0, 128), BF)

    def over_tiles(body):
        for n in range(NT):
            body(slice(n * TILE, (n + 1) * TILE))

    @jax.named_scope("norm")
    def forward_norm(value, index, gain_row, r0, r1):
        center = value - jnp.mean(value, -1, keepdims=True)
        scaled = lax.rsqrt(jnp.mean(center * center, -1, keepdims=True) + EPSILON)
        normed = center * scaled
        NORM[index, r0:r1] = normed
        RSTD[index, r0:r1] = scaled
        return normed * gains[gain_row : gain_row + 1] + shifts[gain_row : gain_row + 1]

    @jax.named_scope("norm_gradient")
    def backward_norm(upstream, index, gain_row, bias_row, r0, r1):
        normed = NORM[index, r0:r1]
        through = upstream * gains[gain_row : gain_row + 1]
        inner = (
            through
            - jnp.mean(through, -1, keepdims=True)
            - normed * jnp.mean(through * normed, -1, keepdims=True)
        )
        result = RSTD[index, r0:r1] * inner
        VG[5 + gain_row : 6 + gain_row] += jnp.sum(upstream * normed, 0, keepdims=True)
        VG[10 + gain_row : 11 + gain_row] += jnp.sum(upstream, 0, keepdims=True)
        VG[bias_row : bias_row + 1] += jnp.sum(result, 0, keepdims=True)
        return result

    def rows_of_group(p, g, stream):
        r0, r1 = stream
        return A[p, 2 * g : 2 * g + 2, r0:r1, :].reshape(2 * (r1 - r0), D_MODEL)

    def project(p, g, stream, w, QV):
        r0, r1 = stream
        for n in range(NT):
            column = slice(n * TILE, (n + 1) * TILE)
            mapped = dot_nn(rows_of_group(p, g, stream), W[w, :, column]) + QB[w : w + 1, column]
            QV[2 * g : 2 * g + 2, r0:r1, column] = mapped.astype(BF).reshape(2, r1 - r0, TILE)

    def attend(g, stream, QV, Cb, PL, PV, crossed):
        for s in (2 * g, 2 * g + 1):
            attend_slab(QV, Cb, PL, PV, crossed, stream, s)

    def expand_rows(g, stream):
        r0, r1 = stream
        rows = r1 - r0
        w = EXPAND[stream]
        for n in range(NT):
            column = slice(n * TILE, (n + 1) * TILE)
            before = dot_nn(rows_of_group(2, g, stream), W[w, :, column]) + QB[w : w + 1, column]
            half = 0.5 * (1.0 + lax.erf(before * math.sqrt(0.5)))
            slope = half + before * jnp.exp(-0.5 * before * before) * (1.0 / math.sqrt(2.0 * math.pi))
            H[2 * g : 2 * g + 2, r0:r1, column] = (before * half).astype(BF).reshape(2, rows, TILE)
            GP[2 * g : 2 * g + 2, r0:r1, column] = slope.astype(BF).reshape(2, rows, TILE)

    def hidden_gradient(g, stream):
        r0, r1 = stream
        rows = r1 - r0
        for n in range(NT):
            column = slice(n * TILE, (n + 1) * TILE)
            up_hidden = dot_nn(rows_of_group(3, g, stream), W[CONTRACT[stream], :, column])
            slope = GP[2 * g : 2 * g + 2, r0:r1, column].reshape(2 * rows, TILE)
            D[2 * g : 2 * g + 2, r0:r1, column] = (
                (up_hidden * slope.astype(F32)).astype(BF).reshape(2, rows, TILE)
            )

    def context_gradient(p, g, stream, w):
        r0, r1 = stream
        upstream = dot_nn(rows_of_group(p, g, stream), W[w, :, 512:768])
        D[2 * g : 2 * g + 2, r0:r1, 512:768] = upstream.astype(BF).reshape(2, r1 - r0, TILE)

    def attend_gradient(g, streams, QV, PL, PV, crossed):
        for s in (2 * g, 2 * g + 1):
            attend_back_slab(QV, PL, PV, crossed, streams, s)

    def all_rows(ref, r0, r1, lanes):
        value = ref[:, r0:r1, lanes]
        return value.reshape(SLOTS * (r1 - r0), value.shape[-1])

    def weight_grad(w, lhs_p, rhs_ref, r0, r1, lanes=slice(0, 768)):
        for m in range(NT):
            column = slice(m * TILE, (m + 1) * TILE)
            left = all_rows(A.at[lhs_p], r0, r1, column)
            G[w, column, lanes] = dot_tn(left, all_rows(rhs_ref, r0, r1, lanes)).astype(BF)

    def attention_weight_grad(w, x_p, b_p, Cb, r0, r1):
        weight_grad(w, x_p, D, r0, r1, slice(0, 512))
        for m in range(NT):
            column = slice(m * TILE, (m + 1) * TILE)
            G[w, column, 512:768] = (
                dot_tn(all_rows(A.at[x_p], r0, r1, column), all_rows(D, r0, r1, slice(512, 768)))
                + dot_tn(all_rows(A.at[b_p], r0, r1, column), all_rows(Cb, r0, r1, slice(0, 256)))
            ).astype(BF)

    def bias_grad(row, r0, r1):
        total = jnp.zeros((1, D_MODEL), F32)
        for s in range(SLOTS):
            total = total + jnp.sum(D[s, r0:r1].astype(F32), 0, keepdims=True)
        QG[row : row + 1] = total

    def grad_first(w):
        for j in range(2):
            half = rows_of_chip(k_flip[2], (1 - j) * SHARE, SHARE)
            send(G.at[w, half], RD.at[j, w], plane[j], gsem.at[2, w])

    def grad_second(w):
        wait_bytes(RD.at[:, w], gsem.at[2, w])
        for j in range(2):
            half = rows_of_chip(k_flip[1 - j], (1 - j) * SHARE, SHARE)
            G[w, half] = (G[w, half].astype(F32) + RD[j, w].astype(F32)).astype(BF)
        for j in range(2):
            send(G.at[w, rows_of_chip(k_flip[j])], RX.at[j, w], plane[j], gsem.at[j, w])

    grad_nears = []

    def grad_third(w):
        for j in range(2):
            wait_bytes(RX.at[j, w], gsem.at[j, w])
        total = G[w, pair_rows].astype(F32) + RX[0, w].astype(F32) + RX[1, w].astype(F32)
        G[w, pair_rows] = total.astype(BF)
        low, high = rows_of_chip(k, 0, SHARE), rows_of_chip(k, SHARE, SHARE)
        slot = counter[0]
        counter[0] += 2
        own = pltpu.make_async_copy(G.at[w, low], R2.at[0, w], gsem2.at[w])
        near = remote(G.at[w, high], R2.at[0, w], ssem.at[slot], gsem2.at[w], sib)
        far_low = remote(G.at[w, low], R2.at[1, w], ssem.at[slot], gsem2.at[w], (2 * k, z2))
        far_high = remote(G.at[w, high], R2.at[1, w], ssem.at[slot + 1], gsem2.at[w], (2 * k + 1, z2))

        @pl.when(c == 0)
        def _():
            own.start()
            near.start()

        @pl.when(c == 1)
        def _():
            far_low.start()
            far_high.start()

        grad_nears.append((near, far_low, far_high))

    def grad_last(w):
        wait_bytes(R2.at[:, w], gsem2.at[w])
        wgrad[w] = R2[0, w].astype(F32) + R2[1, w].astype(F32)

    def count_step(stage, peer):
        count_copies[stage].wait_recv()
        CA[stage + 1] = CA[stage] + CR[stage]
        if peer is not None:
            count_copies.append(send(CA.at[stage + 1], CR.at[stage + 1], peer))

    quarter = jnp.where(c == 0, z, z2)
    vector_peers = [sib, plane[0], plane[1], zp, (d, z2)]
    vector_copies, late_copies = [], []

    def vector_start():
        AVA[0, 0:16] = VG[...]
        for j in range(4):
            AVA[0, 16 + 4 * j : 20 + 4 * j] = jnp.where(quarter == j, QG[1:5], 0.0)
        vector_copies.append(send(AVA.at[0], AVR.at[0], vector_peers[0]))

    def vector_step(stage):
        vector_copies[stage].wait_recv()
        AVA[stage + 1] = AVA[stage] + AVR[stage]
        if stage < 4:
            vector_copies.append(send(AVA.at[stage + 1], AVR.at[stage + 1], vector_peers[stage + 1]))

    def late_start():
        for j in range(4):
            LVA[0, j : j + 1] = jnp.where(quarter == j, QG[0:1], 0.0)
        LVA[0, 4:8] = jnp.zeros((4, D_MODEL), F32)
        late_copies.append(send(LVA.at[0], LVR.at[0], vector_peers[0]))

    def late_step(stage):
        late_copies[stage].wait_recv()
        LVA[stage + 1] = LVA[stage] + LVR[stage]
        if stage < 4:
            late_copies.append(send(LVA.at[stage + 1], LVR.at[stage + 1], vector_peers[stage + 1]))

    VG[...] = jnp.zeros_like(VG)
    QG[...] = jnp.zeros_like(QG)
    cross = (QVK.at[0], C.at[0], PCL, PCV, True)
    inner = (QVK.at[1], C.at[1], PSL, PSV, False)

    weight_second(0)
    attention_share(2)
    nears.append(weight_first(2))
    attention_share(1)
    nears.append(weight_first(1))
    far_x = {stream: gather_forward(rows_x[stream]) for stream in (VIS, LANG)}
    kv_sib.wait_recv()
    kv_zp.wait_recv()
    kv_far = send(KV.at[2], KV.at[3], sib)
    bias_swap.wait_recv()
    QB[...] = jnp.where(c == 1, QR[...], QO[...])
    weight_third(0)
    kv_far.wait_recv()
    arrived("rows", rows_x[VIS][2], rows_x[LANG][2])
    weight_ready(0)

    project(0, 0, BOTH, 0, QVK.at[0])
    weight_second(2)
    nears.append(weight_first(4))
    attend(0, VIS, *cross)
    partial_nt(0, C.at[0], VIS, 0, slice(512, 768))
    near_v = sums_near(VIS)
    weight_second(1)
    nears.append(weight_first(6))
    attend(0, LANG, *cross)
    partial_nt(0, C.at[0], LANG, 0, slice(512, 768))
    near_l = sums_near(LANG)
    arrived("rows", far_x[VIS], far_x[LANG])
    project(0, 1, BOTH, 0, QVK.at[0])
    attend(1, VIS, *cross)
    partial_nt(1, C.at[0], VIS, 0, slice(512, 768))
    far_v = sums_far(VIS)
    attend(1, LANG, *cross)
    z_v = sums_z(VIS, far_v)
    partial_nt(1, C.at[0], LANG, 0, slice(512, 768))
    far_l = sums_far(LANG)
    weight_third(2)
    z_l = sums_z(LANG, far_l)
    count_step(0, plane[0])
    weight_third(1)

    def first_norm(stream, *copies):
        r0, r1 = stream
        value = reduced(stream, *copies) + out_bias[0:1] + A[0, 0, r0:r1].astype(F32)
        A[1, 0, r0:r1] = forward_norm(value, 0, 0, r0, r1).astype(BF)
        return gather_start(1, stream)

    rows_v = first_norm(VIS, near_v, z_v)
    rows_l = first_norm(LANG, near_l, z_l)

    def self_rows(g, stream):
        w = SELF[stream]
        project(1, g, stream, w, QVK.at[1])
        attend(g, stream, *inner)
        partial_nt(g, C.at[1], stream, w, slice(512, 768))

    weight_second(4)
    weight_ready(2)
    arrived("rows", rows_v[2])
    self_rows(0, VIS)
    near_v = sums_near(VIS)
    far_x = gather_forward(rows_v)
    weight_second(6)
    nears.append(weight_first(3))
    weight_ready(1)
    arrived("rows", rows_l[2])
    self_rows(0, LANG)
    near_l = sums_near(LANG)
    far_y = gather_forward(rows_l)
    arrived("rows", far_x)
    self_rows(1, VIS)
    far_v = sums_far(VIS)
    weight_third(4)
    nears.append(weight_first(5))
    arrived("rows", far_y)
    self_rows(1, LANG)
    z_v = sums_z(VIS, far_v)
    far_l = sums_far(LANG)
    count_step(1, plane[1])
    z_l = sums_z(LANG, far_l)
    weight_third(6)

    def second_norm(stream, *copies):
        r0, r1 = stream
        n = 1 if stream == LANG else 2
        value = reduced(stream, *copies) + out_bias[n : n + 1] + A[1, 0, r0:r1].astype(F32)
        A[2, 0, r0:r1] = forward_norm(value, 1, n, r0, r1).astype(BF)
        return gather_start(2, stream)

    rows_v = second_norm(VIS, near_v, z_v)
    rows_l = second_norm(LANG, near_l, z_l)

    weight_second(3)
    weight_ready(4)
    arrived("rows", rows_v[2])
    expand_rows(0, VIS)
    far_x = gather_forward(rows_v)
    weight_second(5)
    arrived("rows", far_x)
    expand_rows(1, VIS)
    far_y = gather_forward(rows_l)
    weight_ready(6)
    partial_nt(1, H, VIS, 6, slice(0, 768))
    far_v = sums_far(VIS)
    weight_third(3)
    partial_nt(0, H, VIS, 6, slice(0, 768))
    near_v = sums_near(VIS)
    z_v = sums_z(VIS, far_v)
    weight_ready(3)
    arrived("rows", rows_l[2], far_y)
    expand_rows(0, LANG)
    expand_rows(1, LANG)
    weight_third(5)
    count_step(2, None)

    def last_norm(stream, *copies):
        r0, r1 = stream
        n = 0 if stream == LANG else 1
        value = reduced(stream, *copies) + contract_b[n : n + 1] + A[2, 0, r0:r1].astype(F32)
        OUTS[r0:r1] = forward_norm(value, 2, 3 + n, r0, r1).astype(BF)
        scale = total_items / CA[3, n : n + 1, 0:1]
        upstream = COT[r0:r1].astype(F32) * (FLAG[r0:r1] * scale)
        result = backward_norm(upstream, 2, 3 + n, 3 + n, r0, r1)
        DZ[r0:r1] = result
        A[3, 0, r0:r1] = result.astype(BF)
        return gather_start(3, stream)

    rows_v = last_norm(VIS, near_v, z_v)
    weight_ready(5)
    partial_nt(1, H, LANG, 5, slice(0, 768))
    far_l = sums_far(LANG)
    partial_nt(0, H, LANG, 5, slice(0, 768))
    near_l = sums_near(LANG)
    z_l = sums_z(LANG, far_l)

    def feed_gradient(g, stream):
        hidden_gradient(g, stream)
        partial_nt(g, D, stream, EXPAND[stream], slice(0, 768))

    arrived("rows", rows_v[2])
    feed_gradient(0, VIS)
    near_v = sums_near(VIS)
    far_x = gather_forward(rows_v)
    rows_l = last_norm(LANG, near_l, z_l)
    arrived("rows", far_x)
    feed_gradient(1, VIS)
    far_v = sums_far(VIS)
    arrived("rows", rows_l[2])
    feed_gradient(0, LANG)
    near_l = sums_near(LANG)
    z_v = sums_z(VIS, far_v)
    far_y = gather_forward(rows_l)
    weight_grad(6, 3, H, *VIS)
    grad_first(6)
    arrived("rows", far_y)
    feed_gradient(1, LANG)
    far_l = sums_far(LANG)
    weight_grad(4, 2, D, *VIS)
    grad_first(4)
    z_l = sums_z(LANG, far_l)
    bias_grad(4, *VIS)

    def second_norm_back(stream, *copies):
        r0, r1 = stream
        n = 1 if stream == LANG else 2
        result = backward_norm(DZ[r0:r1] + reduced(stream, *copies), 1, n, n, r0, r1)
        DZ[r0:r1] = result
        A[4, 0, r0:r1] = result.astype(BF)
        return gather_start(4, stream)

    rows_v = second_norm_back(VIS, near_v, z_v)
    tail_out = [
        send(OUTS.at[pl.ds(RL - LANG_TAIL, LANG_TAIL)], TLO, up),
        send(OUTS.at[pl.ds(ROWS - VIS_TAIL, VIS_TAIL)], TVO, up),
    ]
    weight_grad(5, 3, H, *LANG)
    grad_first(5)
    grad_second(6)
    rows_l = second_norm_back(LANG, near_l, z_l)
    weight_grad(3, 2, D, *LANG)
    grad_first(3)
    bias_grad(3, *LANG)
    grad_second(4)

    def self_gradient(g, stream):
        w = SELF[stream]
        context_gradient(4, g, stream, w)
        attend_gradient(g, (stream,), QVK.at[1], PSL, PSV, False)
        partial_nt(g, D, stream, w, slice(0, 768))

    arrived("rows", rows_v[2])
    self_gradient(0, VIS)
    near_v = sums_near(VIS)
    far_x = gather_forward(rows_v)
    grad_second(5)
    arrived("rows", rows_l[2])
    self_gradient(0, LANG)
    near_l = sums_near(LANG)
    far_y = gather_forward(rows_l)
    arrived("rows", far_x)
    self_gradient(1, VIS)
    far_v = sums_far(VIS)
    grad_second(3)
    arrived("rows", far_y)
    self_gradient(1, LANG)
    z_v = sums_z(VIS, far_v)
    far_l = sums_far(LANG)
    grad_third(6)
    z_l = sums_z(LANG, far_l)
    attention_weight_grad(2, 1, 4, C.at[1], *VIS)
    grad_first(2)
    bias_grad(2, *VIS)
    grad_third(4)

    def first_norm_back(stream, *copies):
        r0, r1 = stream
        result = backward_norm(DZ[r0:r1] + reduced(stream, *copies), 0, 0, 0, r0, r1)
        DZ[r0:r1] = result
        A[5, 0, r0:r1] = result.astype(BF)
        return gather_start(5, stream)

    rows_v = first_norm_back(VIS, near_v, z_v)
    rows_l = first_norm_back(LANG, near_l, z_l)
    attention_weight_grad(1, 1, 4, C.at[1], *LANG)
    grad_first(1)
    bias_grad(1, *LANG)
    grad_third(5)
    grad_second(2)

    vector_start()

    arrived("rows", rows_v[2], rows_l[2])
    for stream in (VIS, LANG):
        context_gradient(5, 0, stream, 0)
    attend_gradient(0, None, QVK.at[0], PCL, PCV, True)
    vector_step(0)
    far_x = gather_forward(rows_v)
    far_y = gather_forward(rows_l)
    for stream in (VIS, LANG):
        partial_nt(0, D, stream, 0, slice(0, 768))
    near_v = sums_near(VIS)
    near_l = sums_near(LANG)
    vector_step(1)
    grad_second(1)
    grad_third(3)
    arrived("rows", far_x, far_y)
    for stream in (VIS, LANG):
        context_gradient(5, 1, stream, 0)
    vector_step(2)
    attend_gradient(1, None, QVK.at[0], PCL, PCV, True)
    attention_weight_grad(0, 0, 5, C.at[0], *BOTH)
    grad_first(0)
    vector_step(3)
    bias_grad(0, *BOTH)
    late_start()
    partial_nt(1, D, VIS, 0, slice(0, 768))
    far_v = sums_far(VIS)
    vector_step(4)
    partial_nt(1, D, LANG, 0, slice(0, 768))
    far_l = sums_far(LANG)
    z_v = sums_z(VIS, far_v)
    z_l = sums_z(LANG, far_l)
    late_step(0)
    grad_second(0)
    grad_third(2)
    late_step(1)
    grad_third(1)
    late_step(2)
    for w in (6, 4, 5, 3):
        grad_last(w)
    grad_third(0)
    late_step(3)
    for stream, copies in ((VIS, (near_v, z_v)), (LANG, (near_l, z_l))):
        r0, r1 = stream
        DZ[r0:r1] = DZ[r0:r1] + reduced(stream, *copies)
    tail_grad = [
        send(DZ.at[pl.ds(RL - LANG_TAIL, LANG_TAIL)], TLG, up),
        send(DZ.at[pl.ds(ROWS - VIS_TAIL, VIS_TAIL)], TVG, up),
    ]
    for w in (2, 1):
        grad_last(w)
    late_step(4)
    vec_out[...] = AVA[5, 0:16]
    for j in range(4):

        @pl.when(z == j)
        def _(j=j):
            qb_out[0:1] = LVA[5, j : j + 1]
            qb_out[1:5] = AVA[5, 16 + 4 * j : 20 + 4 * j]

    arrived("tails", *tail_out, *tail_grad)
    before_l = jnp.where(z == 1, 0, 25 - 5 * z)
    before_v = jnp.where(z == 1, 0, 45 - 9 * z)
    tail_shift_l = own_l - before_l - (RL - LANG_TAIL)
    tail_shift_v = own_v - before_v - (RV - VIS_TAIL)
    for own_rows, off, tail_rows, shift, out_ref, grad_ref, r0, r1, t_out, t_grad in (
        (own_l, off_l, LANG_TAIL, tail_shift_l, lang_out, lang_grad, 0, RL, TLO, TLG),
        (own_v, off_v, VIS_TAIL, tail_shift_v, vis_out, vis_grad, RL, ROWS, TVO, TVG),
    ):
        from_own = select_rows((own_rows, r1 - r0), -off, off, own_rows)
        from_tail = select_rows((own_rows, tail_rows), shift, 0, off)
        out_ref[...] = (
            dot_nn(from_own.astype(BF), OUTS[r0:r1]) + dot_nn(from_tail.astype(BF), t_out[...])
        ).astype(BF)
        exact = lax.Precision.HIGHEST
        grad_ref[...] = jnp.dot(
            from_own, DZ[r0:r1], precision=exact, preferred_element_type=F32
        ) + jnp.dot(from_tail, t_grad[...], precision=exact, preferred_element_type=F32)

    grad_last(0)

    for copy in pending:
        copy.wait_send()
    for index, stream in list(stage_used):
        stage_free(index, stream)

    @pl.when(c == 1)
    def _():
        for copy in nears:
            copy.wait_send()
        for _, far_low, far_high in grad_nears:
            far_low.wait_send()
            far_high.wait_send()

    @pl.when(c == 0)
    def _():
        for near, _, _ in grad_nears:
            near.wait_send()
    assert counter[0] <= ssem.shape[0] and counter[1] <= rsem.shape[0], counter


N_SEND = 192
N_RECV = 112


def fused_layer(total_items, *operands):
    own_l, own_v = operands[0].shape[0], operands[1].shape[0]
    vmem = pl.BlockSpec(memory_space=pltpu.VMEM)
    smem = pl.BlockSpec(memory_space=pltpu.SMEM)
    shapes = [
        ((own_l, D), BF),
        ((own_v, D), BF),
        ((own_l, D), F32),
        ((own_v, D), F32),
        ((7, SHARE, D), F32),
        ((16, D), F32),
        ((8, D), F32),
    ]
    scratch = [
        ((7, D, D), BF),
        ((7, D, D), BF),
        ((2, 7, SHARE, D), BF),
        ((2, 7, HALF_PAIR, D), BF),
        ((2, 7, SHARE, D), BF),
        ((6, SLOTS, ROWS, D), BF),
        ((SLOTS, 8, TILE), F32),
        ((3, ROWS, D), BF),
        ((3, ROWS, D), BF),
        ((2, SLOTS, ROWS, D), BF),
        ((SLOTS, ROWS, D), BF),
        ((2, SLOTS, ROWS, TILE), BF),
        ((SLOTS, ROWS, D), BF),
        ((SLOTS, ROWS, D), BF),
        ((SLOTS, 3 * RL, RV), BF),
        ((SLOTS, 3 * RV, RL), BF),
        ((SLOTS, 3 * RL, RL), BF),
        ((SLOTS, 3 * RV, RV), BF),
        ((ROWS, D), F32),
        ((ROWS, D), F32),
        ((3, ROWS, D), F32),
        ((3, ROWS, 1), F32),
        ((ROWS, D), F32),
        ((ROWS, D), BF),
        ((3, SHARE, D), BF),
        ((ROWS, 1), F32),
        ((8, D), F32),
        ((8, D), F32),
        ((8, D), F32),
        ((4, 8, 128), F32),
        ((3, 8, 128), F32),
        ((16, D), F32),
        ((8, D), F32),
        ((6, N_AR, D), F32),
        ((5, N_AR, D), F32),
        ((6, 8, D), F32),
        ((5, 8, D), F32),
        ((2, LANG_HEAD, D), BF),
        ((2, VIS_HEAD, D), BF),
        ((ROWS, D), BF),
        ((LANG_TAIL, D), BF),
        ((VIS_TAIL, D), BF),
        ((LANG_TAIL, D), F32),
        ((VIS_TAIL, D), F32),
    ]
    dma = pltpu.SemaphoreType.DMA
    return pl.pallas_call(
        partial(layer_kernel, total_items),
        out_shape=[jax.ShapeDtypeStruct(s, t) for s, t in shapes],
        in_specs=[vmem] * 4 + [smem] * 3 + [vmem] * (len(operands) - 7),
        out_specs=[vmem] * len(shapes),
        scratch_shapes=[pltpu.VMEM(s, t) for s, t in scratch]
        + [dma((N_SEND,)), dma((N_RECV,)), dma((3, 7)), dma((7,)), dma((3, 7)), dma((7,)), dma((1,))],
        compiler_params=pltpu.CompilerParams(
            collective_id=0, has_side_effects=True, vmem_limit_bytes=VMEM_LIMIT
        ),
    )(*operands)


def unpack_kernel(lo, vo, lg, vg, wgrad, vec, qb, *outs):
    (lo_out, vo_out, lg_out, vg_out, proj, qv, outw, outb, exp, expb, con, conb, gain, shift) = outs
    lo_out[...] = lo[...]
    vo_out[...] = vo[...]
    lg_out[...] = lg[...]
    vg_out[...] = vg[...]
    width = HALF_PAIR
    for b in range(3):
        for j, lane in enumerate((0, 2 * width, width)):
            proj[b, j] = wgrad[b, :, lane : lane + width]
        outw[b] = wgrad[b, :, 3 * width :].T
        for j in range(2):
            qv[b, j : j + 1] = qb[b : b + 1, j * width : (j + 1) * width]
    for stream in range(2):
        exp[stream] = wgrad[3 + stream]
        con[stream] = wgrad[5 + stream]
    expb[...] = qb[3:5]
    outb[...] = vec[0:3]
    conb[...] = vec[3:5]
    gain[...] = vec[5:10]
    shift[...] = vec[10:15]


def unpack(packed, shapes):
    vmem = pl.BlockSpec(memory_space=pltpu.VMEM)
    return pl.pallas_call(
        unpack_kernel,
        out_shape=shapes,
        in_specs=[vmem] * len(packed),
        out_specs=[vmem] * len(shapes),
        compiler_params=pltpu.CompilerParams(vmem_limit_bytes=VMEM_LIMIT),
    )(*packed)


def on_device_fused(
    language_input,
    vision_input,
    word_lengths,
    region_counts,
    task_flags,
    language_cotangent,
    vision_cotangent,
    projection_weight,
    query_value_bias,
    output_weight,
    output_bias,
    expand_weight,
    expand_bias,
    contract_weight,
    contract_bias,
    norm_gain,
    norm_bias,
):
    packed = fused_layer(
        float(word_lengths.shape[0] * lax.axis_size("dp")),
        language_input,
        vision_input,
        language_cotangent,
        vision_cotangent,
        word_lengths,
        region_counts,
        task_flags.T,
        projection_weight,
        query_value_bias,
        output_weight,
        expand_weight,
        expand_bias,
        contract_weight.transpose(0, 2, 1),
        output_bias,
        contract_bias,
        norm_gain,
        norm_bias,
    )
    like = [
        (language_input, BF),
        (vision_input, BF),
        (language_input, F32),
        (vision_input, F32),
        (projection_weight, F32),
        (query_value_bias, F32),
        (output_weight, F32),
        (output_bias, F32),
        (expand_weight, F32),
        (expand_bias, F32),
        (contract_weight.transpose(0, 2, 1), F32),
        (contract_bias, F32),
        (norm_gain, F32),
        (norm_bias, F32),
    ]
    outs = list(unpack(packed, [jax.ShapeDtypeStruct(a.shape, t) for a, t in like]))
    outs[10] = outs[10].transpose(0, 2, 1)
    return tuple(outs)


def solution(mesh):
    in_specs = (
        P(("dp", "mp"), None),
        P(("dp", "mp"), None),
        P("dp"),
        P("dp"),
        P("dp", None),
        P(("dp", "mp"), None),
        P(("dp", "mp"), None),
        P(None, None, "dp", "mp"),
        P(None, None, "mp"),
        P(None, "mp", "dp"),
        P(),
        P(None, "dp", "mp"),
        P(None, "mp"),
        P(None, "mp", "dp"),
        P(),
        P(),
        P(),
    )
    out_specs = (
        P(("dp", "mp"), None),
        P(("dp", "mp"), None),
        P(("dp", "mp"), None),
        P(("dp", "mp"), None),
        P(None, None, "dp", "mp"),
        P(None, None, "mp"),
        P(None, "mp", "dp"),
        P(),
        P(None, "dp", "mp"),
        P(None, "mp"),
        P(None, "mp", "dp"),
        P(),
        P(),
        P(),
    )
    fused = dict(mesh.shape) == {"dp": 8, "mp": 4}
    return jax.shard_map(
        on_device_fused if fused else on_device, mesh=mesh, in_specs=in_specs, out_specs=out_specs, check_vma=False
    )
```
